32 devices in a mesh: fsdp: 4 (over z), ctx: 2 (over x), tp: 4 (over y, core).
Axes of the slice: x: 2, y: 2, z: 4, core: 2. Of those that a mesh axis runs over, the one named last changes fastest.
Arguments:
- tokens: bfloat16 [4, 2048, 1536], P('fsdp', 'ctx'), may hold values from -6 to 6
- prefix_len: int32 [4], P('fsdp'), may hold values from 204 to 1024
- positions: int32 [4, 2048], P('fsdp', 'ctx'), may hold values from 0 to 3071, as said below
- gain_attend: bfloat16 [1536], P('fsdp'), may hold values from 0.5 to 1.5
- w_query: bfloat16 [1536, 1536], P('fsdp', 'tp'), may hold values from -0.15625 to 0.15625
- w_key: bfloat16 [1536, 768], P('fsdp', 'tp'), may hold values from -0.15625 to 0.15625
- w_value: bfloat16 [1536, 768], P('fsdp', 'tp'), may hold values from -0.15625 to 0.15625
- w_project: bfloat16 [1536, 1536], P('tp', 'fsdp'), may hold values from -2.5 to 2.5
- gain_feed: bfloat16 [1536], P('fsdp'), may hold values from 0.5 to 1.5
- w_gate: bfloat16 [1536, 4096], P('fsdp', 'tp'), may hold values from -0.15625 to 0.15625
- w_up: bfloat16 [1536, 4096], P('fsdp', 'tp'), may hold values from -0.15625 to 0.15625
- w_down: bfloat16 [4096, 1536], P('tp', 'fsdp'), may hold values from -0.09375 to 0.09375
- cotangent: bfloat16 [4, 2048, 1536], P('fsdp', 'ctx'), may hold values from -6 to 6
Outputs:
- layer_output: bfloat16 [4, 2048, 1536], P('fsdp', 'ctx')
- tokens_grad: bfloat16 [4, 2048, 1536], P('fsdp', 'ctx')
- attend_grad: float32 [1536], P('fsdp')
- query_grad: float32 [1536, 1536], P('fsdp', 'tp')
- key_grad: float32 [1536, 768], P('fsdp', 'tp')
- value_grad: float32 [1536, 768], P('fsdp', 'tp')
- project_grad: float32 [1536, 1536], P('tp', 'fsdp')
- feed_grad: float32 [1536], P('fsdp')
- gate_grad: float32 [1536, 4096], P('fsdp', 'tp')
- up_grad: float32 [1536, 4096], P('fsdp', 'tp')
- down_grad: float32 [4096, 1536], P('tp', 'fsdp')
The draws below stay inside these ranges and needn't reach their ends.
Inputs may be any that keep to these rules, and one draw needn't show every extreme that they name: Within each sequence, taken in token order, the positions start at 0 and rise by 1 or 2 from one token to the next, by 2 at exactly 1024 of the steps.
All inputs are finite; a program needn't handle non-finite values.
Results may differ from the reference program's by a relative error of at most 0.023.
Values may be sent and summed in bfloat16 or wider, within the bound.
A program may use at most 192 MiB of HBM per device.

```python
from functools import partial
import jax
import jax.numpy as jnp
from jax import lax

D = 1536
HQ = 16
KVH = 8
HD = 96
FF = 4096
SEQ = 2048
SEQS = 4
QW = 1536
KW = 768
BLK = 512
N_CTX = 2


def draw_positions(key, part):
    key = jax.random.fold_in(key, 11)
    seq_keys = jax.random.split(key, SEQS)

    def one_sequence(seq_key):
        shuffled = jax.random.permutation(seq_key, SEQ - 1)
        strides = 1 + (shuffled < SEQ // 2).astype(jnp.int32)
        natural = jnp.concatenate([jnp.zeros((1,), jnp.int32), jnp.cumsum(strides).astype(jnp.int32)])
        blocks = natural.reshape(2 * N_CTX, BLK)
        return jnp.stack([blocks[:N_CTX], blocks[N_CTX:][::-1]], axis=1).reshape(SEQ)
    return jax.vmap(one_sequence)(seq_keys)


def plant(entries, own_key, least, largest):
    spot = [jax.random.randint(jax.random.fold_in(own_key, axis), (), 0, length) for axis, length in enumerate(entries.shape)]
    main_axis = entries.shape.index(max(entries.shape))
    neighbour = spot[:main_axis] + [(spot[main_axis] + 1) % entries.shape[main_axis]] + spot[main_axis + 1:]
    return entries.at[tuple(spot)].set(least).at[tuple(neighbour)].set(largest)


def block_levels(rng, shape, cuts, least, largest):
    level = 1.0
    for position, blocks in cuts:
        draws = jax.random.uniform(jax.random.fold_in(jax.random.fold_in(rng, 6), position), (blocks,), jnp.float32, least / len(cuts), largest / len(cuts))
        level = level * jnp.repeat(jnp.exp(draws), shape[position] // blocks).reshape((-1,) + (1,) * (len(shape) - 1 - position))
    return level


def noise(stream_key, extent, spread, most, cuts=(), held_as=jnp.bfloat16):
    loudness = block_levels(stream_key, extent, cuts, -0.22, 0.18) if cuts else 1.0
    values = jax.random.normal(stream_key, extent, jnp.float32) * spread * loudness
    return jnp.minimum(jnp.maximum(values, -most), most).astype(held_as)


def setup_inputs(seed: int = 0) -> dict:
    streams_of = jax.random.split(jax.random.key(seed), 14)
    return {
        "tokens": noise(streams_of[0], (SEQS, SEQ, D), 1.0, 6.0, ((0, 4), (1, 2))),
        "prefix_len": plant(jax.random.randint(streams_of[1], (SEQS,), SEQ // 10, SEQ // 2 + 1), jax.random.fold_in(streams_of[1], 1), SEQ // 10, (SEQ // 2 + 1) - 1).astype(jnp.int32),
        "positions": draw_positions(jax.random.fold_in(streams_of[13], 71), 0),
        "gain_attend": jnp.clip(1.0 + 0.1 * jax.random.normal(streams_of[3], (D,), jnp.float32), 0.5, 1.5).astype(jnp.bfloat16),
        "w_query": noise(streams_of[4], (D, QW), D ** -0.5, 0.15625, ((0, 4), (1, 4))),
        "w_key": noise(streams_of[5], (D, KW), D ** -0.5, 0.15625, ((0, 4), (1, 4))),
        "w_value": noise(streams_of[6], (D, KW), D ** -0.5, 0.15625, ((0, 4), (1, 4))),
        "w_project": noise(streams_of[7], (QW, D), (max(QW // 256, 1)) ** -0.5, 2.5, ((0, 4), (1, 4))),
        "gain_feed": jnp.clip(1.0 + 0.1 * jax.random.normal(streams_of[8], (D,), jnp.float32), 0.5, 1.5).astype(jnp.bfloat16),
        "w_gate": noise(streams_of[9], (D, FF), D ** -0.5, 0.15625, ((0, 4), (1, 4))),
        "w_up": noise(streams_of[10], (D, FF), D ** -0.5, 0.15625, ((0, 4), (1, 4))),
        "w_down": noise(streams_of[11], (FF, D), FF ** -0.5, 0.09375, ((0, 4), (1, 4))),
        "cotangent": noise(streams_of[12], (SEQS, SEQ, D), 1.0, 6.0, ((0, 4), (1, 2))),
    }


EPSILON = 1e-05
ROPE_BASE = 100000.0
NEGATIVE = -1e+30

@jax.custom_vjp
def low(v):
    return lax.optimization_barrier(v.astype(jnp.bfloat16)).astype(jnp.float32)

@jax.custom_vjp
def low_back(v):
    return v

def low_keep(v):
    return (low(v), None)

def low_pass(kept, grad):
    return (grad,)

def back_keep(v):
    return (v, None)

def back_low(kept, grad):
    return (low(grad),)
low.defvjp(low_keep, low_pass)
low_back.defvjp(back_keep, back_low)

def matmul(left_side, right_side):
    return jnp.dot(left_side, right_side, precision=lax.Precision.HIGHEST, preferred_element_type=jnp.float32)

def rms_norm(values, gain_row):
    return values * lax.rsqrt(lax.optimization_barrier(jnp.mean(values * values, axis=-1, keepdims=True)) + EPSILON) * gain_row

def rotate(values, cosine_table, sine_table):
    half_width = values.shape[-1] // 2
    leading = values[..., :half_width]
    trailing = values[..., half_width:]
    return jnp.concatenate([leading * cosine_table - trailing * sine_table, trailing * cosine_table + leading * sine_table], axis=-1)

def to_natural(stored):
    paired = stored.reshape((N_CTX, 2, BLK) + stored.shape[1:])
    return jnp.concatenate([paired[:, 0], paired[::-1, 1]], axis=0).reshape(stored.shape)

def to_storage(natural):
    blocks = natural.reshape((2 * N_CTX, BLK) + natural.shape[1:])
    return jnp.stack([blocks[:N_CTX], blocks[N_CTX:][::-1]], axis=1).reshape(natural.shape)

def attend(queries, keys_rot, values_low, prefix):
    group_size = HQ // KVH
    keys_all = jnp.repeat(keys_rot, group_size, axis=1)
    values_all = jnp.repeat(values_low, group_size, axis=1)
    block_rows = min(512, SEQ)
    score_scale = HD ** (-0.5)
    key_order = jnp.arange(SEQ, dtype=jnp.int32)

    def one_block(query_rows, block_start):
        scores = jnp.einsum('qhd,khd->hqk', query_rows, keys_all, precision=lax.Precision.HIGHEST) * score_scale
        scores = low_back(scores)
        query_order = block_start + jnp.arange(block_rows, dtype=jnp.int32)
        visible = (key_order[None, :] <= query_order[:, None]) | (key_order[None, :] < prefix)
        scores = jnp.where(visible[None], scores, NEGATIVE)
        weights_low = low(jax.nn.softmax(scores, axis=-1))
        return jnp.einsum('hqk,khd->qhd', weights_low, values_all, precision=lax.Precision.HIGHEST)
    blocked = queries.reshape(SEQ // block_rows, block_rows, HQ, HD)
    starts = (jnp.arange(SEQ // block_rows, dtype=jnp.int32) * block_rows).astype(jnp.int32)
    outputs = lax.map(lambda item_pair: jax.checkpoint(one_block)(item_pair[0], item_pair[1]), (blocked, starts))
    return outputs.reshape(SEQ, HQ * HD)

def layer(inputs, gain_attend, w_query, w_key, w_value, w_project, gain_feed, w_gate, w_up, w_down, cosine_table, sine_table, prefix):
    normed_hidden = low(rms_norm(inputs, gain_attend))
    queries = low(rotate(low_back(matmul(normed_hidden, w_query).reshape(SEQ, HQ, HD)), cosine_table, sine_table))
    keys_rot = low(rotate(low_back(matmul(normed_hidden, w_key).reshape(SEQ, KVH, HD)), cosine_table, sine_table))
    values_low = low(low_back(matmul(normed_hidden, w_value).reshape(SEQ, KVH, HD)))
    attended = low(low_back(attend(queries, keys_rot, values_low, prefix)))
    middle = inputs + low_back(matmul(attended, w_project))
    normed_feed_input = low(rms_norm(middle, gain_feed))
    gate_activation = low_back(matmul(normed_feed_input, w_gate))
    up_activation = low_back(matmul(normed_feed_input, w_up))
    hidden_state = low(jax.nn.silu(gate_activation) * up_activation)
    return middle + low_back(matmul(hidden_state, w_down))

def reference(tokens, prefix_len, positions, gain_attend, w_query, w_key, w_value, w_project, gain_feed, w_gate, w_up, w_down, cotangent):
    weights = tuple((weight_arg.astype(jnp.float32) for weight_arg in (gain_attend, w_query, w_key, w_value, w_project, gain_feed, w_gate, w_up, w_down)))
    frequency = ROPE_BASE ** (-(jnp.arange(HD // 2, dtype=jnp.float32) * 2.0 / HD))

    def per_sequence(totals, seq_items):
        seq_tokens, seq_prefix, seq_pos, seq_cot = seq_items
        inputs = to_natural(seq_tokens.astype(jnp.float32))
        angles = to_natural(seq_pos).astype(jnp.float32)[:, None] * frequency[None, :]
        cosine_table = jnp.cos(angles)[:, None, :]
        sine_table = jnp.sin(angles)[:, None, :]
        forward_fn = partial(layer, cosine_table=cosine_table, sine_table=sine_table, prefix=seq_prefix)
        output, pullback = jax.vjp(forward_fn, inputs, *weights)
        gradients = pullback(to_natural(seq_cot.astype(jnp.float32)))
        totals = jax.tree.map(jnp.add, totals, tuple(gradients[1:]))
        return (totals, (to_storage(output).astype(jnp.bfloat16), to_storage(gradients[0]).astype(jnp.bfloat16)))
    initial = tuple((jnp.zeros_like(weight_arg) for weight_arg in weights))
    totals, outputs = lax.scan(per_sequence, initial, (tokens, prefix_len, positions, cotangent))
    return (outputs[0], outputs[1], totals[0], totals[1], totals[2], totals[3], totals[4], totals[5], totals[6], totals[7], totals[8])
```

```python
import math

import jax
import jax.numpy as jnp
from jax import lax
from jax.experimental import pallas as pl
from jax.experimental.pallas import tpu as pltpu
from jax.sharding import PartitionSpec as P

HQ = 16
KVH = 8
HD = 96


EPSILON = 1e-05
ROPE_BASE = 100000.0
NEGATIVE = -1e30


def natural_index(stored, block_len, pair_count):
    device = stored // (2 * block_len)
    second_half = stored // block_len % 2
    within = stored % block_len
    block_id = jnp.where(second_half == 0, device, 2 * pair_count - 1 - device)
    return block_id * block_len + within


def rotate(values, cosine_table, sine_table):
    half_width = values.shape[-1] // 2
    leading = values[..., :half_width]
    trailing = values[..., half_width:]
    return jnp.concatenate(
        [
            leading * cosine_table - trailing * sine_table,
            trailing * cosine_table + leading * sine_table,
        ],
        axis=-1,
    )


def rotate_back(incoming, cosine_table, sine_table):
    half_width = incoming.shape[-1] // 2
    leading = incoming[..., :half_width]
    trailing = incoming[..., half_width:]
    return jnp.concatenate(
        [
            leading * cosine_table + trailing * sine_table,
            trailing * cosine_table - leading * sine_table,
        ],
        axis=-1,
    )


def rms_factor(values):
    return lax.rsqrt(jnp.mean(values * values, axis=-1, keepdims=True) + EPSILON)


def rms_back(values, factor, gain_row, incoming):
    scaled = gain_row * incoming
    return factor * scaled - values * factor**3 * jnp.mean(scaled * values, axis=-1, keepdims=True)


def tensor_sum(term_rows):
    return lax.psum(term_rows.astype(jnp.bfloat16), "tp").astype(jnp.float32)


def general_body(
    tokens,
    prefix_len,
    positions,
    gain_attend,
    w_query,
    w_key,
    w_value,
    w_project,
    gain_feed,
    w_gate,
    w_up,
    w_down,
    cotangent,
):
    (
        gain_one,
        query_weight_whole,
        key_weight_whole,
        value_weight_whole,
        project_weight_whole,
        gain_two,
        gate_weight_whole,
        up_weight_whole,
        down_weight_whole,
    ) = (
        lax.all_gather(gain_attend, "fsdp", axis=0, tiled=True),
        lax.all_gather(w_query, "fsdp", axis=0, tiled=True),
        lax.all_gather(w_key, "fsdp", axis=0, tiled=True),
        lax.all_gather(w_value, "fsdp", axis=0, tiled=True),
        lax.all_gather(w_project, "fsdp", axis=1, tiled=True),
        lax.all_gather(gain_feed, "fsdp", axis=0, tiled=True),
        lax.all_gather(w_gate, "fsdp", axis=0, tiled=True),
        lax.all_gather(w_up, "fsdp", axis=0, tiled=True),
        lax.all_gather(w_down, "fsdp", axis=1, tiled=True),
    )
    seq_count, rows_local, _ = tokens.shape
    pair_count = lax.axis_size("ctx")
    block_len = rows_local // 2
    query_width = query_weight_whole.shape[1]
    kv_width = key_weight_whole.shape[1]
    query_heads = query_width // HD
    kv_heads = kv_width // HD
    group_size = HQ // KVH
    score_scale = HD ** (-0.5)
    frequency = ROPE_BASE ** (-(jnp.arange(HD // 2, dtype=jnp.float32) * 2.0 / HD))
    angles = positions.astype(jnp.float32)[:, :, None] * frequency
    cosine_table = jnp.cos(angles)[:, :, None, :]
    sine_table = jnp.sin(angles)[:, :, None, :]
    stored_rows = lax.axis_index("ctx") * rows_local + jnp.arange(rows_local, dtype=jnp.int32)
    query_order = natural_index(stored_rows, block_len, pair_count)

    def visible_mask(key_order):
        causal = key_order[None, None, :] <= query_order[None, :, None]
        opened = key_order[None, None, :] < prefix_len[:, None, None]
        return (causal | opened)[:, :, None, None, :]

    inputs = tokens.astype(jnp.float32)
    factor_one = rms_factor(inputs)
    normed_hidden = (inputs * factor_one * gain_one.astype(jnp.float32)).astype(jnp.bfloat16)
    query_projected = jnp.einsum(
        "rxc,cf->rxf", normed_hidden, query_weight_whole, preferred_element_type=jnp.float32
    )
    key_projected = jnp.einsum(
        "rxc,cf->rxf", normed_hidden, key_weight_whole, preferred_element_type=jnp.float32
    )
    value_projected = jnp.einsum(
        "rxc,cf->rxf", normed_hidden, value_weight_whole, preferred_element_type=jnp.float32
    )
    queries = (
        rotate(
            query_projected.reshape(seq_count, rows_local, query_heads, HD),
            cosine_table,
            sine_table,
        )
        .astype(jnp.bfloat16)
        .reshape(seq_count, rows_local, kv_heads, group_size, HD)
    )
    keys_rot = (
        rotate(key_projected.reshape(seq_count, rows_local, kv_heads, HD), cosine_table, sine_table)
        .astype(jnp.bfloat16)
        .reshape(seq_count, rows_local, kv_width)
    )
    values_low = value_projected.astype(jnp.bfloat16)
    stat_shape = (seq_count, rows_local, kv_heads, group_size)
    initial = (
        jnp.full(stat_shape, NEGATIVE, jnp.float32),
        jnp.zeros(stat_shape, jnp.float32),
        jnp.zeros(stat_shape + (HD,), jnp.float32),
    )
    key_piece = lax.all_gather(keys_rot, "ctx", axis=1, tiled=True)
    value_piece = lax.all_gather(values_low, "ctx", axis=1, tiled=True)
    key_total = key_piece.shape[1]
    span_rows = math.gcd(key_total, rows_local)

    def one_span(span_index, running):
        run_max, run_sum, run_acc = running
        span_start = span_index * span_rows
        key_rows = lax.dynamic_slice_in_dim(key_piece, span_start, span_rows, 1).reshape(
            seq_count, span_rows, kv_heads, HD
        )
        value_rows = lax.dynamic_slice_in_dim(value_piece, span_start, span_rows, 1).reshape(
            seq_count, span_rows, kv_heads, HD
        )
        key_order = natural_index(
            span_start + jnp.arange(span_rows, dtype=jnp.int32), block_len, pair_count
        )
        visible = visible_mask(key_order)
        scores = (
            jnp.einsum("slhgd,skhd->slhgk", queries, key_rows, preferred_element_type=jnp.float32)
            * score_scale
        )
        new_max = jnp.maximum(run_max, jnp.max(jnp.where(visible, scores, NEGATIVE), axis=-1))
        weights_raw = jnp.where(visible, jnp.exp(scores - new_max[..., None]), 0.0)
        rescale = jnp.exp(run_max - new_max)
        run_sum = run_sum * rescale + jnp.sum(weights_raw, axis=-1)
        run_acc = run_acc * rescale[..., None] + jnp.einsum(
            "slhgk,skhd->slhgd",
            weights_raw.astype(jnp.bfloat16),
            value_rows,
            preferred_element_type=jnp.float32,
        )
        return (new_max, run_sum, run_acc)

    run_max, run_sum, run_acc = lax.fori_loop(0, key_total // span_rows, one_span, initial)
    attended = run_acc / run_sum[..., None]
    log_total = run_max + jnp.log(run_sum)
    attended_reduced = attended.reshape(seq_count, rows_local, query_width).astype(jnp.bfloat16)
    project_rows = jnp.einsum(
        "hxz,zm->hxm", attended_reduced, project_weight_whole, preferred_element_type=jnp.float32
    )
    middle = inputs + tensor_sum(project_rows)
    factor_two = rms_factor(middle)
    normed_feed_input = (middle * factor_two * gain_two.astype(jnp.float32)).astype(jnp.bfloat16)
    gate_activation = jnp.einsum(
        "qeh,hj->qej", normed_feed_input, gate_weight_whole, preferred_element_type=jnp.float32
    )
    up_activation = jnp.einsum(
        "qeh,hj->qej", normed_feed_input, up_weight_whole, preferred_element_type=jnp.float32
    )
    sigmoid_gate = jax.nn.sigmoid(gate_activation)
    silu_gate = gate_activation * sigmoid_gate
    hidden_state = (silu_gate * up_activation).astype(jnp.bfloat16)
    down_output_rows = jnp.einsum(
        "nct,tm->ncm", hidden_state, down_weight_whole, preferred_element_type=jnp.float32
    )
    layer_output = (middle + tensor_sum(down_output_rows)).astype(jnp.bfloat16)
    (
        gain_one,
        query_weight_whole,
        key_weight_whole,
        value_weight_whole,
        project_weight_whole,
        gain_two,
        gate_weight_whole,
        up_weight_whole,
        down_weight_whole,
    ) = (
        lax.all_gather(gain_attend, "fsdp", axis=0, tiled=True),
        lax.all_gather(w_query, "fsdp", axis=0, tiled=True),
        lax.all_gather(w_key, "fsdp", axis=0, tiled=True),
        lax.all_gather(w_value, "fsdp", axis=0, tiled=True),
        lax.all_gather(w_project, "fsdp", axis=1, tiled=True),
        lax.all_gather(gain_feed, "fsdp", axis=0, tiled=True),
        lax.all_gather(w_gate, "fsdp", axis=0, tiled=True),
        lax.all_gather(w_up, "fsdp", axis=0, tiled=True),
        lax.all_gather(w_down, "fsdp", axis=1, tiled=True),
    )
    hidden_grad = jnp.einsum(
        "ehv,iv->ehi", cotangent, down_weight_whole, preferred_element_type=jnp.float32
    )
    down_weight_part = jnp.einsum(
        "gqa,gqz->az", hidden_state, cotangent, preferred_element_type=jnp.float32
    )
    gate_reduced = (
        hidden_grad * up_activation * sigmoid_gate * (1.0 + gate_activation * (1.0 - sigmoid_gate))
    ).astype(jnp.bfloat16)
    up_reduced = (hidden_grad * silu_gate).astype(jnp.bfloat16)
    gate_weight_part = jnp.einsum(
        "bic,big->cg", normed_feed_input, gate_reduced, preferred_element_type=jnp.float32
    )
    up_weight_part = jnp.einsum(
        "bic,big->cg", normed_feed_input, up_reduced, preferred_element_type=jnp.float32
    )
    feed_rows = jnp.einsum(
        "vte,ce->vtc", gate_reduced, gate_weight_whole, preferred_element_type=jnp.float32
    ) + jnp.einsum("vte,ce->vtc", up_reduced, up_weight_whole, preferred_element_type=jnp.float32)
    feed_in = tensor_sum(feed_rows)
    gain_two_term = jnp.sum(feed_in * middle * factor_two, axis=(0, 1))
    middle_grad = cotangent.astype(jnp.float32) + rms_back(
        middle, factor_two, gain_two.astype(jnp.float32), feed_in
    )
    middle_reduced = middle_grad.astype(jnp.bfloat16)
    project_term = jnp.einsum(
        "xeh,xec->hc", attended_reduced, middle_reduced, preferred_element_type=jnp.float32
    )
    attended_grad = (
        jnp.einsum(
            "vhk,nk->vhn", middle_reduced, project_weight_whole, preferred_element_type=jnp.float32
        )
        .astype(jnp.bfloat16)
        .reshape(seq_count, rows_local, kv_heads, group_size, HD)
    )
    row_delta = jnp.sum(attended_grad.astype(jnp.float32) * attended, axis=-1)
    whole_keys, whole_values = (
        lax.all_gather(keys_rot[None], "ctx", axis=0, tiled=True),
        lax.all_gather(values_low[None], "ctx", axis=0, tiled=True),
    )

    def key_block(grad_acc, block_items):
        key_rows, value_rows, block_index = block_items
        key_rows = key_rows.reshape(seq_count, rows_local, kv_heads, HD)
        value_rows = value_rows.reshape(seq_count, rows_local, kv_heads, HD)
        key_order = natural_index(
            block_index * rows_local + jnp.arange(rows_local, dtype=jnp.int32),
            block_len,
            pair_count,
        )
        visible = visible_mask(key_order)
        scores = (
            jnp.einsum("slhgd,skhd->slhgk", queries, key_rows, preferred_element_type=jnp.float32)
            * score_scale
        )
        weights_norm = jnp.where(visible, jnp.exp(scores - log_total[..., None]), 0.0)
        prob_grad = jnp.einsum(
            "slhgd,skhd->slhgk", attended_grad, value_rows, preferred_element_type=jnp.float32
        )
        score_grad = (weights_norm * (prob_grad - row_delta[..., None])).astype(jnp.bfloat16)
        grad_acc = (
            grad_acc
            + jnp.einsum(
                "slhgk,skhd->slhgd", score_grad, key_rows, preferred_element_type=jnp.float32
            )
            * score_scale
        )
        key_grad = (
            jnp.einsum("slhgk,slhgd->skhd", score_grad, queries, preferred_element_type=jnp.float32)
            * score_scale
        )
        value_grad = jnp.einsum(
            "slhgk,slhgd->skhd",
            weights_norm.astype(jnp.bfloat16),
            attended_grad,
            preferred_element_type=jnp.float32,
        )
        return (
            grad_acc,
            (
                key_grad.reshape(seq_count, rows_local, kv_width),
                value_grad.reshape(seq_count, rows_local, kv_width),
            ),
        )

    block_ids = jnp.arange(pair_count, dtype=jnp.int32)
    query_grad, (key_terms, value_terms) = lax.scan(
        key_block, jnp.zeros(stat_shape + (HD,), jnp.float32), (whole_keys, whole_values, block_ids)
    )
    key_sum, value_sum = (
        lax.psum_scatter(
            key_terms.astype(jnp.bfloat16), "ctx", scatter_dimension=0, tiled=True
        ).astype(jnp.float32),
        lax.psum_scatter(
            value_terms.astype(jnp.bfloat16), "ctx", scatter_dimension=0, tiled=True
        ).astype(jnp.float32),
    )
    key_reduced = (
        rotate_back(
            key_sum[0].reshape(seq_count, rows_local, kv_heads, HD), cosine_table, sine_table
        )
        .astype(jnp.bfloat16)
        .reshape(seq_count, rows_local, kv_width)
    )
    value_backward = value_sum[0].astype(jnp.bfloat16)
    query_reduced = (
        rotate_back(
            query_grad.reshape(seq_count, rows_local, query_heads, HD), cosine_table, sine_table
        )
        .astype(jnp.bfloat16)
        .reshape(seq_count, rows_local, query_width)
    )
    query_weight_part = jnp.einsum(
        "prb,pro->bo", normed_hidden, query_reduced, preferred_element_type=jnp.float32
    )
    key_weight_part = jnp.einsum(
        "prb,pro->bo", normed_hidden, key_reduced, preferred_element_type=jnp.float32
    )
    value_weight_part = jnp.einsum(
        "prb,pro->bo", normed_hidden, value_backward, preferred_element_type=jnp.float32
    )
    normed_rows = (
        jnp.einsum(
            "kjw,iw->kji", query_reduced, query_weight_whole, preferred_element_type=jnp.float32
        )
        + jnp.einsum(
            "kjw,iw->kji", key_reduced, key_weight_whole, preferred_element_type=jnp.float32
        )
        + jnp.einsum(
            "kjw,iw->kji", value_backward, value_weight_whole, preferred_element_type=jnp.float32
        )
    )
    normed_grad = tensor_sum(normed_rows)
    gain_one_term = jnp.sum(normed_grad * inputs * factor_one, axis=(0, 1))
    tokens_grad = (
        middle_grad + rms_back(inputs, factor_one, gain_one.astype(jnp.float32), normed_grad)
    ).astype(jnp.bfloat16)
    (
        part_one,
        part_query,
        part_key,
        part_value,
        part_project,
        part_two,
        part_gate,
        part_up,
        part_down,
    ) = (
        lax.psum_scatter(gain_one_term, ("fsdp", "ctx"), scatter_dimension=0, tiled=True),
        lax.psum_scatter(query_weight_part, ("fsdp", "ctx"), scatter_dimension=0, tiled=True),
        lax.psum_scatter(key_weight_part, ("fsdp", "ctx"), scatter_dimension=0, tiled=True),
        lax.psum_scatter(value_weight_part, ("fsdp", "ctx"), scatter_dimension=0, tiled=True),
        lax.psum_scatter(project_term, ("fsdp", "ctx"), scatter_dimension=1, tiled=True),
        lax.psum_scatter(gain_two_term, ("fsdp", "ctx"), scatter_dimension=0, tiled=True),
        lax.psum_scatter(gate_weight_part, ("fsdp", "ctx"), scatter_dimension=0, tiled=True),
        lax.psum_scatter(up_weight_part, ("fsdp", "ctx"), scatter_dimension=0, tiled=True),
        lax.psum_scatter(down_weight_part, ("fsdp", "ctx"), scatter_dimension=1, tiled=True),
    )
    reduced = (
        lax.all_gather(part_one.astype(jnp.bfloat16), "ctx", axis=0, tiled=True).astype(
            part_one.dtype
        ),
        lax.all_gather(part_query.astype(jnp.bfloat16), "ctx", axis=0, tiled=True).astype(
            part_query.dtype
        ),
        lax.all_gather(part_key.astype(jnp.bfloat16), "ctx", axis=0, tiled=True).astype(
            part_key.dtype
        ),
        lax.all_gather(part_value.astype(jnp.bfloat16), "ctx", axis=0, tiled=True).astype(
            part_value.dtype
        ),
        lax.all_gather(part_project.astype(jnp.bfloat16), "ctx", axis=1, tiled=True).astype(
            part_project.dtype
        ),
        lax.all_gather(part_two.astype(jnp.bfloat16), "ctx", axis=0, tiled=True).astype(
            part_two.dtype
        ),
        lax.all_gather(part_gate.astype(jnp.bfloat16), "ctx", axis=0, tiled=True).astype(
            part_gate.dtype
        ),
        lax.all_gather(part_up.astype(jnp.bfloat16), "ctx", axis=0, tiled=True).astype(
            part_up.dtype
        ),
        lax.all_gather(part_down.astype(jnp.bfloat16), "ctx", axis=1, tiled=True).astype(
            part_down.dtype
        ),
    )
    return (layer_output, tokens_grad) + tuple(reduced)


LANES = 128
HALF = HD // 2
SPAN = LANES // 2
LOG2E = math.log2(math.e)
VMEM_BYTES = 56 * 1024 * 1024


def swap_ctx(block):
    return lax.ppermute(block, "ctx", [(0, 1), (1, 0)])


def swap_core(block):
    return lax.ppermute(block, "tp", [(0, 1), (1, 0), (2, 3), (3, 2)])


def swap_chip(block):
    return lax.ppermute(block, "tp", [(0, 2), (2, 0), (1, 3), (3, 1)])


def paired_tensor_sum(term_rows):
    half = term_rows.shape[0] // 2
    core = lax.axis_index("tp") % 2
    low = term_rows.astype(jnp.bfloat16)
    keep = lax.dynamic_slice_in_dim(low, core * half, half, 0)
    give = lax.dynamic_slice_in_dim(low, (1 - core) * half, half, 0)
    chip_part = (keep.astype(jnp.float32) + swap_core(give).astype(jnp.float32)).astype(jnp.bfloat16)
    total = (chip_part.astype(jnp.float32) + swap_chip(chip_part).astype(jnp.float32)).astype(
        jnp.bfloat16
    )
    other = swap_core(total)
    return jnp.where(
        core == 0,
        jnp.concatenate([total, other], axis=0),
        jnp.concatenate([other, total], axis=0),
    ).astype(jnp.float32)


def spread_turned(columns):
    rows, width = columns.shape
    parts = columns.reshape(rows, width // HD, 2, HALF)
    return jnp.pad(parts, ((0, 0), (0, 0), (0, 0), (0, SPAN - HALF))).reshape(
        rows, width // HD * LANES
    )


def spread_plain(columns):
    rows, width = columns.shape
    parts = columns.reshape(rows, width // HD, HD)
    return jnp.pad(parts, ((0, 0), (0, 0), (0, LANES - HD))).reshape(rows, width // HD * LANES)


def close_turned(columns):
    rows, width = columns.shape
    return columns.reshape(rows, width // SPAN, SPAN)[..., :HALF].reshape(
        rows, width // SPAN * HALF
    )


def close_plain(columns):
    rows, width = columns.shape
    return columns.reshape(rows, width // LANES, LANES)[..., :HD].reshape(
        rows, width // LANES * HD
    )


def dot(a, b, contract):
    return lax.dot_general(a, b, (contract, ((), ())), preferred_element_type=jnp.float32)


def project_kernel(x_ref, gain_ref, w_ref, cos_ref, sin_ref, normed_ref, q_ref, kv_ref):
    x = x_ref[...].astype(jnp.float32)
    factor = lax.rsqrt(jnp.mean(x * x, axis=-1, keepdims=True) + EPSILON)
    normed = (x * factor * gain_ref[...].astype(jnp.float32)).astype(jnp.bfloat16)
    normed_ref[...] = normed
    cosine = cos_ref[...]
    sine = sin_ref[...]
    q_tiles = q_ref.shape[1] // LANES
    tiles = w_ref.shape[1] // LANES
    turned = q_tiles + (tiles - q_tiles) // 2
    scale = HD ** (-0.5) * LOG2E
    for pair in range(tiles // 2):
        wide = dot(normed, w_ref[:, pair * 2 * LANES : (pair + 1) * 2 * LANES], ((1,), (0,)))
        for side in range(2):
            tile = 2 * pair + side
            part = wide[:, side * LANES : (side + 1) * LANES]
            if tile < turned:
                part = part * cosine + pltpu.roll(part, SPAN, 1) * sine
            if tile < q_tiles:
                q_ref[:, tile * LANES : (tile + 1) * LANES] = (part * scale).astype(jnp.bfloat16)
            else:
                lane = (tile - q_tiles) * LANES
                kv_ref[:, lane : lane + LANES] = part.astype(jnp.bfloat16)


def project_tokens(x, gain, weights, cosine, sine, q_width):
    rows, width = x.shape
    out_width = weights.shape[1]
    tile = min(256, rows)
    return pl.pallas_call(
        project_kernel,
        grid=(rows // tile,),
        in_specs=[
            pl.BlockSpec((tile, width), lambda i: (i, 0)),
            pl.BlockSpec((1, width), lambda i: (0, 0)),
            pl.BlockSpec((width, out_width), lambda i: (0, 0)),
            pl.BlockSpec((tile, LANES), lambda i: (i, 0)),
            pl.BlockSpec((tile, LANES), lambda i: (i, 0)),
        ],
        out_specs=[
            pl.BlockSpec((tile, width), lambda i: (i, 0)),
            pl.BlockSpec((tile, q_width), lambda i: (i, 0)),
            pl.BlockSpec((tile, out_width - q_width), lambda i: (i, 0)),
        ],
        out_shape=[
            jax.ShapeDtypeStruct((rows, width), jnp.bfloat16),
            jax.ShapeDtypeStruct((rows, q_width), jnp.bfloat16),
            jax.ShapeDtypeStruct((rows, out_width - q_width), jnp.bfloat16),
        ],
        compiler_params=pltpu.CompilerParams(vmem_limit_bytes=VMEM_BYTES),
        name="project_tokens",
    )(x, gain, weights, cosine, sine)


def block_kinds(meta_ref, query_tile, key_tile, q_start, k_start):
    prefix = meta_ref[0]
    whole = (k_start + (key_tile - 1) <= q_start) | (k_start + key_tile <= prefix)
    nothing = (k_start > q_start + (query_tile - 1)) & (k_start >= prefix)
    return prefix, whole, nothing


def mask_scores(scores, prefix, q_start, k_start, query_tile):
    key_ids = k_start + lax.broadcasted_iota(jnp.int32, scores.shape, 0)
    column = lax.broadcasted_iota(jnp.int32, scores.shape, 1)
    query_ids = q_start + jnp.bitwise_and(column, query_tile - 1)
    return jnp.where((key_ids <= query_ids) | (key_ids < prefix), scores, NEGATIVE)


def attend_kernel(meta_ref, q_ref, k_ref, v_ref, o_ref, lse_ref, max_ref, sum_ref, acc_ref):
    tile = q_ref.shape[0]
    key_tile = tile
    query_tiles = pl.num_programs(1)
    step = pl.program_id(1)
    q_start = meta_ref[1 + step]
    queries = jnp.concatenate([q_ref[:, :LANES], q_ref[:, LANES:]], axis=0)
    max_ref[...] = jnp.full_like(max_ref, NEGATIVE)
    sum_ref[...] = jnp.zeros_like(sum_ref)
    acc_ref[...] = jnp.zeros_like(acc_ref)

    def absorb(scores, values):
        old = max_ref[...]
        new = jnp.maximum(old, jnp.max(scores, axis=0, keepdims=True))
        weights = jnp.exp2(scores - new)
        rescale = jnp.exp2(old - new)
        max_ref[...] = new
        sum_ref[...] = sum_ref[...] * rescale + jnp.sum(weights, axis=0, keepdims=True)
        acc_ref[...] = acc_ref[...] * rescale + dot(
            values, weights.astype(jnp.bfloat16), ((0,), (0,))
        )

    def one(j, carry):
        k_start = meta_ref[1 + query_tiles + j]
        prefix, whole, nothing = block_kinds(meta_ref, tile, key_tile, q_start, k_start)
        rows = pl.ds(pl.multiple_of(j * key_tile, key_tile), key_tile)

        @pl.when(whole)
        def _():
            absorb(dot(k_ref[rows, :], queries, ((1,), (1,))), v_ref[rows, :])

        @pl.when(jnp.logical_not(whole | nothing))
        def _():
            scores = dot(k_ref[rows, :], queries, ((1,), (1,)))
            absorb(mask_scores(scores, prefix, q_start, k_start, tile), v_ref[rows, :])

        return carry

    lax.fori_loop(0, k_ref.shape[0] // key_tile, one, 0)
    total = sum_ref[...]
    lse_ref[0, 0] = max_ref[...] + jnp.log2(total)
    out = (acc_ref[...] / total).T.astype(jnp.bfloat16)
    o_ref[:, :LANES] = out[:tile]
    o_ref[:, LANES:] = out[tile:]


def attend(meta, q, kv, tile):
    rows, q_width = q.shape
    keys = kv.shape[0]
    groups = q_width // (2 * LANES)
    steps = rows // tile
    return pl.pallas_call(
        attend_kernel,
        grid_spec=pltpu.PrefetchScalarGridSpec(
            num_scalar_prefetch=1,
            grid=(groups, steps),
            in_specs=[
                pl.BlockSpec((tile, 2 * LANES), lambda g, i, m: (i, g)),
                pl.BlockSpec((keys, LANES), lambda g, i, m: (0, g)),
                pl.BlockSpec((keys, LANES), lambda g, i, m: (0, groups + g)),
            ],
            out_specs=[
                pl.BlockSpec((tile, 2 * LANES), lambda g, i, m: (i, g)),
                pl.BlockSpec((1, 1, 1, 2 * tile), lambda g, i, m: (g, i, 0, 0)),
            ],
            scratch_shapes=[
                pltpu.VMEM((1, 2 * tile), jnp.float32),
                pltpu.VMEM((1, 2 * tile), jnp.float32),
                pltpu.VMEM((LANES, 2 * tile), jnp.float32),
            ],
        ),
        out_shape=[
            jax.ShapeDtypeStruct((rows, q_width), jnp.bfloat16),
            jax.ShapeDtypeStruct((groups, steps, 1, 2 * tile), jnp.float32),
        ],
        compiler_params=pltpu.CompilerParams(vmem_limit_bytes=VMEM_BYTES),
        cost_estimate=pl.CostEstimate(
            flops=8 * rows * keys * LANES * groups, bytes_accessed=6_000_000, transcendentals=0
        ),
        name="attend",
    )(meta, q, kv, kv)


def attend_back_kernel(
    meta_ref,
    q_ref,
    k_ref,
    v_ref,
    o_ref,
    do_ref,
    lse_ref,
    cos_ref,
    sin_ref,
    dq_ref,
    dk_ref,
    dv_ref,
    delta_ref,
    acc_ref,
):
    query_tiles = lse_ref.shape[1]
    tile = q_ref.shape[0] // query_tiles
    key_tile = k_ref.shape[0]
    j = pl.program_id(1)

    def stacked(ref, i):
        rows = pl.ds(pl.multiple_of(i * tile, tile), tile)
        return jnp.concatenate([ref[rows, :LANES], ref[rows, LANES:]], axis=0)

    @pl.when(j == 0)
    def _():
        acc_ref[...] = jnp.zeros_like(acc_ref)

        def one_delta(i, carry):
            product = stacked(o_ref, i).astype(jnp.float32) * stacked(do_ref, i).astype(jnp.float32)
            delta_ref[i] = jnp.sum(product.T, axis=0, keepdims=True)
            return carry

        lax.fori_loop(0, query_tiles, one_delta, 0)

    k_start = meta_ref[1 + query_tiles + j]
    keys = k_ref[...]
    values = v_ref[...]

    def one(i, carry):
        q_start = meta_ref[1 + i]
        prefix, whole, nothing = block_kinds(meta_ref, tile, key_tile, q_start, k_start)

        def some(state):
            dk, dv = state
            queries = stacked(q_ref, i)
            d_out = stacked(do_ref, i)
            scores = dot(keys, queries, ((1,), (1,)))
            scores = lax.cond(
                whole,
                lambda s: s,
                lambda s: mask_scores(s, prefix, q_start, k_start, tile),
                scores,
            )
            weights = jnp.exp2(scores - lse_ref[0, i])
            d_weights = dot(values, d_out, ((1,), (1,)))
            d_scores = (weights * (d_weights - delta_ref[i])).astype(jnp.bfloat16)
            dv = dv + dot(weights.astype(jnp.bfloat16), d_out, ((1,), (0,)))
            dk = dk + dot(d_scores, queries, ((1,), (0,)))
            acc_ref[i] += dot(keys, d_scores, ((0,), (0,)))
            return dk, dv

        return lax.cond(nothing, lambda state: state, some, carry)

    zero = jnp.zeros((key_tile, LANES), jnp.float32)
    dk, dv = lax.fori_loop(0, query_tiles, one, (zero, zero))
    dk_ref[...] = (dk * (1.0 / LOG2E)).astype(jnp.bfloat16)
    dv_ref[...] = dv.astype(jnp.bfloat16)

    @pl.when(j == pl.num_programs(1) - 1)
    def _():
        scale = HD ** (-0.5)

        def one_out(i, carry):
            rows = pl.ds(pl.multiple_of(i * tile, tile), tile)
            turned = acc_ref[i].T * scale
            for head in range(2):
                part = turned[head * tile : (head + 1) * tile]
                part = part * cos_ref[rows, :] - pltpu.roll(part, SPAN, 1) * sin_ref[rows, :]
                dq_ref[rows, head * LANES : (head + 1) * LANES] = part.astype(jnp.bfloat16)
            return carry

        lax.fori_loop(0, query_tiles, one_out, 0)


def attend_back(meta, q, kv, o, d_out, lse, cosine, sine, tile):
    rows, q_width = q.shape
    keys = kv.shape[0]
    groups = q_width // (2 * LANES)
    query_tiles = rows // tile
    key_tiles = keys // tile
    whole_q = pl.BlockSpec((rows, 2 * LANES), lambda g, j, m: (0, g))
    return pl.pallas_call(
        attend_back_kernel,
        grid_spec=pltpu.PrefetchScalarGridSpec(
            num_scalar_prefetch=1,
            grid=(groups, key_tiles),
            in_specs=[
                whole_q,
                pl.BlockSpec((tile, LANES), lambda g, j, m: (j, g)),
                pl.BlockSpec((tile, LANES), lambda g, j, m: (j, groups + g)),
                whole_q,
                whole_q,
                pl.BlockSpec((1, query_tiles, 1, 2 * tile), lambda g, j, m: (g, 0, 0, 0)),
                pl.BlockSpec((rows, LANES), lambda g, j, m: (0, 0)),
                pl.BlockSpec((rows, LANES), lambda g, j, m: (0, 0)),
            ],
            out_specs=[
                whole_q,
                pl.BlockSpec((tile, LANES), lambda g, j, m: (j, g)),
                pl.BlockSpec((tile, LANES), lambda g, j, m: (j, g)),
            ],
            scratch_shapes=[
                pltpu.VMEM((query_tiles, 1, 2 * tile), jnp.float32),
                pltpu.VMEM((query_tiles, LANES, 2 * tile), jnp.float32),
            ],
        ),
        out_shape=[
            jax.ShapeDtypeStruct((rows, q_width), jnp.bfloat16),
            jax.ShapeDtypeStruct((keys, groups * LANES), jnp.bfloat16),
            jax.ShapeDtypeStruct((keys, groups * LANES), jnp.bfloat16),
        ],
        compiler_params=pltpu.CompilerParams(vmem_limit_bytes=VMEM_BYTES),
        cost_estimate=pl.CostEstimate(
            flops=20 * rows * keys * LANES * groups, bytes_accessed=8_000_000, transcendentals=0
        ),
        name="attend_back",
    )(meta, q, kv, kv, o, d_out, lse, cosine, sine)


def paired_body(
    tokens,
    prefix_len,
    positions,
    gain_attend,
    w_query,
    w_key,
    w_value,
    w_project,
    gain_feed,
    w_gate,
    w_up,
    w_down,
    cotangent,
):
    seqs, rows, width = tokens.shape
    assert seqs == 1
    c = lax.axis_index("ctx")
    bf16, f32 = jnp.bfloat16, jnp.float32

    def half(array, axis, which=None):
        size = array.shape[axis] // 2
        which = c if which is None else which
        return lax.dynamic_slice_in_dim(array, which * size, size, axis)

    def ordered(mine, other, axis):
        return jnp.where(
            c == 0,
            jnp.concatenate([mine, other], axis=axis),
            jnp.concatenate([other, mine], axis=axis),
        )

    def gathered(mine, axis):
        whole = lax.all_gather(mine, "fsdp", axis=axis, tiled=True)
        return whole, swap_ctx(whole)

    gains = lax.all_gather(jnp.stack([gain_attend, gain_feed]), "fsdp", axis=1, tiled=True)
    gain_one, gain_two = gains[:1].astype(f32), gains[1:].astype(f32)
    qkv_mine, qkv_other = gathered(
        jnp.concatenate([half(w_query, 1), half(w_key, 1), half(w_value, 1)], axis=1), 0
    )
    wp_mine, wp_other = gathered(half(w_project, 0), 1)
    wg_mine, wg_other = gathered(half(w_gate, 1), 0)
    wu_mine, wu_other = gathered(half(w_up, 1), 0)
    wd_mine, wd_other = gathered(half(w_down, 0), 1)

    kv_half = w_key.shape[1] // 2
    q_half = w_query.shape[1] // 2

    def parts(block):
        return (
            block[:, :q_half],
            block[:, q_half : q_half + kv_half],
            block[:, q_half + kv_half :],
        )

    mine, other = parts(qkv_mine), parts(qkv_other)
    w_qkv = jnp.concatenate(
        [spread_turned(jnp.concatenate([mine[0], other[0], mine[1], other[1]], axis=1)),
         spread_plain(jnp.concatenate([mine[2], other[2]], axis=1))],
        axis=1,
    )
    q_width = 2 * q_half // HD * LANES
    kv_width = 2 * kv_half // HD * LANES

    frequency = ROPE_BASE ** (-(jnp.arange(HALF, dtype=f32) * 2.0 / HD))
    frequency = jnp.pad(frequency, (0, SPAN - HALF))
    angles = positions[0].astype(f32)[:, None] * frequency
    cosine = jnp.cos(angles)
    sine = jnp.sin(angles)
    cosine = jnp.concatenate([cosine, cosine], axis=1)
    sine = jnp.concatenate([-sine, sine], axis=1)

    block_len = rows // 2
    tile = min(256, block_len)
    query_tiles = rows // tile
    own = c * rows + tile * jnp.arange(query_tiles, dtype=jnp.int32)
    opposite = (1 - c) * rows + tile * jnp.arange(query_tiles, dtype=jnp.int32)
    own, opposite = natural_index(own, block_len, 2), natural_index(opposite, block_len, 2)
    meta = jnp.concatenate([prefix_len.astype(jnp.int32), own, own, opposite])

    x = tokens[0]
    cot = cotangent[0]
    normed, q, kv = project_tokens(x, gain_one, w_qkv, cosine, sine, q_width)
    kv_away = swap_ctx(kv)
    kv_away = kv_away.reshape(rows, 2, 2, kv_width // 2)[:, :, ::-1].reshape(rows, 2 * kv_width)
    kv_all = jnp.concatenate([kv, kv_away], axis=0)
    o, lse = attend(meta, q, kv_all, tile)
    o_low = close_plain(o)
    w_p = jnp.concatenate([wp_mine, wp_other], axis=0)
    middle = x.astype(f32) + paired_tensor_sum(dot(o_low, w_p, ((1,), (0,))))
    factor_two = rms_factor(middle)
    normed_feed = (middle * factor_two * gain_two).astype(bf16)

    def feed(wg, wu, wd):
        gate = dot(normed_feed, wg, ((1,), (0,)))
        up = dot(normed_feed, wu, ((1,), (0,)))
        sigmoid = jax.nn.sigmoid(gate)
        silu = gate * sigmoid
        hidden = (silu * up).astype(bf16)
        hidden_in = dot(cot, wd, ((1,), (1,)))
        gate_back = (hidden_in * up * sigmoid * (1.0 + gate * (1.0 - sigmoid))).astype(bf16)
        up_back = (hidden_in * silu).astype(bf16)
        feed_rows = dot(gate_back, wg, ((1,), (1,))) + dot(up_back, wu, ((1,), (1,)))
        return hidden, gate_back, up_back, feed_rows

    hidden_m, gate_back_m, up_back_m, feed_m = feed(wg_mine, wu_mine, wd_mine)
    hidden_o, gate_back_o, up_back_o, feed_o = feed(wg_other, wu_other, wd_other)
    feed_in = paired_tensor_sum(feed_m + feed_o)

    def summed(give, keep, axis):
        both = (keep + swap_ctx(give.astype(bf16)).astype(f32)).astype(bf16)
        share = lax.psum_scatter(both, "fsdp", scatter_dimension=axis, tiled=True)
        return share

    def whole_again(share, axis):
        return ordered(share, swap_ctx(share), axis).astype(f32)

    contract_rows = ((0,), (0,))
    gate_share = summed(
        dot(normed_feed, gate_back_o, contract_rows), dot(normed_feed, gate_back_m, contract_rows), 0
    )
    up_share = summed(
        dot(normed_feed, up_back_o, contract_rows), dot(normed_feed, up_back_m, contract_rows), 0
    )
    down_part = jnp.concatenate(
        [dot(hidden_m, cot, contract_rows), dot(hidden_o, cot, contract_rows)], axis=0
    ).astype(bf16)
    down_share = lax.psum_scatter(down_part, "fsdp", scatter_dimension=1, tiled=True)
    down_away = swap_ctx(down_share)
    size = down_share.shape[0] // 2
    down_mine = down_share[:size].astype(f32) + down_away[size:].astype(f32)
    down_other = down_share[size:].astype(f32) + down_away[:size].astype(f32)
    down_grad = ordered(down_mine, down_other, 0)

    layer_output = (
        middle
        + paired_tensor_sum(
            dot(hidden_m, wd_mine, ((1,), (0,))) + dot(hidden_o, wd_other, ((1,), (0,)))
        )
    ).astype(bf16)

    gain_two_term = jnp.sum(feed_in * middle * factor_two, axis=0)
    middle_grad = cot.astype(f32) + rms_back(middle, factor_two, gain_two, feed_in)
    middle_low = middle_grad.astype(bf16)
    project_part = dot(o_low, middle_low, contract_rows)
    rows_half = project_part.shape[0] // 2
    project_share = summed(project_part[rows_half:], project_part[:rows_half], 1)
    d_out = spread_plain(dot(middle_low, w_p, ((1,), (1,))).astype(bf16))
    q_low, dk, dv = attend_back(meta, q, kv_all, o, d_out, lse, cosine, sine, tile)
    d_kv = jnp.concatenate([dk, dv], axis=1)
    d_kv_away = swap_ctx(d_kv[rows:])
    d_kv_away = d_kv_away.reshape(rows, 2, 2, kv_width // 2)[:, :, ::-1].reshape(rows, 2 * kv_width)
    d_kv = d_kv[:rows].astype(f32) + d_kv_away.astype(f32)
    key_turned = d_kv[:, :kv_width].reshape(rows, 2, 2, SPAN)
    sine_half, cosine_half = sine[:, None, SPAN:], cosine[:, None, SPAN:]
    k_low = jnp.stack(
        [
            key_turned[:, :, 0] * cosine_half + key_turned[:, :, 1] * sine_half,
            key_turned[:, :, 1] * cosine_half - key_turned[:, :, 0] * sine_half,
        ],
        axis=2,
    )
    k_low = k_low.reshape(rows, kv_width).astype(bf16)
    v_low = d_kv[:, kv_width:].astype(bf16)
    low = jnp.concatenate([q_low, k_low, v_low], axis=1)
    normed_in = paired_tensor_sum(dot(low, w_qkv, ((1,), (1,))))
    qc, kc, vc = close_turned(q_low), close_turned(k_low), close_plain(v_low)
    low_mine = jnp.concatenate([qc[:, :q_half], kc[:, :kv_half], vc[:, :kv_half]], axis=1)
    low_other = jnp.concatenate([qc[:, q_half:], kc[:, kv_half:], vc[:, kv_half:]], axis=1)
    qkv_share = summed(
        dot(normed, low_other, contract_rows), dot(normed, low_mine, contract_rows), 0
    )
    qkv_away = swap_ctx(qkv_share)
    shares = [
        ordered(a, b, 1).astype(f32) for a, b in zip(parts(qkv_share), parts(qkv_away))
    ]

    inputs = x.astype(f32)
    factor_one = rms_factor(inputs)
    gain_one_term = jnp.sum(normed_in * inputs * factor_one, axis=0)
    tokens_grad = (middle_grad + rms_back(inputs, factor_one, gain_one, normed_in)).astype(bf16)
    gain_terms = jnp.stack([gain_one_term, gain_two_term])
    gain_terms = lax.psum_scatter(
        gain_terms + swap_ctx(gain_terms), "fsdp", scatter_dimension=1, tiled=True
    )
    return (
        layer_output[None],
        tokens_grad[None],
        gain_terms[0],
        shares[0],
        shares[1],
        shares[2],
        whole_again(project_share, 0),
        gain_terms[1],
        whole_again(gate_share, 1),
        whole_again(up_share, 1),
        down_grad,
    )


def solution(mesh):
    paired = mesh.shape["ctx"] == 2 and mesh.shape["tp"] == 4
    return jax.shard_map(
        paired_body if paired else general_body,
        mesh=mesh,
        in_specs=(
            P("fsdp", "ctx", None),
            P("fsdp"),
            P("fsdp", "ctx"),
            P("fsdp"),
            P("fsdp", "tp"),
            P("fsdp", "tp"),
            P("fsdp", "tp"),
            P("tp", "fsdp"),
            P("fsdp"),
            P("fsdp", "tp"),
            P("fsdp", "tp"),
            P("tp", "fsdp"),
            P("fsdp", "ctx", None),
        ),
        out_specs=(
            P("fsdp", "ctx", None),
            P("fsdp", "ctx", None),
            P("fsdp"),
            P("fsdp", "tp"),
            P("fsdp", "tp"),
            P("fsdp", "tp"),
            P("tp", "fsdp"),
            P("fsdp"),
            P("fsdp", "tp"),
            P("fsdp", "tp"),
            P("tp", "fsdp"),
        ),
        check_vma=False,
    )
```

```python
import math

import jax
import jax.numpy as jnp
import numpy as np
from jax import lax
from jax.experimental import pallas as pl
from jax.experimental.pallas import tpu as pltpu
from jax.sharding import PartitionSpec as P

HQ = 16
KVH = 8
HD = 96


EPSILON = 1e-05
ROPE_BASE = 100000.0
NEGATIVE = -1e30


def natural_index(stored, block_len, pair_count):
    device = stored // (2 * block_len)
    second_half = stored // block_len % 2
    within = stored % block_len
    block_id = jnp.where(second_half == 0, device, 2 * pair_count - 1 - device)
    return block_id * block_len + within


def rotate(values, cosine_table, sine_table):
    half_width = values.shape[-1] // 2
    leading = values[..., :half_width]
    trailing = values[..., half_width:]
    return jnp.concatenate(
        [
            leading * cosine_table - trailing * sine_table,
            trailing * cosine_table + leading * sine_table,
        ],
        axis=-1,
    )


def rotate_back(incoming, cosine_table, sine_table):
    half_width = incoming.shape[-1] // 2
    leading = incoming[..., :half_width]
    trailing = incoming[..., half_width:]
    return jnp.concatenate(
        [
            leading * cosine_table + trailing * sine_table,
            trailing * cosine_table - leading * sine_table,
        ],
        axis=-1,
    )


def rms_factor(values):
    return lax.rsqrt(jnp.mean(values * values, axis=-1, keepdims=True) + EPSILON)


def rms_back(values, factor, gain_row, incoming):
    scaled = gain_row * incoming
    return factor * scaled - values * factor**3 * jnp.mean(scaled * values, axis=-1, keepdims=True)


def tensor_sum(term_rows):
    return lax.psum(term_rows.astype(jnp.bfloat16), "tp").astype(jnp.float32)


def general_body(
    tokens,
    prefix_len,
    positions,
    gain_attend,
    w_query,
    w_key,
    w_value,
    w_project,
    gain_feed,
    w_gate,
    w_up,
    w_down,
    cotangent,
):
    (
        gain_one,
        query_weight_whole,
        key_weight_whole,
        value_weight_whole,
        project_weight_whole,
        gain_two,
        gate_weight_whole,
        up_weight_whole,
        down_weight_whole,
    ) = (
        lax.all_gather(gain_attend, "fsdp", axis=0, tiled=True),
        lax.all_gather(w_query, "fsdp", axis=0, tiled=True),
        lax.all_gather(w_key, "fsdp", axis=0, tiled=True),
        lax.all_gather(w_value, "fsdp", axis=0, tiled=True),
        lax.all_gather(w_project, "fsdp", axis=1, tiled=True),
        lax.all_gather(gain_feed, "fsdp", axis=0, tiled=True),
        lax.all_gather(w_gate, "fsdp", axis=0, tiled=True),
        lax.all_gather(w_up, "fsdp", axis=0, tiled=True),
        lax.all_gather(w_down, "fsdp", axis=1, tiled=True),
    )
    seq_count, rows_local, _ = tokens.shape
    pair_count = lax.axis_size("ctx")
    block_len = rows_local // 2
    query_width = query_weight_whole.shape[1]
    kv_width = key_weight_whole.shape[1]
    query_heads = query_width // HD
    kv_heads = kv_width // HD
    group_size = HQ // KVH
    score_scale = HD ** (-0.5)
    frequency = ROPE_BASE ** (-(jnp.arange(HD // 2, dtype=jnp.float32) * 2.0 / HD))
    angles = positions.astype(jnp.float32)[:, :, None] * frequency
    cosine_table = jnp.cos(angles)[:, :, None, :]
    sine_table = jnp.sin(angles)[:, :, None, :]
    stored_rows = lax.axis_index("ctx") * rows_local + jnp.arange(rows_local, dtype=jnp.int32)
    query_order = natural_index(stored_rows, block_len, pair_count)

    def visible_mask(key_order):
        causal = key_order[None, None, :] <= query_order[None, :, None]
        opened = key_order[None, None, :] < prefix_len[:, None, None]
        return (causal | opened)[:, :, None, None, :]

    inputs = tokens.astype(jnp.float32)
    factor_one = rms_factor(inputs)
    normed_hidden = (inputs * factor_one * gain_one.astype(jnp.float32)).astype(jnp.bfloat16)
    query_projected = jnp.einsum(
        "rxc,cf->rxf", normed_hidden, query_weight_whole, preferred_element_type=jnp.float32
    )
    key_projected = jnp.einsum(
        "rxc,cf->rxf", normed_hidden, key_weight_whole, preferred_element_type=jnp.float32
    )
    value_projected = jnp.einsum(
        "rxc,cf->rxf", normed_hidden, value_weight_whole, preferred_element_type=jnp.float32
    )
    queries = (
        rotate(
            query_projected.reshape(seq_count, rows_local, query_heads, HD),
            cosine_table,
            sine_table,
        )
        .astype(jnp.bfloat16)
        .reshape(seq_count, rows_local, kv_heads, group_size, HD)
    )
    keys_rot = (
        rotate(key_projected.reshape(seq_count, rows_local, kv_heads, HD), cosine_table, sine_table)
        .astype(jnp.bfloat16)
        .reshape(seq_count, rows_local, kv_width)
    )
    values_low = value_projected.astype(jnp.bfloat16)
    stat_shape = (seq_count, rows_local, kv_heads, group_size)
    initial = (
        jnp.full(stat_shape, NEGATIVE, jnp.float32),
        jnp.zeros(stat_shape, jnp.float32),
        jnp.zeros(stat_shape + (HD,), jnp.float32),
    )
    key_piece = lax.all_gather(keys_rot, "ctx", axis=1, tiled=True)
    value_piece = lax.all_gather(values_low, "ctx", axis=1, tiled=True)
    key_total = key_piece.shape[1]
    span_rows = math.gcd(key_total, rows_local)

    def one_span(span_index, running):
        run_max, run_sum, run_acc = running
        span_start = span_index * span_rows
        key_rows = lax.dynamic_slice_in_dim(key_piece, span_start, span_rows, 1).reshape(
            seq_count, span_rows, kv_heads, HD
        )
        value_rows = lax.dynamic_slice_in_dim(value_piece, span_start, span_rows, 1).reshape(
            seq_count, span_rows, kv_heads, HD
        )
        key_order = natural_index(
            span_start + jnp.arange(span_rows, dtype=jnp.int32), block_len, pair_count
        )
        visible = visible_mask(key_order)
        scores = (
            jnp.einsum("slhgd,skhd->slhgk", queries, key_rows, preferred_element_type=jnp.float32)
            * score_scale
        )
        new_max = jnp.maximum(run_max, jnp.max(jnp.where(visible, scores, NEGATIVE), axis=-1))
        weights_raw = jnp.where(visible, jnp.exp(scores - new_max[..., None]), 0.0)
        rescale = jnp.exp(run_max - new_max)
        run_sum = run_sum * rescale + jnp.sum(weights_raw, axis=-1)
        run_acc = run_acc * rescale[..., None] + jnp.einsum(
            "slhgk,skhd->slhgd",
            weights_raw.astype(jnp.bfloat16),
            value_rows,
            preferred_element_type=jnp.float32,
        )
        return (new_max, run_sum, run_acc)

    run_max, run_sum, run_acc = lax.fori_loop(0, key_total // span_rows, one_span, initial)
    attended = run_acc / run_sum[..., None]
    log_total = run_max + jnp.log(run_sum)
    attended_reduced = attended.reshape(seq_count, rows_local, query_width).astype(jnp.bfloat16)
    project_rows = jnp.einsum(
        "hxz,zm->hxm", attended_reduced, project_weight_whole, preferred_element_type=jnp.float32
    )
    middle = inputs + tensor_sum(project_rows)
    factor_two = rms_factor(middle)
    normed_feed_input = (middle * factor_two * gain_two.astype(jnp.float32)).astype(jnp.bfloat16)
    gate_activation = jnp.einsum(
        "qeh,hj->qej", normed_feed_input, gate_weight_whole, preferred_element_type=jnp.float32
    )
    up_activation = jnp.einsum(
        "qeh,hj->qej", normed_feed_input, up_weight_whole, preferred_element_type=jnp.float32
    )
    sigmoid_gate = jax.nn.sigmoid(gate_activation)
    silu_gate = gate_activation * sigmoid_gate
    hidden_state = (silu_gate * up_activation).astype(jnp.bfloat16)
    down_output_rows = jnp.einsum(
        "nct,tm->ncm", hidden_state, down_weight_whole, preferred_element_type=jnp.float32
    )
    layer_output = (middle + tensor_sum(down_output_rows)).astype(jnp.bfloat16)
    (
        gain_one,
        query_weight_whole,
        key_weight_whole,
        value_weight_whole,
        project_weight_whole,
        gain_two,
        gate_weight_whole,
        up_weight_whole,
        down_weight_whole,
    ) = (
        lax.all_gather(gain_attend, "fsdp", axis=0, tiled=True),
        lax.all_gather(w_query, "fsdp", axis=0, tiled=True),
        lax.all_gather(w_key, "fsdp", axis=0, tiled=True),
        lax.all_gather(w_value, "fsdp", axis=0, tiled=True),
        lax.all_gather(w_project, "fsdp", axis=1, tiled=True),
        lax.all_gather(gain_feed, "fsdp", axis=0, tiled=True),
        lax.all_gather(w_gate, "fsdp", axis=0, tiled=True),
        lax.all_gather(w_up, "fsdp", axis=0, tiled=True),
        lax.all_gather(w_down, "fsdp", axis=1, tiled=True),
    )
    hidden_grad = jnp.einsum(
        "ehv,iv->ehi", cotangent, down_weight_whole, preferred_element_type=jnp.float32
    )
    down_weight_part = jnp.einsum(
        "gqa,gqz->az", hidden_state, cotangent, preferred_element_type=jnp.float32
    )
    gate_reduced = (
        hidden_grad * up_activation * sigmoid_gate * (1.0 + gate_activation * (1.0 - sigmoid_gate))
    ).astype(jnp.bfloat16)
    up_reduced = (hidden_grad * silu_gate).astype(jnp.bfloat16)
    gate_weight_part = jnp.einsum(
        "bic,big->cg", normed_feed_input, gate_reduced, preferred_element_type=jnp.float32
    )
    up_weight_part = jnp.einsum(
        "bic,big->cg", normed_feed_input, up_reduced, preferred_element_type=jnp.float32
    )
    feed_rows = jnp.einsum(
        "vte,ce->vtc", gate_reduced, gate_weight_whole, preferred_element_type=jnp.float32
    ) + jnp.einsum("vte,ce->vtc", up_reduced, up_weight_whole, preferred_element_type=jnp.float32)
    feed_in = tensor_sum(feed_rows)
    gain_two_term = jnp.sum(feed_in * middle * factor_two, axis=(0, 1))
    middle_grad = cotangent.astype(jnp.float32) + rms_back(
        middle, factor_two, gain_two.astype(jnp.float32), feed_in
    )
    middle_reduced = middle_grad.astype(jnp.bfloat16)
    project_term = jnp.einsum(
        "xeh,xec->hc", attended_reduced, middle_reduced, preferred_element_type=jnp.float32
    )
    attended_grad = (
        jnp.einsum(
            "vhk,nk->vhn", middle_reduced, project_weight_whole, preferred_element_type=jnp.float32
        )
        .astype(jnp.bfloat16)
        .reshape(seq_count, rows_local, kv_heads, group_size, HD)
    )
    row_delta = jnp.sum(attended_grad.astype(jnp.float32) * attended, axis=-1)
    whole_keys, whole_values = (
        lax.all_gather(keys_rot[None], "ctx", axis=0, tiled=True),
        lax.all_gather(values_low[None], "ctx", axis=0, tiled=True),
    )

    def key_block(grad_acc, block_items):
        key_rows, value_rows, block_index = block_items
        key_rows = key_rows.reshape(seq_count, rows_local, kv_heads, HD)
        value_rows = value_rows.reshape(seq_count, rows_local, kv_heads, HD)
        key_order = natural_index(
            block_index * rows_local + jnp.arange(rows_local, dtype=jnp.int32),
            block_len,
            pair_count,
        )
        visible = visible_mask(key_order)
        scores = (
            jnp.einsum("slhgd,skhd->slhgk", queries, key_rows, preferred_element_type=jnp.float32)
            * score_scale
        )
        weights_norm = jnp.where(visible, jnp.exp(scores - log_total[..., None]), 0.0)
        prob_grad = jnp.einsum(
            "slhgd,skhd->slhgk", attended_grad, value_rows, preferred_element_type=jnp.float32
        )
        score_grad = (weights_norm * (prob_grad - row_delta[..., None])).astype(jnp.bfloat16)
        grad_acc = (
            grad_acc
            + jnp.einsum(
                "slhgk,skhd->slhgd", score_grad, key_rows, preferred_element_type=jnp.float32
            )
            * score_scale
        )
        key_grad = (
            jnp.einsum("slhgk,slhgd->skhd", score_grad, queries, preferred_element_type=jnp.float32)
            * score_scale
        )
        value_grad = jnp.einsum(
            "slhgk,slhgd->skhd",
            weights_norm.astype(jnp.bfloat16),
            attended_grad,
            preferred_element_type=jnp.float32,
        )
        return (
            grad_acc,
            (
                key_grad.reshape(seq_count, rows_local, kv_width),
                value_grad.reshape(seq_count, rows_local, kv_width),
            ),
        )

    block_ids = jnp.arange(pair_count, dtype=jnp.int32)
    query_grad, (key_terms, value_terms) = lax.scan(
        key_block, jnp.zeros(stat_shape + (HD,), jnp.float32), (whole_keys, whole_values, block_ids)
    )
    key_sum, value_sum = (
        lax.psum_scatter(
            key_terms.astype(jnp.bfloat16), "ctx", scatter_dimension=0, tiled=True
        ).astype(jnp.float32),
        lax.psum_scatter(
            value_terms.astype(jnp.bfloat16), "ctx", scatter_dimension=0, tiled=True
        ).astype(jnp.float32),
    )
    key_reduced = (
        rotate_back(
            key_sum[0].reshape(seq_count, rows_local, kv_heads, HD), cosine_table, sine_table
        )
        .astype(jnp.bfloat16)
        .reshape(seq_count, rows_local, kv_width)
    )
    value_backward = value_sum[0].astype(jnp.bfloat16)
    query_reduced = (
        rotate_back(
            query_grad.reshape(seq_count, rows_local, query_heads, HD), cosine_table, sine_table
        )
        .astype(jnp.bfloat16)
        .reshape(seq_count, rows_local, query_width)
    )
    query_weight_part = jnp.einsum(
        "prb,pro->bo", normed_hidden, query_reduced, preferred_element_type=jnp.float32
    )
    key_weight_part = jnp.einsum(
        "prb,pro->bo", normed_hidden, key_reduced, preferred_element_type=jnp.float32
    )
    value_weight_part = jnp.einsum(
        "prb,pro->bo", normed_hidden, value_backward, preferred_element_type=jnp.float32
    )
    normed_rows = (
        jnp.einsum(
            "kjw,iw->kji", query_reduced, query_weight_whole, preferred_element_type=jnp.float32
        )
        + jnp.einsum(
            "kjw,iw->kji", key_reduced, key_weight_whole, preferred_element_type=jnp.float32
        )
        + jnp.einsum(
            "kjw,iw->kji", value_backward, value_weight_whole, preferred_element_type=jnp.float32
        )
    )
    normed_grad = tensor_sum(normed_rows)
    gain_one_term = jnp.sum(normed_grad * inputs * factor_one, axis=(0, 1))
    tokens_grad = (
        middle_grad + rms_back(inputs, factor_one, gain_one.astype(jnp.float32), normed_grad)
    ).astype(jnp.bfloat16)
    (
        part_one,
        part_query,
        part_key,
        part_value,
        part_project,
        part_two,
        part_gate,
        part_up,
        part_down,
    ) = (
        lax.psum_scatter(gain_one_term, ("fsdp", "ctx"), scatter_dimension=0, tiled=True),
        lax.psum_scatter(query_weight_part, ("fsdp", "ctx"), scatter_dimension=0, tiled=True),
        lax.psum_scatter(key_weight_part, ("fsdp", "ctx"), scatter_dimension=0, tiled=True),
        lax.psum_scatter(value_weight_part, ("fsdp", "ctx"), scatter_dimension=0, tiled=True),
        lax.psum_scatter(project_term, ("fsdp", "ctx"), scatter_dimension=1, tiled=True),
        lax.psum_scatter(gain_two_term, ("fsdp", "ctx"), scatter_dimension=0, tiled=True),
        lax.psum_scatter(gate_weight_part, ("fsdp", "ctx"), scatter_dimension=0, tiled=True),
        lax.psum_scatter(up_weight_part, ("fsdp", "ctx"), scatter_dimension=0, tiled=True),
        lax.psum_scatter(down_weight_part, ("fsdp", "ctx"), scatter_dimension=1, tiled=True),
    )
    reduced = (
        lax.all_gather(part_one.astype(jnp.bfloat16), "ctx", axis=0, tiled=True).astype(
            part_one.dtype
        ),
        lax.all_gather(part_query.astype(jnp.bfloat16), "ctx", axis=0, tiled=True).astype(
            part_query.dtype
        ),
        lax.all_gather(part_key.astype(jnp.bfloat16), "ctx", axis=0, tiled=True).astype(
            part_key.dtype
        ),
        lax.all_gather(part_value.astype(jnp.bfloat16), "ctx", axis=0, tiled=True).astype(
            part_value.dtype
        ),
        lax.all_gather(part_project.astype(jnp.bfloat16), "ctx", axis=1, tiled=True).astype(
            part_project.dtype
        ),
        lax.all_gather(part_two.astype(jnp.bfloat16), "ctx", axis=0, tiled=True).astype(
            part_two.dtype
        ),
        lax.all_gather(part_gate.astype(jnp.bfloat16), "ctx", axis=0, tiled=True).astype(
            part_gate.dtype
        ),
        lax.all_gather(part_up.astype(jnp.bfloat16), "ctx", axis=0, tiled=True).astype(
            part_up.dtype
        ),
        lax.all_gather(part_down.astype(jnp.bfloat16), "ctx", axis=1, tiled=True).astype(
            part_down.dtype
        ),
    )
    return (layer_output, tokens_grad) + tuple(reduced)


LANES = 128
HALF = HD // 2
SPAN = LANES // 2
LOG2E = math.log2(math.e)
VMEM_BYTES = 56 * 1024 * 1024


def swap_ctx(block):
    return lax.ppermute(block, "ctx", [(0, 1), (1, 0)])


def swap_core(block):
    return lax.ppermute(block, "tp", [(0, 1), (1, 0), (2, 3), (3, 2)])


def swap_chip(block):
    return lax.ppermute(block, "tp", [(0, 2), (2, 0), (1, 3), (3, 1)])


def paired_tensor_sum(term_rows):
    half = term_rows.shape[0] // 2
    core = lax.axis_index("tp") % 2
    low = term_rows.astype(jnp.bfloat16)
    keep = lax.dynamic_slice_in_dim(low, core * half, half, 0)
    give = lax.dynamic_slice_in_dim(low, (1 - core) * half, half, 0)
    chip_part = (keep.astype(jnp.float32) + swap_core(give).astype(jnp.float32)).astype(jnp.bfloat16)
    total = (chip_part.astype(jnp.float32) + swap_chip(chip_part).astype(jnp.float32)).astype(
        jnp.bfloat16
    )
    other = swap_core(total)
    return jnp.where(
        core == 0,
        jnp.concatenate([total, other], axis=0),
        jnp.concatenate([other, total], axis=0),
    ).astype(jnp.float32)


def dot(a, b, contract):
    return lax.dot_general(a, b, (contract, ((), ())), preferred_element_type=jnp.float32)


MESH = pl.DeviceIdType.MESH
GAIN_ROWS = 16


def gather_kernel(
    x_ref,
    pack_ref,
    rest_ref,
    spread_ref,
    cos_ref,
    sin_ref,
    normed_ref,
    q_ref,
    kv_ref,
    wide_ref,
    project_ref,
    gain_ref,
    buf_ref,
    up_send,
    up_recv,
    down_send,
    down_recv,
    x_send,
    x_recv,
    kv_send,
    kv_recv,
):
    planes = buf_ref.shape[0]
    depth = wide_ref.shape[0] // planes
    half_width = wide_ref.shape[1] // 2
    matrix_rows = pack_ref.shape[0] - GAIN_ROWS
    project_rows = matrix_rows - depth
    rows = x_ref.shape[0]
    z = lax.axis_index("fsdp")
    c = lax.axis_index("ctx")
    across = {"ctx": 1 - c}
    has_above = z < planes - 1
    has_below = z > 0

    barrier = pltpu.get_barrier_semaphore()

    @pl.when(has_above)
    def _():
        pl.semaphore_signal(barrier, inc=1, device_id={"fsdp": z + 1}, device_id_type=MESH)

    @pl.when(has_below)
    def _():
        pl.semaphore_signal(barrier, inc=1, device_id={"fsdp": z - 1}, device_id_type=MESH)

    pl.semaphore_signal(barrier, inc=1, device_id=across, device_id_type=MESH)

    @pl.when(has_above & has_below)
    def _():
        pl.semaphore_wait(barrier, 3)

    @pl.when(jnp.logical_not(has_above & has_below))
    def _():
        pl.semaphore_wait(barrier, 2)

    def up(k):
        piece = z - k
        return pltpu.make_async_remote_copy(
            src_ref=pack_ref if k == 0 else buf_ref.at[piece, 0],
            dst_ref=buf_ref.at[piece, 0],
            send_sem=up_send.at[k],
            recv_sem=up_recv.at[k],
            device_id={"fsdp": z + 1},
            device_id_type=MESH,
        )

    def down(k):
        piece = z + k
        return pltpu.make_async_remote_copy(
            src_ref=pack_ref if k == 0 else buf_ref.at[piece, 0],
            dst_ref=buf_ref.at[piece, 0],
            send_sem=down_send.at[k],
            recv_sem=down_recv.at[k],
            device_id={"fsdp": z - 1},
            device_id_type=MESH,
        )

    def from_below(k):
        piece = z - 1 - k
        return pltpu.make_async_remote_copy(
            src_ref=buf_ref.at[piece, 0],
            dst_ref=buf_ref.at[piece, 0],
            send_sem=up_send.at[k],
            recv_sem=up_recv.at[k],
            device_id={"fsdp": z - 1},
            device_id_type=MESH,
        )

    def from_above(k):
        piece = z + 1 + k
        return pltpu.make_async_remote_copy(
            src_ref=buf_ref.at[piece, 0],
            dst_ref=buf_ref.at[piece, 0],
            send_sem=down_send.at[k],
            recv_sem=down_recv.at[k],
            device_id={"fsdp": z + 1},
            device_id_type=MESH,
        )

    def sideways(side, k):
        piece = z - k if side == 0 else z + k
        return pltpu.make_async_remote_copy(
            src_ref=buf_ref.at[piece, 0, pl.ds(0, matrix_rows)],
            dst_ref=buf_ref.at[piece, 1, pl.ds(0, matrix_rows)],
            send_sem=x_send.at[side, k],
            recv_sem=x_recv.at[side, k],
            device_id=across,
            device_id_type=MESH,
        )

    spread = spread_ref[...]

    def place(block, piece, which):
        at = pl.ds(pl.multiple_of(piece * depth, depth), depth)
        wide_ref[at, which * half_width : (which + 1) * half_width] = dot(
            block[:depth], spread, ((1,), (0,))
        ).astype(jnp.bfloat16)
        for head in range(project_rows // HD):
            row = (which * (project_rows // HD) + head) * LANES
            project_ref[row : row + HD, at] = block[depth + head * HD : depth + (head + 1) * HD]

    def place_gain(block, piece):
        at = pl.ds(pl.multiple_of(piece * depth, depth), depth)
        gain_ref[:, at] = block[matrix_rows:]

    @pl.when(has_above)
    def _():
        up(0).start()

    @pl.when(has_below)
    def _():
        down(0).start()

    for head in range(project_ref.shape[0] // LANES):
        row = head * LANES + HD
        project_ref[row : row + LANES - HD, :] = jnp.zeros(
            (LANES - HD, project_ref.shape[1]), jnp.bfloat16
        )
    place(pack_ref, z, 0)
    place_gain(pack_ref, z)
    place(rest_ref, z, 1)

    for k in range(1, planes):
        below = z - k >= 0
        above = z + k <= planes - 1

        @pl.when(below)
        def _():
            from_below(k - 1).wait_recv()
            if k < planes - 1:

                @pl.when(has_above)
                def _():
                    up(k).start()

            sideways(0, k).start()

        @pl.when(above)
        def _():
            from_above(k - 1).wait_recv()
            if k < planes - 1:

                @pl.when(has_below)
                def _():
                    down(k).start()

            sideways(1, k).start()

        @pl.when(below)
        def _():
            place(buf_ref.at[z - k, 0], z - k, 0)
            place_gain(buf_ref.at[z - k, 0], z - k)

        @pl.when(above)
        def _():
            place(buf_ref.at[z + k, 0], z + k, 0)
            place_gain(buf_ref.at[z + k, 0], z + k)

    tile = 128
    gain = gain_ref[0:1, :].astype(jnp.float32)

    def norm_rows(i, carry):
        at = pl.ds(pl.multiple_of(i * tile, tile), tile)
        x = x_ref[at, :].astype(jnp.float32)
        factor = lax.rsqrt(jnp.mean(x * x, axis=-1, keepdims=True) + EPSILON)
        normed_ref[at, :] = (x * factor * gain).astype(jnp.bfloat16)
        return carry

    lax.fori_loop(0, rows // tile, norm_rows, 0)

    for k in range(1, planes):

        @pl.when(z - k >= 0)
        def _():
            sideways(0, k).wait_recv()
            place(buf_ref.at[z - k, 1], z - k, 1)

        @pl.when(z + k <= planes - 1)
        def _():
            sideways(1, k).wait_recv()
            place(buf_ref.at[z + k, 1], z + k, 1)

    block = 256

    def turn(part, at):
        return part * cos_ref[at, :] + pltpu.roll(part, SPAN, 1) * sin_ref[at, :]

    def key_rows(i, carry):
        at = pl.ds(pl.multiple_of(i * block, block), block)
        for which in range(2):
            lane = which * half_width + 2 * LANES
            both = dot(normed_ref[at, :], wide_ref[:, lane : lane + 2 * LANES], ((1,), (0,)))
            kv_ref[which, at, :] = turn(both[:, :LANES], at).astype(jnp.bfloat16)
            kv_ref[2 + which, at, :] = both[:, LANES:].astype(jnp.bfloat16)
        return carry

    lax.fori_loop(0, rows // block, key_rows, 0)

    def exchange(slab):
        return pltpu.make_async_remote_copy(
            src_ref=kv_ref.at[slab, pl.ds(0, rows)],
            dst_ref=kv_ref.at[slab ^ 1, pl.ds(rows, rows)],
            send_sem=kv_send.at[slab],
            recv_sem=kv_recv.at[slab ^ 1],
            device_id=across,
            device_id_type=MESH,
        )

    for slab in range(4):
        exchange(slab).start()
    scale = HD ** (-0.5) * LOG2E

    def query_rows(i, carry):
        at = pl.ds(pl.multiple_of(i * block, block), block)
        for which in range(2):
            lane = which * half_width
            both = dot(normed_ref[at, :], wide_ref[:, lane : lane + 2 * LANES], ((1,), (0,)))
            for head in range(2):
                part = turn(both[:, head * LANES : (head + 1) * LANES], at)
                lane = (2 * which + head) * LANES
                q_ref[at, lane : lane + LANES] = (part * scale).astype(jnp.bfloat16)
        return carry

    lax.fori_loop(0, rows // block, query_rows, 0)

    for k in range(planes - 1):

        @pl.when((z - k >= 0) & has_above)
        def _():
            up(k).wait_send()

        @pl.when((z + k <= planes - 1) & has_below)
        def _():
            down(k).wait_send()

    for k in range(1, planes):

        @pl.when(z - k >= 0)
        def _():
            sideways(0, k).wait_send()

        @pl.when(z + k <= planes - 1)
        def _():
            sideways(1, k).wait_send()

    for slab in range(4):
        exchange(slab).wait_send()
    for slab in range(4):
        exchange(slab).wait_recv()


def gather_project(x, pack, rest, spread, cosine, sine, planes):
    rows, width = x.shape
    depth = width // planes
    half_width = spread.shape[1]
    project_rows = pack.shape[0] - GAIN_ROWS - depth
    vmem = pl.BlockSpec(memory_space=pltpu.VMEM)
    bf16 = jnp.bfloat16
    dma = pltpu.SemaphoreType.DMA
    return pl.pallas_call(
        gather_kernel,
        in_specs=[vmem] * 6,
        out_specs=[vmem] * 6,
        out_shape=[
            jax.ShapeDtypeStruct((rows, width), bf16),
            jax.ShapeDtypeStruct((rows, half_width), bf16),
            jax.ShapeDtypeStruct((4, 2 * rows, LANES), bf16),
            jax.ShapeDtypeStruct((width, 2 * half_width), bf16),
            jax.ShapeDtypeStruct((2 * project_rows // HD * LANES, width), bf16),
            jax.ShapeDtypeStruct((GAIN_ROWS, width), bf16),
        ],
        scratch_shapes=[
            pltpu.VMEM((planes, 2, pack.shape[0], pack.shape[1]), bf16),
            dma((planes - 1,)),
            dma((planes - 1,)),
            dma((planes - 1,)),
            dma((planes - 1,)),
            dma((2, planes)),
            dma((2, planes)),
            dma((4,)),
            dma((4,)),
        ],
        compiler_params=pltpu.CompilerParams(
            collective_id=1, has_side_effects=True, vmem_limit_bytes=VMEM_BYTES
        ),
        cost_estimate=pl.CostEstimate(
            flops=40_000_000_000, bytes_accessed=16_000_000, transcendentals=0
        ),
        name="gather_project",
    )(x, pack, rest, spread, cosine, sine)


def block_kinds(meta_ref, query_tile, key_tile, q_start, k_start):
    prefix = meta_ref[0]
    whole = (k_start + (key_tile - 1) <= q_start) | (k_start + key_tile <= prefix)
    nothing = (k_start > q_start + (query_tile - 1)) & (k_start >= prefix)
    return prefix, whole, nothing


def mask_scores(scores, prefix, q_start, k_start, query_tile):
    key_ids = k_start + lax.broadcasted_iota(jnp.int32, scores.shape, 0)
    column = lax.broadcasted_iota(jnp.int32, scores.shape, 1)
    query_ids = q_start + jnp.bitwise_and(column, query_tile - 1)
    return jnp.where((key_ids <= query_ids) | (key_ids < prefix), scores, NEGATIVE)


def attend_kernel(meta_ref, q_ref, k_ref, v_ref, o_ref, lse_ref, max_ref, sum_ref, acc_ref):
    tile = q_ref.shape[0]
    key_tile = tile
    query_tiles = pl.num_programs(1)
    step = pl.program_id(1)
    q_start = meta_ref[1 + step]
    queries = jnp.concatenate([q_ref[:, :LANES], q_ref[:, LANES:]], axis=0)
    max_ref[...] = jnp.full_like(max_ref, NEGATIVE)
    sum_ref[...] = jnp.zeros_like(sum_ref)
    acc_ref[...] = jnp.zeros_like(acc_ref)

    def absorb(scores, values):
        old = max_ref[...]
        new = jnp.maximum(old, jnp.max(scores, axis=0, keepdims=True))
        weights = jnp.exp2(scores - new)
        rescale = jnp.exp2(old - new)
        max_ref[...] = new
        sum_ref[...] = sum_ref[...] * rescale + jnp.sum(weights, axis=0, keepdims=True)
        acc_ref[...] = acc_ref[...] * rescale + dot(
            values, weights.astype(jnp.bfloat16), ((0,), (0,))
        )

    def one(j, carry):
        k_start = meta_ref[1 + query_tiles + j]
        prefix, whole, nothing = block_kinds(meta_ref, tile, key_tile, q_start, k_start)
        rows = pl.ds(pl.multiple_of(j * key_tile, key_tile), key_tile)

        @pl.when(whole)
        def _():
            absorb(dot(k_ref[0, rows, :], queries, ((1,), (1,))), v_ref[0, rows, :])

        @pl.when(jnp.logical_not(whole | nothing))
        def _():
            scores = dot(k_ref[0, rows, :], queries, ((1,), (1,)))
            absorb(mask_scores(scores, prefix, q_start, k_start, tile), v_ref[0, rows, :])

        return carry

    lax.fori_loop(0, k_ref.shape[1] // key_tile, one, 0)
    total = sum_ref[...]
    lse_ref[0, 0] = max_ref[...] + jnp.log2(total)
    out = (acc_ref[...] / total).T.astype(jnp.bfloat16)
    o_ref[:, :LANES] = out[:tile]
    o_ref[:, LANES:] = out[tile:]


def attend(meta, q, kv, tile):
    rows, q_width = q.shape
    keys = kv.shape[1]
    groups = q_width // (2 * LANES)
    steps = rows // tile
    return pl.pallas_call(
        attend_kernel,
        grid_spec=pltpu.PrefetchScalarGridSpec(
            num_scalar_prefetch=1,
            grid=(groups, steps),
            in_specs=[
                pl.BlockSpec((tile, 2 * LANES), lambda g, i, m: (i, g)),
                pl.BlockSpec((1, keys, LANES), lambda g, i, m: (g, 0, 0)),
                pl.BlockSpec((1, keys, LANES), lambda g, i, m: (groups + g, 0, 0)),
            ],
            out_specs=[
                pl.BlockSpec((tile, 2 * LANES), lambda g, i, m: (i, g)),
                pl.BlockSpec((1, 1, 1, 2 * tile), lambda g, i, m: (g, i, 0, 0)),
            ],
            scratch_shapes=[
                pltpu.VMEM((1, 2 * tile), jnp.float32),
                pltpu.VMEM((1, 2 * tile), jnp.float32),
                pltpu.VMEM((LANES, 2 * tile), jnp.float32),
            ],
        ),
        out_shape=[
            jax.ShapeDtypeStruct((rows, q_width), jnp.bfloat16),
            jax.ShapeDtypeStruct((groups, steps, 1, 2 * tile), jnp.float32),
        ],
        compiler_params=pltpu.CompilerParams(vmem_limit_bytes=VMEM_BYTES),
        cost_estimate=pl.CostEstimate(
            flops=8 * rows * keys * LANES * groups, bytes_accessed=6_000_000, transcendentals=0
        ),
        name="attend",
    )(meta, q, kv, kv)


def attend_back_kernel(
    meta_ref,
    q_ref,
    k_ref,
    v_ref,
    o_ref,
    do_ref,
    lse_ref,
    cos_ref,
    sin_ref,
    dq_ref,
    dk_ref,
    dv_ref,
    delta_ref,
    acc_ref,
):
    query_tiles = lse_ref.shape[1]
    tile = q_ref.shape[0] // query_tiles
    key_tile = k_ref.shape[1]
    j = pl.program_id(1)

    def stacked(ref, i):
        rows = pl.ds(pl.multiple_of(i * tile, tile), tile)
        return jnp.concatenate([ref[rows, :LANES], ref[rows, LANES:]], axis=0)

    @pl.when(j == 0)
    def _():
        acc_ref[...] = jnp.zeros_like(acc_ref)

        def one_delta(i, carry):
            product = stacked(o_ref, i).astype(jnp.float32) * stacked(do_ref, i).astype(jnp.float32)
            delta_ref[i] = jnp.sum(product.T, axis=0, keepdims=True)
            return carry

        lax.fori_loop(0, query_tiles, one_delta, 0)

    k_start = meta_ref[1 + query_tiles + j]
    keys = k_ref[0]
    values = v_ref[0]

    def one(i, carry):
        q_start = meta_ref[1 + i]
        prefix, whole, nothing = block_kinds(meta_ref, tile, key_tile, q_start, k_start)

        def some(state):
            dk, dv = state
            queries = stacked(q_ref, i)
            d_out = stacked(do_ref, i)
            scores = dot(keys, queries, ((1,), (1,)))
            scores = lax.cond(
                whole,
                lambda s: s,
                lambda s: mask_scores(s, prefix, q_start, k_start, tile),
                scores,
            )
            weights = jnp.exp2(scores - lse_ref[0, i])
            d_weights = dot(values, d_out, ((1,), (1,)))
            d_scores = (weights * (d_weights - delta_ref[i])).astype(jnp.bfloat16)
            dv = dv + dot(weights.astype(jnp.bfloat16), d_out, ((1,), (0,)))
            dk = dk + dot(d_scores, queries, ((1,), (0,)))
            acc_ref[i] += dot(keys, d_scores, ((0,), (0,)))
            return dk, dv

        return lax.cond(nothing, lambda state: state, some, carry)

    zero = jnp.zeros((key_tile, LANES), jnp.float32)
    dk, dv = lax.fori_loop(0, query_tiles, one, (zero, zero))
    dk_ref[0] = (dk * (1.0 / LOG2E)).astype(jnp.bfloat16)
    dv_ref[0] = dv.astype(jnp.bfloat16)

    @pl.when(j == pl.num_programs(1) - 1)
    def _():
        scale = HD ** (-0.5)

        def one_out(i, carry):
            rows = pl.ds(pl.multiple_of(i * tile, tile), tile)
            turned = acc_ref[i].T * scale
            for head in range(2):
                part = turned[head * tile : (head + 1) * tile]
                part = part * cos_ref[rows, :] - pltpu.roll(part, SPAN, 1) * sin_ref[rows, :]
                dq_ref[rows, head * LANES : (head + 1) * LANES] = part.astype(jnp.bfloat16)
            return carry

        lax.fori_loop(0, query_tiles, one_out, 0)


def attend_back(meta, q, kv, o, d_out, lse, cosine, sine, tile):
    rows, q_width = q.shape
    keys = kv.shape[1]
    groups = q_width // (2 * LANES)
    query_tiles = rows // tile
    key_tiles = keys // tile
    whole_q = pl.BlockSpec((rows, 2 * LANES), lambda g, j, m: (0, g))
    return pl.pallas_call(
        attend_back_kernel,
        grid_spec=pltpu.PrefetchScalarGridSpec(
            num_scalar_prefetch=1,
            grid=(groups, key_tiles),
            in_specs=[
                whole_q,
                pl.BlockSpec((1, tile, LANES), lambda g, j, m: (g, j, 0)),
                pl.BlockSpec((1, tile, LANES), lambda g, j, m: (groups + g, j, 0)),
                whole_q,
                whole_q,
                pl.BlockSpec((1, query_tiles, 1, 2 * tile), lambda g, j, m: (g, 0, 0, 0)),
                pl.BlockSpec((rows, LANES), lambda g, j, m: (0, 0)),
                pl.BlockSpec((rows, LANES), lambda g, j, m: (0, 0)),
            ],
            out_specs=[
                whole_q,
                pl.BlockSpec((1, tile, LANES), lambda g, j, m: (g, j, 0)),
                pl.BlockSpec((1, tile, LANES), lambda g, j, m: (g, j, 0)),
            ],
            scratch_shapes=[
                pltpu.VMEM((query_tiles, 1, 2 * tile), jnp.float32),
                pltpu.VMEM((query_tiles, LANES, 2 * tile), jnp.float32),
            ],
        ),
        out_shape=[
            jax.ShapeDtypeStruct((rows, q_width), jnp.bfloat16),
            jax.ShapeDtypeStruct((groups, keys, LANES), jnp.bfloat16),
            jax.ShapeDtypeStruct((groups, keys, LANES), jnp.bfloat16),
        ],
        compiler_params=pltpu.CompilerParams(vmem_limit_bytes=VMEM_BYTES),
        cost_estimate=pl.CostEstimate(
            flops=20 * rows * keys * LANES * groups, bytes_accessed=8_000_000, transcendentals=0
        ),
        name="attend_back",
    )(meta, q, kv, kv, o, d_out, lse, cosine, sine)


def paired_body(
    tokens,
    prefix_len,
    positions,
    gain_attend,
    w_query,
    w_key,
    w_value,
    w_project,
    gain_feed,
    w_gate,
    w_up,
    w_down,
    cotangent,
):
    seqs, rows, width = tokens.shape
    assert seqs == 1
    c = lax.axis_index("ctx")
    bf16, f32 = jnp.bfloat16, jnp.float32

    def half(array, axis, which=None):
        size = array.shape[axis] // 2
        which = c if which is None else which
        return lax.dynamic_slice_in_dim(array, which * size, size, axis)

    def ordered(mine, other, axis):
        return jnp.where(
            c == 0,
            jnp.concatenate([mine, other], axis=axis),
            jnp.concatenate([other, mine], axis=axis),
        )

    def gathered(mine, axis):
        whole = lax.all_gather(mine, "fsdp", axis=axis, tiled=True)
        return whole, swap_ctx(whole)

    planes = lax.axis_size("fsdp")
    kv_half = w_key.shape[1] // 2
    q_half = w_query.shape[1] // 2

    def packed(which):
        return jnp.concatenate(
            [
                jnp.concatenate([half(w_query, 1, which), half(w_key, 1, which), half(w_value, 1, which)], axis=1),
                half(w_project, 0, which),
                jnp.pad(jnp.stack([gain_attend, gain_feed]), ((0, GAIN_ROWS - 2), (0, 0))),
            ],
            axis=0,
        )

    wg_mine, wg_other = gathered(half(w_gate, 1), 0)
    wu_mine, wu_other = gathered(half(w_up, 1), 0)
    wd_mine, wd_other = gathered(half(w_down, 0), 1)

    def parts(block):
        return (
            block[:, :q_half],
            block[:, q_half : q_half + kv_half],
            block[:, q_half + kv_half :],
        )

    half_heads = (q_half + 2 * kv_half) // HD
    spread = np.zeros((half_heads * HD, half_heads * LANES), np.float32)
    for head in range(half_heads):
        for lane in range(HD):
            turned = lane if lane < HALF or head == half_heads - 1 else lane - HALF + SPAN
            spread[head * HD + lane, head * LANES + turned] = 1.0
    spread = jnp.asarray(spread, bf16)

    frequency = ROPE_BASE ** (-(jnp.arange(HALF, dtype=f32) * 2.0 / HD))
    frequency = jnp.pad(frequency, (0, SPAN - HALF))
    angles = positions[0].astype(f32)[:, None] * frequency
    cosine = jnp.cos(angles)
    sine = jnp.sin(angles)
    cosine = jnp.concatenate([cosine, cosine], axis=1)
    sine = jnp.concatenate([-sine, sine], axis=1)

    block_len = rows // 2
    tile = min(256, block_len)
    query_tiles = rows // tile
    own = c * rows + tile * jnp.arange(query_tiles, dtype=jnp.int32)
    opposite = (1 - c) * rows + tile * jnp.arange(query_tiles, dtype=jnp.int32)
    own, opposite = natural_index(own, block_len, 2), natural_index(opposite, block_len, 2)
    meta = jnp.concatenate([prefix_len.astype(jnp.int32), own, own, opposite])

    x = tokens[0]
    cot = cotangent[0]
    normed, q, kv_all, w_qkv, w_p, gains = gather_project(
        x, packed(c), packed(1 - c), spread, cosine, sine, planes
    )
    gain_one, gain_two = gains[0:1].astype(f32), gains[1:2].astype(f32)
    o, lse = attend(meta, q, kv_all, tile)
    middle = x.astype(f32) + paired_tensor_sum(dot(o, w_p, ((1,), (0,))))
    factor_two = rms_factor(middle)
    normed_feed = (middle * factor_two * gain_two).astype(bf16)

    def feed(wg, wu, wd):
        gate = dot(normed_feed, wg, ((1,), (0,)))
        up = dot(normed_feed, wu, ((1,), (0,)))
        sigmoid = jax.nn.sigmoid(gate)
        silu = gate * sigmoid
        hidden = (silu * up).astype(bf16)
        hidden_in = dot(cot, wd, ((1,), (1,)))
        gate_back = (hidden_in * up * sigmoid * (1.0 + gate * (1.0 - sigmoid))).astype(bf16)
        up_back = (hidden_in * silu).astype(bf16)
        feed_rows = dot(gate_back, wg, ((1,), (1,))) + dot(up_back, wu, ((1,), (1,)))
        return hidden, gate_back, up_back, feed_rows

    hidden_m, gate_back_m, up_back_m, feed_m = feed(wg_mine, wu_mine, wd_mine)
    hidden_o, gate_back_o, up_back_o, feed_o = feed(wg_other, wu_other, wd_other)
    feed_in = paired_tensor_sum(feed_m + feed_o)

    def summed(give, keep, axis):
        both = (keep + swap_ctx(give.astype(bf16)).astype(f32)).astype(bf16)
        share = lax.psum_scatter(both, "fsdp", scatter_dimension=axis, tiled=True)
        return share

    def whole_again(share, axis):
        return ordered(share, swap_ctx(share), axis).astype(f32)

    contract_rows = ((0,), (0,))
    gate_share = summed(
        dot(normed_feed, gate_back_o, contract_rows), dot(normed_feed, gate_back_m, contract_rows), 0
    )
    up_share = summed(
        dot(normed_feed, up_back_o, contract_rows), dot(normed_feed, up_back_m, contract_rows), 0
    )
    down_part = jnp.concatenate(
        [dot(hidden_m, cot, contract_rows), dot(hidden_o, cot, contract_rows)], axis=0
    ).astype(bf16)
    down_share = lax.psum_scatter(down_part, "fsdp", scatter_dimension=1, tiled=True)
    down_away = swap_ctx(down_share)
    size = down_share.shape[0] // 2
    down_mine = down_share[:size].astype(f32) + down_away[size:].astype(f32)
    down_other = down_share[size:].astype(f32) + down_away[:size].astype(f32)
    down_grad = ordered(down_mine, down_other, 0)

    layer_output = (
        middle
        + paired_tensor_sum(
            dot(hidden_m, wd_mine, ((1,), (0,))) + dot(hidden_o, wd_other, ((1,), (0,)))
        )
    ).astype(bf16)

    gain_two_term = jnp.sum(feed_in * middle * factor_two, axis=0)
    middle_grad = cot.astype(f32) + rms_back(middle, factor_two, gain_two, feed_in)
    middle_low = middle_grad.astype(bf16)
    project_part = dot(o, middle_low, contract_rows)
    project_part = project_part.reshape(-1, LANES, width)[:, :HD].reshape(-1, width)
    rows_half = project_part.shape[0] // 2
    project_share = summed(project_part[rows_half:], project_part[:rows_half], 1)
    d_out = dot(middle_low, w_p, ((1,), (1,))).astype(bf16)
    q_low, dk, dv = attend_back(meta, q, kv_all, o, d_out, lse, cosine, sine, tile)
    d_kv = jnp.concatenate([dk, dv], axis=0)
    d_kv_away = swap_ctx(d_kv[:, rows:])
    d_kv = [
        d_kv[slab, :rows].astype(f32) + d_kv_away[slab ^ 1].astype(f32) for slab in range(4)
    ]

    def turn_back(part):
        return part * cosine - jnp.concatenate([part[:, SPAN:], part[:, :SPAN]], axis=1) * sine

    low_mine = jnp.concatenate(
        [q_low[:, : 2 * LANES], turn_back(d_kv[0]).astype(bf16), d_kv[2].astype(bf16)], axis=1
    )
    low_other = jnp.concatenate(
        [q_low[:, 2 * LANES :], turn_back(d_kv[1]).astype(bf16), d_kv[3].astype(bf16)], axis=1
    )
    half_width = low_mine.shape[1]
    normed_in = paired_tensor_sum(
        dot(low_mine, w_qkv[:, :half_width], ((1,), (1,)))
        + dot(low_other, w_qkv[:, half_width:], ((1,), (1,)))
    )
    close_mine = dot(low_mine, spread, ((1,), (1,))).astype(bf16)
    close_other = dot(low_other, spread, ((1,), (1,))).astype(bf16)
    qkv_share = summed(
        dot(normed, close_other, contract_rows), dot(normed, close_mine, contract_rows), 0
    )
    qkv_away = swap_ctx(qkv_share)
    shares = [
        ordered(a, b, 1).astype(f32) for a, b in zip(parts(qkv_share), parts(qkv_away))
    ]

    inputs = x.astype(f32)
    factor_one = rms_factor(inputs)
    gain_one_term = jnp.sum(normed_in * inputs * factor_one, axis=0)
    tokens_grad = (middle_grad + rms_back(inputs, factor_one, gain_one, normed_in)).astype(bf16)
    gain_terms = jnp.stack([gain_one_term, gain_two_term])
    gain_terms = lax.psum_scatter(
        gain_terms + swap_ctx(gain_terms), "fsdp", scatter_dimension=1, tiled=True
    )
    return (
        layer_output[None],
        tokens_grad[None],
        gain_terms[0],
        shares[0],
        shares[1],
        shares[2],
        whole_again(project_share, 0),
        gain_terms[1],
        whole_again(gate_share, 1),
        whole_again(up_share, 1),
        down_grad,
    )


def solution(mesh):
    paired = mesh.shape["ctx"] == 2 and mesh.shape["tp"] == 4 and mesh.shape["fsdp"] == 4
    return jax.shard_map(
        paired_body if paired else general_body,
        mesh=mesh,
        in_specs=(
            P("fsdp", "ctx", None),
            P("fsdp"),
            P("fsdp", "ctx"),
            P("fsdp"),
            P("fsdp", "tp"),
            P("fsdp", "tp"),
            P("fsdp", "tp"),
            P("tp", "fsdp"),
            P("fsdp"),
            P("fsdp", "tp"),
            P("fsdp", "tp"),
            P("tp", "fsdp"),
            P("fsdp", "ctx", None),
        ),
        out_specs=(
            P("fsdp", "ctx", None),
            P("fsdp", "ctx", None),
            P("fsdp"),
            P("fsdp", "tp"),
            P("fsdp", "tp"),
            P("fsdp", "tp"),
            P("tp", "fsdp"),
            P("fsdp"),
            P("fsdp", "tp"),
            P("fsdp", "tp"),
            P("tp", "fsdp"),
        ),
        check_vma=False,
    )
```

```python
import functools
import math

import jax
import jax.numpy as jnp
import numpy as np
from jax import lax
from jax.experimental import pallas as pl
from jax.experimental.pallas import tpu as pltpu
from jax.sharding import PartitionSpec as P

HQ = 16
KVH = 8
HD = 96


EPSILON = 1e-05
ROPE_BASE = 100000.0
NEGATIVE = -1e30


def natural_index(stored, block_len, pair_count):
    device = stored // (2 * block_len)
    second_half = stored // block_len % 2
    within = stored % block_len
    block_id = jnp.where(second_half == 0, device, 2 * pair_count - 1 - device)
    return block_id * block_len + within


def rotate(values, cosine_table, sine_table):
    half_width = values.shape[-1] // 2
    leading = values[..., :half_width]
    trailing = values[..., half_width:]
    return jnp.concatenate(
        [
            leading * cosine_table - trailing * sine_table,
            trailing * cosine_table + leading * sine_table,
        ],
        axis=-1,
    )


def rotate_back(incoming, cosine_table, sine_table):
    half_width = incoming.shape[-1] // 2
    leading = incoming[..., :half_width]
    trailing = incoming[..., half_width:]
    return jnp.concatenate(
        [
            leading * cosine_table + trailing * sine_table,
            trailing * cosine_table - leading * sine_table,
        ],
        axis=-1,
    )


def rms_factor(values):
    return lax.rsqrt(jnp.mean(values * values, axis=-1, keepdims=True) + EPSILON)


def rms_back(values, factor, gain_row, incoming):
    scaled = gain_row * incoming
    return factor * scaled - values * factor**3 * jnp.mean(scaled * values, axis=-1, keepdims=True)


def tensor_sum(term_rows):
    return lax.psum(term_rows.astype(jnp.bfloat16), "tp").astype(jnp.float32)


def general_body(
    tokens,
    prefix_len,
    positions,
    gain_attend,
    w_query,
    w_key,
    w_value,
    w_project,
    gain_feed,
    w_gate,
    w_up,
    w_down,
    cotangent,
):
    (
        gain_one,
        query_weight_whole,
        key_weight_whole,
        value_weight_whole,
        project_weight_whole,
        gain_two,
        gate_weight_whole,
        up_weight_whole,
        down_weight_whole,
    ) = (
        lax.all_gather(gain_attend, "fsdp", axis=0, tiled=True),
        lax.all_gather(w_query, "fsdp", axis=0, tiled=True),
        lax.all_gather(w_key, "fsdp", axis=0, tiled=True),
        lax.all_gather(w_value, "fsdp", axis=0, tiled=True),
        lax.all_gather(w_project, "fsdp", axis=1, tiled=True),
        lax.all_gather(gain_feed, "fsdp", axis=0, tiled=True),
        lax.all_gather(w_gate, "fsdp", axis=0, tiled=True),
        lax.all_gather(w_up, "fsdp", axis=0, tiled=True),
        lax.all_gather(w_down, "fsdp", axis=1, tiled=True),
    )
    seq_count, rows_local, _ = tokens.shape
    pair_count = lax.axis_size("ctx")
    block_len = rows_local // 2
    query_width = query_weight_whole.shape[1]
    kv_width = key_weight_whole.shape[1]
    query_heads = query_width // HD
    kv_heads = kv_width // HD
    group_size = HQ // KVH
    score_scale = HD ** (-0.5)
    frequency = ROPE_BASE ** (-(jnp.arange(HD // 2, dtype=jnp.float32) * 2.0 / HD))
    angles = positions.astype(jnp.float32)[:, :, None] * frequency
    cosine_table = jnp.cos(angles)[:, :, None, :]
    sine_table = jnp.sin(angles)[:, :, None, :]
    stored_rows = lax.axis_index("ctx") * rows_local + jnp.arange(rows_local, dtype=jnp.int32)
    query_order = natural_index(stored_rows, block_len, pair_count)

    def visible_mask(key_order):
        causal = key_order[None, None, :] <= query_order[None, :, None]
        opened = key_order[None, None, :] < prefix_len[:, None, None]
        return (causal | opened)[:, :, None, None, :]

    inputs = tokens.astype(jnp.float32)
    factor_one = rms_factor(inputs)
    normed_hidden = (inputs * factor_one * gain_one.astype(jnp.float32)).astype(jnp.bfloat16)
    query_projected = jnp.einsum(
        "rxc,cf->rxf", normed_hidden, query_weight_whole, preferred_element_type=jnp.float32
    )
    key_projected = jnp.einsum(
        "rxc,cf->rxf", normed_hidden, key_weight_whole, preferred_element_type=jnp.float32
    )
    value_projected = jnp.einsum(
        "rxc,cf->rxf", normed_hidden, value_weight_whole, preferred_element_type=jnp.float32
    )
    queries = (
        rotate(
            query_projected.reshape(seq_count, rows_local, query_heads, HD),
            cosine_table,
            sine_table,
        )
        .astype(jnp.bfloat16)
        .reshape(seq_count, rows_local, kv_heads, group_size, HD)
    )
    keys_rot = (
        rotate(key_projected.reshape(seq_count, rows_local, kv_heads, HD), cosine_table, sine_table)
        .astype(jnp.bfloat16)
        .reshape(seq_count, rows_local, kv_width)
    )
    values_low = value_projected.astype(jnp.bfloat16)
    stat_shape = (seq_count, rows_local, kv_heads, group_size)
    initial = (
        jnp.full(stat_shape, NEGATIVE, jnp.float32),
        jnp.zeros(stat_shape, jnp.float32),
        jnp.zeros(stat_shape + (HD,), jnp.float32),
    )
    key_piece = lax.all_gather(keys_rot, "ctx", axis=1, tiled=True)
    value_piece = lax.all_gather(values_low, "ctx", axis=1, tiled=True)
    key_total = key_piece.shape[1]
    span_rows = math.gcd(key_total, rows_local)

    def one_span(span_index, running):
        run_max, run_sum, run_acc = running
        span_start = span_index * span_rows
        key_rows = lax.dynamic_slice_in_dim(key_piece, span_start, span_rows, 1).reshape(
            seq_count, span_rows, kv_heads, HD
        )
        value_rows = lax.dynamic_slice_in_dim(value_piece, span_start, span_rows, 1).reshape(
            seq_count, span_rows, kv_heads, HD
        )
        key_order = natural_index(
            span_start + jnp.arange(span_rows, dtype=jnp.int32), block_len, pair_count
        )
        visible = visible_mask(key_order)
        scores = (
            jnp.einsum("slhgd,skhd->slhgk", queries, key_rows, preferred_element_type=jnp.float32)
            * score_scale
        )
        new_max = jnp.maximum(run_max, jnp.max(jnp.where(visible, scores, NEGATIVE), axis=-1))
        weights_raw = jnp.where(visible, jnp.exp(scores - new_max[..., None]), 0.0)
        rescale = jnp.exp(run_max - new_max)
        run_sum = run_sum * rescale + jnp.sum(weights_raw, axis=-1)
        run_acc = run_acc * rescale[..., None] + jnp.einsum(
            "slhgk,skhd->slhgd",
            weights_raw.astype(jnp.bfloat16),
            value_rows,
            preferred_element_type=jnp.float32,
        )
        return (new_max, run_sum, run_acc)

    run_max, run_sum, run_acc = lax.fori_loop(0, key_total // span_rows, one_span, initial)
    attended = run_acc / run_sum[..., None]
    log_total = run_max + jnp.log(run_sum)
    attended_reduced = attended.reshape(seq_count, rows_local, query_width).astype(jnp.bfloat16)
    project_rows = jnp.einsum(
        "hxz,zm->hxm", attended_reduced, project_weight_whole, preferred_element_type=jnp.float32
    )
    middle = inputs + tensor_sum(project_rows)
    factor_two = rms_factor(middle)
    normed_feed_input = (middle * factor_two * gain_two.astype(jnp.float32)).astype(jnp.bfloat16)
    gate_activation = jnp.einsum(
        "qeh,hj->qej", normed_feed_input, gate_weight_whole, preferred_element_type=jnp.float32
    )
    up_activation = jnp.einsum(
        "qeh,hj->qej", normed_feed_input, up_weight_whole, preferred_element_type=jnp.float32
    )
    sigmoid_gate = jax.nn.sigmoid(gate_activation)
    silu_gate = gate_activation * sigmoid_gate
    hidden_state = (silu_gate * up_activation).astype(jnp.bfloat16)
    down_output_rows = jnp.einsum(
        "nct,tm->ncm", hidden_state, down_weight_whole, preferred_element_type=jnp.float32
    )
    layer_output = (middle + tensor_sum(down_output_rows)).astype(jnp.bfloat16)
    (
        gain_one,
        query_weight_whole,
        key_weight_whole,
        value_weight_whole,
        project_weight_whole,
        gain_two,
        gate_weight_whole,
        up_weight_whole,
        down_weight_whole,
    ) = (
        lax.all_gather(gain_attend, "fsdp", axis=0, tiled=True),
        lax.all_gather(w_query, "fsdp", axis=0, tiled=True),
        lax.all_gather(w_key, "fsdp", axis=0, tiled=True),
        lax.all_gather(w_value, "fsdp", axis=0, tiled=True),
        lax.all_gather(w_project, "fsdp", axis=1, tiled=True),
        lax.all_gather(gain_feed, "fsdp", axis=0, tiled=True),
        lax.all_gather(w_gate, "fsdp", axis=0, tiled=True),
        lax.all_gather(w_up, "fsdp", axis=0, tiled=True),
        lax.all_gather(w_down, "fsdp", axis=1, tiled=True),
    )
    hidden_grad = jnp.einsum(
        "ehv,iv->ehi", cotangent, down_weight_whole, preferred_element_type=jnp.float32
    )
    down_weight_part = jnp.einsum(
        "gqa,gqz->az", hidden_state, cotangent, preferred_element_type=jnp.float32
    )
    gate_reduced = (
        hidden_grad * up_activation * sigmoid_gate * (1.0 + gate_activation * (1.0 - sigmoid_gate))
    ).astype(jnp.bfloat16)
    up_reduced = (hidden_grad * silu_gate).astype(jnp.bfloat16)
    gate_weight_part = jnp.einsum(
        "bic,big->cg", normed_feed_input, gate_reduced, preferred_element_type=jnp.float32
    )
    up_weight_part = jnp.einsum(
        "bic,big->cg", normed_feed_input, up_reduced, preferred_element_type=jnp.float32
    )
    feed_rows = jnp.einsum(
        "vte,ce->vtc", gate_reduced, gate_weight_whole, preferred_element_type=jnp.float32
    ) + jnp.einsum("vte,ce->vtc", up_reduced, up_weight_whole, preferred_element_type=jnp.float32)
    feed_in = tensor_sum(feed_rows)
    gain_two_term = jnp.sum(feed_in * middle * factor_two, axis=(0, 1))
    middle_grad = cotangent.astype(jnp.float32) + rms_back(
        middle, factor_two, gain_two.astype(jnp.float32), feed_in
    )
    middle_reduced = middle_grad.astype(jnp.bfloat16)
    project_term = jnp.einsum(
        "xeh,xec->hc", attended_reduced, middle_reduced, preferred_element_type=jnp.float32
    )
    attended_grad = (
        jnp.einsum(
            "vhk,nk->vhn", middle_reduced, project_weight_whole, preferred_element_type=jnp.float32
        )
        .astype(jnp.bfloat16)
        .reshape(seq_count, rows_local, kv_heads, group_size, HD)
    )
    row_delta = jnp.sum(attended_grad.astype(jnp.float32) * attended, axis=-1)
    whole_keys, whole_values = (
        lax.all_gather(keys_rot[None], "ctx", axis=0, tiled=True),
        lax.all_gather(values_low[None], "ctx", axis=0, tiled=True),
    )

    def key_block(grad_acc, block_items):
        key_rows, value_rows, block_index = block_items
        key_rows = key_rows.reshape(seq_count, rows_local, kv_heads, HD)
        value_rows = value_rows.reshape(seq_count, rows_local, kv_heads, HD)
        key_order = natural_index(
            block_index * rows_local + jnp.arange(rows_local, dtype=jnp.int32),
            block_len,
            pair_count,
        )
        visible = visible_mask(key_order)
        scores = (
            jnp.einsum("slhgd,skhd->slhgk", queries, key_rows, preferred_element_type=jnp.float32)
            * score_scale
        )
        weights_norm = jnp.where(visible, jnp.exp(scores - log_total[..., None]), 0.0)
        prob_grad = jnp.einsum(
            "slhgd,skhd->slhgk", attended_grad, value_rows, preferred_element_type=jnp.float32
        )
        score_grad = (weights_norm * (prob_grad - row_delta[..., None])).astype(jnp.bfloat16)
        grad_acc = (
            grad_acc
            + jnp.einsum(
                "slhgk,skhd->slhgd", score_grad, key_rows, preferred_element_type=jnp.float32
            )
            * score_scale
        )
        key_grad = (
            jnp.einsum("slhgk,slhgd->skhd", score_grad, queries, preferred_element_type=jnp.float32)
            * score_scale
        )
        value_grad = jnp.einsum(
            "slhgk,slhgd->skhd",
            weights_norm.astype(jnp.bfloat16),
            attended_grad,
            preferred_element_type=jnp.float32,
        )
        return (
            grad_acc,
            (
                key_grad.reshape(seq_count, rows_local, kv_width),
                value_grad.reshape(seq_count, rows_local, kv_width),
            ),
        )

    block_ids = jnp.arange(pair_count, dtype=jnp.int32)
    query_grad, (key_terms, value_terms) = lax.scan(
        key_block, jnp.zeros(stat_shape + (HD,), jnp.float32), (whole_keys, whole_values, block_ids)
    )
    key_sum, value_sum = (
        lax.psum_scatter(
            key_terms.astype(jnp.bfloat16), "ctx", scatter_dimension=0, tiled=True
        ).astype(jnp.float32),
        lax.psum_scatter(
            value_terms.astype(jnp.bfloat16), "ctx", scatter_dimension=0, tiled=True
        ).astype(jnp.float32),
    )
    key_reduced = (
        rotate_back(
            key_sum[0].reshape(seq_count, rows_local, kv_heads, HD), cosine_table, sine_table
        )
        .astype(jnp.bfloat16)
        .reshape(seq_count, rows_local, kv_width)
    )
    value_backward = value_sum[0].astype(jnp.bfloat16)
    query_reduced = (
        rotate_back(
            query_grad.reshape(seq_count, rows_local, query_heads, HD), cosine_table, sine_table
        )
        .astype(jnp.bfloat16)
        .reshape(seq_count, rows_local, query_width)
    )
    query_weight_part = jnp.einsum(
        "prb,pro->bo", normed_hidden, query_reduced, preferred_element_type=jnp.float32
    )
    key_weight_part = jnp.einsum(
        "prb,pro->bo", normed_hidden, key_reduced, preferred_element_type=jnp.float32
    )
    value_weight_part = jnp.einsum(
        "prb,pro->bo", normed_hidden, value_backward, preferred_element_type=jnp.float32
    )
    normed_rows = (
        jnp.einsum(
            "kjw,iw->kji", query_reduced, query_weight_whole, preferred_element_type=jnp.float32
        )
        + jnp.einsum(
            "kjw,iw->kji", key_reduced, key_weight_whole, preferred_element_type=jnp.float32
        )
        + jnp.einsum(
            "kjw,iw->kji", value_backward, value_weight_whole, preferred_element_type=jnp.float32
        )
    )
    normed_grad = tensor_sum(normed_rows)
    gain_one_term = jnp.sum(normed_grad * inputs * factor_one, axis=(0, 1))
    tokens_grad = (
        middle_grad + rms_back(inputs, factor_one, gain_one.astype(jnp.float32), normed_grad)
    ).astype(jnp.bfloat16)
    (
        part_one,
        part_query,
        part_key,
        part_value,
        part_project,
        part_two,
        part_gate,
        part_up,
        part_down,
    ) = (
        lax.psum_scatter(gain_one_term, ("fsdp", "ctx"), scatter_dimension=0, tiled=True),
        lax.psum_scatter(query_weight_part, ("fsdp", "ctx"), scatter_dimension=0, tiled=True),
        lax.psum_scatter(key_weight_part, ("fsdp", "ctx"), scatter_dimension=0, tiled=True),
        lax.psum_scatter(value_weight_part, ("fsdp", "ctx"), scatter_dimension=0, tiled=True),
        lax.psum_scatter(project_term, ("fsdp", "ctx"), scatter_dimension=1, tiled=True),
        lax.psum_scatter(gain_two_term, ("fsdp", "ctx"), scatter_dimension=0, tiled=True),
        lax.psum_scatter(gate_weight_part, ("fsdp", "ctx"), scatter_dimension=0, tiled=True),
        lax.psum_scatter(up_weight_part, ("fsdp", "ctx"), scatter_dimension=0, tiled=True),
        lax.psum_scatter(down_weight_part, ("fsdp", "ctx"), scatter_dimension=1, tiled=True),
    )
    reduced = (
        lax.all_gather(part_one.astype(jnp.bfloat16), "ctx", axis=0, tiled=True).astype(
            part_one.dtype
        ),
        lax.all_gather(part_query.astype(jnp.bfloat16), "ctx", axis=0, tiled=True).astype(
            part_query.dtype
        ),
        lax.all_gather(part_key.astype(jnp.bfloat16), "ctx", axis=0, tiled=True).astype(
            part_key.dtype
        ),
        lax.all_gather(part_value.astype(jnp.bfloat16), "ctx", axis=0, tiled=True).astype(
            part_value.dtype
        ),
        lax.all_gather(part_project.astype(jnp.bfloat16), "ctx", axis=1, tiled=True).astype(
            part_project.dtype
        ),
        lax.all_gather(part_two.astype(jnp.bfloat16), "ctx", axis=0, tiled=True).astype(
            part_two.dtype
        ),
        lax.all_gather(part_gate.astype(jnp.bfloat16), "ctx", axis=0, tiled=True).astype(
            part_gate.dtype
        ),
        lax.all_gather(part_up.astype(jnp.bfloat16), "ctx", axis=0, tiled=True).astype(
            part_up.dtype
        ),
        lax.all_gather(part_down.astype(jnp.bfloat16), "ctx", axis=1, tiled=True).astype(
            part_down.dtype
        ),
    )
    return (layer_output, tokens_grad) + tuple(reduced)


LANES = 128
HALF = HD // 2
SPAN = LANES // 2
LOG2E = math.log2(math.e)
VMEM_BYTES = 56 * 1024 * 1024


def swap_ctx(block):
    return lax.ppermute(block, "ctx", [(0, 1), (1, 0)])


def swap_core(block):
    return lax.ppermute(block, "tp", [(0, 1), (1, 0), (2, 3), (3, 2)])


def swap_chip(block):
    return lax.ppermute(block, "tp", [(0, 2), (2, 0), (1, 3), (3, 1)])


def paired_tensor_sum(term_rows):
    half = term_rows.shape[0] // 2
    core = lax.axis_index("tp") % 2
    low = term_rows.astype(jnp.bfloat16)
    keep = lax.dynamic_slice_in_dim(low, core * half, half, 0)
    give = lax.dynamic_slice_in_dim(low, (1 - core) * half, half, 0)
    chip_part = (keep.astype(jnp.float32) + swap_core(give).astype(jnp.float32)).astype(jnp.bfloat16)
    total = (chip_part.astype(jnp.float32) + swap_chip(chip_part).astype(jnp.float32)).astype(
        jnp.bfloat16
    )
    other = swap_core(total)
    return jnp.where(
        core == 0,
        jnp.concatenate([total, other], axis=0),
        jnp.concatenate([other, total], axis=0),
    )


def dot(a, b, contract):
    return lax.dot_general(a, b, (contract, ((), ())), preferred_element_type=jnp.float32)


def block_kinds(meta_ref, query_tile, key_tile, q_start, k_start):
    prefix = meta_ref[0]
    whole = (k_start + (key_tile - 1) <= q_start) | (k_start + key_tile <= prefix)
    nothing = (k_start > q_start + (query_tile - 1)) & (k_start >= prefix)
    return prefix, whole, nothing


def mask_scores(scores, prefix, q_start, k_start, query_tile):
    key_ids = k_start + lax.broadcasted_iota(jnp.int32, scores.shape, 0)
    column = lax.broadcasted_iota(jnp.int32, scores.shape, 1)
    query_ids = q_start + jnp.bitwise_and(column, query_tile - 1)
    return jnp.where((key_ids <= query_ids) | (key_ids < prefix), scores, NEGATIVE)


MESH = pl.DeviceIdType.MESH
GAIN_ROWS = 16
PREFIX_MOST = 1024


def front_kernel(
    prefix_ref,
    x_ref,
    pack_ref,
    rest_ref,
    spread_ref,
    cos_ref,
    sin_ref,
    w_project_ref,
    w_gate_ref,
    w_up_ref,
    w_down_ref,
    normed_ref,
    q_ref,
    kv_ref,
    wide_ref,
    project_ref,
    gain_ref,
    o_ref,
    lse_ref,
    total_ref,
    gate_ref,
    up_ref,
    down_ref,
    buf_ref,
    max_ref,
    sum_ref,
    acc_ref,
    give_ref,
    core_in_ref,
    keep_ref,
    chip_in_ref,
    up_send,
    up_recv,
    down_send,
    down_recv,
    x_send,
    x_recv,
    kv_send,
    kv_recv,
    m_up_send,
    m_up_recv,
    m_down_send,
    m_down_recv,
    m_x_send,
    m_x_recv,
    local_sem,
    core_send,
    core_recv,
    chip_send,
    chip_recv,
    back_send,
    back_recv,
):
    bf16, f32 = jnp.bfloat16, jnp.float32
    planes = buf_ref.shape[0]
    rows, width = x_ref.shape
    depth = width // planes
    half_width = wide_ref.shape[1] // 2
    matrix_rows = rest_ref.shape[0]
    heads_half = project_ref.shape[0] // 2
    units = gate_ref.shape[2]
    z = lax.axis_index("fsdp")
    c = lax.axis_index("ctx")
    t = lax.axis_index("tp")
    core = lax.rem(t, 2)
    across = {"ctx": 1 - c}
    sibling = {"tp": t + 1 - 2 * core}
    partner = {"tp": lax.rem(t + 2, 4)}
    has_above = z < planes - 1
    has_below = z > 0

    def remote(src, dst, send, recv, device):
        return pltpu.make_async_remote_copy(
            src_ref=src,
            dst_ref=dst,
            send_sem=send,
            recv_sem=recv,
            device_id=device,
            device_id_type=MESH,
        )

    project_ref[:, HD:, :] = jnp.zeros(
        (project_ref.shape[0], LANES - HD, project_ref.shape[2]), bf16
    )

    barrier = pltpu.get_barrier_semaphore()

    @pl.when(has_above)
    def _():
        pl.semaphore_signal(barrier, inc=1, device_id={"fsdp": z + 1}, device_id_type=MESH)

    @pl.when(has_below)
    def _():
        pl.semaphore_signal(barrier, inc=1, device_id={"fsdp": z - 1}, device_id_type=MESH)

    for device in (across, sibling, partner):
        pl.semaphore_signal(barrier, inc=1, device_id=device, device_id_type=MESH)

    @pl.when(has_above & has_below)
    def _():
        pl.semaphore_wait(barrier, 5)

    @pl.when(jnp.logical_not(has_above & has_below))
    def _():
        pl.semaphore_wait(barrier, 4)

    def up(k):
        piece = z - k
        src = pack_ref if k == 0 else buf_ref.at[piece, 0]
        return remote(src, buf_ref.at[piece, 0], up_send.at[k], up_recv.at[k], {"fsdp": z + 1})

    def down(k):
        piece = z + k
        src = pack_ref if k == 0 else buf_ref.at[piece, 0]
        return remote(src, buf_ref.at[piece, 0], down_send.at[k], down_recv.at[k], {"fsdp": z - 1})

    def from_below(k):
        slot = buf_ref.at[z - 1 - k, 0]
        return remote(slot, slot, up_send.at[k], up_recv.at[k], {"fsdp": z - 1})

    def from_above(k):
        slot = buf_ref.at[z + 1 + k, 0]
        return remote(slot, slot, down_send.at[k], down_recv.at[k], {"fsdp": z + 1})

    def sideways(side, k):
        piece = z - k if side == 0 else z + k
        matrix = pl.ds(0, matrix_rows)
        return remote(
            buf_ref.at[piece, 0, matrix],
            buf_ref.at[piece, 1, matrix],
            x_send.at[side, k],
            x_recv.at[side, k],
            across,
        )

    def own_half(m, half):
        if m == 0:
            return w_gate_ref.at[:, pl.ds(pl.multiple_of(half * units, units), units)]
        if m == 1:
            return w_up_ref.at[:, pl.ds(pl.multiple_of(half * units, units), units)]
        if m == 2:
            return w_down_ref.at[pl.ds(pl.multiple_of(half * units, units), units), :]
        return w_project_ref.at[pl.ds(half * heads_half, heads_half)]

    def slot(m, which, piece):
        at = pl.ds(pl.multiple_of(piece * depth, depth), depth)
        if m == 0:
            return gate_ref.at[which, at]
        if m == 1:
            return up_ref.at[which, at]
        if m == 2:
            return down_ref.at[which, :, at]
        return project_ref.at[pl.ds(which * heads_half, heads_half), pl.ds(0, HD), at]

    def m_up(m, k):
        piece = z - k
        src = own_half(m, c) if k == 0 else slot(m, 0, piece)
        return remote(
            src, slot(m, 0, piece), m_up_send.at[m, k], m_up_recv.at[m, k], {"fsdp": z + 1}
        )

    def m_down(m, k):
        piece = z + k
        src = own_half(m, c) if k == 0 else slot(m, 0, piece)
        return remote(
            src, slot(m, 0, piece), m_down_send.at[m, k], m_down_recv.at[m, k], {"fsdp": z - 1}
        )

    def m_below(m, k):
        at = slot(m, 0, z - 1 - k)
        return remote(at, at, m_up_send.at[m, k], m_up_recv.at[m, k], {"fsdp": z - 1})

    def m_above(m, k):
        at = slot(m, 0, z + 1 + k)
        return remote(at, at, m_down_send.at[m, k], m_down_recv.at[m, k], {"fsdp": z + 1})

    def m_side(m, side, k):
        piece = z - k if side == 0 else z + k
        return remote(
            slot(m, 0, piece),
            slot(m, 1, piece),
            m_x_send.at[m, side, k],
            m_x_recv.at[m, side, k],
            across,
        )

    groups = ((3, 0), (1,), (2,))

    def relay(group, k):
        for m in groups[group]:

            @pl.when(z - k >= 0)
            def _():
                m_below(m, k - 1).wait_recv()
                if k < planes - 1:

                    @pl.when(has_above)
                    def _():
                        m_up(m, k).start()

            @pl.when(z + k <= planes - 1)
            def _():
                m_above(m, k - 1).wait_recv()
                if k < planes - 1:

                    @pl.when(has_below)
                    def _():
                        m_down(m, k).start()

    def cross(group, k):
        for m in groups[group]:

            @pl.when(z - k >= 0)
            def _():
                m_side(m, 0, k).start()

            @pl.when(z + k <= planes - 1)
            def _():
                m_side(m, 1, k).start()

    def crossed(m, k):
        @pl.when(z - k >= 0)
        def _():
            m_side(m, 0, k).wait_recv()

        @pl.when(z + k <= planes - 1)
        def _():
            m_side(m, 1, k).wait_recv()

    def local(m, which):
        half = c if which == 0 else 1 - c
        return pltpu.make_async_copy(own_half(m, half), slot(m, which, z), local_sem.at[m, which])

    spread = spread_ref[...]

    def place(block, piece, which):
        at = pl.ds(pl.multiple_of(piece * depth, depth), depth)
        wide_ref[at, which * half_width : (which + 1) * half_width] = dot(
            block[:depth], spread, ((1,), (0,))
        ).astype(bf16)

    def place_gain(block, piece):
        at = pl.ds(pl.multiple_of(piece * depth, depth), depth)
        gain_ref[:, at] = block[matrix_rows:]

    @pl.when(has_above)
    def _():
        up(0).start()

    @pl.when(has_below)
    def _():
        down(0).start()

    for m in (3, 0, 1, 2):
        for which in range(2):
            local(m, which).start()
    place(pack_ref, z, 0)
    place_gain(pack_ref, z)
    place(rest_ref, z, 1)

    for k in range(1, planes):
        below = z - k >= 0
        above = z + k <= planes - 1

        @pl.when(below)
        def _():
            from_below(k - 1).wait_recv()
            if k < planes - 1:

                @pl.when(has_above)
                def _():
                    up(k).start()

            sideways(0, k).start()

        @pl.when(above)
        def _():
            from_above(k - 1).wait_recv()
            if k < planes - 1:

                @pl.when(has_below)
                def _():
                    down(k).start()

            sideways(1, k).start()

        if k == max(1, planes - 2):
            for m in (3, 0, 1, 2):

                @pl.when(has_above)
                def _():
                    m_up(m, 0).start()

                @pl.when(has_below)
                def _():
                    m_down(m, 0).start()

        @pl.when(below)
        def _():
            place(buf_ref.at[z - k, 0], z - k, 0)
            place_gain(buf_ref.at[z - k, 0], z - k)

        @pl.when(above)
        def _():
            place(buf_ref.at[z + k, 0], z + k, 0)
            place_gain(buf_ref.at[z + k, 0], z + k)

    tile = 128
    gain = gain_ref[0:1, :].astype(f32)

    def norm_rows(i, carry):
        at = pl.ds(pl.multiple_of(i * tile, tile), tile)
        x = x_ref[at, :].astype(f32)
        factor = lax.rsqrt(jnp.mean(x * x, axis=-1, keepdims=True) + EPSILON)
        normed_ref[at, :] = (x * factor * gain).astype(bf16)
        return carry

    lax.fori_loop(0, rows // tile, norm_rows, 0)

    for k in range(1, planes):

        @pl.when(z - k >= 0)
        def _():
            sideways(0, k).wait_recv()
            place(buf_ref.at[z - k, 1], z - k, 1)

        @pl.when(z + k <= planes - 1)
        def _():
            sideways(1, k).wait_recv()
            place(buf_ref.at[z + k, 1], z + k, 1)

    block = 256

    def turn(part, at):
        return part * cos_ref[at, :] + pltpu.roll(part, SPAN, 1) * sin_ref[at, :]

    def key_rows(i, carry):
        at = pl.ds(pl.multiple_of(i * block, block), block)
        for which in range(2):
            lane = which * half_width + 2 * LANES
            both = dot(normed_ref[at, :], wide_ref[:, lane : lane + 2 * LANES], ((1,), (0,)))
            kv_ref[which, at, :] = turn(both[:, :LANES], at).astype(bf16)
            kv_ref[2 + which, at, :] = both[:, LANES:].astype(bf16)
        return carry

    lax.fori_loop(0, rows // block, key_rows, 0)

    def exchange(slab):
        return remote(
            kv_ref.at[slab, pl.ds(0, rows)],
            kv_ref.at[slab ^ 1, pl.ds(rows, rows)],
            kv_send.at[slab],
            kv_recv.at[slab ^ 1],
            across,
        )

    for slab in range(4):
        exchange(slab).start()
    relay(0, 1)
    scale = HD ** (-0.5) * LOG2E

    def query_rows(i, carry):
        at = pl.ds(pl.multiple_of(i * block, block), block)
        for which in range(2):
            lane = which * half_width
            both = dot(normed_ref[at, :], wide_ref[:, lane : lane + 2 * LANES], ((1,), (0,)))
            for head in range(2):
                part = turn(both[:, head * LANES : (head + 1) * LANES], at)
                lane = (2 * which + head) * LANES
                q_ref[at, lane : lane + LANES] = (part * scale).astype(bf16)
        return carry

    lax.fori_loop(0, rows // block, query_rows, 0)
    relay(1, 1)

    tiles = rows // block
    tiles_of_block = tiles // 2
    prefix = prefix_ref[0]
    max_ref[...] = jnp.full_like(max_ref, NEGATIVE)
    sum_ref[...] = jnp.zeros_like(sum_ref)
    acc_ref[...] = jnp.zeros_like(acc_ref)

    def start_of(device, tile_index):
        second = tile_index // tiles_of_block
        block_id = device + second * (3 - 2 * device)
        return (block_id * tiles_of_block + tile_index % tiles_of_block) * block

    def attend_group(g, away):
        key_device = 1 - c if away else c

        def one_tile(i, carry):
            at = pl.ds(pl.multiple_of(i * block, block), block)
            lane = 2 * g * LANES
            queries = jnp.concatenate(
                [q_ref[at, lane : lane + LANES], q_ref[at, lane + LANES : lane + 2 * LANES]],
                axis=0,
            )
            q_start = start_of(c, i)
            u = g * tiles + i

            def absorb(scores, values):
                old = max_ref[u]
                new = jnp.maximum(old, jnp.max(scores, axis=0, keepdims=True))
                weights = jnp.exp2(scores - new)
                rescale = jnp.exp2(old - new)
                max_ref[u] = new
                sum_ref[u] = sum_ref[u] * rescale + jnp.sum(weights, axis=0, keepdims=True)
                acc_ref[u] = acc_ref[u] * rescale + dot(values, weights.astype(bf16), ((0,), (0,)))

            def one(j, carry):
                k_start = start_of(key_device, j)
                first = (tiles if away else 0) + j
                keys_at = pl.ds(pl.multiple_of(first * block, block), block)
                whole = k_start + (block - 1) <= q_start
                nothing = (k_start > q_start + (block - 1)) & (k_start >= PREFIX_MOST)

                @pl.when(whole)
                def _():
                    absorb(dot(kv_ref[g, keys_at, :], queries, ((1,), (1,))), kv_ref[2 + g, keys_at, :])

                @pl.when(jnp.logical_not(whole | nothing))
                def _():
                    scores = dot(kv_ref[g, keys_at, :], queries, ((1,), (1,)))
                    absorb(
                        mask_scores(scores, prefix, q_start, k_start, block),
                        kv_ref[2 + g, keys_at, :],
                    )

                return carry

            lax.fori_loop(0, tiles, one, 0)
            if away:
                total = sum_ref[u]
                lse_ref[g, i] = max_ref[u] + jnp.log2(total)
                out = (acc_ref[u] / total).T.astype(bf16)
                o_ref[at, lane : lane + LANES] = out[:block]
                o_ref[at, lane + LANES : lane + 2 * LANES] = out[block:]
            return carry

        lax.fori_loop(0, tiles, one_tile, 0)

    attend_group(0, False)
    relay(2, 1)
    attend_group(1, False)
    relay(0, 2)
    for slab in range(4):
        exchange(slab).wait_recv()
    cross(0, 1)
    cross(1, 1)
    cross(2, 1)
    attend_group(0, True)
    relay(1, 2)
    cross(0, 2)
    cross(1, 2)
    attend_group(1, True)
    relay(2, 2)
    cross(2, 2)

    chunks, chunk, _ = give_ref.shape
    half_rows = rows // 2
    give_start = (1 - core) * half_rows
    keep_start = core * half_rows
    relay(0, 3)
    cross(0, 3)
    for which in range(2):
        local(3, which).wait()
    for k in range(1, planes):
        crossed(3, k)
    w_project = project_ref[...].reshape(project_ref.shape[0] * LANES, width)

    def feature_rows(start):
        at = pl.ds(pl.multiple_of(start, chunk), chunk)
        return dot(o_ref[at, :], w_project, ((1,), (0,)))

    def to_core(i):
        return remote(give_ref.at[i], core_in_ref.at[i], core_send.at[i], core_recv.at[i], sibling)

    def to_chip(i):
        return remote(keep_ref.at[i], chip_in_ref.at[i], chip_send.at[i], chip_recv.at[i], partner)

    def back(i, start):
        at = pl.ds(pl.multiple_of(start + i * chunk, chunk), chunk)
        return remote(
            total_ref.at[at], total_ref.at[at], back_send.at[i], back_recv.at[i], sibling
        )

    for i in range(chunks):
        give_ref[i] = feature_rows(give_start + i * chunk).astype(bf16)
        to_core(i).start()
    for i in range(chunks):
        kept = feature_rows(keep_start + i * chunk)
        to_core(i).wait_recv()
        keep_ref[i] = (kept + core_in_ref[i].astype(f32)).astype(bf16)
        to_chip(i).start()

    def finish_chunk(i):
        to_chip(i).wait_recv()
        at = pl.ds(pl.multiple_of(keep_start + i * chunk, chunk), chunk)
        total_ref[at, :] = (keep_ref[i].astype(f32) + chip_in_ref[i].astype(f32)).astype(bf16)
        back(i, keep_start).start()

    relay(1, 3)
    cross(1, 3)
    finish_chunk(0)
    relay(2, 3)
    cross(2, 3)
    for i in range(1, chunks):
        finish_chunk(i)

    for k in range(planes - 1):

        @pl.when((z - k >= 0) & has_above)
        def _():
            up(k).wait_send()
            for m in range(4):
                m_up(m, k).wait_send()

        @pl.when((z + k <= planes - 1) & has_below)
        def _():
            down(k).wait_send()
            for m in range(4):
                m_down(m, k).wait_send()

    for k in range(1, planes):

        @pl.when(z - k >= 0)
        def _():
            sideways(0, k).wait_send()
            for m in range(4):
                m_side(m, 0, k).wait_send()

        @pl.when(z + k <= planes - 1)
        def _():
            sideways(1, k).wait_send()
            for m in range(4):
                m_side(m, 1, k).wait_send()

        for m in range(3):
            crossed(m, k)

    for m in range(3):
        for which in range(2):
            local(m, which).wait()
    for slab in range(4):
        exchange(slab).wait_send()
    for i in range(chunks):
        to_core(i).wait_send()
        to_chip(i).wait_send()
        back(i, keep_start).wait_send()
        back(i, give_start).wait_recv()


def front(prefix, x, pack, rest, spread, cosine, sine, w_project, w_gate, w_up, w_down, planes):
    rows, width = x.shape
    half_width = spread.shape[1]
    units = w_gate.shape[1] // 2
    heads = w_project.shape[0]
    block = 256
    tiles = rows // block
    chunks = 4
    chunk = rows // 2 // chunks
    vmem = pl.BlockSpec(memory_space=pltpu.VMEM)
    anywhere = pl.BlockSpec(memory_space=pl.ANY)
    smem = pl.BlockSpec(memory_space=pltpu.SMEM)
    bf16, f32 = jnp.bfloat16, jnp.float32
    dma = pltpu.SemaphoreType.DMA
    piece = pltpu.VMEM((chunks, chunk, width), bf16)
    return pl.pallas_call(
        front_kernel,
        in_specs=[smem] + [vmem] * 6 + [anywhere] * 4,
        out_specs=[vmem] * 9 + [anywhere] * 3,
        out_shape=[
            jax.ShapeDtypeStruct((rows, width), bf16),
            jax.ShapeDtypeStruct((rows, half_width), bf16),
            jax.ShapeDtypeStruct((4, 2 * rows, LANES), bf16),
            jax.ShapeDtypeStruct((width, 2 * half_width), bf16),
            jax.ShapeDtypeStruct((heads, LANES, width), bf16),
            jax.ShapeDtypeStruct((GAIN_ROWS, width), bf16),
            jax.ShapeDtypeStruct((rows, half_width), bf16),
            jax.ShapeDtypeStruct((2, tiles, 1, 2 * block), f32),
            jax.ShapeDtypeStruct((rows, width), bf16),
            jax.ShapeDtypeStruct((2, width, units), bf16),
            jax.ShapeDtypeStruct((2, width, units), bf16),
            jax.ShapeDtypeStruct((2, units, width), bf16),
        ],
        scratch_shapes=[
            pltpu.VMEM((planes, 2, pack.shape[0], pack.shape[1]), bf16),
            pltpu.VMEM((2 * tiles, 1, 2 * block), f32),
            pltpu.VMEM((2 * tiles, 1, 2 * block), f32),
            pltpu.VMEM((2 * tiles, LANES, 2 * block), f32),
            piece,
            piece,
            piece,
            piece,
        ]
        + [dma((planes - 1,))] * 4
        + [dma((2, planes))] * 2
        + [dma((4,))] * 2
        + [dma((4, planes - 1))] * 4
        + [dma((4, 2, planes))] * 2
        + [dma((4, 2))]
        + [dma((chunks,))] * 6,
        compiler_params=pltpu.CompilerParams(
            collective_id=1, has_side_effects=True, vmem_limit_bytes=VMEM_BYTES
        ),
        cost_estimate=pl.CostEstimate(
            flops=120_000_000_000, bytes_accessed=60_000_000, transcendentals=0
        ),
        name="front",
    )(prefix, x, pack, rest, spread, cosine, sine, w_project, w_gate, w_up, w_down)


def attend_back_kernel(
    final,
    meta_ref,
    carry_ref,
    q_ref,
    k_ref,
    v_ref,
    o_ref,
    do_ref,
    lse_ref,
    cos_ref,
    sin_ref,
    dq_ref,
    dk_ref,
    dv_ref,
    delta_ref,
    acc_ref,
):
    query_tiles = lse_ref.shape[1]
    tile = q_ref.shape[0] // query_tiles
    key_tile = k_ref.shape[1]
    j = pl.program_id(1)

    def stacked(ref, i):
        rows = pl.ds(pl.multiple_of(i * tile, tile), tile)
        return jnp.concatenate([ref[rows, :LANES], ref[rows, LANES:]], axis=0)

    @pl.when(j == 0)
    def _():
        acc_ref[...] = carry_ref[0] if final else jnp.zeros_like(acc_ref)

        def one_delta(i, carry):
            product = stacked(o_ref, i).astype(jnp.float32) * stacked(do_ref, i).astype(jnp.float32)
            delta_ref[i] = jnp.sum(product.T, axis=0, keepdims=True)
            return carry

        lax.fori_loop(0, query_tiles, one_delta, 0)

    k_start = meta_ref[1 + query_tiles + (0 if final else pl.num_programs(1)) + j]
    keys = k_ref[0]
    values = v_ref[0]

    def one(i, carry):
        q_start = meta_ref[1 + i]
        prefix, whole, nothing = block_kinds(meta_ref, tile, key_tile, q_start, k_start)

        def some(state):
            dk, dv = state
            queries = stacked(q_ref, i)
            d_out = stacked(do_ref, i)
            scores = dot(keys, queries, ((1,), (1,)))
            scores = lax.cond(
                whole,
                lambda s: s,
                lambda s: mask_scores(s, prefix, q_start, k_start, tile),
                scores,
            )
            weights = jnp.exp2(scores - lse_ref[0, i])
            d_weights = dot(values, d_out, ((1,), (1,)))
            d_scores = (weights * (d_weights - delta_ref[i])).astype(jnp.bfloat16)
            dv = dv + dot(weights.astype(jnp.bfloat16), d_out, ((1,), (0,)))
            dk = dk + dot(d_scores, queries, ((1,), (0,)))
            acc_ref[i] += dot(keys, d_scores, ((0,), (0,)))
            return dk, dv

        return lax.cond(nothing, lambda state: state, some, carry)

    zero = jnp.zeros((key_tile, LANES), jnp.float32)
    dk, dv = lax.fori_loop(0, query_tiles, one, (zero, zero))
    dk_ref[0] = (dk * (1.0 / LOG2E)).astype(jnp.bfloat16)
    dv_ref[0] = dv.astype(jnp.bfloat16)

    @pl.when(j == pl.num_programs(1) - 1)
    def _():
        scale = HD ** (-0.5)
        if not final:
            dq_ref[0] = acc_ref[...]
            return

        def one_out(i, carry):
            rows = pl.ds(pl.multiple_of(i * tile, tile), tile)
            turned = acc_ref[i].T * scale
            for head in range(2):
                part = turned[head * tile : (head + 1) * tile]
                part = part * cos_ref[rows, :] - pltpu.roll(part, SPAN, 1) * sin_ref[rows, :]
                dq_ref[rows, head * LANES : (head + 1) * LANES] = part.astype(jnp.bfloat16)
            return carry

        lax.fori_loop(0, query_tiles, one_out, 0)


def attend_back(meta, carry, q, kv, away, o, d_out, lse, cosine, sine, tile):
    rows, q_width = q.shape
    keys = kv.shape[1] // 2
    groups = q_width // (2 * LANES)
    query_tiles = rows // tile
    key_tiles = keys // tile
    skip = key_tiles if away else 0
    acc_block = pl.BlockSpec((1, query_tiles, LANES, 2 * tile), lambda g, j, m: (g, 0, 0, 0))
    acc_shape = jax.ShapeDtypeStruct((groups, query_tiles, LANES, 2 * tile), jnp.float32)
    if away:
        carry = jnp.zeros((1, 1, 8, LANES), jnp.float32)
        carry_block = pl.BlockSpec((1, 1, 8, LANES), lambda g, j, m: (0, 0, 0, 0))
    else:
        carry_block = acc_block
    whole_q = pl.BlockSpec((rows, 2 * LANES), lambda g, j, m: (0, g))
    return pl.pallas_call(
        functools.partial(attend_back_kernel, not away),
        grid_spec=pltpu.PrefetchScalarGridSpec(
            num_scalar_prefetch=1,
            grid=(groups, key_tiles),
            in_specs=[
                carry_block,
                whole_q,
                pl.BlockSpec((1, tile, LANES), lambda g, j, m: (g, skip + j, 0)),
                pl.BlockSpec((1, tile, LANES), lambda g, j, m: (groups + g, skip + j, 0)),
                whole_q,
                whole_q,
                pl.BlockSpec((1, query_tiles, 1, 2 * tile), lambda g, j, m: (g, 0, 0, 0)),
                pl.BlockSpec((rows, LANES), lambda g, j, m: (0, 0)),
                pl.BlockSpec((rows, LANES), lambda g, j, m: (0, 0)),
            ],
            out_specs=[
                acc_block if away else whole_q,
                pl.BlockSpec((1, tile, LANES), lambda g, j, m: (g, j, 0)),
                pl.BlockSpec((1, tile, LANES), lambda g, j, m: (g, j, 0)),
            ],
            scratch_shapes=[
                pltpu.VMEM((query_tiles, 1, 2 * tile), jnp.float32),
                pltpu.VMEM((query_tiles, LANES, 2 * tile), jnp.float32),
            ],
        ),
        out_shape=[
            acc_shape if away else jax.ShapeDtypeStruct((rows, q_width), jnp.bfloat16),
            jax.ShapeDtypeStruct((groups, keys, LANES), jnp.bfloat16),
            jax.ShapeDtypeStruct((groups, keys, LANES), jnp.bfloat16),
        ],
        compiler_params=pltpu.CompilerParams(vmem_limit_bytes=VMEM_BYTES),
        cost_estimate=pl.CostEstimate(
            flops=20 * rows * keys * LANES * groups * 2, bytes_accessed=8_000_000, transcendentals=0
        ),
        name="attend_back_away" if away else "attend_back_own",
    )(meta, carry, q, kv, kv, o, d_out, lse, cosine, sine)


def middle_back_kernel(
    x_ref,
    project_ref,
    feed_ref,
    cot_ref,
    gain_ref,
    hidden_ref,
    down_w_ref,
    o_ref,
    wp_ref,
    grad_ref,
    d_out_ref,
    down_ref,
    wp_grad_ref,
    gain_grad_ref,
    acc_ref,
):
    step = pl.program_id(0)
    last = pl.num_programs(0) - 1
    bf16, f32 = jnp.bfloat16, jnp.float32

    @pl.when(step == 0)
    def _():
        acc_ref[...] = jnp.zeros_like(acc_ref)
        gain_grad_ref[...] = jnp.zeros_like(gain_grad_ref)

    middle = x_ref[...].astype(f32) + project_ref[...].astype(f32)
    factor = lax.rsqrt(jnp.mean(middle * middle, axis=-1, keepdims=True) + EPSILON)
    feed_in = feed_ref[...].astype(f32)
    gain_grad_ref[...] += jnp.sum(feed_in * middle * factor, axis=0, keepdims=True)
    scaled = gain_ref[1:2, :].astype(f32) * feed_in
    grad = (
        cot_ref[...].astype(f32)
        + factor * scaled
        - middle * (factor * factor * factor * jnp.mean(scaled * middle, axis=-1, keepdims=True))
    )
    grad_ref[...] = grad
    low = grad.astype(bf16)
    d_out_ref[...] = dot(low, wp_ref[...], ((1,), (1,))).astype(bf16)
    acc_ref[...] += dot(o_ref[...], low, ((0,), (0,)))
    half = hidden_ref.shape[1] // 2
    down_ref[...] = (
        dot(hidden_ref[:, :half], down_w_ref[0], ((1,), (0,)))
        + dot(hidden_ref[:, half:], down_w_ref[1], ((1,), (0,)))
    ).astype(bf16)

    @pl.when(step == last)
    def _():
        for head in range(acc_ref.shape[0] // LANES):
            wp_grad_ref[head * HD : (head + 1) * HD, :] = acc_ref[
                head * LANES : head * LANES + HD, :
            ].astype(bf16)


def middle_back(x, project_sum, feed_sum, cot, gains, hidden, down_w, o, w_p):
    rows, width = x.shape
    tile = 256
    units = hidden.shape[1]
    heads = o.shape[1] // LANES
    bf16, f32 = jnp.bfloat16, jnp.float32

    def rows_of(columns):
        return pl.BlockSpec((tile, columns), lambda i: (i, 0))

    def whole(array):
        return pl.BlockSpec(array.shape, lambda i: (0, 0))

    return pl.pallas_call(
        middle_back_kernel,
        grid=(rows // tile,),
        in_specs=[
            rows_of(width),
            rows_of(width),
            rows_of(width),
            rows_of(width),
            whole(gains),
            rows_of(units),
            pl.BlockSpec(down_w.shape, lambda i: (0, 0, 0)),
            rows_of(o.shape[1]),
            whole(w_p),
        ],
        out_specs=[
            rows_of(width),
            rows_of(o.shape[1]),
            rows_of(width),
            pl.BlockSpec((heads * HD, width), lambda i: (0, 0)),
            pl.BlockSpec((1, width), lambda i: (0, 0)),
        ],
        out_shape=[
            jax.ShapeDtypeStruct((rows, width), f32),
            jax.ShapeDtypeStruct(o.shape, bf16),
            jax.ShapeDtypeStruct((rows, width), bf16),
            jax.ShapeDtypeStruct((heads * HD, width), bf16),
            jax.ShapeDtypeStruct((1, width), f32),
        ],
        scratch_shapes=[pltpu.VMEM((o.shape[1], width), f32)],
        compiler_params=pltpu.CompilerParams(vmem_limit_bytes=VMEM_BYTES),
        cost_estimate=pl.CostEstimate(
            flops=8_000_000_000, bytes_accessed=30_000_000, transcendentals=0
        ),
        name="middle_back",
    )(x, project_sum, feed_sum, cot, gains, hidden, down_w, o, w_p)


def tail_kernel(
    first_ref,
    second_ref,
    q_low_ref,
    own_ref,
    away_ref,
    normed_ref,
    wide_ref,
    x_ref,
    grad_ref,
    gain_term_ref,
    gain_ref,
    project_ref,
    spread_ref,
    cos_ref,
    sin_ref,
    out_ref,
    share_ref,
    gain_share_ref,
    low_ref,
    close_ref,
    part_ref,
    x_in_ref,
    up_ref,
    down_ref,
    give_ref,
    core_in_ref,
    keep_ref,
    chip_in_ref,
    total_ref,
    gain_sum_ref,
    gain_x_ref,
    gain_z_ref,
    x_send,
    x_recv,
    up_send,
    up_recv,
    down_send,
    down_recv,
    core_send,
    core_recv,
    chip_send,
    chip_recv,
    back_send,
    back_recv,
    last_send,
    last_recv,
    gain_send,
    gain_recv,
):
    bf16, f32 = jnp.bfloat16, jnp.float32
    planes = part_ref.shape[1]
    rows, width = x_ref.shape
    depth = width // planes
    project_rows = project_ref.shape[0] // 2
    half_rows = rows // 2
    chunks = give_ref.shape[0]
    chunk = half_rows // chunks
    half_width = low_ref.shape[2]
    z = lax.axis_index("fsdp")
    c = lax.axis_index("ctx")
    t = lax.axis_index("tp")
    core = lax.rem(t, 2)
    across = {"ctx": 1 - c}
    sibling = {"tp": t + 1 - 2 * core}
    partner = {"tp": lax.rem(t + 2, 4)}
    has_above = z < planes - 1
    has_below = z > 0

    barrier = pltpu.get_barrier_semaphore()
    for device in (across, sibling, partner):
        pl.semaphore_signal(barrier, inc=1, device_id=device, device_id_type=MESH)
    for k in range(1, planes):
        pl.semaphore_signal(
            barrier, inc=1, device_id={"fsdp": lax.rem(z + k, planes)}, device_id_type=MESH
        )
    pl.semaphore_wait(barrier, 3 + planes - 1)

    def remote(src, dst, send, recv, device):
        return pltpu.make_async_remote_copy(
            src_ref=src,
            dst_ref=dst,
            send_sem=send,
            recv_sem=recv,
            device_id=device,
            device_id_type=MESH,
        )

    block = 256

    def lower(i, carry):
        at = pl.ds(pl.multiple_of(i * block, block), block)
        for which in range(2):
            low_ref[which, at, : 2 * LANES] = q_low_ref[
                at, which * 2 * LANES : (which + 1) * 2 * LANES
            ]
            key = own_ref[which, at, :].astype(f32) + away_ref[1 - which, at, :].astype(f32)
            key = key * cos_ref[at, :] - pltpu.roll(key, SPAN, 1) * sin_ref[at, :]
            low_ref[which, at, 2 * LANES : 3 * LANES] = key.astype(bf16)
            value = own_ref[2 + which, at, :].astype(f32) + away_ref[3 - which, at, :].astype(f32)
            low_ref[which, at, 3 * LANES :] = value.astype(bf16)
            close_ref[which, at, :] = dot(
                low_ref[which, at, :], spread_ref[...], ((1,), (1,))
            ).astype(bf16)
        return carry

    lax.fori_loop(0, rows // block, lower, 0)

    order = []
    for k in range((planes + 1) // 2):
        order += [planes - 1 - k, k]
    order = order[:planes]

    def weight_part(which, d):
        at = slice(d * depth, (d + 1) * depth)
        part_ref[which, d, :depth] = dot(
            normed_ref[:, at], close_ref[which], ((0,), (0,))
        ).astype(bf16)
        part_ref[which, d, depth:] = project_ref[
            which * project_rows : (which + 1) * project_rows, at
        ]

    def to_neighbour(d):
        return remote(part_ref.at[1, d], x_in_ref.at[d], x_send.at[d], x_recv.at[d], across)

    for d in order:
        weight_part(1, d)
        to_neighbour(d).start()

    def feature_rows(start):
        at = pl.ds(pl.multiple_of(start, chunk), chunk)
        return dot(low_ref[0, at, :], wide_ref[:, :half_width], ((1,), (1,))) + dot(
            low_ref[1, at, :], wide_ref[:, half_width:], ((1,), (1,))
        )

    give_start = (1 - core) * half_rows
    keep_start = core * half_rows

    def to_core(i):
        return remote(give_ref.at[i], core_in_ref.at[i], core_send.at[i], core_recv.at[i], sibling)

    def to_chip(i):
        return remote(keep_ref.at[i], chip_in_ref.at[i], chip_send.at[i], chip_recv.at[i], partner)

    def keep_at(i):
        return pl.ds(pl.multiple_of(keep_start + i * chunk, chunk), chunk)

    def give_at(i):
        return pl.ds(pl.multiple_of(give_start + i * chunk, chunk), chunk)

    def back(i):
        return remote(
            total_ref.at[keep_at(i)],
            total_ref.at[keep_at(i)],
            back_send.at[i],
            back_recv.at[i],
            sibling,
        )

    def from_core(i):
        return remote(
            total_ref.at[give_at(i)],
            total_ref.at[give_at(i)],
            back_send.at[i],
            back_recv.at[i],
            sibling,
        )

    for i in range(chunks):
        give_ref[i] = feature_rows(give_start + i * chunk).astype(bf16)
        to_core(i).start()
    for i in range(chunks):
        kept = feature_rows(keep_start + i * chunk)
        to_core(i).wait_recv()
        keep_ref[i] = (kept + core_in_ref[i].astype(f32)).astype(bf16)
        to_chip(i).start()

    for d in order:
        weight_part(0, d)

    def add_neighbour(d):
        to_neighbour(d).wait_recv()
        part_ref[0, d] = (part_ref[0, d].astype(f32) + x_in_ref[d].astype(f32)).astype(bf16)

    def up(d):
        return remote(up_ref.at[d], up_ref.at[d], up_send.at[d], up_recv.at[d], {"fsdp": z + 1})

    def down(d):
        return remote(
            down_ref.at[d], down_ref.at[d], down_send.at[d], down_recv.at[d], {"fsdp": z - 1}
        )

    def upward(d):
        @pl.when(z == 0)
        def _():
            up_ref[d] = part_ref[0, d]

        @pl.when((z > 0) & (z < d))
        def _():
            up(d).wait_recv()
            up_ref[d] = (up_ref[d].astype(f32) + part_ref[0, d].astype(f32)).astype(bf16)

        @pl.when(z < d)
        def _():
            up(d).start()

    def downward(d):
        @pl.when(z == planes - 1)
        def _():
            down_ref[d] = part_ref[0, d]

        @pl.when((z < planes - 1) & (z > d))
        def _():
            down(d).wait_recv()
            down_ref[d] = (down_ref[d].astype(f32) + part_ref[0, d].astype(f32)).astype(bf16)

        @pl.when(z > d)
        def _():
            down(d).start()

    def finish_chunk(i):
        to_chip(i).wait_recv()
        total_ref[keep_at(i)] = (keep_ref[i].astype(f32) + chip_in_ref[i].astype(f32)).astype(bf16)
        back(i).start()

    def last_share():
        return remote(
            share_ref.at[0], share_ref.at[1], last_send.at[0], last_recv.at[0], across
        )

    added = set()

    def line_step(k):
        for d in (planes - 1 - k, k):
            if d not in added:
                added.add(d)
                add_neighbour(d)
        upward(planes - 1 - k)
        downward(k)

    per_step = -(-chunks // planes)
    done = 0
    for k in range(planes - 1):
        line_step(k)
        for i in range(done, min(chunks, done + per_step)):
            finish_chunk(i)
        done = min(chunks, done + per_step)

    own = part_ref[0, pl.ds(z, 1)][0].astype(f32)
    share_ref[0] = own.astype(bf16)

    @pl.when(has_below)
    def _():
        up(z).wait_recv()
        share_ref[0] = (share_ref[0].astype(f32) + up_ref[pl.ds(z, 1)][0].astype(f32)).astype(bf16)

    @pl.when(has_above)
    def _():
        down(z).wait_recv()
        share_ref[0] = (share_ref[0].astype(f32) + down_ref[pl.ds(z, 1)][0].astype(f32)).astype(bf16)

    last_share().start()
    for i in range(done, chunks):
        finish_chunk(i)

    gain_sum_ref[...] = jnp.zeros_like(gain_sum_ref)
    gain_sum_ref[1:2, :] = gain_term_ref[...]
    gain = gain_ref[0:1, :].astype(f32)

    def finish_rows(start):
        at = pl.ds(pl.multiple_of(start, chunk), chunk)
        x = x_ref[at, :].astype(f32)
        factor = lax.rsqrt(jnp.mean(x * x, axis=-1, keepdims=True) + EPSILON)
        normed_in = total_ref[at, :].astype(f32)
        gain_sum_ref[0:1, :] += jnp.sum(normed_in * x * factor, axis=0, keepdims=True)
        scaled = gain * normed_in
        out_ref[at, :] = (
            grad_ref[at, :]
            + factor * scaled
            - x * (factor * factor * factor * jnp.mean(scaled * x, axis=-1, keepdims=True))
        ).astype(bf16)

    for i in range(chunks):
        finish_rows(keep_start + i * chunk)
    for i in range(chunks):
        from_core(i).wait_recv()
        finish_rows(give_start + i * chunk)

    gain_over = remote(gain_sum_ref, gain_x_ref, gain_send.at[0], gain_recv.at[0], across)
    gain_over.start()
    gain_over.wait()
    gain_sum_ref[...] = gain_sum_ref[...] + gain_x_ref[...]

    def gain_to(k):
        plane = lax.rem(z + k, planes)
        return remote(
            gain_sum_ref.at[:, pl.ds(pl.multiple_of(plane * depth, depth), depth)],
            gain_z_ref.at[k],
            gain_send.at[k],
            gain_recv.at[k],
            {"fsdp": plane},
        )

    for k in range(1, planes):
        gain_to(k).start()
    gain_share_ref[...] = gain_sum_ref[:, pl.ds(pl.multiple_of(z * depth, depth), depth)]
    for k in range(1, planes):
        gain_to(k).wait_recv()
        gain_share_ref[...] += gain_z_ref[k]

    last_share().wait()
    for k in range(1, planes):
        gain_to(k).wait_send()
    for i in range(chunks):
        to_core(i).wait_send()
        to_chip(i).wait_send()
        back(i).wait_send()
    for d in range(planes):
        to_neighbour(d).wait_send()

        @pl.when(z < d)
        def _():
            up(d).wait_send()

        @pl.when(z > d)
        def _():
            down(d).wait_send()


def tail(
    first, second, q_low, own, away, normed, wide, x, grad, gain_term, gains, project,
    spread, cosine, sine, planes,
):
    rows, width = x.shape
    depth = width // planes
    half_width = wide.shape[1] // 2
    close_width = spread.shape[0]
    chunks = 4
    chunk = rows // 2 // chunks
    bf16, f32 = jnp.bfloat16, jnp.float32
    vmem = pl.BlockSpec(memory_space=pltpu.VMEM)
    dma = pltpu.SemaphoreType.DMA
    operands = (
        first, second, q_low, own, away, normed, wide, x, grad, gain_term, gains, project,
        spread, cosine, sine,
    )
    anywhere = pl.BlockSpec(memory_space=pl.ANY)
    piece_rows = depth + project.shape[0] // 2
    return pl.pallas_call(
        tail_kernel,
        in_specs=[anywhere] * 2 + [vmem] * (len(operands) - 2),
        out_specs=[vmem] * 3,
        out_shape=[
            jax.ShapeDtypeStruct((rows, width), bf16),
            jax.ShapeDtypeStruct((2, piece_rows, close_width), bf16),
            jax.ShapeDtypeStruct((8, depth), f32),
        ],
        scratch_shapes=[
            pltpu.VMEM((2, rows, half_width), bf16),
            pltpu.VMEM((2, rows, close_width), bf16),
            pltpu.VMEM((2, planes, piece_rows, close_width), bf16),
            pltpu.VMEM((planes, piece_rows, close_width), bf16),
            pltpu.VMEM((planes, piece_rows, close_width), bf16),
            pltpu.VMEM((planes, piece_rows, close_width), bf16),
            pltpu.VMEM((chunks, chunk, width), bf16),
            pltpu.VMEM((chunks, chunk, width), bf16),
            pltpu.VMEM((chunks, chunk, width), bf16),
            pltpu.VMEM((chunks, chunk, width), bf16),
            pltpu.VMEM((rows, width), bf16),
            pltpu.VMEM((8, width), f32),
            pltpu.VMEM((8, width), f32),
            pltpu.VMEM((planes, 8, depth), f32),
            dma((planes,)),
            dma((planes,)),
            dma((planes,)),
            dma((planes,)),
            dma((planes,)),
            dma((planes,)),
            dma((chunks,)),
            dma((chunks,)),
            dma((chunks,)),
            dma((chunks,)),
            dma((chunks,)),
            dma((chunks,)),
            dma((1,)),
            dma((1,)),
            dma((planes,)),
            dma((planes,)),
        ],
        compiler_params=pltpu.CompilerParams(
            collective_id=2, has_side_effects=True, vmem_limit_bytes=VMEM_BYTES
        ),
        cost_estimate=pl.CostEstimate(
            flops=60_000_000_000, bytes_accessed=24_000_000, transcendentals=0
        ),
        name="tail",
    )(*operands)


def feed_kernel(
    x_ref,
    project_ref,
    cot_ref,
    gain_ref,
    gate_ref,
    up_ref,
    down_ref,
    total_ref,
    hidden_ref,
    gate_grad_ref,
    up_grad_ref,
    down_grad_ref,
    normed_ref,
    gate_back_ref,
    up_back_ref,
    give_ref,
    core_in_ref,
    keep_ref,
    chip_in_ref,
    core_send,
    core_recv,
    chip_send,
    chip_recv,
    back_send,
    back_recv,
):
    bf16, f32 = jnp.bfloat16, jnp.float32
    rows, width = x_ref.shape
    half_rows = rows // 2
    chunks, chunk, _ = give_ref.shape
    units = gate_ref.shape[2]
    t = lax.axis_index("tp")
    core = lax.rem(t, 2)
    sibling = {"tp": t + 1 - 2 * core}
    partner = {"tp": lax.rem(t + 2, 4)}

    barrier = pltpu.get_barrier_semaphore()
    for device in (sibling, partner):
        pl.semaphore_signal(barrier, inc=1, device_id=device, device_id_type=MESH)
    pl.semaphore_wait(barrier, 2)

    def remote(src, dst, send, recv, device):
        return pltpu.make_async_remote_copy(
            src_ref=src,
            dst_ref=dst,
            send_sem=send,
            recv_sem=recv,
            device_id=device,
            device_id_type=MESH,
        )

    give_start = (1 - core) * half_rows
    keep_start = core * half_rows
    gain = gain_ref[1:2, :].astype(f32)
    halves = tuple((gate_ref.at[i], up_ref.at[i], down_ref.at[i]) for i in range(2))

    def feature_rows(start):
        at = pl.ds(pl.multiple_of(start, chunk), chunk)
        middle = x_ref[at, :].astype(f32) + project_ref[at, :].astype(f32)
        factor = lax.rsqrt(jnp.mean(middle * middle, axis=-1, keepdims=True) + EPSILON)
        normed_ref[at, :] = (middle * factor * gain).astype(bf16)
        for which, (gate_w, up_w, down_w) in enumerate(halves):
            cols = slice(which * units, (which + 1) * units)
            gate = dot(normed_ref[at, :], gate_w[...], ((1,), (0,)))
            up = dot(normed_ref[at, :], up_w[...], ((1,), (0,)))
            hidden_in = dot(cot_ref[at, :], down_w[...], ((1,), (1,)))
            sigmoid = jax.nn.sigmoid(gate)
            silu = gate * sigmoid
            hidden_ref[at, cols] = (silu * up).astype(bf16)
            gate_back_ref[at, cols] = (
                hidden_in * up * sigmoid * (1.0 + gate * (1.0 - sigmoid))
            ).astype(bf16)
            up_back_ref[at, cols] = (hidden_in * silu).astype(bf16)
        return sum(
            dot(back_ref[at, which * units : (which + 1) * units], weight[...], ((1,), (1,)))
            for which, (gate_w, up_w, _) in enumerate(halves)
            for back_ref, weight in ((gate_back_ref, gate_w), (up_back_ref, up_w))
        )

    def to_core(i):
        return remote(give_ref.at[i], core_in_ref.at[i], core_send.at[i], core_recv.at[i], sibling)

    def to_chip(i):
        return remote(keep_ref.at[i], chip_in_ref.at[i], chip_send.at[i], chip_recv.at[i], partner)

    def back(i, start):
        at = pl.ds(pl.multiple_of(start + i * chunk, chunk), chunk)
        return remote(
            total_ref.at[at], total_ref.at[at], back_send.at[i], back_recv.at[i], sibling
        )

    for i in range(chunks):
        give_ref[i] = feature_rows(give_start + i * chunk).astype(bf16)
        to_core(i).start()
        kept = feature_rows(keep_start + i * chunk)
        to_core(i).wait_recv()
        keep_ref[i] = (kept + core_in_ref[i].astype(f32)).astype(bf16)
        to_chip(i).start()

    block = 256

    def input_grads(back_ref, grad_ref):
        def some(i, carry):
            at = pl.ds(pl.multiple_of(i * block, block), block)
            for which in (1, 0):
                grad_ref[which, at, :] = dot(
                    normed_ref[:, at],
                    back_ref[:, which * units : (which + 1) * units],
                    ((0,), (0,)),
                ).astype(bf16)
            return carry

        lax.fori_loop(0, width // block, some, 0)

    def down_grads(i, carry):
        at = pl.ds(pl.multiple_of(i * block, block), block)
        down_grad_ref[at, :] = dot(hidden_ref[:, at], cot_ref[...], ((0,), (0,))).astype(bf16)
        return carry

    def finish_chunk(i):
        to_chip(i).wait_recv()
        at = pl.ds(pl.multiple_of(keep_start + i * chunk, chunk), chunk)
        total_ref[at, :] = (keep_ref[i].astype(f32) + chip_in_ref[i].astype(f32)).astype(bf16)
        back(i, keep_start).start()

    input_grads(gate_back_ref, gate_grad_ref)
    for i in range(chunks // 2):
        finish_chunk(i)
    input_grads(up_back_ref, up_grad_ref)
    lax.fori_loop(0, down_grad_ref.shape[0] // block, down_grads, 0)
    for i in range(chunks // 2, chunks):
        finish_chunk(i)
    for i in range(chunks):
        to_core(i).wait_send()
        to_chip(i).wait_send()
        back(i, keep_start).wait_send()
    for i in range(chunks):
        back(i, give_start).wait_recv()


def feed(x, project_sum, cot, gains, gate_w, up_w, down_w):
    rows, width = x.shape
    units = gate_w.shape[2]
    chunk = 256
    chunks = rows // 2 // chunk
    bf16 = jnp.bfloat16
    vmem = pl.BlockSpec(memory_space=pltpu.VMEM)
    dma = pltpu.SemaphoreType.DMA
    operands = (x, project_sum, cot, gains, gate_w, up_w, down_w)
    piece = pltpu.VMEM((chunks, chunk, width), bf16)
    return pl.pallas_call(
        feed_kernel,
        in_specs=[vmem] * len(operands),
        out_specs=[vmem] * 5,
        out_shape=[
            jax.ShapeDtypeStruct((rows, width), bf16),
            jax.ShapeDtypeStruct((rows, 2 * units), bf16),
            jax.ShapeDtypeStruct((2, width, units), bf16),
            jax.ShapeDtypeStruct((2, width, units), bf16),
            jax.ShapeDtypeStruct((2 * units, width), bf16),
        ],
        scratch_shapes=[
            pltpu.VMEM((rows, width), bf16),
            pltpu.VMEM((rows, 2 * units), bf16),
            pltpu.VMEM((rows, 2 * units), bf16),
            piece,
            piece,
            piece,
            piece,
        ]
        + [dma((chunks,))] * 6,
        compiler_params=pltpu.CompilerParams(
            collective_id=3, has_side_effects=True, vmem_limit_bytes=VMEM_BYTES
        ),
        cost_estimate=pl.CostEstimate(
            flops=50_000_000_000, bytes_accessed=40_000_000, transcendentals=0
        ),
        name="feed",
    )(*operands)


def paired_body(
    tokens,
    prefix_len,
    positions,
    gain_attend,
    w_query,
    w_key,
    w_value,
    w_project,
    gain_feed,
    w_gate,
    w_up,
    w_down,
    cotangent,
):
    seqs, rows, width = tokens.shape
    assert seqs == 1
    c = lax.axis_index("ctx")
    bf16, f32 = jnp.bfloat16, jnp.float32

    def half(array, axis, which=None):
        size = array.shape[axis] // 2
        which = c if which is None else which
        return lax.dynamic_slice_in_dim(array, which * size, size, axis)

    def ordered(mine, other, axis):
        return jnp.where(
            c == 0,
            jnp.concatenate([mine, other], axis=axis),
            jnp.concatenate([other, mine], axis=axis),
        )

    planes = lax.axis_size("fsdp")
    kv_half = w_key.shape[1] // 2
    q_half = w_query.shape[1] // 2

    def packed(which):
        return jnp.concatenate(
            [half(w_query, 1, which), half(w_key, 1, which), half(w_value, 1, which)], axis=1
        )

    gain_rows = jnp.pad(jnp.stack([gain_attend, gain_feed]), ((0, GAIN_ROWS - 2), (0, 0)))
    pack = jnp.concatenate([packed(c), gain_rows], axis=0)

    def parts(block):
        return (
            block[:, :q_half],
            block[:, q_half : q_half + kv_half],
            block[:, q_half + kv_half :],
        )

    half_heads = (q_half + 2 * kv_half) // HD
    spread = np.zeros((half_heads * HD, half_heads * LANES), np.float32)
    for head in range(half_heads):
        for lane in range(HD):
            turned = lane if lane < HALF or head == half_heads - 1 else lane - HALF + SPAN
            spread[head * HD + lane, head * LANES + turned] = 1.0
    spread = jnp.asarray(spread, bf16)

    frequency = ROPE_BASE ** (-(jnp.arange(HALF, dtype=f32) * 2.0 / HD))
    frequency = jnp.pad(frequency, (0, SPAN - HALF))
    angles = positions[0].astype(f32)[:, None] * frequency
    cosine = jnp.cos(angles)
    sine = jnp.sin(angles)
    cosine = jnp.concatenate([cosine, cosine], axis=1)
    sine = jnp.concatenate([-sine, sine], axis=1)

    block_len = rows // 2
    tile = min(256, block_len)
    query_tiles = rows // tile
    own = c * rows + tile * jnp.arange(query_tiles, dtype=jnp.int32)
    opposite = (1 - c) * rows + tile * jnp.arange(query_tiles, dtype=jnp.int32)
    own, opposite = natural_index(own, block_len, 2), natural_index(opposite, block_len, 2)
    meta = jnp.concatenate([prefix_len.astype(jnp.int32), own, own, opposite])

    x = tokens[0]
    cot = cotangent[0]
    (
        normed, q, kv_all, w_qkv, w_p, gains, o, lse, project_sum, wg, wu, wd,
    ) = front(
        prefix_len, x, pack, packed(1 - c), spread, cosine, sine,
        w_project.reshape(-1, HD, w_project.shape[1]), w_gate, w_up, w_down, planes,
    )
    w_p = w_p.reshape(-1, width)
    feed_sum, hidden, gate_grad, up_grad, down_part = feed(
        x, project_sum, cot, gains, wg, wu, wd
    )

    gate_away, up_away = swap_ctx(gate_grad[1]), swap_ctx(up_grad[1])

    def added(a, b):
        return (a.astype(f32) + b.astype(f32)).astype(bf16)

    both = jnp.concatenate([added(gate_grad[0], gate_away), added(up_grad[0], up_away)], axis=1)
    both_share = lax.psum_scatter(both, "fsdp", scatter_dimension=0, tiled=True)
    both_away = swap_ctx(both_share)
    units_half = gate_grad.shape[2]
    down_share = lax.psum_scatter(down_part, "fsdp", scatter_dimension=1, tiled=True)
    down_away = swap_ctx(down_share)
    size = down_share.shape[0] // 2
    down_mine = down_share[:size].astype(f32) + down_away[size:].astype(f32)
    down_other = down_share[size:].astype(f32) + down_away[:size].astype(f32)
    down_grad = ordered(down_mine, down_other, 0)

    middle_grad, d_out, down_rows, project_part, gain_two_term = middle_back(
        x, project_sum, feed_sum, cot, gains, hidden, wd, o, w_p
    )
    layer_output = (x.astype(f32) + project_sum.astype(f32)
                    + paired_tensor_sum(down_rows).astype(f32)).astype(bf16)
    dq_away, dk_away, dv_away = attend_back(
        meta, None, q, kv_all, True, o, d_out, lse, cosine, sine, tile
    )
    d_kv_away = swap_ctx(jnp.concatenate([dk_away, dv_away], axis=0))
    q_low, dk_own, dv_own = attend_back(
        meta, dq_away, q, kv_all, False, o, d_out, lse, cosine, sine, tile
    )
    d_kv_own = jnp.concatenate([dk_own, dv_own], axis=0)
    tokens_grad, share, gain_share = tail(
        both, down_share, q_low, d_kv_own, d_kv_away, normed, w_qkv, x, middle_grad,
        gain_two_term, gains, project_part, spread, cosine, sine, planes,
    )
    shares = [
        ordered(a, b, 1).astype(f32) for a, b in zip(parts(share[0, : width // planes]), parts(share[1, : width // planes]))
    ]
    return (
        layer_output[None],
        tokens_grad[None],
        gain_share[0],
        shares[0],
        shares[1],
        shares[2],
        ordered(share[0, width // planes :], share[1, width // planes :], 0).astype(f32),
        gain_share[1],
        ordered(both_share[:, :units_half], both_away[:, :units_half], 1).astype(f32),
        ordered(both_share[:, units_half:], both_away[:, units_half:], 1).astype(f32),
        down_grad,
    )


def solution(mesh):
    paired = mesh.shape["ctx"] == 2 and mesh.shape["tp"] == 4 and mesh.shape["fsdp"] == 4
    return jax.shard_map(
        paired_body if paired else general_body,
        mesh=mesh,
        in_specs=(
            P("fsdp", "ctx", None),
            P("fsdp"),
            P("fsdp", "ctx"),
            P("fsdp"),
            P("fsdp", "tp"),
            P("fsdp", "tp"),
            P("fsdp", "tp"),
            P("tp", "fsdp"),
            P("fsdp"),
            P("fsdp", "tp"),
            P("fsdp", "tp"),
            P("tp", "fsdp"),
            P("fsdp", "ctx", None),
        ),
        out_specs=(
            P("fsdp", "ctx", None),
            P("fsdp", "ctx", None),
            P("fsdp"),
            P("fsdp", "tp"),
            P("fsdp", "tp"),
            P("fsdp", "tp"),
            P("tp", "fsdp"),
            P("fsdp"),
            P("fsdp", "tp"),
            P("fsdp", "tp"),
            P("tp", "fsdp"),
        ),
        check_vma=False,
    )
```

```python
import functools
import math

import jax
import jax.numpy as jnp
import numpy as np
from jax import lax
from jax.experimental import pallas as pl
from jax.experimental.pallas import tpu as pltpu
from jax.sharding import PartitionSpec as P

HQ = 16
KVH = 8
HD = 96


EPSILON = 1e-05
ROPE_BASE = 100000.0
NEGATIVE = -1e30


def natural_index(stored, block_len, pair_count):
    device = stored // (2 * block_len)
    second_half = stored // block_len % 2
    within = stored % block_len
    block_id = jnp.where(second_half == 0, device, 2 * pair_count - 1 - device)
    return block_id * block_len + within


def rotate(values, cosine_table, sine_table):
    half_width = values.shape[-1] // 2
    leading = values[..., :half_width]
    trailing = values[..., half_width:]
    return jnp.concatenate(
        [
            leading * cosine_table - trailing * sine_table,
            trailing * cosine_table + leading * sine_table,
        ],
        axis=-1,
    )


def rotate_back(incoming, cosine_table, sine_table):
    half_width = incoming.shape[-1] // 2
    leading = incoming[..., :half_width]
    trailing = incoming[..., half_width:]
    return jnp.concatenate(
        [
            leading * cosine_table + trailing * sine_table,
            trailing * cosine_table - leading * sine_table,
        ],
        axis=-1,
    )


def rms_factor(values):
    return lax.rsqrt(jnp.mean(values * values, axis=-1, keepdims=True) + EPSILON)


def rms_back(values, factor, gain_row, incoming):
    scaled = gain_row * incoming
    return factor * scaled - values * factor**3 * jnp.mean(scaled * values, axis=-1, keepdims=True)


def tensor_sum(term_rows):
    return lax.psum(term_rows.astype(jnp.bfloat16), "tp").astype(jnp.float32)


def general_body(
    tokens,
    prefix_len,
    positions,
    gain_attend,
    w_query,
    w_key,
    w_value,
    w_project,
    gain_feed,
    w_gate,
    w_up,
    w_down,
    cotangent,
):
    (
        gain_one,
        query_weight_whole,
        key_weight_whole,
        value_weight_whole,
        project_weight_whole,
        gain_two,
        gate_weight_whole,
        up_weight_whole,
        down_weight_whole,
    ) = (
        lax.all_gather(gain_attend, "fsdp", axis=0, tiled=True),
        lax.all_gather(w_query, "fsdp", axis=0, tiled=True),
        lax.all_gather(w_key, "fsdp", axis=0, tiled=True),
        lax.all_gather(w_value, "fsdp", axis=0, tiled=True),
        lax.all_gather(w_project, "fsdp", axis=1, tiled=True),
        lax.all_gather(gain_feed, "fsdp", axis=0, tiled=True),
        lax.all_gather(w_gate, "fsdp", axis=0, tiled=True),
        lax.all_gather(w_up, "fsdp", axis=0, tiled=True),
        lax.all_gather(w_down, "fsdp", axis=1, tiled=True),
    )
    seq_count, rows_local, _ = tokens.shape
    pair_count = lax.axis_size("ctx")
    block_len = rows_local // 2
    query_width = query_weight_whole.shape[1]
    kv_width = key_weight_whole.shape[1]
    query_heads = query_width // HD
    kv_heads = kv_width // HD
    group_size = HQ // KVH
    score_scale = HD ** (-0.5)
    frequency = ROPE_BASE ** (-(jnp.arange(HD // 2, dtype=jnp.float32) * 2.0 / HD))
    angles = positions.astype(jnp.float32)[:, :, None] * frequency
    cosine_table = jnp.cos(angles)[:, :, None, :]
    sine_table = jnp.sin(angles)[:, :, None, :]
    stored_rows = lax.axis_index("ctx") * rows_local + jnp.arange(rows_local, dtype=jnp.int32)
    query_order = natural_index(stored_rows, block_len, pair_count)

    def visible_mask(key_order):
        causal = key_order[None, None, :] <= query_order[None, :, None]
        opened = key_order[None, None, :] < prefix_len[:, None, None]
        return (causal | opened)[:, :, None, None, :]

    inputs = tokens.astype(jnp.float32)
    factor_one = rms_factor(inputs)
    normed_hidden = (inputs * factor_one * gain_one.astype(jnp.float32)).astype(jnp.bfloat16)
    query_projected = jnp.einsum(
        "rxc,cf->rxf", normed_hidden, query_weight_whole, preferred_element_type=jnp.float32
    )
    key_projected = jnp.einsum(
        "rxc,cf->rxf", normed_hidden, key_weight_whole, preferred_element_type=jnp.float32
    )
    value_projected = jnp.einsum(
        "rxc,cf->rxf", normed_hidden, value_weight_whole, preferred_element_type=jnp.float32
    )
    queries = (
        rotate(
            query_projected.reshape(seq_count, rows_local, query_heads, HD),
            cosine_table,
            sine_table,
        )
        .astype(jnp.bfloat16)
        .reshape(seq_count, rows_local, kv_heads, group_size, HD)
    )
    keys_rot = (
        rotate(key_projected.reshape(seq_count, rows_local, kv_heads, HD), cosine_table, sine_table)
        .astype(jnp.bfloat16)
        .reshape(seq_count, rows_local, kv_width)
    )
    values_low = value_projected.astype(jnp.bfloat16)
    stat_shape = (seq_count, rows_local, kv_heads, group_size)
    initial = (
        jnp.full(stat_shape, NEGATIVE, jnp.float32),
        jnp.zeros(stat_shape, jnp.float32),
        jnp.zeros(stat_shape + (HD,), jnp.float32),
    )
    key_piece = lax.all_gather(keys_rot, "ctx", axis=1, tiled=True)
    value_piece = lax.all_gather(values_low, "ctx", axis=1, tiled=True)
    key_total = key_piece.shape[1]
    span_rows = math.gcd(key_total, rows_local)

    def one_span(span_index, running):
        run_max, run_sum, run_acc = running
        span_start = span_index * span_rows
        key_rows = lax.dynamic_slice_in_dim(key_piece, span_start, span_rows, 1).reshape(
            seq_count, span_rows, kv_heads, HD
        )
        value_rows = lax.dynamic_slice_in_dim(value_piece, span_start, span_rows, 1).reshape(
            seq_count, span_rows, kv_heads, HD
        )
        key_order = natural_index(
            span_start + jnp.arange(span_rows, dtype=jnp.int32), block_len, pair_count
        )
        visible = visible_mask(key_order)
        scores = (
            jnp.einsum("slhgd,skhd->slhgk", queries, key_rows, preferred_element_type=jnp.float32)
            * score_scale
        )
        new_max = jnp.maximum(run_max, jnp.max(jnp.where(visible, scores, NEGATIVE), axis=-1))
        weights_raw = jnp.where(visible, jnp.exp(scores - new_max[..., None]), 0.0)
        rescale = jnp.exp(run_max - new_max)
        run_sum = run_sum * rescale + jnp.sum(weights_raw, axis=-1)
        run_acc = run_acc * rescale[..., None] + jnp.einsum(
            "slhgk,skhd->slhgd",
            weights_raw.astype(jnp.bfloat16),
            value_rows,
            preferred_element_type=jnp.float32,
        )
        return (new_max, run_sum, run_acc)

    run_max, run_sum, run_acc = lax.fori_loop(0, key_total // span_rows, one_span, initial)
    attended = run_acc / run_sum[..., None]
    log_total = run_max + jnp.log(run_sum)
    attended_reduced = attended.reshape(seq_count, rows_local, query_width).astype(jnp.bfloat16)
    project_rows = jnp.einsum(
        "hxz,zm->hxm", attended_reduced, project_weight_whole, preferred_element_type=jnp.float32
    )
    middle = inputs + tensor_sum(project_rows)
    factor_two = rms_factor(middle)
    normed_feed_input = (middle * factor_two * gain_two.astype(jnp.float32)).astype(jnp.bfloat16)
    gate_activation = jnp.einsum(
        "qeh,hj->qej", normed_feed_input, gate_weight_whole, preferred_element_type=jnp.float32
    )
    up_activation = jnp.einsum(
        "qeh,hj->qej", normed_feed_input, up_weight_whole, preferred_element_type=jnp.float32
    )
    sigmoid_gate = jax.nn.sigmoid(gate_activation)
    silu_gate = gate_activation * sigmoid_gate
    hidden_state = (silu_gate * up_activation).astype(jnp.bfloat16)
    down_output_rows = jnp.einsum(
        "nct,tm->ncm", hidden_state, down_weight_whole, preferred_element_type=jnp.float32
    )
    layer_output = (middle + tensor_sum(down_output_rows)).astype(jnp.bfloat16)
    (
        gain_one,
        query_weight_whole,
        key_weight_whole,
        value_weight_whole,
        project_weight_whole,
        gain_two,
        gate_weight_whole,
        up_weight_whole,
        down_weight_whole,
    ) = (
        lax.all_gather(gain_attend, "fsdp", axis=0, tiled=True),
        lax.all_gather(w_query, "fsdp", axis=0, tiled=True),
        lax.all_gather(w_key, "fsdp", axis=0, tiled=True),
        lax.all_gather(w_value, "fsdp", axis=0, tiled=True),
        lax.all_gather(w_project, "fsdp", axis=1, tiled=True),
        lax.all_gather(gain_feed, "fsdp", axis=0, tiled=True),
        lax.all_gather(w_gate, "fsdp", axis=0, tiled=True),
        lax.all_gather(w_up, "fsdp", axis=0, tiled=True),
        lax.all_gather(w_down, "fsdp", axis=1, tiled=True),
    )
    hidden_grad = jnp.einsum(
        "ehv,iv->ehi", cotangent, down_weight_whole, preferred_element_type=jnp.float32
    )
    down_weight_part = jnp.einsum(
        "gqa,gqz->az", hidden_state, cotangent, preferred_element_type=jnp.float32
    )
    gate_reduced = (
        hidden_grad * up_activation * sigmoid_gate * (1.0 + gate_activation * (1.0 - sigmoid_gate))
    ).astype(jnp.bfloat16)
    up_reduced = (hidden_grad * silu_gate).astype(jnp.bfloat16)
    gate_weight_part = jnp.einsum(
        "bic,big->cg", normed_feed_input, gate_reduced, preferred_element_type=jnp.float32
    )
    up_weight_part = jnp.einsum(
        "bic,big->cg", normed_feed_input, up_reduced, preferred_element_type=jnp.float32
    )
    feed_rows = jnp.einsum(
        "vte,ce->vtc", gate_reduced, gate_weight_whole, preferred_element_type=jnp.float32
    ) + jnp.einsum("vte,ce->vtc", up_reduced, up_weight_whole, preferred_element_type=jnp.float32)
    feed_in = tensor_sum(feed_rows)
    gain_two_term = jnp.sum(feed_in * middle * factor_two, axis=(0, 1))
    middle_grad = cotangent.astype(jnp.float32) + rms_back(
        middle, factor_two, gain_two.astype(jnp.float32), feed_in
    )
    middle_reduced = middle_grad.astype(jnp.bfloat16)
    project_term = jnp.einsum(
        "xeh,xec->hc", attended_reduced, middle_reduced, preferred_element_type=jnp.float32
    )
    attended_grad = (
        jnp.einsum(
            "vhk,nk->vhn", middle_reduced, project_weight_whole, preferred_element_type=jnp.float32
        )
        .astype(jnp.bfloat16)
        .reshape(seq_count, rows_local, kv_heads, group_size, HD)
    )
    row_delta = jnp.sum(attended_grad.astype(jnp.float32) * attended, axis=-1)
    whole_keys, whole_values = (
        lax.all_gather(keys_rot[None], "ctx", axis=0, tiled=True),
        lax.all_gather(values_low[None], "ctx", axis=0, tiled=True),
    )

    def key_block(grad_acc, block_items):
        key_rows, value_rows, block_index = block_items
        key_rows = key_rows.reshape(seq_count, rows_local, kv_heads, HD)
        value_rows = value_rows.reshape(seq_count, rows_local, kv_heads, HD)
        key_order = natural_index(
            block_index * rows_local + jnp.arange(rows_local, dtype=jnp.int32),
            block_len,
            pair_count,
        )
        visible = visible_mask(key_order)
        scores = (
            jnp.einsum("slhgd,skhd->slhgk", queries, key_rows, preferred_element_type=jnp.float32)
            * score_scale
        )
        weights_norm = jnp.where(visible, jnp.exp(scores - log_total[..., None]), 0.0)
        prob_grad = jnp.einsum(
            "slhgd,skhd->slhgk", attended_grad, value_rows, preferred_element_type=jnp.float32
        )
        score_grad = (weights_norm * (prob_grad - row_delta[..., None])).astype(jnp.bfloat16)
        grad_acc = (
            grad_acc
            + jnp.einsum(
                "slhgk,skhd->slhgd", score_grad, key_rows, preferred_element_type=jnp.float32
            )
            * score_scale
        )
        key_grad = (
            jnp.einsum("slhgk,slhgd->skhd", score_grad, queries, preferred_element_type=jnp.float32)
            * score_scale
        )
        value_grad = jnp.einsum(
            "slhgk,slhgd->skhd",
            weights_norm.astype(jnp.bfloat16),
            attended_grad,
            preferred_element_type=jnp.float32,
        )
        return (
            grad_acc,
            (
                key_grad.reshape(seq_count, rows_local, kv_width),
                value_grad.reshape(seq_count, rows_local, kv_width),
            ),
        )

    block_ids = jnp.arange(pair_count, dtype=jnp.int32)
    query_grad, (key_terms, value_terms) = lax.scan(
        key_block, jnp.zeros(stat_shape + (HD,), jnp.float32), (whole_keys, whole_values, block_ids)
    )
    key_sum, value_sum = (
        lax.psum_scatter(
            key_terms.astype(jnp.bfloat16), "ctx", scatter_dimension=0, tiled=True
        ).astype(jnp.float32),
        lax.psum_scatter(
            value_terms.astype(jnp.bfloat16), "ctx", scatter_dimension=0, tiled=True
        ).astype(jnp.float32),
    )
    key_reduced = (
        rotate_back(
            key_sum[0].reshape(seq_count, rows_local, kv_heads, HD), cosine_table, sine_table
        )
        .astype(jnp.bfloat16)
        .reshape(seq_count, rows_local, kv_width)
    )
    value_backward = value_sum[0].astype(jnp.bfloat16)
    query_reduced = (
        rotate_back(
            query_grad.reshape(seq_count, rows_local, query_heads, HD), cosine_table, sine_table
        )
        .astype(jnp.bfloat16)
        .reshape(seq_count, rows_local, query_width)
    )
    query_weight_part = jnp.einsum(
        "prb,pro->bo", normed_hidden, query_reduced, preferred_element_type=jnp.float32
    )
    key_weight_part = jnp.einsum(
        "prb,pro->bo", normed_hidden, key_reduced, preferred_element_type=jnp.float32
    )
    value_weight_part = jnp.einsum(
        "prb,pro->bo", normed_hidden, value_backward, preferred_element_type=jnp.float32
    )
    normed_rows = (
        jnp.einsum(
            "kjw,iw->kji", query_reduced, query_weight_whole, preferred_element_type=jnp.float32
        )
        + jnp.einsum(
            "kjw,iw->kji", key_reduced, key_weight_whole, preferred_element_type=jnp.float32
        )
        + jnp.einsum(
            "kjw,iw->kji", value_backward, value_weight_whole, preferred_element_type=jnp.float32
        )
    )
    normed_grad = tensor_sum(normed_rows)
    gain_one_term = jnp.sum(normed_grad * inputs * factor_one, axis=(0, 1))
    tokens_grad = (
        middle_grad + rms_back(inputs, factor_one, gain_one.astype(jnp.float32), normed_grad)
    ).astype(jnp.bfloat16)
    (
        part_one,
        part_query,
        part_key,
        part_value,
        part_project,
        part_two,
        part_gate,
        part_up,
        part_down,
    ) = (
        lax.psum_scatter(gain_one_term, ("fsdp", "ctx"), scatter_dimension=0, tiled=True),
        lax.psum_scatter(query_weight_part, ("fsdp", "ctx"), scatter_dimension=0, tiled=True),
        lax.psum_scatter(key_weight_part, ("fsdp", "ctx"), scatter_dimension=0, tiled=True),
        lax.psum_scatter(value_weight_part, ("fsdp", "ctx"), scatter_dimension=0, tiled=True),
        lax.psum_scatter(project_term, ("fsdp", "ctx"), scatter_dimension=1, tiled=True),
        lax.psum_scatter(gain_two_term, ("fsdp", "ctx"), scatter_dimension=0, tiled=True),
        lax.psum_scatter(gate_weight_part, ("fsdp", "ctx"), scatter_dimension=0, tiled=True),
        lax.psum_scatter(up_weight_part, ("fsdp", "ctx"), scatter_dimension=0, tiled=True),
        lax.psum_scatter(down_weight_part, ("fsdp", "ctx"), scatter_dimension=1, tiled=True),
    )
    reduced = (
        lax.all_gather(part_one.astype(jnp.bfloat16), "ctx", axis=0, tiled=True).astype(
            part_one.dtype
        ),
        lax.all_gather(part_query.astype(jnp.bfloat16), "ctx", axis=0, tiled=True).astype(
            part_query.dtype
        ),
        lax.all_gather(part_key.astype(jnp.bfloat16), "ctx", axis=0, tiled=True).astype(
            part_key.dtype
        ),
        lax.all_gather(part_value.astype(jnp.bfloat16), "ctx", axis=0, tiled=True).astype(
            part_value.dtype
        ),
        lax.all_gather(part_project.astype(jnp.bfloat16), "ctx", axis=1, tiled=True).astype(
            part_project.dtype
        ),
        lax.all_gather(part_two.astype(jnp.bfloat16), "ctx", axis=0, tiled=True).astype(
            part_two.dtype
        ),
        lax.all_gather(part_gate.astype(jnp.bfloat16), "ctx", axis=0, tiled=True).astype(
            part_gate.dtype
        ),
        lax.all_gather(part_up.astype(jnp.bfloat16), "ctx", axis=0, tiled=True).astype(
            part_up.dtype
        ),
        lax.all_gather(part_down.astype(jnp.bfloat16), "ctx", axis=1, tiled=True).astype(
            part_down.dtype
        ),
    )
    return (layer_output, tokens_grad) + tuple(reduced)


LANES = 128
HALF = HD // 2
SPAN = LANES // 2
LOG2E = math.log2(math.e)
VMEM_BYTES = 60 * 1024 * 1024


def swap_ctx(block):
    return lax.ppermute(block, "ctx", [(0, 1), (1, 0)])


def swap_core(block):
    return lax.ppermute(block, "tp", [(0, 1), (1, 0), (2, 3), (3, 2)])


def swap_chip(block):
    return lax.ppermute(block, "tp", [(0, 2), (2, 0), (1, 3), (3, 1)])


def by_core(total, other):
    return jnp.where(
        lax.axis_index("tp") % 2 == 0,
        jnp.concatenate([total, other], axis=0),
        jnp.concatenate([other, total], axis=0),
    )


def dot(a, b, contract):
    return lax.dot_general(a, b, (contract, ((), ())), preferred_element_type=jnp.float32)


def block_kinds(meta_ref, query_tile, key_tile, q_start, k_start):
    prefix = meta_ref[0]
    whole = (k_start + (key_tile - 1) <= q_start) | (k_start + key_tile <= prefix)
    nothing = (k_start > q_start + (query_tile - 1)) & (k_start >= prefix)
    return prefix, whole, nothing


def mask_scores(scores, prefix, q_start, k_start, query_tile):
    key_ids = k_start + lax.broadcasted_iota(jnp.int32, scores.shape, 0)
    column = lax.broadcasted_iota(jnp.int32, scores.shape, 1)
    query_ids = q_start + jnp.bitwise_and(column, query_tile - 1)
    return jnp.where((key_ids <= query_ids) | (key_ids < prefix), scores, NEGATIVE)


MESH = pl.DeviceIdType.MESH
GAIN_ROWS = 16
PREFIX_MOST = 1024


def line_sum(z, planes, source, up_ref, down_ref, up_send, up_recv, down_send, down_recv):
    f32 = jnp.float32

    def up(d):
        return pltpu.make_async_remote_copy(
            src_ref=up_ref.at[d - 1],
            dst_ref=up_ref.at[d - 1],
            send_sem=up_send.at[d],
            recv_sem=up_recv.at[d],
            device_id={"fsdp": z + 1},
            device_id_type=MESH,
        )

    def down(d):
        return pltpu.make_async_remote_copy(
            src_ref=down_ref.at[d],
            dst_ref=down_ref.at[d],
            send_sem=down_send.at[d],
            recv_sem=down_recv.at[d],
            device_id={"fsdp": z - 1},
            device_id_type=MESH,
        )

    def begin(k):
        high, low = planes - 1 - k, k

        @pl.when(z == 0)
        def _():
            up_ref[high - 1] = source(high)
            up(high).start()

        @pl.when(z == planes - 1)
        def _():
            down_ref[low] = source(low)
            down(low).start()

    def relay(k):
        high, low = planes - 1 - k, k

        def pass_up():
            @pl.when((z > 0) & (z < high))
            def _():
                up(high).wait_recv()
                up_ref[high - 1] = (
                    up_ref[high - 1].astype(f32) + source(high).astype(f32)
                ).astype(up_ref.dtype)
                up(high).start()

        def pass_down():
            @pl.when((z < planes - 1) & (z > low))
            def _():
                down(low).wait_recv()
                down_ref[low] = (
                    down_ref[low].astype(f32) + source(low).astype(f32)
                ).astype(down_ref.dtype)
                down(low).start()

        @pl.when(2 * z < planes)
        def _():
            pass_up()
            pass_down()

        @pl.when(2 * z >= planes)
        def _():
            pass_down()
            pass_up()

    def finish(out_ref):
        out_ref[...] = source(z)

        @pl.when(z > 0)
        def _():
            up(z).wait_recv()
            out_ref[...] = (
                out_ref[...].astype(f32) + up_ref[pl.ds(z - 1, 1)][0].astype(f32)
            ).astype(out_ref.dtype)

        @pl.when(z < planes - 1)
        def _():
            down(z).wait_recv()
            out_ref[...] = (
                out_ref[...].astype(f32) + down_ref[pl.ds(z, 1)][0].astype(f32)
            ).astype(out_ref.dtype)

    def sent():
        for d in range(planes):

            @pl.when(z < d)
            def _():
                up(d).wait_send()

            @pl.when(z > d)
            def _():
                down(d).wait_send()

    return begin, relay, finish, sent


def front_kernel(
    prefix_ref,
    x_ref,
    pack_ref,
    rest_ref,
    spread_ref,
    cos_ref,
    sin_ref,
    w_project_ref,
    w_gate_ref,
    w_up_ref,
    w_down_ref,
    normed_ref,
    q_ref,
    kv_ref,
    wide_ref,
    project_ref,
    gain_ref,
    o_ref,
    lse_ref,
    total_ref,
    gate_ref,
    up_ref,
    down_ref,
    buf_ref,
    max_ref,
    sum_ref,
    acc_ref,
    give_ref,
    core_in_ref,
    keep_ref,
    chip_in_ref,
    up_send,
    up_recv,
    down_send,
    down_recv,
    x_send,
    x_recv,
    kv_send,
    kv_recv,
    m_up_send,
    m_up_recv,
    m_down_send,
    m_down_recv,
    m_x_send,
    m_x_recv,
    local_sem,
    core_send,
    core_recv,
    chip_send,
    chip_recv,
    back_send,
    back_recv,
):
    bf16, f32 = jnp.bfloat16, jnp.float32
    planes = buf_ref.shape[0]
    rows, width = x_ref.shape
    depth = width // planes
    half_width = wide_ref.shape[1] // 2
    matrix_rows = rest_ref.shape[0]
    heads_half = project_ref.shape[0] // 2
    units = gate_ref.shape[2]
    direct = units // 2
    z = lax.axis_index("fsdp")
    c = lax.axis_index("ctx")
    t = lax.axis_index("tp")
    core = lax.rem(t, 2)
    across = {"ctx": 1 - c}
    sibling = {"tp": t + 1 - 2 * core}
    partner = {"tp": lax.rem(t + 2, 4)}
    has_above = z < planes - 1
    has_below = z > 0

    def remote(src, dst, send, recv, device):
        return pltpu.make_async_remote_copy(
            src_ref=src,
            dst_ref=dst,
            send_sem=send,
            recv_sem=recv,
            device_id=device,
            device_id_type=MESH,
        )

    project_ref[:, HD:, :] = jnp.zeros(
        (project_ref.shape[0], LANES - HD, project_ref.shape[2]), bf16
    )

    barrier = pltpu.get_barrier_semaphore()

    @pl.when(has_above)
    def _():
        pl.semaphore_signal(barrier, inc=1, device_id={"fsdp": z + 1}, device_id_type=MESH)

    @pl.when(has_below)
    def _():
        pl.semaphore_signal(barrier, inc=1, device_id={"fsdp": z - 1}, device_id_type=MESH)

    for device in (across, sibling, partner):
        pl.semaphore_signal(barrier, inc=1, device_id=device, device_id_type=MESH)

    @pl.when(has_above & has_below)
    def _():
        pl.semaphore_wait(barrier, 5)

    @pl.when(jnp.logical_not(has_above & has_below))
    def _():
        pl.semaphore_wait(barrier, 4)

    def up(k):
        piece = z - k
        src = pack_ref if k == 0 else buf_ref.at[piece, 0]
        return remote(src, buf_ref.at[piece, 0], up_send.at[k], up_recv.at[k], {"fsdp": z + 1})

    def down(k):
        piece = z + k
        src = pack_ref if k == 0 else buf_ref.at[piece, 0]
        return remote(src, buf_ref.at[piece, 0], down_send.at[k], down_recv.at[k], {"fsdp": z - 1})

    def from_below(k):
        slot = buf_ref.at[z - 1 - k, 0]
        return remote(slot, slot, up_send.at[k], up_recv.at[k], {"fsdp": z - 1})

    def from_above(k):
        slot = buf_ref.at[z + 1 + k, 0]
        return remote(slot, slot, down_send.at[k], down_recv.at[k], {"fsdp": z + 1})

    def sideways(side, k):
        piece = z - k if side == 0 else z + k
        matrix = pl.ds(0, matrix_rows)
        return remote(
            buf_ref.at[piece, 0, matrix],
            buf_ref.at[piece, 1, matrix],
            x_send.at[side, k],
            x_recv.at[side, k],
            across,
        )

    def own_half(m, half):
        if m == 0:
            return w_gate_ref.at[:, pl.ds(pl.multiple_of(half * units, units), units)]
        if m == 1:
            return w_up_ref.at[:, pl.ds(pl.multiple_of(half * units, units), units)]
        if m == 2:
            return w_down_ref.at[pl.ds(pl.multiple_of(half * units, units), units), :]
        if m == 4:
            return w_down_ref.at[pl.ds(pl.multiple_of((1 - half) * units, units), direct), :]
        return w_project_ref.at[pl.ds(half * heads_half, heads_half)]

    def slot(m, which, piece):
        at = pl.ds(pl.multiple_of(piece * depth, depth), depth)
        if m == 0:
            return gate_ref.at[which, at]
        if m == 1:
            return up_ref.at[which, at]
        if m == 2:
            return down_ref.at[which, :, at]
        if m == 4:
            return down_ref.at[1, pl.ds(0, direct), at]
        return project_ref.at[pl.ds(which * heads_half, heads_half), pl.ds(0, HD), at]

    def m_up(m, k):
        piece = z - k
        src = own_half(m, c) if k == 0 else slot(m, 0, piece)
        return remote(
            src, slot(m, 0, piece), m_up_send.at[m, k], m_up_recv.at[m, k], {"fsdp": z + 1}
        )

    def m_down(m, k):
        piece = z + k
        src = own_half(m, c) if k == 0 else slot(m, 0, piece)
        return remote(
            src, slot(m, 0, piece), m_down_send.at[m, k], m_down_recv.at[m, k], {"fsdp": z - 1}
        )

    def m_below(m, k):
        at = slot(m, 0, z - 1 - k)
        return remote(at, at, m_up_send.at[m, k], m_up_recv.at[m, k], {"fsdp": z - 1})

    def m_above(m, k):
        at = slot(m, 0, z + 1 + k)
        return remote(at, at, m_down_send.at[m, k], m_down_recv.at[m, k], {"fsdp": z + 1})

    def m_side(m, side, k):
        piece = z - k if side == 0 else z + k
        src, dst = slot(m, 0, piece), slot(m, 1, piece)
        if m == 2:
            left = pl.ds(direct, units - direct)
            src, dst = src.at[left], dst.at[left]
        return remote(
            src,
            dst,
            m_x_send.at[m, side, k],
            m_x_recv.at[m, side, k],
            across,
        )

    groups = ((3,), (0,), (1,), (2, 4))

    def relay(group, k):
        for m in groups[group]:

            @pl.when(z - k >= 0)
            def _():
                m_below(m, k - 1).wait_recv()
                if k < planes - 1:

                    @pl.when(has_above)
                    def _():
                        m_up(m, k).start()

            @pl.when(z + k <= planes - 1)
            def _():
                m_above(m, k - 1).wait_recv()
                if k < planes - 1:

                    @pl.when(has_below)
                    def _():
                        m_down(m, k).start()

    def launch(group):
        for m in groups[group]:

            @pl.when(has_above)
            def _():
                m_up(m, 0).start()

            @pl.when(has_below)
            def _():
                m_down(m, 0).start()

    def cross(group, k):
        for m in groups[group]:
            if m == 4:
                continue

            @pl.when(z - k >= 0)
            def _():
                m_side(m, 0, k).start()

            @pl.when(z + k <= planes - 1)
            def _():
                m_side(m, 1, k).start()

    def crossed(m, k):
        @pl.when(z - k >= 0)
        def _():
            m_side(m, 0, k).wait_recv()

        @pl.when(z + k <= planes - 1)
        def _():
            m_side(m, 1, k).wait_recv()

    def local(m, which):
        half = c if which == 0 else 1 - c
        return pltpu.make_async_copy(own_half(m, half), slot(m, which, z), local_sem.at[m, which])

    spread = spread_ref[...]

    def place(block, piece, which):
        at = pl.ds(pl.multiple_of(piece * depth, depth), depth)
        wide_ref[at, which * half_width : (which + 1) * half_width] = dot(
            block[:depth], spread, ((1,), (0,))
        ).astype(bf16)

    def place_gain(block, piece):
        at = pl.ds(pl.multiple_of(piece * depth, depth), depth)
        gain_ref[:, at] = block[matrix_rows:]

    @pl.when(has_above)
    def _():
        up(0).start()

    @pl.when(has_below)
    def _():
        down(0).start()

    for m in (3, 0, 1, 2):
        for which in range(2):
            local(m, which).start()
    place(pack_ref, z, 0)
    place_gain(pack_ref, z)
    place(rest_ref, z, 1)

    for k in range(1, planes):
        below = z - k >= 0
        above = z + k <= planes - 1

        @pl.when(below)
        def _():
            from_below(k - 1).wait_recv()
            if k < planes - 1:

                @pl.when(has_above)
                def _():
                    up(k).start()

            sideways(0, k).start()

        @pl.when(above)
        def _():
            from_above(k - 1).wait_recv()
            if k < planes - 1:

                @pl.when(has_below)
                def _():
                    down(k).start()

            sideways(1, k).start()

        if k == max(1, planes - 2):
            launch(0)
            launch(1)

        @pl.when(below)
        def _():
            place(buf_ref.at[z - k, 0], z - k, 0)
            place_gain(buf_ref.at[z - k, 0], z - k)

        @pl.when(above)
        def _():
            place(buf_ref.at[z + k, 0], z + k, 0)
            place_gain(buf_ref.at[z + k, 0], z + k)

    relay(0, 1)
    cross(0, 1)
    tile = 128
    gain = gain_ref[0:1, :].astype(f32)

    def norm_rows(i, carry):
        at = pl.ds(pl.multiple_of(i * tile, tile), tile)
        x = x_ref[at, :].astype(f32)
        factor = lax.rsqrt(jnp.mean(x * x, axis=-1, keepdims=True) + EPSILON)
        normed_ref[at, :] = (x * factor * gain).astype(bf16)
        return carry

    lax.fori_loop(0, rows // tile, norm_rows, 0)
    relay(0, 2)
    cross(0, 2)
    launch(2)

    for k in range(1, planes):

        @pl.when(z - k >= 0)
        def _():
            sideways(0, k).wait_recv()
            place(buf_ref.at[z - k, 1], z - k, 1)

        @pl.when(z + k <= planes - 1)
        def _():
            sideways(1, k).wait_recv()
            place(buf_ref.at[z + k, 1], z + k, 1)

    block = 256

    def turn(part, at):
        return part * cos_ref[at, :] + pltpu.roll(part, SPAN, 1) * sin_ref[at, :]

    def key_rows(i, carry):
        at = pl.ds(pl.multiple_of(i * block, block), block)
        for which in range(2):
            lane = which * half_width + 2 * LANES
            both = dot(normed_ref[at, :], wide_ref[:, lane : lane + 2 * LANES], ((1,), (0,)))
            kv_ref[which, at, :] = turn(both[:, :LANES], at).astype(bf16)
            kv_ref[2 + which, at, :] = both[:, LANES:].astype(bf16)
        return carry

    lax.fori_loop(0, rows // block, key_rows, 0)

    def exchange(slab):
        return remote(
            kv_ref.at[slab, pl.ds(0, rows)],
            kv_ref.at[slab ^ 1, pl.ds(rows, rows)],
            kv_send.at[slab],
            kv_recv.at[slab ^ 1],
            across,
        )

    for slab in range(4):
        exchange(slab).start()
    relay(0, 3)
    cross(0, 3)
    relay(1, 1)
    launch(3)
    scale = HD ** (-0.5) * LOG2E

    def query_rows(i, carry):
        at = pl.ds(pl.multiple_of(i * block, block), block)
        for which in range(2):
            lane = which * half_width
            both = dot(normed_ref[at, :], wide_ref[:, lane : lane + 2 * LANES], ((1,), (0,)))
            for head in range(2):
                part = turn(both[:, head * LANES : (head + 1) * LANES], at)
                lane = (2 * which + head) * LANES
                q_ref[at, lane : lane + LANES] = (part * scale).astype(bf16)
        return carry

    lax.fori_loop(0, rows // block, query_rows, 0)

    tiles = rows // block
    tiles_of_block = tiles // 2
    prefix = prefix_ref[0]
    max_ref[...] = jnp.full_like(max_ref, NEGATIVE)
    sum_ref[...] = jnp.zeros_like(sum_ref)
    acc_ref[...] = jnp.zeros_like(acc_ref)

    def start_of(device, tile_index):
        second = tile_index // tiles_of_block
        block_id = device + second * (3 - 2 * device)
        return (block_id * tiles_of_block + tile_index % tiles_of_block) * block

    def attend_group(g, away):
        key_device = 1 - c if away else c

        def one_tile(i, carry):
            at = pl.ds(pl.multiple_of(i * block, block), block)
            lane = 2 * g * LANES
            queries = jnp.concatenate(
                [q_ref[at, lane : lane + LANES], q_ref[at, lane + LANES : lane + 2 * LANES]],
                axis=0,
            )
            q_start = start_of(c, i)
            u = g * tiles + i

            def absorb(scores, values):
                old = max_ref[u]
                new = jnp.maximum(old, jnp.max(scores, axis=0, keepdims=True))
                weights = jnp.exp2(scores - new)
                rescale = jnp.exp2(old - new)
                max_ref[u] = new
                sum_ref[u] = sum_ref[u] * rescale + jnp.sum(weights, axis=0, keepdims=True)
                acc_ref[u] = acc_ref[u] * rescale + dot(values, weights.astype(bf16), ((0,), (0,)))

            def one(j, carry):
                k_start = start_of(key_device, j)
                first = (tiles if away else 0) + j
                keys_at = pl.ds(pl.multiple_of(first * block, block), block)
                whole = k_start + (block - 1) <= q_start
                nothing = (k_start > q_start + (block - 1)) & (k_start >= PREFIX_MOST)

                @pl.when(whole)
                def _():
                    absorb(dot(kv_ref[g, keys_at, :], queries, ((1,), (1,))), kv_ref[2 + g, keys_at, :])

                @pl.when(jnp.logical_not(whole | nothing))
                def _():
                    scores = dot(kv_ref[g, keys_at, :], queries, ((1,), (1,)))
                    absorb(
                        mask_scores(scores, prefix, q_start, k_start, block),
                        kv_ref[2 + g, keys_at, :],
                    )

                return carry

            lax.fori_loop(0, tiles, one, 0)
            if away:
                total = sum_ref[u]
                lse_ref[g, i] = max_ref[u] + jnp.log2(total)
                out = (acc_ref[u] / total).T.astype(bf16)
                o_ref[at, lane : lane + LANES] = out[:block]
                o_ref[at, lane + LANES : lane + 2 * LANES] = out[block:]
            return carry

        lax.fori_loop(0, tiles, one_tile, 0)

    attend_group(0, False)
    relay(2, 1)
    attend_group(1, False)
    relay(3, 1)
    for slab in range(4):
        exchange(slab).wait_recv()
    cross(1, 1)
    cross(2, 1)
    cross(3, 1)
    attend_group(0, True)
    relay(1, 2)
    cross(1, 2)
    attend_group(1, True)
    relay(2, 2)
    cross(2, 2)

    chunks, chunk, _ = give_ref.shape
    half_rows = rows // 2
    give_start = (1 - core) * half_rows
    keep_start = core * half_rows
    for which in range(2):
        local(3, which).wait()
    for k in range(1, planes):
        crossed(3, k)
    w_project = project_ref[...].reshape(project_ref.shape[0] * LANES, width)

    def feature_rows(start):
        at = pl.ds(pl.multiple_of(start, chunk), chunk)
        return dot(o_ref[at, :], w_project, ((1,), (0,)))

    def to_core(i):
        return remote(give_ref.at[i], core_in_ref.at[i], core_send.at[i], core_recv.at[i], sibling)

    def to_chip(i):
        return remote(keep_ref.at[i], chip_in_ref.at[i], chip_send.at[i], chip_recv.at[i], partner)

    def back(i, start):
        at = pl.ds(pl.multiple_of(start + i * chunk, chunk), chunk)
        return remote(
            total_ref.at[at], total_ref.at[at], back_send.at[i], back_recv.at[i], sibling
        )

    for i in range(chunks):
        give_ref[i] = feature_rows(give_start + i * chunk).astype(bf16)
        to_core(i).start()
    for i in range(chunks):
        kept = feature_rows(keep_start + i * chunk)
        to_core(i).wait_recv()
        keep_ref[i] = (kept + core_in_ref[i].astype(f32)).astype(bf16)
        to_chip(i).start()

    def finish_chunk(i):
        to_chip(i).wait_recv()
        at = pl.ds(pl.multiple_of(keep_start + i * chunk, chunk), chunk)
        total_ref[at, :] = (keep_ref[i].astype(f32) + chip_in_ref[i].astype(f32)).astype(bf16)
        back(i, keep_start).start()

    relay(3, 2)
    cross(3, 2)
    for i in range(chunks):
        finish_chunk(i)
        if i < planes - 1:
            relay(i + 1, planes - 1)
            cross(i + 1, planes - 1)

    for k in range(planes - 1):

        @pl.when((z - k >= 0) & has_above)
        def _():
            up(k).wait_send()
            for m in range(5):
                m_up(m, k).wait_send()

        @pl.when((z + k <= planes - 1) & has_below)
        def _():
            down(k).wait_send()
            for m in range(5):
                m_down(m, k).wait_send()

    for k in range(1, planes):

        @pl.when(z - k >= 0)
        def _():
            sideways(0, k).wait_send()
            for m in range(4):
                m_side(m, 0, k).wait_send()

        @pl.when(z + k <= planes - 1)
        def _():
            sideways(1, k).wait_send()
            for m in range(4):
                m_side(m, 1, k).wait_send()

        for m in range(3):
            crossed(m, k)

    for m in range(3):
        for which in range(2):
            local(m, which).wait()
    for slab in range(4):
        exchange(slab).wait_send()
    for i in range(chunks):
        to_core(i).wait_send()
        to_chip(i).wait_send()
        back(i, keep_start).wait_send()
        back(i, give_start).wait_recv()


def front(prefix, x, pack, rest, spread, cosine, sine, w_project, w_gate, w_up, w_down, planes):
    rows, width = x.shape
    half_width = spread.shape[1]
    units = w_gate.shape[1] // 2
    heads = w_project.shape[0]
    block = 256
    tiles = rows // block
    chunks = 4
    chunk = rows // 2 // chunks
    vmem = pl.BlockSpec(memory_space=pltpu.VMEM)
    anywhere = pl.BlockSpec(memory_space=pl.ANY)
    smem = pl.BlockSpec(memory_space=pltpu.SMEM)
    bf16, f32 = jnp.bfloat16, jnp.float32
    dma = pltpu.SemaphoreType.DMA
    piece = pltpu.VMEM((chunks, chunk, width), bf16)
    return pl.pallas_call(
        front_kernel,
        in_specs=[smem] + [vmem] * 6 + [anywhere] * 4,
        out_specs=[vmem] * 9 + [anywhere] * 3,
        out_shape=[
            jax.ShapeDtypeStruct((rows, width), bf16),
            jax.ShapeDtypeStruct((rows, half_width), bf16),
            jax.ShapeDtypeStruct((4, 2 * rows, LANES), bf16),
            jax.ShapeDtypeStruct((width, 2 * half_width), bf16),
            jax.ShapeDtypeStruct((heads, LANES, width), bf16),
            jax.ShapeDtypeStruct((GAIN_ROWS, width), bf16),
            jax.ShapeDtypeStruct((rows, half_width), bf16),
            jax.ShapeDtypeStruct((2, tiles, 1, 2 * block), f32),
            jax.ShapeDtypeStruct((rows, width), bf16),
            jax.ShapeDtypeStruct((2, width, units), bf16),
            jax.ShapeDtypeStruct((2, width, units), bf16),
            jax.ShapeDtypeStruct((2, units, width), bf16),
        ],
        scratch_shapes=[
            pltpu.VMEM((planes, 2, pack.shape[0], pack.shape[1]), bf16),
            pltpu.VMEM((2 * tiles, 1, 2 * block), f32),
            pltpu.VMEM((2 * tiles, 1, 2 * block), f32),
            pltpu.VMEM((2 * tiles, LANES, 2 * block), f32),
            piece,
            piece,
            piece,
            piece,
        ]
        + [dma((planes - 1,))] * 4
        + [dma((2, planes))] * 2
        + [dma((4,))] * 2
        + [dma((5, planes - 1))] * 4
        + [dma((4, 2, planes))] * 2
        + [dma((4, 2))]
        + [dma((chunks,))] * 6,
        compiler_params=pltpu.CompilerParams(
            collective_id=1, has_side_effects=True, vmem_limit_bytes=VMEM_BYTES
        ),
        cost_estimate=pl.CostEstimate(
            flops=120_000_000_000, bytes_accessed=60_000_000, transcendentals=0
        ),
        name="front",
    )(prefix, x, pack, rest, spread, cosine, sine, w_project, w_gate, w_up, w_down)


def attend_back_kernel(
    final,
    meta_ref,
    carry_ref,
    first_ref,
    second_ref,
    q_ref,
    k_ref,
    v_ref,
    o_ref,
    do_ref,
    lse_ref,
    cos_ref,
    sin_ref,
    dq_ref,
    dkv_ref,
    delta_ref,
    acc_ref,
    dk_acc_ref,
    dv_acc_ref,
):
    query_tiles = lse_ref.shape[1]
    tile = q_ref.shape[0] // query_tiles
    key_tile = k_ref.shape[1]
    j = pl.program_id(1)

    def stacked(ref, i):
        rows = pl.ds(pl.multiple_of(i * tile, tile), tile)
        return jnp.concatenate([ref[rows, :LANES], ref[rows, LANES:]], axis=0)

    @pl.when(j == 0)
    def _():
        acc_ref[...] = carry_ref[0] if final else jnp.zeros_like(acc_ref)

        def one_delta(i, carry):
            product = stacked(o_ref, i).astype(jnp.float32) * stacked(do_ref, i).astype(jnp.float32)
            delta_ref[i] = jnp.sum(product.T, axis=0, keepdims=True)
            return carry

        lax.fori_loop(0, query_tiles, one_delta, 0)

    k_start = meta_ref[1 + query_tiles + (0 if final else pl.num_programs(1)) + j]
    keys = k_ref[0]
    values = v_ref[0]

    dk_acc_ref[...] = jnp.zeros_like(dk_acc_ref)
    dv_acc_ref[...] = jnp.zeros_like(dv_acc_ref)

    def one(i, carry):
        q_start = meta_ref[1 + i]
        prefix, whole, nothing = block_kinds(meta_ref, tile, key_tile, q_start, k_start)

        def some(masked):
            queries = stacked(q_ref, i)
            d_out = stacked(do_ref, i)
            scores = dot(keys, queries, ((1,), (1,)))
            if masked:
                scores = mask_scores(scores, prefix, q_start, k_start, tile)
            weights = jnp.exp2(scores - lse_ref[0, i])
            d_weights = dot(values, d_out, ((1,), (1,)))
            d_scores = (weights * (d_weights - delta_ref[i])).astype(jnp.bfloat16)
            dv_acc_ref[...] += dot(weights.astype(jnp.bfloat16), d_out, ((1,), (0,)))
            dk_acc_ref[...] += dot(d_scores, queries, ((1,), (0,)))
            acc_ref[i] += dot(keys, d_scores, ((0,), (0,)))

        @pl.when(whole)
        def _():
            some(False)

        @pl.when(jnp.logical_not(whole | nothing))
        def _():
            some(True)

        return carry

    lax.fori_loop(0, query_tiles, one, 0)
    dkv_ref[0, 0] = (dk_acc_ref[...] * (1.0 / LOG2E)).astype(jnp.bfloat16)
    dkv_ref[0, 1] = dv_acc_ref[...].astype(jnp.bfloat16)

    @pl.when(j == pl.num_programs(1) - 1)
    def _():
        scale = HD ** (-0.5)
        if not final:
            dq_ref[0] = acc_ref[...]
            return

        def one_out(i, carry):
            rows = pl.ds(pl.multiple_of(i * tile, tile), tile)
            turned = acc_ref[i].T * scale
            for head in range(2):
                part = turned[head * tile : (head + 1) * tile]
                part = part * cos_ref[rows, :] - pltpu.roll(part, SPAN, 1) * sin_ref[rows, :]
                dq_ref[rows, head * LANES : (head + 1) * LANES] = part.astype(jnp.bfloat16)
            return carry

        lax.fori_loop(0, query_tiles, one_out, 0)


def attend_back(meta, carry, first, second, q, kv, away, o, d_out, lse, cosine, sine, tile):
    rows, q_width = q.shape
    keys = kv.shape[1] // 2
    groups = q_width // (2 * LANES)
    query_tiles = rows // tile
    key_tiles = keys // tile
    skip = key_tiles if away else 0
    acc_block = pl.BlockSpec((1, query_tiles, LANES, 2 * tile), lambda g, j, m: (g, 0, 0, 0))
    acc_shape = jax.ShapeDtypeStruct((groups, query_tiles, LANES, 2 * tile), jnp.float32)
    if away:
        carry = jnp.zeros((1, 1, 8, LANES), jnp.float32)
        carry_block = pl.BlockSpec((1, 1, 8, LANES), lambda g, j, m: (0, 0, 0, 0))
    else:
        carry_block = acc_block
    whole_q = pl.BlockSpec((rows, 2 * LANES), lambda g, j, m: (0, g))
    return pl.pallas_call(
        functools.partial(attend_back_kernel, not away),
        grid_spec=pltpu.PrefetchScalarGridSpec(
            num_scalar_prefetch=1,
            grid=(groups, key_tiles),
            in_specs=[
                carry_block,
                pl.BlockSpec(memory_space=pl.ANY),
                pl.BlockSpec(memory_space=pl.ANY),
                whole_q,
                pl.BlockSpec((1, tile, LANES), lambda g, j, m: (g, skip + j, 0)),
                pl.BlockSpec((1, tile, LANES), lambda g, j, m: (groups + g, skip + j, 0)),
                whole_q,
                whole_q,
                pl.BlockSpec((1, query_tiles, 1, 2 * tile), lambda g, j, m: (g, 0, 0, 0)),
                pl.BlockSpec((rows, LANES), lambda g, j, m: (0, 0)),
                pl.BlockSpec((rows, LANES), lambda g, j, m: (0, 0)),
            ],
            out_specs=[
                acc_block if away else whole_q,
                pl.BlockSpec((1, 2, tile, LANES), lambda g, j, m: (g, 0, j, 0)),
            ],
            scratch_shapes=[
                pltpu.VMEM((query_tiles, 1, 2 * tile), jnp.float32),
                pltpu.VMEM((query_tiles, LANES, 2 * tile), jnp.float32),
                pltpu.VMEM((tile, LANES), jnp.float32),
                pltpu.VMEM((tile, LANES), jnp.float32),
            ],
        ),
        out_shape=[
            acc_shape if away else jax.ShapeDtypeStruct((rows, q_width), jnp.bfloat16),
            jax.ShapeDtypeStruct((groups, 2, keys, LANES), jnp.bfloat16),
        ],
        compiler_params=pltpu.CompilerParams(vmem_limit_bytes=VMEM_BYTES),
        cost_estimate=pl.CostEstimate(
            flops=20 * rows * keys * LANES * groups * 2, bytes_accessed=8_000_000, transcendentals=0
        ),
        name="attend_back_away" if away else "attend_back_own",
    )(meta, carry, first, second, q, kv, kv, o, d_out, lse, cosine, sine)


def middle_back_kernel(
    x_ref,
    project_ref,
    feed_ref,
    cot_ref,
    gain_ref,
    o_ref,
    wp_ref,
    grad_ref,
    d_out_ref,
    wp_grad_ref,
    gain_grad_ref,
    acc_ref,
):
    step = pl.program_id(0)
    last = pl.num_programs(0) - 1
    bf16, f32 = jnp.bfloat16, jnp.float32

    @pl.when(step == 0)
    def _():
        acc_ref[...] = jnp.zeros_like(acc_ref)
        gain_grad_ref[...] = jnp.zeros_like(gain_grad_ref)

    middle = x_ref[...].astype(f32) + project_ref[...].astype(f32)
    factor = lax.rsqrt(jnp.mean(middle * middle, axis=-1, keepdims=True) + EPSILON)
    feed_in = feed_ref[...].astype(f32)
    gain_grad_ref[...] += jnp.sum(feed_in * middle * factor, axis=0, keepdims=True)
    scaled = gain_ref[1:2, :].astype(f32) * feed_in
    grad = (
        cot_ref[...].astype(f32)
        + factor * scaled
        - middle * (factor * factor * factor * jnp.mean(scaled * middle, axis=-1, keepdims=True))
    )
    grad_ref[...] = grad
    low = grad.astype(bf16)
    d_out_ref[...] = dot(low, wp_ref[...], ((1,), (1,))).astype(bf16)
    acc_ref[...] += dot(o_ref[...], low, ((0,), (0,)))

    @pl.when(step == last)
    def _():
        for head in range(acc_ref.shape[0] // LANES):
            wp_grad_ref[head * HD : (head + 1) * HD, :] = acc_ref[
                head * LANES : head * LANES + HD, :
            ].astype(bf16)


def middle_back(x, project_sum, feed_sum, cot, gains, o, w_p):
    rows, width = x.shape
    tile = 256
    heads = o.shape[1] // LANES
    bf16, f32 = jnp.bfloat16, jnp.float32

    def rows_of(columns):
        return pl.BlockSpec((tile, columns), lambda i: (i, 0))

    def whole(array):
        return pl.BlockSpec(array.shape, lambda i: (0, 0))

    return pl.pallas_call(
        middle_back_kernel,
        grid=(rows // tile,),
        in_specs=[
            rows_of(width),
            rows_of(width),
            rows_of(width),
            rows_of(width),
            whole(gains),
            rows_of(o.shape[1]),
            whole(w_p),
        ],
        out_specs=[
            rows_of(width),
            rows_of(o.shape[1]),
            pl.BlockSpec((heads * HD, width), lambda i: (0, 0)),
            pl.BlockSpec((1, width), lambda i: (0, 0)),
        ],
        out_shape=[
            jax.ShapeDtypeStruct((rows, width), f32),
            jax.ShapeDtypeStruct(o.shape, bf16),
            jax.ShapeDtypeStruct((heads * HD, width), bf16),
            jax.ShapeDtypeStruct((1, width), f32),
        ],
        scratch_shapes=[pltpu.VMEM((o.shape[1], width), f32)],
        compiler_params=pltpu.CompilerParams(vmem_limit_bytes=VMEM_BYTES),
        cost_estimate=pl.CostEstimate(
            flops=5_000_000_000, bytes_accessed=26_000_000, transcendentals=0
        ),
        name="middle_back",
    )(x, project_sum, feed_sum, cot, gains, o, w_p)


def tail_kernel(
    first_ref,
    gate_hbm,
    gate_away_hbm,
    gate_rest_hbm,
    up_hbm,
    up_away_hbm,
    q_low_ref,
    own_ref,
    away_ref,
    normed_hbm,
    wide_hbm,
    x_hbm,
    grad_hbm,
    gain_term_ref,
    gain_ref,
    project_ref,
    spread_ref,
    cos_ref,
    sin_ref,
    out_hbm,
    share_ref,
    project_share_ref,
    gate_share_ref,
    up_share_ref,
    gain_share_ref,
    normed_ref,
    wide_ref,
    x_ref,
    grad_ref,
    gate_ref,
    gate_away_ref,
    upw_ref,
    upw_away_ref,
    low_ref,
    close_ref,
    part_ref,
    x_in_ref,
    up_ref,
    down_ref,
    p_in_ref,
    p_up_ref,
    p_down_ref,
    g_up_ref,
    g_down_ref,
    u_up_ref,
    u_down_ref,
    give_ref,
    core_in_ref,
    chip_in_ref,
    total_ref,
    gain_sum_ref,
    gain_x_ref,
    gain_z_ref,
    x_send,
    x_recv,
    up_send,
    up_recv,
    down_send,
    down_recv,
    p_up_send,
    p_up_recv,
    p_down_send,
    p_down_recv,
    g_up_send,
    g_up_recv,
    g_down_send,
    g_down_recv,
    u_up_send,
    u_up_recv,
    u_down_send,
    u_down_recv,
    core_send,
    core_recv,
    chip_send,
    chip_recv,
    back_send,
    back_recv,
    last_send,
    last_recv,
    gain_send,
    gain_recv,
    load_sem,
):
    bf16, f32 = jnp.bfloat16, jnp.float32
    planes = part_ref.shape[1]
    rows, width = x_ref.shape
    depth = width // planes
    sent_rows = gate_away_hbm.shape[0]
    loads = [
        pltpu.make_async_copy(src, dst, load_sem.at[i])
        for i, (src, dst) in enumerate(
            (
                (gate_hbm, gate_ref),
                (gate_away_hbm, gate_away_ref.at[pl.ds(0, sent_rows)]),
                (gate_rest_hbm, gate_away_ref.at[pl.ds(sent_rows, width - sent_rows)]),
                (up_hbm, upw_ref),
                (up_away_hbm, upw_away_ref),
                (normed_hbm, normed_ref),
                (wide_hbm, wide_ref),
                (x_hbm, x_ref),
                (grad_hbm, grad_ref),
            )
        )
    ]
    for load in loads:
        load.start()
    half_rows = rows // 2
    chunks = give_ref.shape[0]
    chunk = half_rows // chunks
    half_width = low_ref.shape[2]
    z = lax.axis_index("fsdp")
    c = lax.axis_index("ctx")
    t = lax.axis_index("tp")
    core = lax.rem(t, 2)
    across = {"ctx": 1 - c}
    sibling = {"tp": t + 1 - 2 * core}
    partner = {"tp": lax.rem(t + 2, 4)}

    barrier = pltpu.get_barrier_semaphore()
    for device in (across, sibling, partner):
        pl.semaphore_signal(barrier, inc=1, device_id=device, device_id_type=MESH)
    for k in range(1, planes):
        pl.semaphore_signal(
            barrier, inc=1, device_id={"fsdp": lax.rem(z + k, planes)}, device_id_type=MESH
        )
    pl.semaphore_wait(barrier, 3 + planes - 1)

    def remote(src, dst, send, recv, device):
        return pltpu.make_async_remote_copy(
            src_ref=src,
            dst_ref=dst,
            send_sem=send,
            recv_sem=recv,
            device_id=device,
            device_id_type=MESH,
        )

    def plane_rows(d):
        return pl.ds(pl.multiple_of(d * depth, depth), depth)

    def pair_source(mine_ref, away_ref):
        def source(d):
            at = plane_rows(d)
            return (mine_ref[at, :].astype(f32) + away_ref[at, :].astype(f32)).astype(bf16)

        return source

    g_begin, g_relay, g_finish, g_sent = line_sum(
        z, planes, pair_source(gate_ref, gate_away_ref),
        g_up_ref, g_down_ref, g_up_send, g_up_recv, g_down_send, g_down_recv,
    )
    u_begin, u_relay, u_finish, u_sent = line_sum(
        z, planes, pair_source(upw_ref, upw_away_ref),
        u_up_ref, u_down_ref, u_up_send, u_up_recv, u_down_send, u_down_recv,
    )

    project_half = project_ref.shape[0] // 2

    def project_over():
        return remote(
            project_ref.at[pl.ds(project_half, project_half)], p_in_ref,
            last_send.at[2], last_recv.at[2], across,
        )

    def project_source(d):
        at = plane_rows(d)
        return (
            project_ref[0:project_half, at].astype(f32) + p_in_ref[:, at].astype(f32)
        ).astype(bf16)

    p_begin, p_relay, p_finish, p_sent = line_sum(
        z, planes, project_source, p_up_ref, p_down_ref, p_up_send, p_up_recv, p_down_send, p_down_recv
    )
    order = []
    for step in range((planes + 1) // 2):
        order += [planes - 1 - step, step]
    order = order[:planes]
    project_over().start()
    for load in loads[:3]:
        load.wait()
    g_begin(0)
    for load in loads[3:5]:
        load.wait()
    u_begin(0)

    block = 256

    def lower(i, carry):
        at = pl.ds(pl.multiple_of(i * block, block), block)
        for which in range(2):
            low_ref[which, at, : 2 * LANES] = q_low_ref[
                at, which * 2 * LANES : (which + 1) * 2 * LANES
            ]
            key = own_ref[which, 0, at, :].astype(f32) + away_ref[1 - which, 0, at, :].astype(f32)
            key = key * cos_ref[at, :] - pltpu.roll(key, SPAN, 1) * sin_ref[at, :]
            low_ref[which, at, 2 * LANES : 3 * LANES] = key.astype(bf16)
            value = own_ref[which, 1, at, :].astype(f32) + away_ref[1 - which, 1, at, :].astype(f32)
            low_ref[which, at, 3 * LANES :] = value.astype(bf16)
            close_ref[which, at, :] = dot(
                low_ref[which, at, :], spread_ref[...], ((1,), (1,))
            ).astype(bf16)
        return carry

    lax.fori_loop(0, rows // block, lower, 0)

    def weight_part(which, d):
        part_ref[which, d] = dot(
            normed_ref[:, d * depth : (d + 1) * depth], close_ref[which], ((0,), (0,))
        ).astype(bf16)

    def to_neighbour(d):
        return remote(part_ref.at[1, d], x_in_ref.at[d], x_send.at[d], x_recv.at[d], across)

    loads[5].wait()
    for d in order:
        weight_part(1, d)
        to_neighbour(d).start()

    def feature_rows(start):
        at = pl.ds(pl.multiple_of(start, chunk), chunk)
        return dot(low_ref[0, at, :], wide_ref[:, :half_width], ((1,), (1,))) + dot(
            low_ref[1, at, :], wide_ref[:, half_width:], ((1,), (1,))
        )

    loads[6].wait()
    give_start = (1 - core) * half_rows
    keep_start = core * half_rows

    def to_core(i):
        return remote(give_ref.at[i], core_in_ref.at[i], core_send.at[i], core_recv.at[i], sibling)

    def to_chip(i):
        return remote(total_ref.at[keep_at(i)], chip_in_ref.at[i], chip_send.at[i], chip_recv.at[i], partner)

    def keep_at(i):
        return pl.ds(pl.multiple_of(keep_start + i * chunk, chunk), chunk)

    def give_at(i):
        return pl.ds(pl.multiple_of(give_start + i * chunk, chunk), chunk)

    def back(i):
        return remote(
            total_ref.at[keep_at(i)],
            total_ref.at[keep_at(i)],
            back_send.at[i],
            back_recv.at[i],
            sibling,
        )

    def from_core(i):
        return remote(
            total_ref.at[give_at(i)],
            total_ref.at[give_at(i)],
            back_send.at[i],
            back_recv.at[i],
            sibling,
        )

    for i in range(chunks):
        give_ref[i] = feature_rows(give_start + i * chunk).astype(bf16)
        to_core(i).start()
    for i in range(chunks):
        kept = feature_rows(keep_start + i * chunk)
        to_core(i).wait_recv()
        total_ref[keep_at(i)] = (kept + core_in_ref[i].astype(f32)).astype(bf16)
        to_chip(i).start()

    g_begin(1)
    g_relay(0)
    u_begin(1)
    u_relay(0)
    for d in order:
        weight_part(0, d)

    def add_neighbour(d):
        to_neighbour(d).wait_recv()
        part_ref[0, d] = (part_ref[0, d].astype(f32) + x_in_ref[d].astype(f32)).astype(bf16)

    q_begin, q_relay, q_finish, q_sent = line_sum(
        z, planes, lambda d: part_ref[0, pl.ds(d, 1)][0], up_ref, down_ref, up_send, up_recv, down_send, down_recv
    )

    def finish_chunk(i):
        to_chip(i).wait()
        total_ref[keep_at(i)] = (
            total_ref[keep_at(i)].astype(f32) + chip_in_ref[i].astype(f32)
        ).astype(bf16)
        back(i).start()

    def last_share():
        return remote(
            share_ref.at[0], share_ref.at[1], last_send.at[0], last_recv.at[0], across
        )

    def last_project():
        return remote(
            project_share_ref.at[0], project_share_ref.at[1], last_send.at[1], last_recv.at[1], across
        )

    def last_of(ref, i):
        return remote(ref.at[0], ref.at[1], last_send.at[i], last_recv.at[i], across)

    g_begin(2)
    u_begin(2)
    g_relay(1)
    finish_chunk(0)
    u_relay(1)
    project_over().wait_recv()
    for step in range(planes - 1):
        p_begin(step)
    for d in order:
        add_neighbour(d)
    for step in range(planes - 1):
        q_begin(step)
    for i in range(1, chunks):
        finish_chunk(i)
    g_finish(gate_share_ref.at[0])
    last_of(gate_share_ref, 3).start()
    p_relay(0)
    u_finish(up_share_ref.at[0])
    last_of(up_share_ref, 4).start()
    q_relay(0)
    for load in loads[7:]:
        load.wait()

    gain_sum_ref[...] = jnp.zeros_like(gain_sum_ref)
    gain_sum_ref[1:2, :] = gain_term_ref[...]
    gain = gain_ref[0:1, :].astype(f32)

    def finish_rows(start):
        at = pl.ds(pl.multiple_of(start, chunk), chunk)
        x = x_ref[at, :].astype(f32)
        factor = lax.rsqrt(jnp.mean(x * x, axis=-1, keepdims=True) + EPSILON)
        normed_in = total_ref[at, :].astype(f32)
        gain_sum_ref[0:1, :] += jnp.sum(normed_in * x * factor, axis=0, keepdims=True)
        scaled = gain * normed_in
        x_ref[at, :] = (
            grad_ref[at, :]
            + factor * scaled
            - x * (factor * factor * factor * jnp.mean(scaled * x, axis=-1, keepdims=True))
        ).astype(bf16)

    for i in range(chunks):
        finish_rows(keep_start + i * chunk)
    p_relay(1)
    q_relay(1)
    for i in range(chunks):
        from_core(i).wait_recv()
        finish_rows(give_start + i * chunk)
    p_finish(project_share_ref.at[0])
    last_project().start()
    q_finish(share_ref.at[0])
    last_share().start()
    out_copy = pltpu.make_async_copy(x_ref, out_hbm, load_sem.at[0])
    out_copy.start()

    gain_over = remote(gain_sum_ref, gain_x_ref, gain_send.at[0], gain_recv.at[0], across)
    gain_over.start()
    gain_over.wait()
    gain_sum_ref[...] = gain_sum_ref[...] + gain_x_ref[...]

    def gain_to(k):
        plane = lax.rem(z + k, planes)
        return remote(
            gain_sum_ref.at[:, pl.ds(pl.multiple_of(plane * depth, depth), depth)],
            gain_z_ref.at[k],
            gain_send.at[k],
            gain_recv.at[k],
            {"fsdp": plane},
        )

    for k in range(1, planes):
        gain_to(k).start()
    gain_share_ref[...] = gain_sum_ref[:, pl.ds(pl.multiple_of(z * depth, depth), depth)]
    for k in range(1, planes):
        gain_to(k).wait_recv()
        gain_share_ref[...] += gain_z_ref[k]

    last_share().wait()
    last_project().wait()
    last_of(gate_share_ref, 3).wait()
    last_of(up_share_ref, 4).wait()
    project_over().wait_send()
    p_sent()
    g_sent()
    u_sent()
    q_sent()
    out_copy.wait()
    for k in range(1, planes):
        gain_to(k).wait_send()
    for i in range(chunks):
        to_core(i).wait_send()
        back(i).wait_send()
    for d in range(planes):
        to_neighbour(d).wait_send()


def tail(
    first, gate, gate_away, gate_rest, upw, up_away, q_low, own, away, normed, wide, x, grad,
    gain_term, gains, project, spread, cosine, sine, planes,
):
    rows, width = x.shape
    depth = width // planes
    half_width = wide.shape[1] // 2
    close_width = spread.shape[0]
    chunks = 2
    chunk = rows // 2 // chunks
    bf16, f32 = jnp.bfloat16, jnp.float32
    vmem = pl.BlockSpec(memory_space=pltpu.VMEM)
    dma = pltpu.SemaphoreType.DMA
    operands = (
        first, gate, gate_away, gate_rest, upw, up_away, q_low, own, away, normed, wide, x, grad,
        gain_term, gains, project, spread, cosine, sine,
    )
    units = gate.shape[1]
    unit_line = pltpu.VMEM((planes - 1, depth, units), bf16)
    anywhere = pl.BlockSpec(memory_space=pl.ANY)
    line = pltpu.VMEM((planes, depth, close_width), bf16)
    short_line = pltpu.VMEM((planes - 1, depth, close_width), bf16)
    project_line = pltpu.VMEM((planes - 1, project.shape[0] // 2, depth), bf16)
    return pl.pallas_call(
        tail_kernel,
        in_specs=[anywhere] * 6 + [vmem] * 3 + [anywhere] * 4 + [vmem] * (len(operands) - 13),
        out_specs=[anywhere] + [vmem] * 5,
        out_shape=[
            jax.ShapeDtypeStruct((rows, width), bf16),
            jax.ShapeDtypeStruct((2, depth, close_width), bf16),
            jax.ShapeDtypeStruct((2, project.shape[0] // 2, depth), bf16),
            jax.ShapeDtypeStruct((2, depth, units), bf16),
            jax.ShapeDtypeStruct((2, depth, units), bf16),
            jax.ShapeDtypeStruct((8, depth), f32),
        ],
        scratch_shapes=[
            pltpu.VMEM((rows, width), bf16),
            pltpu.VMEM(wide.shape, bf16),
            pltpu.VMEM((rows, width), bf16),
            pltpu.VMEM((rows, width), f32),
            pltpu.VMEM((width, units), bf16),
            pltpu.VMEM((width, units), bf16),
            pltpu.VMEM((width, units), bf16),
            pltpu.VMEM((width, units), bf16),
            pltpu.VMEM((2, rows, half_width), bf16),
            pltpu.VMEM((2, rows, close_width), bf16),
            pltpu.VMEM((2, planes, depth, close_width), bf16),
            line,
            short_line,
            short_line,
            pltpu.VMEM((project.shape[0] // 2, width), bf16),
            project_line,
            project_line,
            unit_line,
            unit_line,
            unit_line,
            unit_line,
            pltpu.VMEM((chunks, chunk, width), bf16),
            pltpu.VMEM((chunks, chunk, width), bf16),
            pltpu.VMEM((chunks, chunk, width), bf16),
            pltpu.VMEM((rows, width), bf16),
            pltpu.VMEM((8, width), f32),
            pltpu.VMEM((8, width), f32),
            pltpu.VMEM((planes, 8, depth), f32),
        ]
        + [dma((planes,))] * 18
        + [dma((chunks,))] * 6
        + [dma((5,))] * 2
        + [dma((planes,))] * 2
        + [dma((9,))],
        compiler_params=pltpu.CompilerParams(
            collective_id=2, has_side_effects=True, vmem_limit_bytes=VMEM_BYTES + (3 << 19)
        ),
        cost_estimate=pl.CostEstimate(
            flops=60_000_000_000, bytes_accessed=24_000_000, transcendentals=0
        ),
        name="tail",
    )(*operands)


def feed_kernel(
    x_hbm,
    project_hbm,
    cot_hbm,
    gain_ref,
    gate_hbm,
    up_hbm,
    down_hbm,
    total_hbm,
    gate_m_hbm,
    gate_away_hbm,
    gate_rest_hbm,
    up_m_hbm,
    up_o_hbm,
    down_grad_hbm,
    down_rows_hbm,
    x_ref,
    project_ref,
    cot_ref,
    gate_ref,
    up_ref,
    down_ref,
    total_ref,
    grad_ref,
    down_grad_ref,
    down_rows_ref,
    gate_o_ref,
    normed_ref,
    turned_ref,
    hidden_ref,
    gate_back_ref,
    up_back_ref,
    give_ref,
    core_in_ref,
    keep_ref,
    chip_in_ref,
    load_sem,
    store_sem,
    core_send,
    core_recv,
    chip_send,
    chip_recv,
    back_send,
    back_recv,
    x_send,
    x_recv,
    over_send,
    over_recv,
):
    bf16, f32 = jnp.bfloat16, jnp.float32
    rows, width = x_ref.shape
    half_rows = rows // 2
    chunks, chunk, _ = give_ref.shape
    units = gate_ref.shape[2]
    c = lax.axis_index("ctx")
    t = lax.axis_index("tp")
    core = lax.rem(t, 2)
    across = {"ctx": 1 - c}
    sibling = {"tp": t + 1 - 2 * core}
    partner = {"tp": lax.rem(t + 2, 4)}

    loads = [
        pltpu.make_async_copy(src, dst, load_sem.at[i])
        for i, (src, dst) in enumerate(
            (
                (x_hbm, x_ref),
                (project_hbm, project_ref),
                (gate_hbm, gate_ref),
                (up_hbm, up_ref),
                (cot_hbm, cot_ref),
                (down_hbm, down_ref),
            )
        )
    ]
    for load in loads:
        load.start()

    barrier = pltpu.get_barrier_semaphore()
    for device in (across, sibling, partner):
        pl.semaphore_signal(barrier, inc=1, device_id=device, device_id_type=MESH)
    pl.semaphore_wait(barrier, 3)

    def remote(src, dst, send, recv, device):
        return pltpu.make_async_remote_copy(
            src_ref=src,
            dst_ref=dst,
            send_sem=send,
            recv_sem=recv,
            device_id=device,
            device_id_type=MESH,
        )

    give_start = (1 - core) * half_rows
    keep_start = core * half_rows
    gain = gain_ref[1:2, :].astype(f32)

    def feature_rows(start, first):
        at = pl.ds(pl.multiple_of(start, chunk), chunk)
        if first:
            loads[0].wait()
            loads[1].wait()
        middle = x_ref[at, :].astype(f32) + project_ref[at, :].astype(f32)
        factor = lax.rsqrt(jnp.mean(middle * middle, axis=-1, keepdims=True) + EPSILON)
        normed = (middle * factor * gain).astype(bf16)
        normed_ref[...] = normed
        turned_ref[:, at] = normed.T
        if first:
            for load in loads[2:]:
                load.wait()
        for which in range(2):
            cols = slice(which * units, (which + 1) * units)
            gate = dot(normed_ref[...], gate_ref[which], ((1,), (0,)))
            up = dot(normed_ref[...], up_ref[which], ((1,), (0,)))
            hidden_in = dot(cot_ref[at, :], down_ref[which], ((1,), (1,)))
            sigmoid = jax.nn.sigmoid(gate)
            silu = gate * sigmoid
            hidden_ref[at, cols] = (silu * up).astype(bf16)
            gate_back_ref[at, cols] = (
                hidden_in * up * sigmoid * (1.0 + gate * (1.0 - sigmoid))
            ).astype(bf16)
            up_back_ref[at, cols] = (hidden_in * silu).astype(bf16)
        return sum(
            dot(back_ref[at, which * units : (which + 1) * units], weight[which], ((1,), (1,)))
            for which in range(2)
            for back_ref, weight in ((gate_back_ref, gate_ref), (up_back_ref, up_ref))
        )

    def to_core(i):
        return remote(give_ref.at[i], core_in_ref.at[i], core_send.at[i], core_recv.at[i], sibling)

    def to_chip(i):
        return remote(keep_ref.at[i], chip_in_ref.at[i], chip_send.at[i], chip_recv.at[i], partner)

    def back(i, start):
        at = pl.ds(pl.multiple_of(start + i * chunk, chunk), chunk)
        return remote(
            total_ref.at[at], total_ref.at[at], back_send.at[i], back_recv.at[i], sibling
        )

    for i in range(chunks):
        give_ref[i] = feature_rows(give_start + i * chunk, i == 0).astype(bf16)
        to_core(i).start()
        kept = feature_rows(keep_start + i * chunk, False)
        to_core(i).wait_recv()
        keep_ref[i] = (kept + core_in_ref[i].astype(f32)).astype(bf16)
        to_chip(i).start()

    block = 256

    def weight_rows(back_ref, which, out_ref, begin, count, block=256):
        def some(i, carry):
            at = pl.ds(pl.multiple_of(i * block, block), block)
            out_ref[at, :] = dot(
                turned_ref[at, :], back_ref[:, which * units : (which + 1) * units], ((1,), (0,))
            ).astype(bf16)
            return carry

        lax.fori_loop(begin // block, (begin + count) // block, some, 0)

    def finish_chunk(i):
        to_chip(i).wait()
        at = pl.ds(pl.multiple_of(keep_start + i * chunk, chunk), chunk)
        total_ref[at, :] = (keep_ref[i].astype(f32) + chip_in_ref[i].astype(f32)).astype(bf16)
        back(i, keep_start).start()

    planes, _, depth = down_grad_ref.shape
    pieces = gate_away_hbm.shape[0] // depth

    def over(i):
        at = pl.ds(i * depth, depth)
        return remote(gate_o_ref.at[at], gate_away_hbm.at[at], x_send.at[i], x_recv.at[i], across)

    def down_over(i):
        at = pl.ds(pl.multiple_of(give_start + i * chunk, chunk), chunk)
        return remote(
            down_rows_ref.at[at], core_in_ref.at[i], over_send.at[i], over_recv.at[i], sibling
        )

    stores = []

    def store(src, dst):
        copy = pltpu.make_async_copy(src, dst, store_sem.at[len(stores)])
        copy.start()
        stores.append(copy)

    for i in range(pieces):
        weight_rows(gate_back_ref, 1, gate_o_ref, i * depth, depth, depth)
        over(i).start()
    weight_rows(gate_back_ref, 1, gate_o_ref, pieces * depth, width - pieces * depth, depth)
    store(gate_o_ref.at[pl.ds(pieces * depth, width - pieces * depth)], gate_rest_hbm)
    weight_rows(up_back_ref, 1, grad_ref.at[0], 0, width)
    store(grad_ref.at[0], up_o_hbm)
    for i in range(chunks // 2):
        finish_chunk(i)
    weight_rows(gate_back_ref, 0, grad_ref.at[1], 0, width)
    store(grad_ref.at[1], gate_m_hbm)
    weight_rows(up_back_ref, 0, grad_ref.at[2], 0, width)
    store(grad_ref.at[2], up_m_hbm)

    def down_grads(i, carry):
        at = pl.ds(pl.multiple_of(i * block, block), block)
        part = dot(hidden_ref[:, at], cot_ref[...], ((0,), (0,))).astype(bf16)
        planes, _, depth = down_grad_ref.shape
        for d in range(planes):
            down_grad_ref[d, at, :] = part[:, d * depth : (d + 1) * depth]
        return carry

    lax.fori_loop(0, 2 * units // block, down_grads, 0)
    store(down_grad_ref, down_grad_hbm)

    def down_features(i, carry):
        at = pl.ds(pl.multiple_of(i * block, block), block)
        down_rows_ref[at, :] = (
            dot(hidden_ref[at, :units], down_ref[0], ((1,), (0,)))
            + dot(hidden_ref[at, units:], down_ref[1], ((1,), (0,)))
        ).astype(bf16)
        return carry

    lax.fori_loop(0, rows // block, down_features, 0)
    for i in range(chunks // 2):
        back(i, give_start).wait_recv()
    for i in range(chunks // 2, chunks):
        finish_chunk(i)
    for i in range(chunks // 2, chunks):
        back(i, give_start).wait_recv()
    store(total_ref, total_hbm)
    for i in range(chunks):
        down_over(i).start()
    for i in range(chunks):
        down_over(i).wait()
        at = pl.ds(pl.multiple_of(keep_start + i * chunk, chunk), chunk)
        keep_ref[i] = (down_rows_ref[at, :].astype(f32) + core_in_ref[i].astype(f32)).astype(bf16)
    store(keep_ref, down_rows_hbm)
    for i in range(chunks):
        to_core(i).wait_send()
        back(i, keep_start).wait_send()
    for i in range(pieces):
        over(i).wait()
    for copy in stores:
        copy.wait()


def feed(x, project_sum, cot, gains, gate_w, up_w, down_w, planes):
    rows, width = x.shape
    units = gate_w.shape[2]
    chunk = 256
    chunks = rows // 2 // chunk
    depth = width // planes
    sent = 2 * depth
    bf16 = jnp.bfloat16
    vmem = pl.BlockSpec(memory_space=pltpu.VMEM)
    anywhere = pl.BlockSpec(memory_space=pl.ANY)
    dma = pltpu.SemaphoreType.DMA
    operands = (x, project_sum, cot, gains, gate_w, up_w, down_w)
    piece = pltpu.VMEM((chunks, chunk, width), bf16)
    rows_by_width = pltpu.VMEM((rows, width), bf16)
    rows_by_units = pltpu.VMEM((rows, 2 * units), bf16)
    weight = jax.ShapeDtypeStruct((width, units), bf16)
    return pl.pallas_call(
        feed_kernel,
        in_specs=[anywhere] * 3 + [vmem] + [anywhere] * 3,
        out_specs=[anywhere] * 8,
        out_shape=[
            jax.ShapeDtypeStruct((rows, width), bf16),
            weight,
            jax.ShapeDtypeStruct((sent, units), bf16),
            jax.ShapeDtypeStruct((width - sent, units), bf16),
            weight,
            weight,
            jax.ShapeDtypeStruct((planes, 2 * units, width // planes), bf16),
            jax.ShapeDtypeStruct((chunks, chunk, width), bf16),
        ],
        scratch_shapes=[
            rows_by_width,
            rows_by_width,
            rows_by_width,
            pltpu.VMEM(gate_w.shape, bf16),
            pltpu.VMEM(up_w.shape, bf16),
            pltpu.VMEM(down_w.shape, bf16),
            rows_by_width,
            pltpu.VMEM((3, width, units), bf16),
            pltpu.VMEM((planes, 2 * units, width // planes), bf16),
            rows_by_width,
            pltpu.VMEM((width, units), bf16),
            pltpu.VMEM((chunk, width), bf16),
            pltpu.VMEM((width, rows), bf16),
            rows_by_units,
            rows_by_units,
            rows_by_units,
            piece,
            piece,
            piece,
            piece,
            dma((6,)),
            dma((7,)),
        ]
        + [dma((chunks,))] * 6
        + [dma((sent // depth,))] * 2
        + [dma((chunks,))] * 2,
        compiler_params=pltpu.CompilerParams(
            collective_id=3, has_side_effects=True, vmem_limit_bytes=VMEM_BYTES
        ),
        cost_estimate=pl.CostEstimate(
            flops=50_000_000_000, bytes_accessed=40_000_000, transcendentals=0
        ),
        name="feed",
    )(*operands)


def paired_body(
    tokens,
    prefix_len,
    positions,
    gain_attend,
    w_query,
    w_key,
    w_value,
    w_project,
    gain_feed,
    w_gate,
    w_up,
    w_down,
    cotangent,
):
    seqs, rows, width = tokens.shape
    assert seqs == 1
    c = lax.axis_index("ctx")
    bf16, f32 = jnp.bfloat16, jnp.float32

    def half(array, axis, which=None):
        size = array.shape[axis] // 2
        which = c if which is None else which
        return lax.dynamic_slice_in_dim(array, which * size, size, axis)

    def ordered(mine, other, axis):
        return jnp.where(
            c == 0,
            jnp.concatenate([mine, other], axis=axis),
            jnp.concatenate([other, mine], axis=axis),
        )

    planes = lax.axis_size("fsdp")
    kv_half = w_key.shape[1] // 2
    q_half = w_query.shape[1] // 2

    def packed(which):
        return jnp.concatenate(
            [half(w_query, 1, which), half(w_key, 1, which), half(w_value, 1, which)], axis=1
        )

    gain_rows = jnp.pad(jnp.stack([gain_attend, gain_feed]), ((0, GAIN_ROWS - 2), (0, 0)))
    pack = jnp.concatenate([packed(c), gain_rows], axis=0)

    def parts(block):
        return (
            block[:, :q_half],
            block[:, q_half : q_half + kv_half],
            block[:, q_half + kv_half :],
        )

    half_heads = (q_half + 2 * kv_half) // HD
    spread = np.zeros((half_heads * HD, half_heads * LANES), np.float32)
    for head in range(half_heads):
        for lane in range(HD):
            turned = lane if lane < HALF or head == half_heads - 1 else lane - HALF + SPAN
            spread[head * HD + lane, head * LANES + turned] = 1.0
    spread = jnp.asarray(spread, bf16)

    frequency = ROPE_BASE ** (-(jnp.arange(HALF, dtype=f32) * 2.0 / HD))
    frequency = jnp.pad(frequency, (0, SPAN - HALF))
    angles = positions[0].astype(f32)[:, None] * frequency
    cosine = jnp.cos(angles)
    sine = jnp.sin(angles)
    cosine = jnp.concatenate([cosine, cosine], axis=1)
    sine = jnp.concatenate([-sine, sine], axis=1)

    block_len = rows // 2
    tile = min(256, block_len)
    query_tiles = rows // tile
    own = c * rows + tile * jnp.arange(query_tiles, dtype=jnp.int32)
    opposite = (1 - c) * rows + tile * jnp.arange(query_tiles, dtype=jnp.int32)
    own, opposite = natural_index(own, block_len, 2), natural_index(opposite, block_len, 2)
    meta = jnp.concatenate([prefix_len.astype(jnp.int32), own, own, opposite])

    x = tokens[0]
    cot = cotangent[0]
    (
        normed, q, kv_all, w_qkv, w_p, gains, o, lse, project_sum, wg, wu, wd,
    ) = front(
        prefix_len, x, pack, packed(1 - c), spread, cosine, sine,
        w_project.reshape(-1, HD, w_project.shape[1]), w_gate, w_up, w_down, planes,
    )
    w_p = w_p.reshape(-1, width)
    (
        feed_sum, gate_mine, gate_away, gate_rest, up_mine, up_other, down_part, down_rows,
    ) = feed(x, project_sum, cot, gains, wg, wu, wd, planes)

    gate_rest, up_away = swap_ctx(gate_rest), swap_ctx(up_other)
    down_share = lax.psum_scatter(down_part, "fsdp", scatter_dimension=0, tiled=False)
    down_away = swap_ctx(down_share)
    size = down_share.shape[0] // 2
    down_mine = down_share[:size].astype(f32) + down_away[size:].astype(f32)
    down_other = down_share[size:].astype(f32) + down_away[:size].astype(f32)
    down_grad = ordered(down_mine, down_other, 0)

    middle_grad, d_out, project_part, gain_two_term = middle_back(
        x, project_sum, feed_sum, cot, gains, o, w_p
    )
    def added(a, b):
        return (a.astype(f32) + b.astype(f32)).astype(bf16)

    down_total = added(down_rows, swap_chip(down_rows)).reshape(rows // 2, width)
    down_sum = by_core(down_total, swap_core(down_total))
    layer_output = (
        x.astype(f32) + project_sum.astype(f32) + down_sum.astype(f32)
    ).astype(bf16)
    dq_away, d_kv_away = attend_back(
        meta, None, d_out, d_out, q, kv_all, True, o, d_out, lse, cosine, sine, tile
    )
    d_kv_away = swap_ctx(d_kv_away)
    q_low, d_kv_own = attend_back(
        meta, dq_away, gate_rest, up_away, q, kv_all, False, o, d_out, lse, cosine, sine, tile
    )
    tokens_grad, share, project_share, gate_share, up_share, gain_share = tail(
        down_share, gate_mine, gate_away, gate_rest, up_mine, up_away, q_low, d_kv_own, d_kv_away, normed, w_qkv, x, middle_grad,
        gain_two_term, gains, project_part, spread, cosine, sine, planes,
    )
    shares = [
        ordered(a, b, 1).astype(f32) for a, b in zip(parts(share[0]), parts(share[1]))
    ]
    return (
        layer_output[None],
        tokens_grad[None],
        gain_share[0],
        shares[0],
        shares[1],
        shares[2],
        ordered(project_share[0], project_share[1], 0).astype(f32),
        gain_share[1],
        ordered(gate_share[0], gate_share[1], 1).astype(f32),
        ordered(up_share[0], up_share[1], 1).astype(f32),
        down_grad,
    )


def solution(mesh):
    paired = mesh.shape["ctx"] == 2 and mesh.shape["tp"] == 4 and mesh.shape["fsdp"] == 4
    return jax.shard_map(
        paired_body if paired else general_body,
        mesh=mesh,
        in_specs=(
            P("fsdp", "ctx", None),
            P("fsdp"),
            P("fsdp", "ctx"),
            P("fsdp"),
            P("fsdp", "tp"),
            P("fsdp", "tp"),
            P("fsdp", "tp"),
            P("tp", "fsdp"),
            P("fsdp"),
            P("fsdp", "tp"),
            P("fsdp", "tp"),
            P("tp", "fsdp"),
            P("fsdp", "ctx", None),
        ),
        out_specs=(
            P("fsdp", "ctx", None),
            P("fsdp", "ctx", None),
            P("fsdp"),
            P("fsdp", "tp"),
            P("fsdp", "tp"),
            P("fsdp", "tp"),
            P("tp", "fsdp"),
            P("fsdp"),
            P("fsdp", "tp"),
            P("fsdp", "tp"),
            P("tp", "fsdp"),
        ),
        check_vma=False,
    )
```

```python
import functools
import math

import jax
import jax.numpy as jnp
import numpy as np
from jax import lax
from jax.experimental import pallas as pl
from jax.experimental.pallas import tpu as pltpu
from jax.sharding import PartitionSpec as P

HQ = 16
KVH = 8
HD = 96


EPSILON = 1e-05
ROPE_BASE = 100000.0
NEGATIVE = -1e30


def natural_index(stored, block_len, pair_count):
    device = stored // (2 * block_len)
    second_half = stored // block_len % 2
    within = stored % block_len
    block_id = jnp.where(second_half == 0, device, 2 * pair_count - 1 - device)
    return block_id * block_len + within


def rotate(values, cosine_table, sine_table):
    half_width = values.shape[-1] // 2
    leading = values[..., :half_width]
    trailing = values[..., half_width:]
    return jnp.concatenate(
        [
            leading * cosine_table - trailing * sine_table,
            trailing * cosine_table + leading * sine_table,
        ],
        axis=-1,
    )


def rotate_back(incoming, cosine_table, sine_table):
    half_width = incoming.shape[-1] // 2
    leading = incoming[..., :half_width]
    trailing = incoming[..., half_width:]
    return jnp.concatenate(
        [
            leading * cosine_table + trailing * sine_table,
            trailing * cosine_table - leading * sine_table,
        ],
        axis=-1,
    )


def rms_factor(values):
    return lax.rsqrt(jnp.mean(values * values, axis=-1, keepdims=True) + EPSILON)


def rms_back(values, factor, gain_row, incoming):
    scaled = gain_row * incoming
    return factor * scaled - values * factor**3 * jnp.mean(scaled * values, axis=-1, keepdims=True)


def tensor_sum(term_rows):
    return lax.psum(term_rows.astype(jnp.bfloat16), "tp").astype(jnp.float32)


def general_body(
    tokens,
    prefix_len,
    positions,
    gain_attend,
    w_query,
    w_key,
    w_value,
    w_project,
    gain_feed,
    w_gate,
    w_up,
    w_down,
    cotangent,
):
    (
        gain_one,
        query_weight_whole,
        key_weight_whole,
        value_weight_whole,
        project_weight_whole,
        gain_two,
        gate_weight_whole,
        up_weight_whole,
        down_weight_whole,
    ) = (
        lax.all_gather(gain_attend, "fsdp", axis=0, tiled=True),
        lax.all_gather(w_query, "fsdp", axis=0, tiled=True),
        lax.all_gather(w_key, "fsdp", axis=0, tiled=True),
        lax.all_gather(w_value, "fsdp", axis=0, tiled=True),
        lax.all_gather(w_project, "fsdp", axis=1, tiled=True),
        lax.all_gather(gain_feed, "fsdp", axis=0, tiled=True),
        lax.all_gather(w_gate, "fsdp", axis=0, tiled=True),
        lax.all_gather(w_up, "fsdp", axis=0, tiled=True),
        lax.all_gather(w_down, "fsdp", axis=1, tiled=True),
    )
    seq_count, rows_local, _ = tokens.shape
    pair_count = lax.axis_size("ctx")
    block_len = rows_local // 2
    query_width = query_weight_whole.shape[1]
    kv_width = key_weight_whole.shape[1]
    query_heads = query_width // HD
    kv_heads = kv_width // HD
    group_size = HQ // KVH
    score_scale = HD ** (-0.5)
    frequency = ROPE_BASE ** (-(jnp.arange(HD // 2, dtype=jnp.float32) * 2.0 / HD))
    angles = positions.astype(jnp.float32)[:, :, None] * frequency
    cosine_table = jnp.cos(angles)[:, :, None, :]
    sine_table = jnp.sin(angles)[:, :, None, :]
    stored_rows = lax.axis_index("ctx") * rows_local + jnp.arange(rows_local, dtype=jnp.int32)
    query_order = natural_index(stored_rows, block_len, pair_count)

    def visible_mask(key_order):
        causal = key_order[None, None, :] <= query_order[None, :, None]
        opened = key_order[None, None, :] < prefix_len[:, None, None]
        return (causal | opened)[:, :, None, None, :]

    inputs = tokens.astype(jnp.float32)
    factor_one = rms_factor(inputs)
    normed_hidden = (inputs * factor_one * gain_one.astype(jnp.float32)).astype(jnp.bfloat16)
    query_projected = jnp.einsum(
        "rxc,cf->rxf", normed_hidden, query_weight_whole, preferred_element_type=jnp.float32
    )
    key_projected = jnp.einsum(
        "rxc,cf->rxf", normed_hidden, key_weight_whole, preferred_element_type=jnp.float32
    )
    value_projected = jnp.einsum(
        "rxc,cf->rxf", normed_hidden, value_weight_whole, preferred_element_type=jnp.float32
    )
    queries = (
        rotate(
            query_projected.reshape(seq_count, rows_local, query_heads, HD),
            cosine_table,
            sine_table,
        )
        .astype(jnp.bfloat16)
        .reshape(seq_count, rows_local, kv_heads, group_size, HD)
    )
    keys_rot = (
        rotate(key_projected.reshape(seq_count, rows_local, kv_heads, HD), cosine_table, sine_table)
        .astype(jnp.bfloat16)
        .reshape(seq_count, rows_local, kv_width)
    )
    values_low = value_projected.astype(jnp.bfloat16)
    stat_shape = (seq_count, rows_local, kv_heads, group_size)
    initial = (
        jnp.full(stat_shape, NEGATIVE, jnp.float32),
        jnp.zeros(stat_shape, jnp.float32),
        jnp.zeros(stat_shape + (HD,), jnp.float32),
    )
    key_piece = lax.all_gather(keys_rot, "ctx", axis=1, tiled=True)
    value_piece = lax.all_gather(values_low, "ctx", axis=1, tiled=True)
    key_total = key_piece.shape[1]
    span_rows = math.gcd(key_total, rows_local)

    def one_span(span_index, running):
        run_max, run_sum, run_acc = running
        span_start = span_index * span_rows
        key_rows = lax.dynamic_slice_in_dim(key_piece, span_start, span_rows, 1).reshape(
            seq_count, span_rows, kv_heads, HD
        )
        value_rows = lax.dynamic_slice_in_dim(value_piece, span_start, span_rows, 1).reshape(
            seq_count, span_rows, kv_heads, HD
        )
        key_order = natural_index(
            span_start + jnp.arange(span_rows, dtype=jnp.int32), block_len, pair_count
        )
        visible = visible_mask(key_order)
        scores = (
            jnp.einsum("slhgd,skhd->slhgk", queries, key_rows, preferred_element_type=jnp.float32)
            * score_scale
        )
        new_max = jnp.maximum(run_max, jnp.max(jnp.where(visible, scores, NEGATIVE), axis=-1))
        weights_raw = jnp.where(visible, jnp.exp(scores - new_max[..., None]), 0.0)
        rescale = jnp.exp(run_max - new_max)
        run_sum = run_sum * rescale + jnp.sum(weights_raw, axis=-1)
        run_acc = run_acc * rescale[..., None] + jnp.einsum(
            "slhgk,skhd->slhgd",
            weights_raw.astype(jnp.bfloat16),
            value_rows,
            preferred_element_type=jnp.float32,
        )
        return (new_max, run_sum, run_acc)

    run_max, run_sum, run_acc = lax.fori_loop(0, key_total // span_rows, one_span, initial)
    attended = run_acc / run_sum[..., None]
    log_total = run_max + jnp.log(run_sum)
    attended_reduced = attended.reshape(seq_count, rows_local, query_width).astype(jnp.bfloat16)
    project_rows = jnp.einsum(
        "hxz,zm->hxm", attended_reduced, project_weight_whole, preferred_element_type=jnp.float32
    )
    middle = inputs + tensor_sum(project_rows)
    factor_two = rms_factor(middle)
    normed_feed_input = (middle * factor_two * gain_two.astype(jnp.float32)).astype(jnp.bfloat16)
    gate_activation = jnp.einsum(
        "qeh,hj->qej", normed_feed_input, gate_weight_whole, preferred_element_type=jnp.float32
    )
    up_activation = jnp.einsum(
        "qeh,hj->qej", normed_feed_input, up_weight_whole, preferred_element_type=jnp.float32
    )
    sigmoid_gate = jax.nn.sigmoid(gate_activation)
    silu_gate = gate_activation * sigmoid_gate
    hidden_state = (silu_gate * up_activation).astype(jnp.bfloat16)
    down_output_rows = jnp.einsum(
        "nct,tm->ncm", hidden_state, down_weight_whole, preferred_element_type=jnp.float32
    )
    layer_output = (middle + tensor_sum(down_output_rows)).astype(jnp.bfloat16)
    (
        gain_one,
        query_weight_whole,
        key_weight_whole,
        value_weight_whole,
        project_weight_whole,
        gain_two,
        gate_weight_whole,
        up_weight_whole,
        down_weight_whole,
    ) = (
        lax.all_gather(gain_attend, "fsdp", axis=0, tiled=True),
        lax.all_gather(w_query, "fsdp", axis=0, tiled=True),
        lax.all_gather(w_key, "fsdp", axis=0, tiled=True),
        lax.all_gather(w_value, "fsdp", axis=0, tiled=True),
        lax.all_gather(w_project, "fsdp", axis=1, tiled=True),
        lax.all_gather(gain_feed, "fsdp", axis=0, tiled=True),
        lax.all_gather(w_gate, "fsdp", axis=0, tiled=True),
        lax.all_gather(w_up, "fsdp", axis=0, tiled=True),
        lax.all_gather(w_down, "fsdp", axis=1, tiled=True),
    )
    hidden_grad = jnp.einsum(
        "ehv,iv->ehi", cotangent, down_weight_whole, preferred_element_type=jnp.float32
    )
    down_weight_part = jnp.einsum(
        "gqa,gqz->az", hidden_state, cotangent, preferred_element_type=jnp.float32
    )
    gate_reduced = (
        hidden_grad * up_activation * sigmoid_gate * (1.0 + gate_activation * (1.0 - sigmoid_gate))
    ).astype(jnp.bfloat16)
    up_reduced = (hidden_grad * silu_gate).astype(jnp.bfloat16)
    gate_weight_part = jnp.einsum(
        "bic,big->cg", normed_feed_input, gate_reduced, preferred_element_type=jnp.float32
    )
    up_weight_part = jnp.einsum(
        "bic,big->cg", normed_feed_input, up_reduced, preferred_element_type=jnp.float32
    )
    feed_rows = jnp.einsum(
        "vte,ce->vtc", gate_reduced, gate_weight_whole, preferred_element_type=jnp.float32
    ) + jnp.einsum("vte,ce->vtc", up_reduced, up_weight_whole, preferred_element_type=jnp.float32)
    feed_in = tensor_sum(feed_rows)
    gain_two_term = jnp.sum(feed_in * middle * factor_two, axis=(0, 1))
    middle_grad = cotangent.astype(jnp.float32) + rms_back(
        middle, factor_two, gain_two.astype(jnp.float32), feed_in
    )
    middle_reduced = middle_grad.astype(jnp.bfloat16)
    project_term = jnp.einsum(
        "xeh,xec->hc", attended_reduced, middle_reduced, preferred_element_type=jnp.float32
    )
    attended_grad = (
        jnp.einsum(
            "vhk,nk->vhn", middle_reduced, project_weight_whole, preferred_element_type=jnp.float32
        )
        .astype(jnp.bfloat16)
        .reshape(seq_count, rows_local, kv_heads, group_size, HD)
    )
    row_delta = jnp.sum(attended_grad.astype(jnp.float32) * attended, axis=-1)
    whole_keys, whole_values = (
        lax.all_gather(keys_rot[None], "ctx", axis=0, tiled=True),
        lax.all_gather(values_low[None], "ctx", axis=0, tiled=True),
    )

    def key_block(grad_acc, block_items):
        key_rows, value_rows, block_index = block_items
        key_rows = key_rows.reshape(seq_count, rows_local, kv_heads, HD)
        value_rows = value_rows.reshape(seq_count, rows_local, kv_heads, HD)
        key_order = natural_index(
            block_index * rows_local + jnp.arange(rows_local, dtype=jnp.int32),
            block_len,
            pair_count,
        )
        visible = visible_mask(key_order)
        scores = (
            jnp.einsum("slhgd,skhd->slhgk", queries, key_rows, preferred_element_type=jnp.float32)
            * score_scale
        )
        weights_norm = jnp.where(visible, jnp.exp(scores - log_total[..., None]), 0.0)
        prob_grad = jnp.einsum(
            "slhgd,skhd->slhgk", attended_grad, value_rows, preferred_element_type=jnp.float32
        )
        score_grad = (weights_norm * (prob_grad - row_delta[..., None])).astype(jnp.bfloat16)
        grad_acc = (
            grad_acc
            + jnp.einsum(
                "slhgk,skhd->slhgd", score_grad, key_rows, preferred_element_type=jnp.float32
            )
            * score_scale
        )
        key_grad = (
            jnp.einsum("slhgk,slhgd->skhd", score_grad, queries, preferred_element_type=jnp.float32)
            * score_scale
        )
        value_grad = jnp.einsum(
            "slhgk,slhgd->skhd",
            weights_norm.astype(jnp.bfloat16),
            attended_grad,
            preferred_element_type=jnp.float32,
        )
        return (
            grad_acc,
            (
                key_grad.reshape(seq_count, rows_local, kv_width),
                value_grad.reshape(seq_count, rows_local, kv_width),
            ),
        )

    block_ids = jnp.arange(pair_count, dtype=jnp.int32)
    query_grad, (key_terms, value_terms) = lax.scan(
        key_block, jnp.zeros(stat_shape + (HD,), jnp.float32), (whole_keys, whole_values, block_ids)
    )
    key_sum, value_sum = (
        lax.psum_scatter(
            key_terms.astype(jnp.bfloat16), "ctx", scatter_dimension=0, tiled=True
        ).astype(jnp.float32),
        lax.psum_scatter(
            value_terms.astype(jnp.bfloat16), "ctx", scatter_dimension=0, tiled=True
        ).astype(jnp.float32),
    )
    key_reduced = (
        rotate_back(
            key_sum[0].reshape(seq_count, rows_local, kv_heads, HD), cosine_table, sine_table
        )
        .astype(jnp.bfloat16)
        .reshape(seq_count, rows_local, kv_width)
    )
    value_backward = value_sum[0].astype(jnp.bfloat16)
    query_reduced = (
        rotate_back(
            query_grad.reshape(seq_count, rows_local, query_heads, HD), cosine_table, sine_table
        )
        .astype(jnp.bfloat16)
        .reshape(seq_count, rows_local, query_width)
    )
    query_weight_part = jnp.einsum(
        "prb,pro->bo", normed_hidden, query_reduced, preferred_element_type=jnp.float32
    )
    key_weight_part = jnp.einsum(
        "prb,pro->bo", normed_hidden, key_reduced, preferred_element_type=jnp.float32
    )
    value_weight_part = jnp.einsum(
        "prb,pro->bo", normed_hidden, value_backward, preferred_element_type=jnp.float32
    )
    normed_rows = (
        jnp.einsum(
            "kjw,iw->kji", query_reduced, query_weight_whole, preferred_element_type=jnp.float32
        )
        + jnp.einsum(
            "kjw,iw->kji", key_reduced, key_weight_whole, preferred_element_type=jnp.float32
        )
        + jnp.einsum(
            "kjw,iw->kji", value_backward, value_weight_whole, preferred_element_type=jnp.float32
        )
    )
    normed_grad = tensor_sum(normed_rows)
    gain_one_term = jnp.sum(normed_grad * inputs * factor_one, axis=(0, 1))
    tokens_grad = (
        middle_grad + rms_back(inputs, factor_one, gain_one.astype(jnp.float32), normed_grad)
    ).astype(jnp.bfloat16)
    (
        part_one,
        part_query,
        part_key,
        part_value,
        part_project,
        part_two,
        part_gate,
        part_up,
        part_down,
    ) = (
        lax.psum_scatter(gain_one_term, ("fsdp", "ctx"), scatter_dimension=0, tiled=True),
        lax.psum_scatter(query_weight_part, ("fsdp", "ctx"), scatter_dimension=0, tiled=True),
        lax.psum_scatter(key_weight_part, ("fsdp", "ctx"), scatter_dimension=0, tiled=True),
        lax.psum_scatter(value_weight_part, ("fsdp", "ctx"), scatter_dimension=0, tiled=True),
        lax.psum_scatter(project_term, ("fsdp", "ctx"), scatter_dimension=1, tiled=True),
        lax.psum_scatter(gain_two_term, ("fsdp", "ctx"), scatter_dimension=0, tiled=True),
        lax.psum_scatter(gate_weight_part, ("fsdp", "ctx"), scatter_dimension=0, tiled=True),
        lax.psum_scatter(up_weight_part, ("fsdp", "ctx"), scatter_dimension=0, tiled=True),
        lax.psum_scatter(down_weight_part, ("fsdp", "ctx"), scatter_dimension=1, tiled=True),
    )
    reduced = (
        lax.all_gather(part_one.astype(jnp.bfloat16), "ctx", axis=0, tiled=True).astype(
            part_one.dtype
        ),
        lax.all_gather(part_query.astype(jnp.bfloat16), "ctx", axis=0, tiled=True).astype(
            part_query.dtype
        ),
        lax.all_gather(part_key.astype(jnp.bfloat16), "ctx", axis=0, tiled=True).astype(
            part_key.dtype
        ),
        lax.all_gather(part_value.astype(jnp.bfloat16), "ctx", axis=0, tiled=True).astype(
            part_value.dtype
        ),
        lax.all_gather(part_project.astype(jnp.bfloat16), "ctx", axis=1, tiled=True).astype(
            part_project.dtype
        ),
        lax.all_gather(part_two.astype(jnp.bfloat16), "ctx", axis=0, tiled=True).astype(
            part_two.dtype
        ),
        lax.all_gather(part_gate.astype(jnp.bfloat16), "ctx", axis=0, tiled=True).astype(
            part_gate.dtype
        ),
        lax.all_gather(part_up.astype(jnp.bfloat16), "ctx", axis=0, tiled=True).astype(
            part_up.dtype
        ),
        lax.all_gather(part_down.astype(jnp.bfloat16), "ctx", axis=1, tiled=True).astype(
            part_down.dtype
        ),
    )
    return (layer_output, tokens_grad) + tuple(reduced)


LANES = 128
HALF = HD // 2
SPAN = LANES // 2
LOG2E = math.log2(math.e)
VMEM_BYTES = 60 * 1024 * 1024


def swap_ctx(block):
    return lax.ppermute(block, "ctx", [(0, 1), (1, 0)])


def swap_core(block):
    return lax.ppermute(block, "tp", [(0, 1), (1, 0), (2, 3), (3, 2)])


def swap_chip(block):
    return lax.ppermute(block, "tp", [(0, 2), (2, 0), (1, 3), (3, 1)])


def by_core(total, other):
    return jnp.where(
        lax.axis_index("tp") % 2 == 0,
        jnp.concatenate([total, other], axis=0),
        jnp.concatenate([other, total], axis=0),
    )


def dot(a, b, contract):
    return lax.dot_general(a, b, (contract, ((), ())), preferred_element_type=jnp.float32)


def block_kinds(meta_ref, query_tile, key_tile, q_start, k_start):
    prefix = meta_ref[0]
    whole = (k_start + (key_tile - 1) <= q_start) | (k_start + key_tile <= prefix)
    nothing = (k_start > q_start + (query_tile - 1)) & (k_start >= prefix)
    return prefix, whole, nothing


def mask_scores(scores, prefix, q_start, k_start, query_tile):
    key_ids = k_start + lax.broadcasted_iota(jnp.int32, scores.shape, 0)
    column = lax.broadcasted_iota(jnp.int32, scores.shape, 1)
    query_ids = q_start + jnp.bitwise_and(column, query_tile - 1)
    return jnp.where((key_ids <= query_ids) | (key_ids < prefix), scores, NEGATIVE)


MESH = pl.DeviceIdType.MESH
GAIN_ROWS = 16
PREFIX_MOST = 1024


def line_sum(z, planes, source, up_ref, down_ref, up_send, up_recv, down_send, down_recv):
    f32 = jnp.float32

    def up(d):
        return pltpu.make_async_remote_copy(
            src_ref=up_ref.at[d - 1],
            dst_ref=up_ref.at[d - 1],
            send_sem=up_send.at[d],
            recv_sem=up_recv.at[d],
            device_id={"fsdp": z + 1},
            device_id_type=MESH,
        )

    def down(d):
        return pltpu.make_async_remote_copy(
            src_ref=down_ref.at[d],
            dst_ref=down_ref.at[d],
            send_sem=down_send.at[d],
            recv_sem=down_recv.at[d],
            device_id={"fsdp": z - 1},
            device_id_type=MESH,
        )

    def begin(k):
        high, low = planes - 1 - k, k

        @pl.when(z == 0)
        def _():
            up_ref[high - 1] = source(high)
            up(high).start()

        @pl.when(z == planes - 1)
        def _():
            down_ref[low] = source(low)
            down(low).start()

    def relay(k):
        high, low = planes - 1 - k, k

        def pass_up():
            @pl.when((z > 0) & (z < high))
            def _():
                up(high).wait_recv()
                up_ref[high - 1] = (
                    up_ref[high - 1].astype(f32) + source(high).astype(f32)
                ).astype(up_ref.dtype)
                up(high).start()

        def pass_down():
            @pl.when((z < planes - 1) & (z > low))
            def _():
                down(low).wait_recv()
                down_ref[low] = (
                    down_ref[low].astype(f32) + source(low).astype(f32)
                ).astype(down_ref.dtype)
                down(low).start()

        @pl.when(2 * z < planes)
        def _():
            pass_up()
            pass_down()

        @pl.when(2 * z >= planes)
        def _():
            pass_down()
            pass_up()

    def finish(out_ref):
        out_ref[...] = source(z)

        @pl.when(z > 0)
        def _():
            up(z).wait_recv()
            out_ref[...] = (
                out_ref[...].astype(f32) + up_ref[pl.ds(z - 1, 1)][0].astype(f32)
            ).astype(out_ref.dtype)

        @pl.when(z < planes - 1)
        def _():
            down(z).wait_recv()
            out_ref[...] = (
                out_ref[...].astype(f32) + down_ref[pl.ds(z, 1)][0].astype(f32)
            ).astype(out_ref.dtype)

    def sent():
        for d in range(planes):

            @pl.when(z < d)
            def _():
                up(d).wait_send()

            @pl.when(z > d)
            def _():
                down(d).wait_send()

    return begin, relay, finish, sent


def front_kernel(
    prefix_ref,
    x_ref,
    pack_ref,
    rest_ref,
    spread_ref,
    cos_ref,
    sin_ref,
    w_project_ref,
    w_gate_ref,
    w_up_ref,
    w_down_ref,
    normed_hbm,
    q_hbm,
    kv_hbm,
    wide_hbm,
    project_ref,
    gain_ref,
    o_ref,
    lse_ref,
    total_ref,
    gate_ref,
    up_ref,
    down_ref,
    normed_ref,
    q_ref,
    kv_ref,
    wide_ref,
    buf_ref,
    max_ref,
    sum_ref,
    acc_ref,
    give_ref,
    core_in_ref,
    keep_ref,
    chip_in_ref,
    up_send,
    up_recv,
    down_send,
    down_recv,
    x_send,
    x_recv,
    kv_send,
    kv_recv,
    m_up_send,
    m_up_recv,
    m_down_send,
    m_down_recv,
    m_x_send,
    m_x_recv,
    local_sem,
    core_send,
    core_recv,
    chip_send,
    chip_recv,
    back_send,
    back_recv,
    store_sem,
):
    bf16, f32 = jnp.bfloat16, jnp.float32
    planes = buf_ref.shape[0]
    rows, width = x_ref.shape
    depth = width // planes
    half_width = wide_ref.shape[1] // 2
    matrix_rows = rest_ref.shape[0]
    heads_half = project_ref.shape[0] // 2
    units = gate_ref.shape[2]
    direct = units // 2
    z = lax.axis_index("fsdp")
    c = lax.axis_index("ctx")
    t = lax.axis_index("tp")
    core = lax.rem(t, 2)
    across = {"ctx": 1 - c}
    sibling = {"tp": t + 1 - 2 * core}
    partner = {"tp": lax.rem(t + 2, 4)}
    has_above = z < planes - 1
    has_below = z > 0

    def remote(src, dst, send, recv, device):
        return pltpu.make_async_remote_copy(
            src_ref=src,
            dst_ref=dst,
            send_sem=send,
            recv_sem=recv,
            device_id=device,
            device_id_type=MESH,
        )

    project_ref[:, HD:, :] = jnp.zeros(
        (project_ref.shape[0], LANES - HD, project_ref.shape[2]), bf16
    )

    barrier = pltpu.get_barrier_semaphore()

    @pl.when(has_above)
    def _():
        pl.semaphore_signal(barrier, inc=1, device_id={"fsdp": z + 1}, device_id_type=MESH)

    @pl.when(has_below)
    def _():
        pl.semaphore_signal(barrier, inc=1, device_id={"fsdp": z - 1}, device_id_type=MESH)

    for device in (across, sibling, partner):
        pl.semaphore_signal(barrier, inc=1, device_id=device, device_id_type=MESH)

    @pl.when(has_above & has_below)
    def _():
        pl.semaphore_wait(barrier, 5)

    @pl.when(jnp.logical_not(has_above & has_below))
    def _():
        pl.semaphore_wait(barrier, 4)

    def up(k):
        piece = z - k
        src = pack_ref if k == 0 else buf_ref.at[piece, 0]
        return remote(src, buf_ref.at[piece, 0], up_send.at[k], up_recv.at[k], {"fsdp": z + 1})

    def down(k):
        piece = z + k
        src = pack_ref if k == 0 else buf_ref.at[piece, 0]
        return remote(src, buf_ref.at[piece, 0], down_send.at[k], down_recv.at[k], {"fsdp": z - 1})

    def from_below(k):
        slot = buf_ref.at[z - 1 - k, 0]
        return remote(slot, slot, up_send.at[k], up_recv.at[k], {"fsdp": z - 1})

    def from_above(k):
        slot = buf_ref.at[z + 1 + k, 0]
        return remote(slot, slot, down_send.at[k], down_recv.at[k], {"fsdp": z + 1})

    def sideways(side, k):
        piece = z - k if side == 0 else z + k
        matrix = pl.ds(0, matrix_rows)
        return remote(
            buf_ref.at[piece, 0, matrix],
            buf_ref.at[piece, 1, matrix],
            x_send.at[side, k],
            x_recv.at[side, k],
            across,
        )

    def own_half(m, half):
        if m == 0:
            return w_gate_ref.at[:, pl.ds(pl.multiple_of(half * units, units), units)]
        if m == 1:
            return w_up_ref.at[:, pl.ds(pl.multiple_of(half * units, units), units)]
        if m == 2:
            return w_down_ref.at[pl.ds(pl.multiple_of(half * units, units), units), :]
        if m == 4:
            return w_down_ref.at[pl.ds(pl.multiple_of((1 - half) * units, units), direct), :]
        return w_project_ref.at[pl.ds(half * heads_half, heads_half)]

    def slot(m, which, piece):
        at = pl.ds(pl.multiple_of(piece * depth, depth), depth)
        if m == 0:
            return gate_ref.at[which, at]
        if m == 1:
            return up_ref.at[which, at]
        if m == 2:
            return down_ref.at[which, :, at]
        if m == 4:
            return down_ref.at[1, pl.ds(0, direct), at]
        return project_ref.at[pl.ds(which * heads_half, heads_half), pl.ds(0, HD), at]

    def m_up(m, k):
        piece = z - k
        src = own_half(m, c) if k == 0 else slot(m, 0, piece)
        return remote(
            src, slot(m, 0, piece), m_up_send.at[m, k], m_up_recv.at[m, k], {"fsdp": z + 1}
        )

    def m_down(m, k):
        piece = z + k
        src = own_half(m, c) if k == 0 else slot(m, 0, piece)
        return remote(
            src, slot(m, 0, piece), m_down_send.at[m, k], m_down_recv.at[m, k], {"fsdp": z - 1}
        )

    def m_below(m, k):
        at = slot(m, 0, z - 1 - k)
        return remote(at, at, m_up_send.at[m, k], m_up_recv.at[m, k], {"fsdp": z - 1})

    def m_above(m, k):
        at = slot(m, 0, z + 1 + k)
        return remote(at, at, m_down_send.at[m, k], m_down_recv.at[m, k], {"fsdp": z + 1})

    def m_side(m, side, k):
        piece = z - k if side == 0 else z + k
        src, dst = slot(m, 0, piece), slot(m, 1, piece)
        if m == 2:
            left = pl.ds(direct, units - direct)
            src, dst = src.at[left], dst.at[left]
        return remote(
            src,
            dst,
            m_x_send.at[m, side, k],
            m_x_recv.at[m, side, k],
            across,
        )

    groups = ((3,), (0,), (1,), (2, 4))

    def relay(group, k):
        for m in groups[group]:

            @pl.when(z - k >= 0)
            def _():
                m_below(m, k - 1).wait_recv()
                if k < planes - 1:

                    @pl.when(has_above)
                    def _():
                        m_up(m, k).start()

            @pl.when(z + k <= planes - 1)
            def _():
                m_above(m, k - 1).wait_recv()
                if k < planes - 1:

                    @pl.when(has_below)
                    def _():
                        m_down(m, k).start()

    def launch(group):
        for m in groups[group]:

            @pl.when(has_above)
            def _():
                m_up(m, 0).start()

            @pl.when(has_below)
            def _():
                m_down(m, 0).start()

    def cross(group, k):
        for m in groups[group]:
            if m == 4:
                continue

            @pl.when(z - k >= 0)
            def _():
                m_side(m, 0, k).start()

            @pl.when(z + k <= planes - 1)
            def _():
                m_side(m, 1, k).start()

    def crossed(m, k):
        @pl.when(z - k >= 0)
        def _():
            m_side(m, 0, k).wait_recv()

        @pl.when(z + k <= planes - 1)
        def _():
            m_side(m, 1, k).wait_recv()

    def local(m, which):
        half = c if which == 0 else 1 - c
        return pltpu.make_async_copy(own_half(m, half), slot(m, which, z), local_sem.at[m, which])

    spread = spread_ref[...]

    def place(block, piece, which):
        at = pl.ds(pl.multiple_of(piece * depth, depth), depth)
        wide_ref[at, which * half_width : (which + 1) * half_width] = dot(
            block[:depth], spread, ((1,), (0,))
        ).astype(bf16)

    def place_gain(block, piece):
        at = pl.ds(pl.multiple_of(piece * depth, depth), depth)
        gain_ref[:, at] = block[matrix_rows:]

    @pl.when(has_above)
    def _():
        up(0).start()

    @pl.when(has_below)
    def _():
        down(0).start()

    for m in (3, 0, 1, 2):
        for which in range(2):
            local(m, which).start()
    place(pack_ref, z, 0)
    place_gain(pack_ref, z)
    place(rest_ref, z, 1)

    for k in range(1, planes):
        below = z - k >= 0
        above = z + k <= planes - 1

        @pl.when(below)
        def _():
            from_below(k - 1).wait_recv()
            if k < planes - 1:

                @pl.when(has_above)
                def _():
                    up(k).start()

            sideways(0, k).start()

        @pl.when(above)
        def _():
            from_above(k - 1).wait_recv()
            if k < planes - 1:

                @pl.when(has_below)
                def _():
                    down(k).start()

            sideways(1, k).start()

        if k == max(1, planes - 2):
            launch(0)
            launch(1)

        @pl.when(below)
        def _():
            place(buf_ref.at[z - k, 0], z - k, 0)
            place_gain(buf_ref.at[z - k, 0], z - k)

        @pl.when(above)
        def _():
            place(buf_ref.at[z + k, 0], z + k, 0)
            place_gain(buf_ref.at[z + k, 0], z + k)

    relay(0, 1)
    cross(0, 1)
    tile = 128
    gain = gain_ref[0:1, :].astype(f32)

    def norm_rows(i, carry):
        at = pl.ds(pl.multiple_of(i * tile, tile), tile)
        x = x_ref[at, :].astype(f32)
        factor = lax.rsqrt(jnp.mean(x * x, axis=-1, keepdims=True) + EPSILON)
        normed_ref[at, :] = (x * factor * gain).astype(bf16)
        return carry

    lax.fori_loop(0, rows // tile, norm_rows, 0)
    relay(0, 2)
    cross(0, 2)
    launch(2)

    for k in range(1, planes):

        @pl.when(z - k >= 0)
        def _():
            sideways(0, k).wait_recv()
            place(buf_ref.at[z - k, 1], z - k, 1)

        @pl.when(z + k <= planes - 1)
        def _():
            sideways(1, k).wait_recv()
            place(buf_ref.at[z + k, 1], z + k, 1)

    block = 256

    def turn(part, at):
        return part * cos_ref[at, :] + pltpu.roll(part, SPAN, 1) * sin_ref[at, :]

    def key_rows(i, carry):
        at = pl.ds(pl.multiple_of(i * block, block), block)
        for which in range(2):
            lane = which * half_width + 2 * LANES
            both = dot(normed_ref[at, :], wide_ref[:, lane : lane + 2 * LANES], ((1,), (0,)))
            kv_ref[which, at, :] = turn(both[:, :LANES], at).astype(bf16)
            kv_ref[2 + which, at, :] = both[:, LANES:].astype(bf16)
        return carry

    lax.fori_loop(0, rows // block, key_rows, 0)

    def exchange(slab):
        return remote(
            kv_ref.at[slab, pl.ds(0, rows)],
            kv_ref.at[slab ^ 1, pl.ds(rows, rows)],
            kv_send.at[slab],
            kv_recv.at[slab ^ 1],
            across,
        )

    for slab in range(4):
        exchange(slab).start()
    relay(0, 3)
    cross(0, 3)
    relay(1, 1)
    launch(3)
    scale = HD ** (-0.5) * LOG2E

    def query_rows(i, carry):
        at = pl.ds(pl.multiple_of(i * block, block), block)
        for which in range(2):
            lane = which * half_width
            both = dot(normed_ref[at, :], wide_ref[:, lane : lane + 2 * LANES], ((1,), (0,)))
            for head in range(2):
                part = turn(both[:, head * LANES : (head + 1) * LANES], at)
                lane = (2 * which + head) * LANES
                q_ref[at, lane : lane + LANES] = (part * scale).astype(bf16)
        return carry

    lax.fori_loop(0, rows // block, query_rows, 0)
    stores = [
        pltpu.make_async_copy(src, dst, store_sem.at[i])
        for i, (src, dst) in enumerate(
            ((normed_ref, normed_hbm), (q_ref, q_hbm), (wide_ref, wide_hbm), (kv_ref, kv_hbm))
        )
    ]
    for store in stores[:3]:
        store.start()

    tiles = rows // block
    tiles_of_block = tiles // 2
    prefix = prefix_ref[0]
    max_ref[...] = jnp.full_like(max_ref, NEGATIVE)
    sum_ref[...] = jnp.zeros_like(sum_ref)
    acc_ref[...] = jnp.zeros_like(acc_ref)

    def start_of(device, tile_index):
        second = tile_index // tiles_of_block
        block_id = device + second * (3 - 2 * device)
        return (block_id * tiles_of_block + tile_index % tiles_of_block) * block

    def attend_group(g, away):
        key_device = 1 - c if away else c

        def one_tile(i, carry):
            at = pl.ds(pl.multiple_of(i * block, block), block)
            lane = 2 * g * LANES
            queries = jnp.concatenate(
                [q_ref[at, lane : lane + LANES], q_ref[at, lane + LANES : lane + 2 * LANES]],
                axis=0,
            )
            q_start = start_of(c, i)
            u = g * tiles + i

            def absorb(scores, values):
                old = max_ref[u]
                new = jnp.maximum(old, jnp.max(scores, axis=0, keepdims=True))
                weights = jnp.exp2(scores - new)
                rescale = jnp.exp2(old - new)
                max_ref[u] = new
                sum_ref[u] = sum_ref[u] * rescale + jnp.sum(weights, axis=0, keepdims=True)
                acc_ref[u] = acc_ref[u] * rescale + dot(values, weights.astype(bf16), ((0,), (0,)))

            def one(j, carry):
                k_start = start_of(key_device, j)
                first = (tiles if away else 0) + j
                keys_at = pl.ds(pl.multiple_of(first * block, block), block)
                whole = k_start + (block - 1) <= q_start
                nothing = (k_start > q_start + (block - 1)) & (k_start >= PREFIX_MOST)

                @pl.when(whole)
                def _():
                    absorb(dot(kv_ref[g, keys_at, :], queries, ((1,), (1,))), kv_ref[2 + g, keys_at, :])

                @pl.when(jnp.logical_not(whole | nothing))
                def _():
                    scores = dot(kv_ref[g, keys_at, :], queries, ((1,), (1,)))
                    absorb(
                        mask_scores(scores, prefix, q_start, k_start, block),
                        kv_ref[2 + g, keys_at, :],
                    )

                return carry

            lax.fori_loop(0, tiles, one, 0)
            if away:
                total = sum_ref[u]
                lse_ref[g, i] = max_ref[u] + jnp.log2(total)
                out = (acc_ref[u] / total).T.astype(bf16)
                o_ref[at, lane : lane + LANES] = out[:block]
                o_ref[at, lane + LANES : lane + 2 * LANES] = out[block:]
            return carry

        lax.fori_loop(0, tiles, one_tile, 0)

    attend_group(0, False)
    relay(2, 1)
    attend_group(1, False)
    relay(3, 1)
    for slab in range(4):
        exchange(slab).wait_recv()
    stores[3].start()
    cross(1, 1)
    cross(2, 1)
    cross(3, 1)
    attend_group(0, True)
    relay(1, 2)
    cross(1, 2)
    attend_group(1, True)
    relay(2, 2)
    cross(2, 2)

    chunks, chunk, _ = give_ref.shape
    half_rows = rows // 2
    give_start = (1 - core) * half_rows
    keep_start = core * half_rows
    for which in range(2):
        local(3, which).wait()
    for k in range(1, planes):
        crossed(3, k)
    w_project = project_ref[...].reshape(project_ref.shape[0] * LANES, width)

    def feature_rows(start):
        at = pl.ds(pl.multiple_of(start, chunk), chunk)
        return dot(o_ref[at, :], w_project, ((1,), (0,)))

    def to_core(i):
        return remote(give_ref.at[i], core_in_ref.at[i], core_send.at[i], core_recv.at[i], sibling)

    def to_chip(i):
        return remote(keep_ref.at[i], chip_in_ref.at[i], chip_send.at[i], chip_recv.at[i], partner)

    def back(i, start):
        at = pl.ds(pl.multiple_of(start + i * chunk, chunk), chunk)
        return remote(
            total_ref.at[at], total_ref.at[at], back_send.at[i], back_recv.at[i], sibling
        )

    for i in range(chunks):
        give_ref[i] = feature_rows(give_start + i * chunk).astype(bf16)
        to_core(i).start()
    for i in range(chunks):
        kept = feature_rows(keep_start + i * chunk)
        to_core(i).wait_recv()
        keep_ref[i] = (kept + core_in_ref[i].astype(f32)).astype(bf16)
        to_chip(i).start()

    def finish_chunk(i):
        to_chip(i).wait_recv()
        at = pl.ds(pl.multiple_of(keep_start + i * chunk, chunk), chunk)
        total_ref[at, :] = (keep_ref[i].astype(f32) + chip_in_ref[i].astype(f32)).astype(bf16)
        back(i, keep_start).start()

    relay(3, 2)
    cross(3, 2)
    for i in range(chunks):
        finish_chunk(i)
        if i < planes - 1:
            relay(i + 1, planes - 1)
            cross(i + 1, planes - 1)

    for store in stores:
        store.wait()
    for k in range(planes - 1):

        @pl.when((z - k >= 0) & has_above)
        def _():
            up(k).wait_send()
            for m in range(5):
                m_up(m, k).wait_send()

        @pl.when((z + k <= planes - 1) & has_below)
        def _():
            down(k).wait_send()
            for m in range(5):
                m_down(m, k).wait_send()

    for k in range(1, planes):

        @pl.when(z - k >= 0)
        def _():
            sideways(0, k).wait_send()
            for m in range(4):
                m_side(m, 0, k).wait_send()

        @pl.when(z + k <= planes - 1)
        def _():
            sideways(1, k).wait_send()
            for m in range(4):
                m_side(m, 1, k).wait_send()

        for m in range(3):
            crossed(m, k)

    for m in range(3):
        for which in range(2):
            local(m, which).wait()
    for slab in range(4):
        exchange(slab).wait_send()
    for i in range(chunks):
        to_core(i).wait_send()
        to_chip(i).wait_send()
        back(i, keep_start).wait_send()
        back(i, give_start).wait_recv()


def front(prefix, x, pack, rest, spread, cosine, sine, w_project, w_gate, w_up, w_down, planes):
    rows, width = x.shape
    half_width = spread.shape[1]
    units = w_gate.shape[1] // 2
    heads = w_project.shape[0]
    block = 256
    tiles = rows // block
    chunks = 4
    chunk = rows // 2 // chunks
    vmem = pl.BlockSpec(memory_space=pltpu.VMEM)
    anywhere = pl.BlockSpec(memory_space=pl.ANY)
    smem = pl.BlockSpec(memory_space=pltpu.SMEM)
    bf16, f32 = jnp.bfloat16, jnp.float32
    dma = pltpu.SemaphoreType.DMA
    piece = pltpu.VMEM((chunks, chunk, width), bf16)
    return pl.pallas_call(
        front_kernel,
        in_specs=[smem] + [vmem] * 6 + [anywhere] * 4,
        out_specs=[anywhere] * 4 + [vmem] * 5 + [anywhere] * 3,
        out_shape=[
            jax.ShapeDtypeStruct((rows, width), bf16),
            jax.ShapeDtypeStruct((rows, half_width), bf16),
            jax.ShapeDtypeStruct((4, 2 * rows, LANES), bf16),
            jax.ShapeDtypeStruct((width, 2 * half_width), bf16),
            jax.ShapeDtypeStruct((heads, LANES, width), bf16),
            jax.ShapeDtypeStruct((GAIN_ROWS, width), bf16),
            jax.ShapeDtypeStruct((rows, half_width), bf16),
            jax.ShapeDtypeStruct((2, tiles, 1, 2 * block), f32),
            jax.ShapeDtypeStruct((rows, width), bf16),
            jax.ShapeDtypeStruct((2, width, units), bf16),
            jax.ShapeDtypeStruct((2, width, units), bf16),
            jax.ShapeDtypeStruct((2, units, width), bf16),
        ],
        scratch_shapes=[
            pltpu.VMEM((rows, width), bf16),
            pltpu.VMEM((rows, half_width), bf16),
            pltpu.VMEM((4, 2 * rows, LANES), bf16),
            pltpu.VMEM((width, 2 * half_width), bf16),
            pltpu.VMEM((planes, 2, pack.shape[0], pack.shape[1]), bf16),
            pltpu.VMEM((2 * tiles, 1, 2 * block), f32),
            pltpu.VMEM((2 * tiles, 1, 2 * block), f32),
            pltpu.VMEM((2 * tiles, LANES, 2 * block), f32),
            piece,
            piece,
            piece,
            piece,
        ]
        + [dma((planes - 1,))] * 4
        + [dma((2, planes))] * 2
        + [dma((4,))] * 2
        + [dma((5, planes - 1))] * 4
        + [dma((4, 2, planes))] * 2
        + [dma((4, 2))]
        + [dma((chunks,))] * 6
        + [dma((4,))],
        compiler_params=pltpu.CompilerParams(
            collective_id=1, has_side_effects=True, vmem_limit_bytes=VMEM_BYTES
        ),
        cost_estimate=pl.CostEstimate(
            flops=120_000_000_000, bytes_accessed=60_000_000, transcendentals=0
        ),
        name="front",
    )(prefix, x, pack, rest, spread, cosine, sine, w_project, w_gate, w_up, w_down)


def attend_back_kernel(
    final,
    meta_ref,
    carry_ref,
    first_ref,
    second_ref,
    q_ref,
    k_ref,
    v_ref,
    o_ref,
    do_ref,
    lse_ref,
    cos_ref,
    sin_ref,
    dq_ref,
    dkv_ref,
    delta_ref,
    acc_ref,
    dk_acc_ref,
    dv_acc_ref,
):
    query_tiles = lse_ref.shape[1]
    tile = q_ref.shape[0] // query_tiles
    key_tile = k_ref.shape[1]
    j = pl.program_id(1)

    def stacked(ref, i):
        rows = pl.ds(pl.multiple_of(i * tile, tile), tile)
        return jnp.concatenate([ref[rows, :LANES], ref[rows, LANES:]], axis=0)

    @pl.when(j == 0)
    def _():
        acc_ref[...] = carry_ref[0] if final else jnp.zeros_like(acc_ref)

        def one_delta(i, carry):
            product = stacked(o_ref, i).astype(jnp.float32) * stacked(do_ref, i).astype(jnp.float32)
            delta_ref[i] = jnp.sum(product.T, axis=0, keepdims=True)
            return carry

        lax.fori_loop(0, query_tiles, one_delta, 0)

    k_start = meta_ref[1 + query_tiles + (0 if final else pl.num_programs(1)) + j]
    keys = k_ref[0]
    values = v_ref[0]

    dk_acc_ref[...] = jnp.zeros_like(dk_acc_ref)
    dv_acc_ref[...] = jnp.zeros_like(dv_acc_ref)

    def one(i, carry):
        q_start = meta_ref[1 + i]
        prefix, whole, nothing = block_kinds(meta_ref, tile, key_tile, q_start, k_start)

        def some(masked):
            queries = stacked(q_ref, i)
            d_out = stacked(do_ref, i)
            scores = dot(keys, queries, ((1,), (1,)))
            if masked:
                scores = mask_scores(scores, prefix, q_start, k_start, tile)
            weights = jnp.exp2(scores - lse_ref[0, i])
            d_weights = dot(values, d_out, ((1,), (1,)))
            d_scores = (weights * (d_weights - delta_ref[i])).astype(jnp.bfloat16)
            dv_acc_ref[...] += dot(weights.astype(jnp.bfloat16), d_out, ((1,), (0,)))
            dk_acc_ref[...] += dot(d_scores, queries, ((1,), (0,)))
            acc_ref[i] += dot(keys, d_scores, ((0,), (0,)))

        @pl.when(whole)
        def _():
            some(False)

        @pl.when(jnp.logical_not(whole | nothing))
        def _():
            some(True)

        return carry

    lax.fori_loop(0, query_tiles, one, 0)
    dkv_ref[0, 0] = (dk_acc_ref[...] * (1.0 / LOG2E)).astype(jnp.bfloat16)
    dkv_ref[0, 1] = dv_acc_ref[...].astype(jnp.bfloat16)

    @pl.when(j == pl.num_programs(1) - 1)
    def _():
        scale = HD ** (-0.5)
        if not final:
            dq_ref[0] = acc_ref[...]
            return

        def one_out(i, carry):
            rows = pl.ds(pl.multiple_of(i * tile, tile), tile)
            turned = acc_ref[i].T * scale
            for head in range(2):
                part = turned[head * tile : (head + 1) * tile]
                part = part * cos_ref[rows, :] - pltpu.roll(part, SPAN, 1) * sin_ref[rows, :]
                dq_ref[rows, head * LANES : (head + 1) * LANES] = part.astype(jnp.bfloat16)
            return carry

        lax.fori_loop(0, query_tiles, one_out, 0)


def attend_back(meta, carry, first, second, q, kv, away, o, d_out, lse, cosine, sine, tile):
    rows, q_width = q.shape
    keys = kv.shape[1] // 2
    groups = q_width // (2 * LANES)
    query_tiles = rows // tile
    key_tiles = keys // tile
    skip = key_tiles if away else 0
    acc_block = pl.BlockSpec((1, query_tiles, LANES, 2 * tile), lambda g, j, m: (g, 0, 0, 0))
    acc_shape = jax.ShapeDtypeStruct((groups, query_tiles, LANES, 2 * tile), jnp.float32)
    if away:
        carry = jnp.zeros((1, 1, 8, LANES), jnp.float32)
        carry_block = pl.BlockSpec((1, 1, 8, LANES), lambda g, j, m: (0, 0, 0, 0))
    else:
        carry_block = acc_block
    whole_q = pl.BlockSpec((rows, 2 * LANES), lambda g, j, m: (0, g))
    return pl.pallas_call(
        functools.partial(attend_back_kernel, not away),
        grid_spec=pltpu.PrefetchScalarGridSpec(
            num_scalar_prefetch=1,
            grid=(groups, key_tiles),
            in_specs=[
                carry_block,
                pl.BlockSpec(memory_space=pl.ANY),
                pl.BlockSpec(memory_space=pl.ANY),
                whole_q,
                pl.BlockSpec((1, tile, LANES), lambda g, j, m: (g, skip + j, 0)),
                pl.BlockSpec((1, tile, LANES), lambda g, j, m: (groups + g, skip + j, 0)),
                whole_q,
                whole_q,
                pl.BlockSpec((1, query_tiles, 1, 2 * tile), lambda g, j, m: (g, 0, 0, 0)),
                pl.BlockSpec((rows, LANES), lambda g, j, m: (0, 0)),
                pl.BlockSpec((rows, LANES), lambda g, j, m: (0, 0)),
            ],
            out_specs=[
                acc_block if away else whole_q,
                pl.BlockSpec((1, 2, tile, LANES), lambda g, j, m: (g, 0, j, 0)),
            ],
            scratch_shapes=[
                pltpu.VMEM((query_tiles, 1, 2 * tile), jnp.float32),
                pltpu.VMEM((query_tiles, LANES, 2 * tile), jnp.float32),
                pltpu.VMEM((tile, LANES), jnp.float32),
                pltpu.VMEM((tile, LANES), jnp.float32),
            ],
        ),
        out_shape=[
            acc_shape if away else jax.ShapeDtypeStruct((rows, q_width), jnp.bfloat16),
            jax.ShapeDtypeStruct((groups, 2, keys, LANES), jnp.bfloat16),
        ],
        compiler_params=pltpu.CompilerParams(vmem_limit_bytes=VMEM_BYTES),
        cost_estimate=pl.CostEstimate(
            flops=20 * rows * keys * LANES * groups * 2, bytes_accessed=8_000_000, transcendentals=0
        ),
        name="attend_back_away" if away else "attend_back_own",
    )(meta, carry, first, second, q, kv, kv, o, d_out, lse, cosine, sine)


def middle_back_kernel(
    x_ref,
    project_ref,
    feed_ref,
    cot_ref,
    gain_ref,
    o_ref,
    wp_ref,
    grad_ref,
    d_out_ref,
    wp_grad_ref,
    gain_grad_ref,
    acc_ref,
):
    step = pl.program_id(0)
    last = pl.num_programs(0) - 1
    bf16, f32 = jnp.bfloat16, jnp.float32

    @pl.when(step == 0)
    def _():
        acc_ref[...] = jnp.zeros_like(acc_ref)
        gain_grad_ref[...] = jnp.zeros_like(gain_grad_ref)

    middle = x_ref[...].astype(f32) + project_ref[...].astype(f32)
    factor = lax.rsqrt(jnp.mean(middle * middle, axis=-1, keepdims=True) + EPSILON)
    feed_in = feed_ref[...].astype(f32)
    gain_grad_ref[...] += jnp.sum(feed_in * middle * factor, axis=0, keepdims=True)
    scaled = gain_ref[1:2, :].astype(f32) * feed_in
    grad = (
        cot_ref[...].astype(f32)
        + factor * scaled
        - middle * (factor * factor * factor * jnp.mean(scaled * middle, axis=-1, keepdims=True))
    )
    grad_ref[...] = grad
    low = grad.astype(bf16)
    d_out_ref[...] = dot(low, wp_ref[...], ((1,), (1,))).astype(bf16)
    acc_ref[...] += dot(o_ref[...], low, ((0,), (0,)))

    @pl.when(step == last)
    def _():
        for head in range(acc_ref.shape[0] // LANES):
            wp_grad_ref[head * HD : (head + 1) * HD, :] = acc_ref[
                head * LANES : head * LANES + HD, :
            ].astype(bf16)


def middle_back(x, project_sum, feed_sum, cot, gains, o, w_p):
    rows, width = x.shape
    tile = 256
    heads = o.shape[1] // LANES
    bf16, f32 = jnp.bfloat16, jnp.float32

    def rows_of(columns):
        return pl.BlockSpec((tile, columns), lambda i: (i, 0))

    def whole(array):
        return pl.BlockSpec(array.shape, lambda i: (0, 0))

    return pl.pallas_call(
        middle_back_kernel,
        grid=(rows // tile,),
        in_specs=[
            rows_of(width),
            rows_of(width),
            rows_of(width),
            rows_of(width),
            whole(gains),
            rows_of(o.shape[1]),
            whole(w_p),
        ],
        out_specs=[
            rows_of(width),
            rows_of(o.shape[1]),
            pl.BlockSpec((heads * HD, width), lambda i: (0, 0)),
            pl.BlockSpec((1, width), lambda i: (0, 0)),
        ],
        out_shape=[
            jax.ShapeDtypeStruct((rows, width), f32),
            jax.ShapeDtypeStruct(o.shape, bf16),
            jax.ShapeDtypeStruct((heads * HD, width), bf16),
            jax.ShapeDtypeStruct((1, width), f32),
        ],
        scratch_shapes=[pltpu.VMEM((o.shape[1], width), f32)],
        compiler_params=pltpu.CompilerParams(vmem_limit_bytes=VMEM_BYTES),
        cost_estimate=pl.CostEstimate(
            flops=5_000_000_000, bytes_accessed=26_000_000, transcendentals=0
        ),
        name="middle_back",
    )(x, project_sum, feed_sum, cot, gains, o, w_p)


def tail_kernel(
    down_hbm,
    gate_hbm,
    gate_away_hbm,
    gate_rest_hbm,
    up_hbm,
    up_away_hbm,
    q_low_ref,
    own_ref,
    away_ref,
    normed_hbm,
    wide_hbm,
    x_hbm,
    grad_hbm,
    gain_term_ref,
    gain_ref,
    project_ref,
    spread_ref,
    cos_ref,
    sin_ref,
    out_hbm,
    share_ref,
    project_share_ref,
    gate_share_ref,
    up_share_ref,
    gain_share_ref,
    down_away_hbm,
    normed_ref,
    wide_ref,
    x_ref,
    grad_ref,
    gate_ref,
    gate_away_ref,
    upw_ref,
    upw_away_ref,
    low_ref,
    close_ref,
    part_ref,
    x_in_ref,
    up_ref,
    down_ref,
    p_in_ref,
    p_up_ref,
    p_down_ref,
    g_up_ref,
    g_down_ref,
    u_up_ref,
    u_down_ref,
    give_ref,
    core_in_ref,
    chip_in_ref,
    total_ref,
    gain_sum_ref,
    gain_x_ref,
    gain_z_ref,
    x_send,
    x_recv,
    up_send,
    up_recv,
    down_send,
    down_recv,
    p_up_send,
    p_up_recv,
    p_down_send,
    p_down_recv,
    g_up_send,
    g_up_recv,
    g_down_send,
    g_down_recv,
    u_up_send,
    u_up_recv,
    u_down_send,
    u_down_recv,
    core_send,
    core_recv,
    chip_send,
    chip_recv,
    back_send,
    back_recv,
    last_send,
    last_recv,
    gain_send,
    gain_recv,
    load_sem,
):
    bf16, f32 = jnp.bfloat16, jnp.float32
    planes = part_ref.shape[1]
    rows, width = x_ref.shape
    depth = width // planes
    sent_rows = gate_away_hbm.shape[0]
    loads = [
        pltpu.make_async_copy(src, dst, load_sem.at[i])
        for i, (src, dst) in enumerate(
            (
                (gate_hbm, gate_ref),
                (gate_away_hbm, gate_away_ref.at[pl.ds(0, sent_rows)]),
                (gate_rest_hbm, gate_away_ref.at[pl.ds(sent_rows, width - sent_rows)]),
                (up_hbm, upw_ref),
                (up_away_hbm, upw_away_ref),
                (normed_hbm, normed_ref),
                (wide_hbm, wide_ref),
                (x_hbm, x_ref),
                (grad_hbm, grad_ref),
            )
        )
    ]
    for load in loads:
        load.start()
    half_rows = rows // 2
    chunks = give_ref.shape[0]
    chunk = half_rows // chunks
    half_width = low_ref.shape[2]
    z = lax.axis_index("fsdp")
    c = lax.axis_index("ctx")
    t = lax.axis_index("tp")
    core = lax.rem(t, 2)
    across = {"ctx": 1 - c}
    sibling = {"tp": t + 1 - 2 * core}
    partner = {"tp": lax.rem(t + 2, 4)}

    barrier = pltpu.get_barrier_semaphore()
    for device in (across, sibling, partner):
        pl.semaphore_signal(barrier, inc=1, device_id=device, device_id_type=MESH)
    for k in range(1, planes):
        pl.semaphore_signal(
            barrier, inc=1, device_id={"fsdp": lax.rem(z + k, planes)}, device_id_type=MESH
        )
    pl.semaphore_wait(barrier, 3 + planes - 1)

    def remote(src, dst, send, recv, device):
        return pltpu.make_async_remote_copy(
            src_ref=src,
            dst_ref=dst,
            send_sem=send,
            recv_sem=recv,
            device_id=device,
            device_id_type=MESH,
        )

    def plane_rows(d):
        return pl.ds(pl.multiple_of(d * depth, depth), depth)

    def pair_source(mine_ref, away_ref):
        def source(d):
            at = plane_rows(d)
            return (mine_ref[at, :].astype(f32) + away_ref[at, :].astype(f32)).astype(bf16)

        return source

    g_begin, g_relay, g_finish, g_sent = line_sum(
        z, planes, pair_source(gate_ref, gate_away_ref),
        g_up_ref, g_down_ref, g_up_send, g_up_recv, g_down_send, g_down_recv,
    )
    u_begin, u_relay, u_finish, u_sent = line_sum(
        z, planes, pair_source(upw_ref, upw_away_ref),
        u_up_ref, u_down_ref, u_up_send, u_up_recv, u_down_send, u_down_recv,
    )

    project_half = project_ref.shape[0] // 2

    def project_over():
        return remote(
            project_ref.at[pl.ds(project_half, project_half)], p_in_ref,
            last_send.at[2], last_recv.at[2], across,
        )

    def project_source(d):
        at = plane_rows(d)
        return (
            project_ref[0:project_half, at].astype(f32) + p_in_ref[:, at].astype(f32)
        ).astype(bf16)

    p_begin, p_relay, p_finish, p_sent = line_sum(
        z, planes, project_source, p_up_ref, p_down_ref, p_up_send, p_up_recv, p_down_send, p_down_recv
    )
    order = []
    for step in range((planes + 1) // 2):
        order += [planes - 1 - step, step]
    order = order[:planes]
    project_over().start()
    for load in loads[:3]:
        load.wait()
    g_begin(0)
    for load in loads[3:5]:
        load.wait()
    u_begin(0)

    block = 256

    def lower(i, carry):
        at = pl.ds(pl.multiple_of(i * block, block), block)
        for which in range(2):
            low_ref[which, at, : 2 * LANES] = q_low_ref[
                at, which * 2 * LANES : (which + 1) * 2 * LANES
            ]
            key = own_ref[which, 0, at, :].astype(f32) + away_ref[1 - which, 0, at, :].astype(f32)
            key = key * cos_ref[at, :] - pltpu.roll(key, SPAN, 1) * sin_ref[at, :]
            low_ref[which, at, 2 * LANES : 3 * LANES] = key.astype(bf16)
            value = own_ref[which, 1, at, :].astype(f32) + away_ref[1 - which, 1, at, :].astype(f32)
            low_ref[which, at, 3 * LANES :] = value.astype(bf16)
            close_ref[which, at, :] = dot(
                low_ref[which, at, :], spread_ref[...], ((1,), (1,))
            ).astype(bf16)
        return carry

    lax.fori_loop(0, rows // block, lower, 0)

    def weight_part(which, d):
        part_ref[which, d] = dot(
            normed_ref[:, d * depth : (d + 1) * depth], close_ref[which], ((0,), (0,))
        ).astype(bf16)

    def to_neighbour(d):
        return remote(part_ref.at[1, d], x_in_ref.at[d], x_send.at[d], x_recv.at[d], across)

    loads[5].wait()
    for d in order:
        weight_part(1, d)
        to_neighbour(d).start()

    def feature_rows(start):
        at = pl.ds(pl.multiple_of(start, chunk), chunk)
        return dot(low_ref[0, at, :], wide_ref[:, :half_width], ((1,), (1,))) + dot(
            low_ref[1, at, :], wide_ref[:, half_width:], ((1,), (1,))
        )

    loads[6].wait()
    give_start = (1 - core) * half_rows
    keep_start = core * half_rows

    def to_core(i):
        return remote(give_ref.at[i], core_in_ref.at[i], core_send.at[i], core_recv.at[i], sibling)

    def to_chip(i):
        return remote(total_ref.at[keep_at(i)], chip_in_ref.at[i], chip_send.at[i], chip_recv.at[i], partner)

    def keep_at(i):
        return pl.ds(pl.multiple_of(keep_start + i * chunk, chunk), chunk)

    def give_at(i):
        return pl.ds(pl.multiple_of(give_start + i * chunk, chunk), chunk)

    def back(i):
        return remote(
            total_ref.at[keep_at(i)],
            total_ref.at[keep_at(i)],
            back_send.at[i],
            back_recv.at[i],
            sibling,
        )

    def from_core(i):
        return remote(
            total_ref.at[give_at(i)],
            total_ref.at[give_at(i)],
            back_send.at[i],
            back_recv.at[i],
            sibling,
        )

    for i in range(chunks):
        give_ref[i] = feature_rows(give_start + i * chunk).astype(bf16)
        to_core(i).start()
    for i in range(chunks):
        kept = feature_rows(keep_start + i * chunk)
        to_core(i).wait_recv()
        total_ref[keep_at(i)] = (kept + core_in_ref[i].astype(f32)).astype(bf16)
        to_chip(i).start()

    g_begin(1)
    g_relay(0)
    u_begin(1)
    u_relay(0)
    for d in order:
        weight_part(0, d)

    def add_neighbour(d):
        to_neighbour(d).wait_recv()
        part_ref[0, d] = (part_ref[0, d].astype(f32) + x_in_ref[d].astype(f32)).astype(bf16)

    q_begin, q_relay, q_finish, q_sent = line_sum(
        z, planes, lambda d: part_ref[0, pl.ds(d, 1)][0], up_ref, down_ref, up_send, up_recv, down_send, down_recv
    )

    def finish_chunk(i):
        to_chip(i).wait()
        total_ref[keep_at(i)] = (
            total_ref[keep_at(i)].astype(f32) + chip_in_ref[i].astype(f32)
        ).astype(bf16)
        back(i).start()

    def last_share():
        return remote(
            share_ref.at[0], share_ref.at[1], last_send.at[0], last_recv.at[0], across
        )

    def last_project():
        return remote(
            project_share_ref.at[0], project_share_ref.at[1], last_send.at[1], last_recv.at[1], across
        )

    def down_over():
        return remote(down_hbm, down_away_hbm, last_send.at[5], last_recv.at[5], across)

    def last_of(ref, i):
        return remote(ref.at[0], ref.at[1], last_send.at[i], last_recv.at[i], across)

    g_begin(2)
    u_begin(2)
    g_relay(1)
    finish_chunk(0)
    u_relay(1)
    project_over().wait_recv()
    for step in range(planes - 1):
        p_begin(step)
    for d in order:
        add_neighbour(d)
    for step in range(planes - 1):
        q_begin(step)
    down_over().start()
    for i in range(1, chunks):
        finish_chunk(i)
    g_finish(gate_share_ref.at[0])
    last_of(gate_share_ref, 3).start()
    p_relay(0)
    u_finish(up_share_ref.at[0])
    last_of(up_share_ref, 4).start()
    q_relay(0)
    for load in loads[7:]:
        load.wait()

    gain_sum_ref[...] = jnp.zeros_like(gain_sum_ref)
    gain_sum_ref[1:2, :] = gain_term_ref[...]
    gain = gain_ref[0:1, :].astype(f32)

    def finish_rows(start):
        at = pl.ds(pl.multiple_of(start, chunk), chunk)
        x = x_ref[at, :].astype(f32)
        factor = lax.rsqrt(jnp.mean(x * x, axis=-1, keepdims=True) + EPSILON)
        normed_in = total_ref[at, :].astype(f32)
        gain_sum_ref[0:1, :] += jnp.sum(normed_in * x * factor, axis=0, keepdims=True)
        scaled = gain * normed_in
        x_ref[at, :] = (
            grad_ref[at, :]
            + factor * scaled
            - x * (factor * factor * factor * jnp.mean(scaled * x, axis=-1, keepdims=True))
        ).astype(bf16)

    for i in range(chunks):
        finish_rows(keep_start + i * chunk)
    p_relay(1)
    q_relay(1)
    for i in range(chunks):
        from_core(i).wait_recv()
        finish_rows(give_start + i * chunk)
    p_finish(project_share_ref.at[0])
    last_project().start()
    q_finish(share_ref.at[0])
    last_share().start()
    out_copy = pltpu.make_async_copy(x_ref, out_hbm, load_sem.at[0])
    out_copy.start()

    gain_over = remote(gain_sum_ref, gain_x_ref, gain_send.at[0], gain_recv.at[0], across)
    gain_over.start()
    gain_over.wait()
    gain_sum_ref[...] = gain_sum_ref[...] + gain_x_ref[...]

    def gain_to(k):
        plane = lax.rem(z + k, planes)
        return remote(
            gain_sum_ref.at[:, pl.ds(pl.multiple_of(plane * depth, depth), depth)],
            gain_z_ref.at[k],
            gain_send.at[k],
            gain_recv.at[k],
            {"fsdp": plane},
        )

    for k in range(1, planes):
        gain_to(k).start()
    gain_share_ref[...] = gain_sum_ref[:, pl.ds(pl.multiple_of(z * depth, depth), depth)]
    for k in range(1, planes):
        gain_to(k).wait_recv()
        gain_share_ref[...] += gain_z_ref[k]

    last_share().wait()
    last_project().wait()
    last_of(gate_share_ref, 3).wait()
    last_of(up_share_ref, 4).wait()
    project_over().wait_send()
    down_over().wait()
    p_sent()
    g_sent()
    u_sent()
    q_sent()
    out_copy.wait()
    for k in range(1, planes):
        gain_to(k).wait_send()
    for i in range(chunks):
        to_core(i).wait_send()
        back(i).wait_send()
    for d in range(planes):
        to_neighbour(d).wait_send()


def tail(
    down_share, gate, gate_away, gate_rest, upw, up_away, q_low, own, away, normed, wide, x, grad,
    gain_term, gains, project, spread, cosine, sine, planes,
):
    rows, width = x.shape
    depth = width // planes
    half_width = wide.shape[1] // 2
    close_width = spread.shape[0]
    chunks = 2
    chunk = rows // 2 // chunks
    bf16, f32 = jnp.bfloat16, jnp.float32
    vmem = pl.BlockSpec(memory_space=pltpu.VMEM)
    dma = pltpu.SemaphoreType.DMA
    operands = (
        down_share, gate, gate_away, gate_rest, upw, up_away, q_low, own, away, normed, wide, x, grad,
        gain_term, gains, project, spread, cosine, sine,
    )
    units = gate.shape[1]
    unit_line = pltpu.VMEM((planes - 1, depth, units), bf16)
    anywhere = pl.BlockSpec(memory_space=pl.ANY)
    line = pltpu.VMEM((planes, depth, close_width), bf16)
    short_line = pltpu.VMEM((planes - 1, depth, close_width), bf16)
    project_line = pltpu.VMEM((planes - 1, project.shape[0] // 2, depth), bf16)
    return pl.pallas_call(
        tail_kernel,
        in_specs=[anywhere] * 6 + [vmem] * 3 + [anywhere] * 4 + [vmem] * (len(operands) - 13),
        out_specs=[anywhere] + [vmem] * 5 + [anywhere],
        out_shape=[
            jax.ShapeDtypeStruct((rows, width), bf16),
            jax.ShapeDtypeStruct((2, depth, close_width), bf16),
            jax.ShapeDtypeStruct((2, project.shape[0] // 2, depth), bf16),
            jax.ShapeDtypeStruct((2, depth, units), bf16),
            jax.ShapeDtypeStruct((2, depth, units), bf16),
            jax.ShapeDtypeStruct((8, depth), f32),
            jax.ShapeDtypeStruct(down_share.shape, bf16),
        ],
        scratch_shapes=[
            pltpu.VMEM((rows, width), bf16),
            pltpu.VMEM(wide.shape, bf16),
            pltpu.VMEM((rows, width), bf16),
            pltpu.VMEM((rows, width), f32),
            pltpu.VMEM((width, units), bf16),
            pltpu.VMEM((width, units), bf16),
            pltpu.VMEM((width, units), bf16),
            pltpu.VMEM((width, units), bf16),
            pltpu.VMEM((2, rows, half_width), bf16),
            pltpu.VMEM((2, rows, close_width), bf16),
            pltpu.VMEM((2, planes, depth, close_width), bf16),
            line,
            short_line,
            short_line,
            pltpu.VMEM((project.shape[0] // 2, width), bf16),
            project_line,
            project_line,
            unit_line,
            unit_line,
            unit_line,
            unit_line,
            pltpu.VMEM((chunks, chunk, width), bf16),
            pltpu.VMEM((chunks, chunk, width), bf16),
            pltpu.VMEM((chunks, chunk, width), bf16),
            pltpu.VMEM((rows, width), bf16),
            pltpu.VMEM((8, width), f32),
            pltpu.VMEM((8, width), f32),
            pltpu.VMEM((planes, 8, depth), f32),
        ]
        + [dma((planes,))] * 18
        + [dma((chunks,))] * 6
        + [dma((6,))] * 2
        + [dma((planes,))] * 2
        + [dma((9,))],
        compiler_params=pltpu.CompilerParams(
            collective_id=2, has_side_effects=True, vmem_limit_bytes=VMEM_BYTES + (3 << 19)
        ),
        cost_estimate=pl.CostEstimate(
            flops=60_000_000_000, bytes_accessed=24_000_000, transcendentals=0
        ),
        name="tail",
    )(*operands)


def feed_kernel(
    x_hbm,
    project_hbm,
    cot_hbm,
    gain_ref,
    gate_hbm,
    up_hbm,
    down_hbm,
    total_hbm,
    gate_m_hbm,
    gate_away_hbm,
    gate_rest_hbm,
    up_m_hbm,
    up_o_hbm,
    down_grad_hbm,
    down_rows_hbm,
    x_ref,
    project_ref,
    cot_ref,
    gate_ref,
    up_ref,
    down_ref,
    total_ref,
    grad_ref,
    down_grad_ref,
    down_rows_ref,
    gate_o_ref,
    normed_ref,
    turned_ref,
    hidden_ref,
    gate_back_ref,
    up_back_ref,
    give_ref,
    core_in_ref,
    keep_ref,
    chip_in_ref,
    load_sem,
    store_sem,
    core_send,
    core_recv,
    chip_send,
    chip_recv,
    back_send,
    back_recv,
    x_send,
    x_recv,
    over_send,
    over_recv,
):
    bf16, f32 = jnp.bfloat16, jnp.float32
    rows, width = x_ref.shape
    half_rows = rows // 2
    chunks, chunk, _ = give_ref.shape
    units = gate_ref.shape[2]
    c = lax.axis_index("ctx")
    t = lax.axis_index("tp")
    core = lax.rem(t, 2)
    across = {"ctx": 1 - c}
    sibling = {"tp": t + 1 - 2 * core}
    partner = {"tp": lax.rem(t + 2, 4)}

    loads = [
        pltpu.make_async_copy(src, dst, load_sem.at[i])
        for i, (src, dst) in enumerate(
            (
                (x_hbm, x_ref),
                (project_hbm, project_ref),
                (gate_hbm, gate_ref),
                (up_hbm, up_ref),
                (cot_hbm, cot_ref),
                (down_hbm, down_ref),
            )
        )
    ]
    for load in loads:
        load.start()

    barrier = pltpu.get_barrier_semaphore()
    for device in (across, sibling, partner):
        pl.semaphore_signal(barrier, inc=1, device_id=device, device_id_type=MESH)
    pl.semaphore_wait(barrier, 3)

    def remote(src, dst, send, recv, device):
        return pltpu.make_async_remote_copy(
            src_ref=src,
            dst_ref=dst,
            send_sem=send,
            recv_sem=recv,
            device_id=device,
            device_id_type=MESH,
        )

    give_start = (1 - core) * half_rows
    keep_start = core * half_rows
    gain = gain_ref[1:2, :].astype(f32)

    def feature_rows(start, first):
        at = pl.ds(pl.multiple_of(start, chunk), chunk)
        if first:
            loads[0].wait()
            loads[1].wait()
        middle = x_ref[at, :].astype(f32) + project_ref[at, :].astype(f32)
        factor = lax.rsqrt(jnp.mean(middle * middle, axis=-1, keepdims=True) + EPSILON)
        normed = (middle * factor * gain).astype(bf16)
        normed_ref[...] = normed
        turned_ref[:, at] = normed.T
        if first:
            for load in loads[2:]:
                load.wait()
        for which in range(2):
            cols = slice(which * units, (which + 1) * units)
            gate = dot(normed_ref[...], gate_ref[which], ((1,), (0,)))
            up = dot(normed_ref[...], up_ref[which], ((1,), (0,)))
            hidden_in = dot(cot_ref[at, :], down_ref[which], ((1,), (1,)))
            sigmoid = jax.nn.sigmoid(gate)
            silu = gate * sigmoid
            hidden_ref[at, cols] = (silu * up).astype(bf16)
            gate_back_ref[at, cols] = (
                hidden_in * up * sigmoid * (1.0 + gate * (1.0 - sigmoid))
            ).astype(bf16)
            up_back_ref[at, cols] = (hidden_in * silu).astype(bf16)
        return sum(
            dot(back_ref[at, which * units : (which + 1) * units], weight[which], ((1,), (1,)))
            for which in range(2)
            for back_ref, weight in ((gate_back_ref, gate_ref), (up_back_ref, up_ref))
        )

    def to_core(i):
        return remote(give_ref.at[i], core_in_ref.at[i], core_send.at[i], core_recv.at[i], sibling)

    def to_chip(i):
        return remote(keep_ref.at[i], chip_in_ref.at[i], chip_send.at[i], chip_recv.at[i], partner)

    def back(i, start):
        at = pl.ds(pl.multiple_of(start + i * chunk, chunk), chunk)
        return remote(
            total_ref.at[at], total_ref.at[at], back_send.at[i], back_recv.at[i], sibling
        )

    for i in range(chunks):
        give_ref[i] = feature_rows(give_start + i * chunk, i == 0).astype(bf16)
        to_core(i).start()
        kept = feature_rows(keep_start + i * chunk, False)
        to_core(i).wait_recv()
        keep_ref[i] = (kept + core_in_ref[i].astype(f32)).astype(bf16)
        to_chip(i).start()

    block = 256

    def weight_rows(back_ref, which, out_ref, begin, count, block=256):
        def some(i, carry):
            at = pl.ds(pl.multiple_of(i * block, block), block)
            out_ref[at, :] = dot(
                turned_ref[at, :], back_ref[:, which * units : (which + 1) * units], ((1,), (0,))
            ).astype(bf16)
            return carry

        lax.fori_loop(begin // block, (begin + count) // block, some, 0)

    def finish_chunk(i):
        to_chip(i).wait()
        at = pl.ds(pl.multiple_of(keep_start + i * chunk, chunk), chunk)
        total_ref[at, :] = (keep_ref[i].astype(f32) + chip_in_ref[i].astype(f32)).astype(bf16)
        back(i, keep_start).start()

    planes, _, depth = down_grad_ref.shape
    pieces = gate_away_hbm.shape[0] // depth

    def over(i):
        at = pl.ds(i * depth, depth)
        return remote(gate_o_ref.at[at], gate_away_hbm.at[at], x_send.at[i], x_recv.at[i], across)

    def down_over(i):
        at = pl.ds(pl.multiple_of(give_start + i * chunk, chunk), chunk)
        return remote(
            down_rows_ref.at[at], core_in_ref.at[i], over_send.at[i], over_recv.at[i], sibling
        )

    stores = []

    def store(src, dst):
        copy = pltpu.make_async_copy(src, dst, store_sem.at[len(stores)])
        copy.start()
        stores.append(copy)

    for i in range(pieces):
        weight_rows(gate_back_ref, 1, gate_o_ref, i * depth, depth, depth)
        over(i).start()
    weight_rows(gate_back_ref, 1, gate_o_ref, pieces * depth, width - pieces * depth, depth)
    store(gate_o_ref.at[pl.ds(pieces * depth, width - pieces * depth)], gate_rest_hbm)
    weight_rows(up_back_ref, 1, grad_ref.at[0], 0, width)
    store(grad_ref.at[0], up_o_hbm)
    for i in range(chunks // 2):
        finish_chunk(i)
    weight_rows(gate_back_ref, 0, grad_ref.at[1], 0, width)
    store(grad_ref.at[1], gate_m_hbm)
    weight_rows(up_back_ref, 0, grad_ref.at[2], 0, width)
    store(grad_ref.at[2], up_m_hbm)

    def down_grads(i, carry):
        at = pl.ds(pl.multiple_of(i * block, block), block)
        part = dot(hidden_ref[:, at], cot_ref[...], ((0,), (0,))).astype(bf16)
        planes, _, depth = down_grad_ref.shape
        for d in range(planes):
            down_grad_ref[d, at, :] = part[:, d * depth : (d + 1) * depth]
        return carry

    lax.fori_loop(0, 2 * units // block, down_grads, 0)
    store(down_grad_ref, down_grad_hbm)

    def down_features(i, carry):
        at = pl.ds(pl.multiple_of(i * block, block), block)
        down_rows_ref[at, :] = (
            dot(hidden_ref[at, :units], down_ref[0], ((1,), (0,)))
            + dot(hidden_ref[at, units:], down_ref[1], ((1,), (0,)))
        ).astype(bf16)
        return carry

    lax.fori_loop(0, rows // block, down_features, 0)
    for i in range(chunks // 2):
        back(i, give_start).wait_recv()
    for i in range(chunks):
        down_over(i).start()
    for i in range(chunks):
        to_core(i).wait_send()
        down_over(i).wait()
        at = pl.ds(pl.multiple_of(keep_start + i * chunk, chunk), chunk)
        give_ref[i] = (down_rows_ref[at, :].astype(f32) + core_in_ref[i].astype(f32)).astype(bf16)
    store(give_ref, down_rows_hbm)
    for i in range(chunks // 2, chunks):
        finish_chunk(i)
    for i in range(chunks // 2, chunks):
        back(i, give_start).wait_recv()
    store(total_ref, total_hbm)
    for i in range(chunks):
        back(i, keep_start).wait_send()
    for i in range(pieces):
        over(i).wait()
    for copy in stores:
        copy.wait()


def feed(x, project_sum, cot, gains, gate_w, up_w, down_w, planes):
    rows, width = x.shape
    units = gate_w.shape[2]
    chunk = 256
    chunks = rows // 2 // chunk
    depth = width // planes
    sent = 3 * depth
    bf16 = jnp.bfloat16
    vmem = pl.BlockSpec(memory_space=pltpu.VMEM)
    anywhere = pl.BlockSpec(memory_space=pl.ANY)
    dma = pltpu.SemaphoreType.DMA
    operands = (x, project_sum, cot, gains, gate_w, up_w, down_w)
    piece = pltpu.VMEM((chunks, chunk, width), bf16)
    rows_by_width = pltpu.VMEM((rows, width), bf16)
    rows_by_units = pltpu.VMEM((rows, 2 * units), bf16)
    weight = jax.ShapeDtypeStruct((width, units), bf16)
    return pl.pallas_call(
        feed_kernel,
        in_specs=[anywhere] * 3 + [vmem] + [anywhere] * 3,
        out_specs=[anywhere] * 8,
        out_shape=[
            jax.ShapeDtypeStruct((rows, width), bf16),
            weight,
            jax.ShapeDtypeStruct((sent, units), bf16),
            jax.ShapeDtypeStruct((width - sent, units), bf16),
            weight,
            weight,
            jax.ShapeDtypeStruct((planes, 2 * units, width // planes), bf16),
            jax.ShapeDtypeStruct((chunks, chunk, width), bf16),
        ],
        scratch_shapes=[
            rows_by_width,
            rows_by_width,
            rows_by_width,
            pltpu.VMEM(gate_w.shape, bf16),
            pltpu.VMEM(up_w.shape, bf16),
            pltpu.VMEM(down_w.shape, bf16),
            rows_by_width,
            pltpu.VMEM((3, width, units), bf16),
            pltpu.VMEM((planes, 2 * units, width // planes), bf16),
            rows_by_width,
            pltpu.VMEM((width, units), bf16),
            pltpu.VMEM((chunk, width), bf16),
            pltpu.VMEM((width, rows), bf16),
            rows_by_units,
            rows_by_units,
            rows_by_units,
            piece,
            piece,
            piece,
            piece,
            dma((6,)),
            dma((7,)),
        ]
        + [dma((chunks,))] * 6
        + [dma((sent // depth,))] * 2
        + [dma((chunks,))] * 2,
        compiler_params=pltpu.CompilerParams(
            collective_id=3, has_side_effects=True, vmem_limit_bytes=VMEM_BYTES
        ),
        cost_estimate=pl.CostEstimate(
            flops=50_000_000_000, bytes_accessed=40_000_000, transcendentals=0
        ),
        name="feed",
    )(*operands)


def add_kernel(first_ref, a_ref, b_ref, out_ref):
    out_ref[...] = (a_ref[...].astype(jnp.float32) + b_ref[...].astype(jnp.float32)).astype(
        out_ref.dtype
    )


def add_after(first, a, b):
    rows, width = a.shape
    tile = 256
    spec = pl.BlockSpec((tile, width), lambda i: (i, 0))
    return pl.pallas_call(
        add_kernel,
        grid=(rows // tile,),
        in_specs=[pl.BlockSpec(memory_space=pl.ANY), spec, spec],
        out_specs=spec,
        out_shape=jax.ShapeDtypeStruct(a.shape, a.dtype),
        name="add_after",
    )(first, a, b)


def paired_body(
    tokens,
    prefix_len,
    positions,
    gain_attend,
    w_query,
    w_key,
    w_value,
    w_project,
    gain_feed,
    w_gate,
    w_up,
    w_down,
    cotangent,
):
    seqs, rows, width = tokens.shape
    assert seqs == 1
    c = lax.axis_index("ctx")
    bf16, f32 = jnp.bfloat16, jnp.float32

    def half(array, axis, which=None):
        size = array.shape[axis] // 2
        which = c if which is None else which
        return lax.dynamic_slice_in_dim(array, which * size, size, axis)

    def ordered(mine, other, axis):
        return jnp.where(
            c == 0,
            jnp.concatenate([mine, other], axis=axis),
            jnp.concatenate([other, mine], axis=axis),
        )

    planes = lax.axis_size("fsdp")
    kv_half = w_key.shape[1] // 2
    q_half = w_query.shape[1] // 2

    def packed(which):
        return jnp.concatenate(
            [half(w_query, 1, which), half(w_key, 1, which), half(w_value, 1, which)], axis=1
        )

    gain_rows = jnp.pad(jnp.stack([gain_attend, gain_feed]), ((0, GAIN_ROWS - 2), (0, 0)))
    pack = jnp.concatenate([packed(c), gain_rows], axis=0)

    def parts(block):
        return (
            block[:, :q_half],
            block[:, q_half : q_half + kv_half],
            block[:, q_half + kv_half :],
        )

    half_heads = (q_half + 2 * kv_half) // HD
    spread = np.zeros((half_heads * HD, half_heads * LANES), np.float32)
    for head in range(half_heads):
        for lane in range(HD):
            turned = lane if lane < HALF or head == half_heads - 1 else lane - HALF + SPAN
            spread[head * HD + lane, head * LANES + turned] = 1.0
    spread = jnp.asarray(spread, bf16)

    frequency = ROPE_BASE ** (-(jnp.arange(HALF, dtype=f32) * 2.0 / HD))
    frequency = jnp.pad(frequency, (0, SPAN - HALF))
    angles = positions[0].astype(f32)[:, None] * frequency
    cosine = jnp.cos(angles)
    sine = jnp.sin(angles)
    cosine = jnp.concatenate([cosine, cosine], axis=1)
    sine = jnp.concatenate([-sine, sine], axis=1)

    block_len = rows // 2
    tile = min(256, block_len)
    query_tiles = rows // tile
    own = c * rows + tile * jnp.arange(query_tiles, dtype=jnp.int32)
    opposite = (1 - c) * rows + tile * jnp.arange(query_tiles, dtype=jnp.int32)
    own, opposite = natural_index(own, block_len, 2), natural_index(opposite, block_len, 2)
    meta = jnp.concatenate([prefix_len.astype(jnp.int32), own, own, opposite])

    x = tokens[0]
    cot = cotangent[0]
    (
        normed, q, kv_all, w_qkv, w_p, gains, o, lse, project_sum, wg, wu, wd,
    ) = front(
        prefix_len, x, pack, packed(1 - c), spread, cosine, sine,
        w_project.reshape(-1, HD, w_project.shape[1]), w_gate, w_up, w_down, planes,
    )
    w_p = w_p.reshape(-1, width)
    (
        feed_sum, gate_mine, gate_away, gate_rest, up_mine, up_other, down_part, down_rows,
    ) = feed(x, project_sum, cot, gains, wg, wu, wd, planes)

    gate_rest, up_away = swap_ctx(gate_rest), swap_ctx(up_other)
    down_share = lax.psum_scatter(down_part, "fsdp", scatter_dimension=0, tiled=False)
    middle_grad, d_out, project_part, gain_two_term = middle_back(
        x, project_sum, feed_sum, cot, gains, o, w_p
    )
    down_rows = down_rows.reshape(rows // 2, width)
    down_away = swap_chip(down_rows)
    dq_away, d_kv_away = attend_back(
        meta, None, d_out, d_out, q, kv_all, True, o, d_out, lse, cosine, sine, tile
    )
    d_kv_away = swap_ctx(d_kv_away)
    down_total = add_after(dq_away, down_rows, down_away)
    down_sum = by_core(down_total, swap_core(down_total))
    layer_output = (
        x.astype(f32) + project_sum.astype(f32) + down_sum.astype(f32)
    ).astype(bf16)
    q_low, d_kv_own = attend_back(
        meta, dq_away, gate_rest, up_away, q, kv_all, False, o, d_out, lse, cosine, sine, tile
    )
    tokens_grad, share, project_share, gate_share, up_share, gain_share, down_other_share = tail(
        down_share, gate_mine, gate_away, gate_rest, up_mine, up_away, q_low, d_kv_own, d_kv_away, normed, w_qkv, x, middle_grad,
        gain_two_term, gains, project_part, spread, cosine, sine, planes,
    )
    size = down_share.shape[0] // 2
    down_mine = down_share[:size].astype(f32) + down_other_share[size:].astype(f32)
    down_other = down_share[size:].astype(f32) + down_other_share[:size].astype(f32)
    down_grad = ordered(down_mine, down_other, 0)
    shares = [
        ordered(a, b, 1).astype(f32) for a, b in zip(parts(share[0]), parts(share[1]))
    ]
    return (
        layer_output[None],
        tokens_grad[None],
        gain_share[0],
        shares[0],
        shares[1],
        shares[2],
        ordered(project_share[0], project_share[1], 0).astype(f32),
        gain_share[1],
        ordered(gate_share[0], gate_share[1], 1).astype(f32),
        ordered(up_share[0], up_share[1], 1).astype(f32),
        down_grad,
    )


def solution(mesh):
    paired = mesh.shape["ctx"] == 2 and mesh.shape["tp"] == 4 and mesh.shape["fsdp"] == 4
    return jax.shard_map(
        paired_body if paired else general_body,
        mesh=mesh,
        in_specs=(
            P("fsdp", "ctx", None),
            P("fsdp"),
            P("fsdp", "ctx"),
            P("fsdp"),
            P("fsdp", "tp"),
            P("fsdp", "tp"),
            P("fsdp", "tp"),
            P("tp", "fsdp"),
            P("fsdp"),
            P("fsdp", "tp"),
            P("fsdp", "tp"),
            P("tp", "fsdp"),
            P("fsdp", "ctx", None),
        ),
        out_specs=(
            P("fsdp", "ctx", None),
            P("fsdp", "ctx", None),
            P("fsdp"),
            P("fsdp", "tp"),
            P("fsdp", "tp"),
            P("fsdp", "tp"),
            P("tp", "fsdp"),
            P("fsdp"),
            P("fsdp", "tp"),
            P("fsdp", "tp"),
            P("tp", "fsdp"),
        ),
        check_vma=False,
    )
```

```python
import functools
import math

import jax
import jax.numpy as jnp
import numpy as np
from jax import lax
from jax.experimental import pallas as pl
from jax.experimental.pallas import tpu as pltpu
from jax.sharding import PartitionSpec as P

HQ = 16
KVH = 8
HD = 96


EPSILON = 1e-05
ROPE_BASE = 100000.0
NEGATIVE = -1e30


def natural_index(stored, block_len, pair_count):
    device = stored // (2 * block_len)
    second_half = stored // block_len % 2
    within = stored % block_len
    block_id = jnp.where(second_half == 0, device, 2 * pair_count - 1 - device)
    return block_id * block_len + within


def rotate(values, cosine_table, sine_table):
    half_width = values.shape[-1] // 2
    leading = values[..., :half_width]
    trailing = values[..., half_width:]
    return jnp.concatenate(
        [
            leading * cosine_table - trailing * sine_table,
            trailing * cosine_table + leading * sine_table,
        ],
        axis=-1,
    )


def rotate_back(incoming, cosine_table, sine_table):
    half_width = incoming.shape[-1] // 2
    leading = incoming[..., :half_width]
    trailing = incoming[..., half_width:]
    return jnp.concatenate(
        [
            leading * cosine_table + trailing * sine_table,
            trailing * cosine_table - leading * sine_table,
        ],
        axis=-1,
    )


def rms_factor(values):
    return lax.rsqrt(jnp.mean(values * values, axis=-1, keepdims=True) + EPSILON)


def rms_back(values, factor, gain_row, incoming):
    scaled = gain_row * incoming
    return factor * scaled - values * factor**3 * jnp.mean(scaled * values, axis=-1, keepdims=True)


def tensor_sum(term_rows):
    return lax.psum(term_rows.astype(jnp.bfloat16), "tp").astype(jnp.float32)


def general_body(
    tokens,
    prefix_len,
    positions,
    gain_attend,
    w_query,
    w_key,
    w_value,
    w_project,
    gain_feed,
    w_gate,
    w_up,
    w_down,
    cotangent,
):
    (
        gain_one,
        query_weight_whole,
        key_weight_whole,
        value_weight_whole,
        project_weight_whole,
        gain_two,
        gate_weight_whole,
        up_weight_whole,
        down_weight_whole,
    ) = (
        lax.all_gather(gain_attend, "fsdp", axis=0, tiled=True),
        lax.all_gather(w_query, "fsdp", axis=0, tiled=True),
        lax.all_gather(w_key, "fsdp", axis=0, tiled=True),
        lax.all_gather(w_value, "fsdp", axis=0, tiled=True),
        lax.all_gather(w_project, "fsdp", axis=1, tiled=True),
        lax.all_gather(gain_feed, "fsdp", axis=0, tiled=True),
        lax.all_gather(w_gate, "fsdp", axis=0, tiled=True),
        lax.all_gather(w_up, "fsdp", axis=0, tiled=True),
        lax.all_gather(w_down, "fsdp", axis=1, tiled=True),
    )
    seq_count, rows_local, _ = tokens.shape
    pair_count = lax.axis_size("ctx")
    block_len = rows_local // 2
    query_width = query_weight_whole.shape[1]
    kv_width = key_weight_whole.shape[1]
    query_heads = query_width // HD
    kv_heads = kv_width // HD
    group_size = HQ // KVH
    score_scale = HD ** (-0.5)
    frequency = ROPE_BASE ** (-(jnp.arange(HD // 2, dtype=jnp.float32) * 2.0 / HD))
    angles = positions.astype(jnp.float32)[:, :, None] * frequency
    cosine_table = jnp.cos(angles)[:, :, None, :]
    sine_table = jnp.sin(angles)[:, :, None, :]
    stored_rows = lax.axis_index("ctx") * rows_local + jnp.arange(rows_local, dtype=jnp.int32)
    query_order = natural_index(stored_rows, block_len, pair_count)

    def visible_mask(key_order):
        causal = key_order[None, None, :] <= query_order[None, :, None]
        opened = key_order[None, None, :] < prefix_len[:, None, None]
        return (causal | opened)[:, :, None, None, :]

    inputs = tokens.astype(jnp.float32)
    factor_one = rms_factor(inputs)
    normed_hidden = (inputs * factor_one * gain_one.astype(jnp.float32)).astype(jnp.bfloat16)
    query_projected = jnp.einsum(
        "rxc,cf->rxf", normed_hidden, query_weight_whole, preferred_element_type=jnp.float32
    )
    key_projected = jnp.einsum(
        "rxc,cf->rxf", normed_hidden, key_weight_whole, preferred_element_type=jnp.float32
    )
    value_projected = jnp.einsum(
        "rxc,cf->rxf", normed_hidden, value_weight_whole, preferred_element_type=jnp.float32
    )
    queries = (
        rotate(
            query_projected.reshape(seq_count, rows_local, query_heads, HD),
            cosine_table,
            sine_table,
        )
        .astype(jnp.bfloat16)
        .reshape(seq_count, rows_local, kv_heads, group_size, HD)
    )
    keys_rot = (
        rotate(key_projected.reshape(seq_count, rows_local, kv_heads, HD), cosine_table, sine_table)
        .astype(jnp.bfloat16)
        .reshape(seq_count, rows_local, kv_width)
    )
    values_low = value_projected.astype(jnp.bfloat16)
    stat_shape = (seq_count, rows_local, kv_heads, group_size)
    initial = (
        jnp.full(stat_shape, NEGATIVE, jnp.float32),
        jnp.zeros(stat_shape, jnp.float32),
        jnp.zeros(stat_shape + (HD,), jnp.float32),
    )
    key_piece = lax.all_gather(keys_rot, "ctx", axis=1, tiled=True)
    value_piece = lax.all_gather(values_low, "ctx", axis=1, tiled=True)
    key_total = key_piece.shape[1]
    span_rows = math.gcd(key_total, rows_local)

    def one_span(span_index, running):
        run_max, run_sum, run_acc = running
        span_start = span_index * span_rows
        key_rows = lax.dynamic_slice_in_dim(key_piece, span_start, span_rows, 1).reshape(
            seq_count, span_rows, kv_heads, HD
        )
        value_rows = lax.dynamic_slice_in_dim(value_piece, span_start, span_rows, 1).reshape(
            seq_count, span_rows, kv_heads, HD
        )
        key_order = natural_index(
            span_start + jnp.arange(span_rows, dtype=jnp.int32), block_len, pair_count
        )
        visible = visible_mask(key_order)
        scores = (
            jnp.einsum("slhgd,skhd->slhgk", queries, key_rows, preferred_element_type=jnp.float32)
            * score_scale
        )
        new_max = jnp.maximum(run_max, jnp.max(jnp.where(visible, scores, NEGATIVE), axis=-1))
        weights_raw = jnp.where(visible, jnp.exp(scores - new_max[..., None]), 0.0)
        rescale = jnp.exp(run_max - new_max)
        run_sum = run_sum * rescale + jnp.sum(weights_raw, axis=-1)
        run_acc = run_acc * rescale[..., None] + jnp.einsum(
            "slhgk,skhd->slhgd",
            weights_raw.astype(jnp.bfloat16),
            value_rows,
            preferred_element_type=jnp.float32,
        )
        return (new_max, run_sum, run_acc)

    run_max, run_sum, run_acc = lax.fori_loop(0, key_total // span_rows, one_span, initial)
    attended = run_acc / run_sum[..., None]
    log_total = run_max + jnp.log(run_sum)
    attended_reduced = attended.reshape(seq_count, rows_local, query_width).astype(jnp.bfloat16)
    project_rows = jnp.einsum(
        "hxz,zm->hxm", attended_reduced, project_weight_whole, preferred_element_type=jnp.float32
    )
    middle = inputs + tensor_sum(project_rows)
    factor_two = rms_factor(middle)
    normed_feed_input = (middle * factor_two * gain_two.astype(jnp.float32)).astype(jnp.bfloat16)
    gate_activation = jnp.einsum(
        "qeh,hj->qej", normed_feed_input, gate_weight_whole, preferred_element_type=jnp.float32
    )
    up_activation = jnp.einsum(
        "qeh,hj->qej", normed_feed_input, up_weight_whole, preferred_element_type=jnp.float32
    )
    sigmoid_gate = jax.nn.sigmoid(gate_activation)
    silu_gate = gate_activation * sigmoid_gate
    hidden_state = (silu_gate * up_activation).astype(jnp.bfloat16)
    down_output_rows = jnp.einsum(
        "nct,tm->ncm", hidden_state, down_weight_whole, preferred_element_type=jnp.float32
    )
    layer_output = (middle + tensor_sum(down_output_rows)).astype(jnp.bfloat16)
    (
        gain_one,
        query_weight_whole,
        key_weight_whole,
        value_weight_whole,
        project_weight_whole,
        gain_two,
        gate_weight_whole,
        up_weight_whole,
        down_weight_whole,
    ) = (
        lax.all_gather(gain_attend, "fsdp", axis=0, tiled=True),
        lax.all_gather(w_query, "fsdp", axis=0, tiled=True),
        lax.all_gather(w_key, "fsdp", axis=0, tiled=True),
        lax.all_gather(w_value, "fsdp", axis=0, tiled=True),
        lax.all_gather(w_project, "fsdp", axis=1, tiled=True),
        lax.all_gather(gain_feed, "fsdp", axis=0, tiled=True),
        lax.all_gather(w_gate, "fsdp", axis=0, tiled=True),
        lax.all_gather(w_up, "fsdp", axis=0, tiled=True),
        lax.all_gather(w_down, "fsdp", axis=1, tiled=True),
    )
    hidden_grad = jnp.einsum(
        "ehv,iv->ehi", cotangent, down_weight_whole, preferred_element_type=jnp.float32
    )
    down_weight_part = jnp.einsum(
        "gqa,gqz->az", hidden_state, cotangent, preferred_element_type=jnp.float32
    )
    gate_reduced = (
        hidden_grad * up_activation * sigmoid_gate * (1.0 + gate_activation * (1.0 - sigmoid_gate))
    ).astype(jnp.bfloat16)
    up_reduced = (hidden_grad * silu_gate).astype(jnp.bfloat16)
    gate_weight_part = jnp.einsum(
        "bic,big->cg", normed_feed_input, gate_reduced, preferred_element_type=jnp.float32
    )
    up_weight_part = jnp.einsum(
        "bic,big->cg", normed_feed_input, up_reduced, preferred_element_type=jnp.float32
    )
    feed_rows = jnp.einsum(
        "vte,ce->vtc", gate_reduced, gate_weight_whole, preferred_element_type=jnp.float32
    ) + jnp.einsum("vte,ce->vtc", up_reduced, up_weight_whole, preferred_element_type=jnp.float32)
    feed_in = tensor_sum(feed_rows)
    gain_two_term = jnp.sum(feed_in * middle * factor_two, axis=(0, 1))
    middle_grad = cotangent.astype(jnp.float32) + rms_back(
        middle, factor_two, gain_two.astype(jnp.float32), feed_in
    )
    middle_reduced = middle_grad.astype(jnp.bfloat16)
    project_term = jnp.einsum(
        "xeh,xec->hc", attended_reduced, middle_reduced, preferred_element_type=jnp.float32
    )
    attended_grad = (
        jnp.einsum(
            "vhk,nk->vhn", middle_reduced, project_weight_whole, preferred_element_type=jnp.float32
        )
        .astype(jnp.bfloat16)
        .reshape(seq_count, rows_local, kv_heads, group_size, HD)
    )
    row_delta = jnp.sum(attended_grad.astype(jnp.float32) * attended, axis=-1)
    whole_keys, whole_values = (
        lax.all_gather(keys_rot[None], "ctx", axis=0, tiled=True),
        lax.all_gather(values_low[None], "ctx", axis=0, tiled=True),
    )

    def key_block(grad_acc, block_items):
        key_rows, value_rows, block_index = block_items
        key_rows = key_rows.reshape(seq_count, rows_local, kv_heads, HD)
        value_rows = value_rows.reshape(seq_count, rows_local, kv_heads, HD)
        key_order = natural_index(
            block_index * rows_local + jnp.arange(rows_local, dtype=jnp.int32),
            block_len,
            pair_count,
        )
        visible = visible_mask(key_order)
        scores = (
            jnp.einsum("slhgd,skhd->slhgk", queries, key_rows, preferred_element_type=jnp.float32)
            * score_scale
        )
        weights_norm = jnp.where(visible, jnp.exp(scores - log_total[..., None]), 0.0)
        prob_grad = jnp.einsum(
            "slhgd,skhd->slhgk", attended_grad, value_rows, preferred_element_type=jnp.float32
        )
        score_grad = (weights_norm * (prob_grad - row_delta[..., None])).astype(jnp.bfloat16)
        grad_acc = (
            grad_acc
            + jnp.einsum(
                "slhgk,skhd->slhgd", score_grad, key_rows, preferred_element_type=jnp.float32
            )
            * score_scale
        )
        key_grad = (
            jnp.einsum("slhgk,slhgd->skhd", score_grad, queries, preferred_element_type=jnp.float32)
            * score_scale
        )
        value_grad = jnp.einsum(
            "slhgk,slhgd->skhd",
            weights_norm.astype(jnp.bfloat16),
            attended_grad,
            preferred_element_type=jnp.float32,
        )
        return (
            grad_acc,
            (
                key_grad.reshape(seq_count, rows_local, kv_width),
                value_grad.reshape(seq_count, rows_local, kv_width),
            ),
        )

    block_ids = jnp.arange(pair_count, dtype=jnp.int32)
    query_grad, (key_terms, value_terms) = lax.scan(
        key_block, jnp.zeros(stat_shape + (HD,), jnp.float32), (whole_keys, whole_values, block_ids)
    )
    key_sum, value_sum = (
        lax.psum_scatter(
            key_terms.astype(jnp.bfloat16), "ctx", scatter_dimension=0, tiled=True
        ).astype(jnp.float32),
        lax.psum_scatter(
            value_terms.astype(jnp.bfloat16), "ctx", scatter_dimension=0, tiled=True
        ).astype(jnp.float32),
    )
    key_reduced = (
        rotate_back(
            key_sum[0].reshape(seq_count, rows_local, kv_heads, HD), cosine_table, sine_table
        )
        .astype(jnp.bfloat16)
        .reshape(seq_count, rows_local, kv_width)
    )
    value_backward = value_sum[0].astype(jnp.bfloat16)
    query_reduced = (
        rotate_back(
            query_grad.reshape(seq_count, rows_local, query_heads, HD), cosine_table, sine_table
        )
        .astype(jnp.bfloat16)
        .reshape(seq_count, rows_local, query_width)
    )
    query_weight_part = jnp.einsum(
        "prb,pro->bo", normed_hidden, query_reduced, preferred_element_type=jnp.float32
    )
    key_weight_part = jnp.einsum(
        "prb,pro->bo", normed_hidden, key_reduced, preferred_element_type=jnp.float32
    )
    value_weight_part = jnp.einsum(
        "prb,pro->bo", normed_hidden, value_backward, preferred_element_type=jnp.float32
    )
    normed_rows = (
        jnp.einsum(
            "kjw,iw->kji", query_reduced, query_weight_whole, preferred_element_type=jnp.float32
        )
        + jnp.einsum(
            "kjw,iw->kji", key_reduced, key_weight_whole, preferred_element_type=jnp.float32
        )
        + jnp.einsum(
            "kjw,iw->kji", value_backward, value_weight_whole, preferred_element_type=jnp.float32
        )
    )
    normed_grad = tensor_sum(normed_rows)
    gain_one_term = jnp.sum(normed_grad * inputs * factor_one, axis=(0, 1))
    tokens_grad = (
        middle_grad + rms_back(inputs, factor_one, gain_one.astype(jnp.float32), normed_grad)
    ).astype(jnp.bfloat16)
    (
        part_one,
        part_query,
        part_key,
        part_value,
        part_project,
        part_two,
        part_gate,
        part_up,
        part_down,
    ) = (
        lax.psum_scatter(gain_one_term, ("fsdp", "ctx"), scatter_dimension=0, tiled=True),
        lax.psum_scatter(query_weight_part, ("fsdp", "ctx"), scatter_dimension=0, tiled=True),
        lax.psum_scatter(key_weight_part, ("fsdp", "ctx"), scatter_dimension=0, tiled=True),
        lax.psum_scatter(value_weight_part, ("fsdp", "ctx"), scatter_dimension=0, tiled=True),
        lax.psum_scatter(project_term, ("fsdp", "ctx"), scatter_dimension=1, tiled=True),
        lax.psum_scatter(gain_two_term, ("fsdp", "ctx"), scatter_dimension=0, tiled=True),
        lax.psum_scatter(gate_weight_part, ("fsdp", "ctx"), scatter_dimension=0, tiled=True),
        lax.psum_scatter(up_weight_part, ("fsdp", "ctx"), scatter_dimension=0, tiled=True),
        lax.psum_scatter(down_weight_part, ("fsdp", "ctx"), scatter_dimension=1, tiled=True),
    )
    reduced = (
        lax.all_gather(part_one.astype(jnp.bfloat16), "ctx", axis=0, tiled=True).astype(
            part_one.dtype
        ),
        lax.all_gather(part_query.astype(jnp.bfloat16), "ctx", axis=0, tiled=True).astype(
            part_query.dtype
        ),
        lax.all_gather(part_key.astype(jnp.bfloat16), "ctx", axis=0, tiled=True).astype(
            part_key.dtype
        ),
        lax.all_gather(part_value.astype(jnp.bfloat16), "ctx", axis=0, tiled=True).astype(
            part_value.dtype
        ),
        lax.all_gather(part_project.astype(jnp.bfloat16), "ctx", axis=1, tiled=True).astype(
            part_project.dtype
        ),
        lax.all_gather(part_two.astype(jnp.bfloat16), "ctx", axis=0, tiled=True).astype(
            part_two.dtype
        ),
        lax.all_gather(part_gate.astype(jnp.bfloat16), "ctx", axis=0, tiled=True).astype(
            part_gate.dtype
        ),
        lax.all_gather(part_up.astype(jnp.bfloat16), "ctx", axis=0, tiled=True).astype(
            part_up.dtype
        ),
        lax.all_gather(part_down.astype(jnp.bfloat16), "ctx", axis=1, tiled=True).astype(
            part_down.dtype
        ),
    )
    return (layer_output, tokens_grad) + tuple(reduced)


LANES = 128
HALF = HD // 2
SPAN = LANES // 2
LOG2E = math.log2(math.e)
VMEM_BYTES = 60 * 1024 * 1024


def swap_ctx(block):
    return lax.ppermute(block, "ctx", [(0, 1), (1, 0)])


def swap_core(block):
    return lax.ppermute(block, "tp", [(0, 1), (1, 0), (2, 3), (3, 2)])


def swap_chip(block):
    return lax.ppermute(block, "tp", [(0, 2), (2, 0), (1, 3), (3, 1)])


def by_core(total, other):
    return jnp.where(
        lax.axis_index("tp") % 2 == 0,
        jnp.concatenate([total, other], axis=0),
        jnp.concatenate([other, total], axis=0),
    )


def dot(a, b, contract):
    return lax.dot_general(a, b, (contract, ((), ())), preferred_element_type=jnp.float32)


def block_kinds(meta_ref, query_tile, key_tile, q_start, k_start):
    prefix = meta_ref[0]
    whole = (k_start + (key_tile - 1) <= q_start) | (k_start + key_tile <= prefix)
    nothing = (k_start > q_start + (query_tile - 1)) & (k_start >= prefix)
    return prefix, whole, nothing


def mask_scores(scores, prefix, q_start, k_start, query_tile):
    key_ids = k_start + lax.broadcasted_iota(jnp.int32, scores.shape, 0)
    column = lax.broadcasted_iota(jnp.int32, scores.shape, 1)
    query_ids = q_start + jnp.bitwise_and(column, query_tile - 1)
    return jnp.where((key_ids <= query_ids) | (key_ids < prefix), scores, NEGATIVE)


MESH = pl.DeviceIdType.MESH
GAIN_ROWS = 16
PREFIX_MOST = 1024


def line_sum(z, planes, source, up_ref, down_ref, up_send, up_recv, down_send, down_recv):
    f32 = jnp.float32

    def up(d):
        return pltpu.make_async_remote_copy(
            src_ref=up_ref.at[d - 1],
            dst_ref=up_ref.at[d - 1],
            send_sem=up_send.at[d],
            recv_sem=up_recv.at[d],
            device_id={"fsdp": z + 1},
            device_id_type=MESH,
        )

    def down(d):
        return pltpu.make_async_remote_copy(
            src_ref=down_ref.at[d],
            dst_ref=down_ref.at[d],
            send_sem=down_send.at[d],
            recv_sem=down_recv.at[d],
            device_id={"fsdp": z - 1},
            device_id_type=MESH,
        )

    def begin(k):
        high, low = planes - 1 - k, k

        @pl.when(z == 0)
        def _():
            up_ref[high - 1] = source(high)
            up(high).start()

        @pl.when(z == planes - 1)
        def _():
            down_ref[low] = source(low)
            down(low).start()

    def relay(k):
        high, low = planes - 1 - k, k

        def pass_up():
            @pl.when((z > 0) & (z < high))
            def _():
                up(high).wait_recv()
                up_ref[high - 1] = (
                    up_ref[high - 1].astype(f32) + source(high).astype(f32)
                ).astype(up_ref.dtype)
                up(high).start()

        def pass_down():
            @pl.when((z < planes - 1) & (z > low))
            def _():
                down(low).wait_recv()
                down_ref[low] = (
                    down_ref[low].astype(f32) + source(low).astype(f32)
                ).astype(down_ref.dtype)
                down(low).start()

        @pl.when(2 * z < planes)
        def _():
            pass_up()
            pass_down()

        @pl.when(2 * z >= planes)
        def _():
            pass_down()
            pass_up()

    def finish(out_ref):
        out_ref[...] = source(z)

        @pl.when(z > 0)
        def _():
            up(z).wait_recv()
            out_ref[...] = (
                out_ref[...].astype(f32) + up_ref[pl.ds(z - 1, 1)][0].astype(f32)
            ).astype(out_ref.dtype)

        @pl.when(z < planes - 1)
        def _():
            down(z).wait_recv()
            out_ref[...] = (
                out_ref[...].astype(f32) + down_ref[pl.ds(z, 1)][0].astype(f32)
            ).astype(out_ref.dtype)

    def sent():
        for d in range(planes):

            @pl.when(z < d)
            def _():
                up(d).wait_send()

            @pl.when(z > d)
            def _():
                down(d).wait_send()

    return begin, relay, finish, sent


def front_kernel(
    prefix_ref,
    x_ref,
    pack_ref,
    rest_ref,
    spread_ref,
    cos_ref,
    sin_ref,
    w_project_ref,
    w_gate_ref,
    w_up_ref,
    w_down_ref,
    normed_hbm,
    q_hbm,
    kv_hbm,
    wide_hbm,
    project_ref,
    gain_ref,
    o_ref,
    lse_ref,
    total_ref,
    gate_ref,
    up_ref,
    down_ref,
    normed_ref,
    q_ref,
    kv_ref,
    wide_ref,
    buf_ref,
    max_ref,
    sum_ref,
    acc_ref,
    give_ref,
    core_in_ref,
    keep_ref,
    chip_in_ref,
    up_send,
    up_recv,
    down_send,
    down_recv,
    x_send,
    x_recv,
    kv_send,
    kv_recv,
    m_up_send,
    m_up_recv,
    m_down_send,
    m_down_recv,
    m_x_send,
    m_x_recv,
    local_sem,
    core_send,
    core_recv,
    chip_send,
    chip_recv,
    back_send,
    back_recv,
    store_sem,
):
    bf16, f32 = jnp.bfloat16, jnp.float32
    planes = buf_ref.shape[0]
    rows, width = x_ref.shape
    depth = width // planes
    half_width = wide_ref.shape[1] // 2
    matrix_rows = rest_ref.shape[0]
    heads_half = project_ref.shape[0] // 2
    units = gate_ref.shape[2]
    direct = units // 2
    z = lax.axis_index("fsdp")
    c = lax.axis_index("ctx")
    t = lax.axis_index("tp")
    core = lax.rem(t, 2)
    across = {"ctx": 1 - c}
    sibling = {"tp": t + 1 - 2 * core}
    partner = {"tp": lax.rem(t + 2, 4)}
    has_above = z < planes - 1
    has_below = z > 0

    def remote(src, dst, send, recv, device):
        return pltpu.make_async_remote_copy(
            src_ref=src,
            dst_ref=dst,
            send_sem=send,
            recv_sem=recv,
            device_id=device,
            device_id_type=MESH,
        )

    project_ref[:, HD:, :] = jnp.zeros(
        (project_ref.shape[0], LANES - HD, project_ref.shape[2]), bf16
    )

    barrier = pltpu.get_barrier_semaphore()

    @pl.when(has_above)
    def _():
        pl.semaphore_signal(barrier, inc=1, device_id={"fsdp": z + 1}, device_id_type=MESH)

    @pl.when(has_below)
    def _():
        pl.semaphore_signal(barrier, inc=1, device_id={"fsdp": z - 1}, device_id_type=MESH)

    for device in (across, sibling, partner):
        pl.semaphore_signal(barrier, inc=1, device_id=device, device_id_type=MESH)

    @pl.when(has_above & has_below)
    def _():
        pl.semaphore_wait(barrier, 5)

    @pl.when(jnp.logical_not(has_above & has_below))
    def _():
        pl.semaphore_wait(barrier, 4)

    def up(k):
        piece = z - k
        src = pack_ref if k == 0 else buf_ref.at[piece, 0]
        return remote(src, buf_ref.at[piece, 0], up_send.at[k], up_recv.at[k], {"fsdp": z + 1})

    def down(k):
        piece = z + k
        src = pack_ref if k == 0 else buf_ref.at[piece, 0]
        return remote(src, buf_ref.at[piece, 0], down_send.at[k], down_recv.at[k], {"fsdp": z - 1})

    def from_below(k):
        slot = buf_ref.at[z - 1 - k, 0]
        return remote(slot, slot, up_send.at[k], up_recv.at[k], {"fsdp": z - 1})

    def from_above(k):
        slot = buf_ref.at[z + 1 + k, 0]
        return remote(slot, slot, down_send.at[k], down_recv.at[k], {"fsdp": z + 1})

    def sideways(side, k):
        piece = z - k if side == 0 else z + k
        matrix = pl.ds(0, matrix_rows)
        return remote(
            buf_ref.at[piece, 0, matrix],
            buf_ref.at[piece, 1, matrix],
            x_send.at[side, k],
            x_recv.at[side, k],
            across,
        )

    def own_half(m, half):
        if m == 0:
            return w_gate_ref.at[:, pl.ds(pl.multiple_of(half * units, units), units)]
        if m == 1:
            return w_up_ref.at[:, pl.ds(pl.multiple_of(half * units, units), units)]
        if m == 2:
            return w_down_ref.at[pl.ds(pl.multiple_of(half * units, units), units), :]
        if m == 4:
            return w_down_ref.at[pl.ds(pl.multiple_of((1 - half) * units, units), direct), :]
        return w_project_ref.at[pl.ds(half * heads_half, heads_half)]

    def slot(m, which, piece):
        at = pl.ds(pl.multiple_of(piece * depth, depth), depth)
        if m == 0:
            return gate_ref.at[which, at]
        if m == 1:
            return up_ref.at[which, at]
        if m == 2:
            return down_ref.at[which, :, at]
        if m == 4:
            return down_ref.at[1, pl.ds(0, direct), at]
        return project_ref.at[pl.ds(which * heads_half, heads_half), pl.ds(0, HD), at]

    def m_up(m, k):
        piece = z - k
        src = own_half(m, c) if k == 0 else slot(m, 0, piece)
        return remote(
            src, slot(m, 0, piece), m_up_send.at[m, k], m_up_recv.at[m, k], {"fsdp": z + 1}
        )

    def m_down(m, k):
        piece = z + k
        src = own_half(m, c) if k == 0 else slot(m, 0, piece)
        return remote(
            src, slot(m, 0, piece), m_down_send.at[m, k], m_down_recv.at[m, k], {"fsdp": z - 1}
        )

    def m_below(m, k):
        at = slot(m, 0, z - 1 - k)
        return remote(at, at, m_up_send.at[m, k], m_up_recv.at[m, k], {"fsdp": z - 1})

    def m_above(m, k):
        at = slot(m, 0, z + 1 + k)
        return remote(at, at, m_down_send.at[m, k], m_down_recv.at[m, k], {"fsdp": z + 1})

    def m_side(m, side, k):
        piece = z - k if side == 0 else z + k
        src, dst = slot(m, 0, piece), slot(m, 1, piece)
        if m == 2:
            left = pl.ds(direct, units - direct)
            src, dst = src.at[left], dst.at[left]
        return remote(
            src,
            dst,
            m_x_send.at[m, side, k],
            m_x_recv.at[m, side, k],
            across,
        )

    groups = ((3,), (0,), (1,), (2, 4))

    def relay(group, k):
        for m in groups[group]:

            @pl.when(z - k >= 0)
            def _():
                m_below(m, k - 1).wait_recv()
                if k < planes - 1:

                    @pl.when(has_above)
                    def _():
                        m_up(m, k).start()

            @pl.when(z + k <= planes - 1)
            def _():
                m_above(m, k - 1).wait_recv()
                if k < planes - 1:

                    @pl.when(has_below)
                    def _():
                        m_down(m, k).start()

    def launch(group):
        for m in groups[group]:

            @pl.when(has_above)
            def _():
                m_up(m, 0).start()

            @pl.when(has_below)
            def _():
                m_down(m, 0).start()

    def cross(group, k):
        for m in groups[group]:
            if m == 4:
                continue

            @pl.when(z - k >= 0)
            def _():
                m_side(m, 0, k).start()

            @pl.when(z + k <= planes - 1)
            def _():
                m_side(m, 1, k).start()

    def crossed(m, k):
        @pl.when(z - k >= 0)
        def _():
            m_side(m, 0, k).wait_recv()

        @pl.when(z + k <= planes - 1)
        def _():
            m_side(m, 1, k).wait_recv()

    def local(m, which):
        half = c if which == 0 else 1 - c
        return pltpu.make_async_copy(own_half(m, half), slot(m, which, z), local_sem.at[m, which])

    spread = spread_ref[...]

    def place(block, piece, which):
        at = pl.ds(pl.multiple_of(piece * depth, depth), depth)
        wide_ref[at, which * half_width : (which + 1) * half_width] = dot(
            block[:depth], spread, ((1,), (0,))
        ).astype(bf16)

    def place_gain(block, piece):
        at = pl.ds(pl.multiple_of(piece * depth, depth), depth)
        gain_ref[:, at] = block[matrix_rows:]

    @pl.when(has_above)
    def _():
        up(0).start()

    @pl.when(has_below)
    def _():
        down(0).start()

    for m in (3, 0, 1, 2):
        for which in range(2):
            local(m, which).start()
    place(pack_ref, z, 0)
    place_gain(pack_ref, z)
    place(rest_ref, z, 1)

    for k in range(1, planes):
        below = z - k >= 0
        above = z + k <= planes - 1

        @pl.when(below)
        def _():
            from_below(k - 1).wait_recv()
            if k < planes - 1:

                @pl.when(has_above)
                def _():
                    up(k).start()

            sideways(0, k).start()

        @pl.when(above)
        def _():
            from_above(k - 1).wait_recv()
            if k < planes - 1:

                @pl.when(has_below)
                def _():
                    down(k).start()

            sideways(1, k).start()

        if k == max(1, planes - 2):
            launch(0)
            launch(1)

        @pl.when(below)
        def _():
            place(buf_ref.at[z - k, 0], z - k, 0)
            place_gain(buf_ref.at[z - k, 0], z - k)

        @pl.when(above)
        def _():
            place(buf_ref.at[z + k, 0], z + k, 0)
            place_gain(buf_ref.at[z + k, 0], z + k)

    relay(0, 1)
    cross(0, 1)
    tile = 128
    gain = gain_ref[0:1, :].astype(f32)

    def norm_rows(i, carry):
        at = pl.ds(pl.multiple_of(i * tile, tile), tile)
        x = x_ref[at, :].astype(f32)
        factor = lax.rsqrt(jnp.mean(x * x, axis=-1, keepdims=True) + EPSILON)
        normed_ref[at, :] = (x * factor * gain).astype(bf16)
        return carry

    lax.fori_loop(0, rows // tile, norm_rows, 0)
    relay(0, 2)
    cross(0, 2)
    launch(2)

    for k in range(1, planes):

        @pl.when(z - k >= 0)
        def _():
            sideways(0, k).wait_recv()
            place(buf_ref.at[z - k, 1], z - k, 1)

        @pl.when(z + k <= planes - 1)
        def _():
            sideways(1, k).wait_recv()
            place(buf_ref.at[z + k, 1], z + k, 1)

    block = 256

    def turn(part, at):
        return part * cos_ref[at, :] + pltpu.roll(part, SPAN, 1) * sin_ref[at, :]

    def key_rows(i, carry):
        at = pl.ds(pl.multiple_of(i * block, block), block)
        for which in range(2):
            lane = which * half_width + 2 * LANES
            both = dot(normed_ref[at, :], wide_ref[:, lane : lane + 2 * LANES], ((1,), (0,)))
            kv_ref[which, at, :] = turn(both[:, :LANES], at).astype(bf16)
            kv_ref[2 + which, at, :] = both[:, LANES:].astype(bf16)
        return carry

    lax.fori_loop(0, rows // block, key_rows, 0)

    def exchange(slab):
        return remote(
            kv_ref.at[slab, pl.ds(0, rows)],
            kv_ref.at[slab ^ 1, pl.ds(rows, rows)],
            kv_send.at[slab],
            kv_recv.at[slab ^ 1],
            across,
        )

    for slab in range(4):
        exchange(slab).start()
    relay(0, 3)
    cross(0, 3)
    relay(1, 1)
    launch(3)
    scale = HD ** (-0.5) * LOG2E

    def query_rows(i, carry):
        at = pl.ds(pl.multiple_of(i * block, block), block)
        for which in range(2):
            lane = which * half_width
            both = dot(normed_ref[at, :], wide_ref[:, lane : lane + 2 * LANES], ((1,), (0,)))
            for head in range(2):
                part = turn(both[:, head * LANES : (head + 1) * LANES], at)
                lane = (2 * which + head) * LANES
                q_ref[at, lane : lane + LANES] = (part * scale).astype(bf16)
        return carry

    lax.fori_loop(0, rows // block, query_rows, 0)
    stores = [
        pltpu.make_async_copy(src, dst, store_sem.at[i])
        for i, (src, dst) in enumerate(
            ((normed_ref, normed_hbm), (q_ref, q_hbm), (wide_ref, wide_hbm), (kv_ref, kv_hbm))
        )
    ]
    for store in stores[:3]:
        store.start()

    tiles = rows // block
    tiles_of_block = tiles // 2
    prefix = prefix_ref[0]
    max_ref[...] = jnp.full_like(max_ref, NEGATIVE)
    sum_ref[...] = jnp.zeros_like(sum_ref)
    acc_ref[...] = jnp.zeros_like(acc_ref)

    def start_of(device, tile_index):
        second = tile_index // tiles_of_block
        block_id = device + second * (3 - 2 * device)
        return (block_id * tiles_of_block + tile_index % tiles_of_block) * block

    def attend_group(g, away):
        key_device = 1 - c if away else c

        def one_tile(i, carry):
            at = pl.ds(pl.multiple_of(i * block, block), block)
            lane = 2 * g * LANES
            queries = jnp.concatenate(
                [q_ref[at, lane : lane + LANES], q_ref[at, lane + LANES : lane + 2 * LANES]],
                axis=0,
            )
            q_start = start_of(c, i)
            u = g * tiles + i

            def absorb(scores, values):
                old = max_ref[u]
                new = jnp.maximum(old, jnp.max(scores, axis=0, keepdims=True))
                weights = jnp.exp2(scores - new)
                rescale = jnp.exp2(old - new)
                max_ref[u] = new
                sum_ref[u] = sum_ref[u] * rescale + jnp.sum(weights, axis=0, keepdims=True)
                acc_ref[u] = acc_ref[u] * rescale + dot(values, weights.astype(bf16), ((0,), (0,)))

            def one(j, carry):
                k_start = start_of(key_device, j)
                first = (tiles if away else 0) + j
                keys_at = pl.ds(pl.multiple_of(first * block, block), block)
                whole = k_start + (block - 1) <= q_start
                nothing = (k_start > q_start + (block - 1)) & (k_start >= PREFIX_MOST)

                @pl.when(whole)
                def _():
                    absorb(dot(kv_ref[g, keys_at, :], queries, ((1,), (1,))), kv_ref[2 + g, keys_at, :])

                @pl.when(jnp.logical_not(whole | nothing))
                def _():
                    scores = dot(kv_ref[g, keys_at, :], queries, ((1,), (1,)))
                    absorb(
                        mask_scores(scores, prefix, q_start, k_start, block),
                        kv_ref[2 + g, keys_at, :],
                    )

                return carry

            lax.fori_loop(0, tiles, one, 0)
            if away:
                total = sum_ref[u]
                lse_ref[g, i] = max_ref[u] + jnp.log2(total)
                out = (acc_ref[u] / total).T.astype(bf16)
                o_ref[at, lane : lane + LANES] = out[:block]
                o_ref[at, lane + LANES : lane + 2 * LANES] = out[block:]
            return carry

        lax.fori_loop(0, tiles, one_tile, 0)

    attend_group(0, False)
    relay(2, 1)
    cross(1, 1)
    attend_group(1, False)
    relay(3, 1)
    for slab in range(4):
        exchange(slab).wait_recv()
    stores[3].start()
    cross(2, 1)
    cross(3, 1)
    attend_group(0, True)
    relay(1, 2)
    cross(1, 2)
    attend_group(1, True)
    relay(2, 2)
    cross(2, 2)

    chunks, chunk, _ = give_ref.shape
    half_rows = rows // 2
    give_start = (1 - core) * half_rows
    keep_start = core * half_rows
    for which in range(2):
        local(3, which).wait()
    for k in range(1, planes):
        crossed(3, k)
    w_project = project_ref[...].reshape(project_ref.shape[0] * LANES, width)

    def feature_rows(start):
        at = pl.ds(pl.multiple_of(start, chunk), chunk)
        return dot(o_ref[at, :], w_project, ((1,), (0,)))

    def to_core(i):
        return remote(give_ref.at[i], core_in_ref.at[i], core_send.at[i], core_recv.at[i], sibling)

    def to_chip(i):
        return remote(keep_ref.at[i], chip_in_ref.at[i], chip_send.at[i], chip_recv.at[i], partner)

    def back(i, start):
        at = pl.ds(pl.multiple_of(start + i * chunk, chunk), chunk)
        return remote(
            total_ref.at[at], total_ref.at[at], back_send.at[i], back_recv.at[i], sibling
        )

    for i in range(chunks):
        give_ref[i] = feature_rows(give_start + i * chunk).astype(bf16)
        to_core(i).start()
    for i in range(chunks):
        kept = feature_rows(keep_start + i * chunk)
        to_core(i).wait_recv()
        keep_ref[i] = (kept + core_in_ref[i].astype(f32)).astype(bf16)
        to_chip(i).start()

    def finish_chunk(i):
        to_chip(i).wait_recv()
        at = pl.ds(pl.multiple_of(keep_start + i * chunk, chunk), chunk)
        total_ref[at, :] = (keep_ref[i].astype(f32) + chip_in_ref[i].astype(f32)).astype(bf16)
        back(i, keep_start).start()

    relay(3, 2)
    cross(3, 2)
    for i in range(chunks):
        finish_chunk(i)
        if i < planes - 1:
            relay(i + 1, planes - 1)
            cross(i + 1, planes - 1)

    for store in stores:
        store.wait()
    for k in range(planes - 1):

        @pl.when((z - k >= 0) & has_above)
        def _():
            up(k).wait_send()
            for m in range(5):
                m_up(m, k).wait_send()

        @pl.when((z + k <= planes - 1) & has_below)
        def _():
            down(k).wait_send()
            for m in range(5):
                m_down(m, k).wait_send()

    for k in range(1, planes):

        @pl.when(z - k >= 0)
        def _():
            sideways(0, k).wait_send()
            for m in range(4):
                m_side(m, 0, k).wait_send()

        @pl.when(z + k <= planes - 1)
        def _():
            sideways(1, k).wait_send()
            for m in range(4):
                m_side(m, 1, k).wait_send()

        for m in range(3):
            crossed(m, k)

    for m in range(3):
        for which in range(2):
            local(m, which).wait()
    for slab in range(4):
        exchange(slab).wait_send()
    for i in range(chunks):
        to_core(i).wait_send()
        to_chip(i).wait_send()
        back(i, keep_start).wait_send()
        back(i, give_start).wait_recv()


def front(prefix, x, pack, rest, spread, cosine, sine, w_project, w_gate, w_up, w_down, planes):
    rows, width = x.shape
    half_width = spread.shape[1]
    units = w_gate.shape[1] // 2
    heads = w_project.shape[0]
    block = 256
    tiles = rows // block
    chunks = 4
    chunk = rows // 2 // chunks
    vmem = pl.BlockSpec(memory_space=pltpu.VMEM)
    anywhere = pl.BlockSpec(memory_space=pl.ANY)
    smem = pl.BlockSpec(memory_space=pltpu.SMEM)
    bf16, f32 = jnp.bfloat16, jnp.float32
    dma = pltpu.SemaphoreType.DMA
    piece = pltpu.VMEM((chunks, chunk, width), bf16)
    return pl.pallas_call(
        front_kernel,
        in_specs=[smem] + [vmem] * 6 + [anywhere] * 4,
        out_specs=[anywhere] * 4 + [vmem] * 5 + [anywhere] * 3,
        out_shape=[
            jax.ShapeDtypeStruct((rows, width), bf16),
            jax.ShapeDtypeStruct((rows, half_width), bf16),
            jax.ShapeDtypeStruct((4, 2 * rows, LANES), bf16),
            jax.ShapeDtypeStruct((width, 2 * half_width), bf16),
            jax.ShapeDtypeStruct((heads, LANES, width), bf16),
            jax.ShapeDtypeStruct((GAIN_ROWS, width), bf16),
            jax.ShapeDtypeStruct((rows, half_width), bf16),
            jax.ShapeDtypeStruct((2, tiles, 1, 2 * block), f32),
            jax.ShapeDtypeStruct((rows, width), bf16),
            jax.ShapeDtypeStruct((2, width, units), bf16),
            jax.ShapeDtypeStruct((2, width, units), bf16),
            jax.ShapeDtypeStruct((2, units, width), bf16),
        ],
        scratch_shapes=[
            pltpu.VMEM((rows, width), bf16),
            pltpu.VMEM((rows, half_width), bf16),
            pltpu.VMEM((4, 2 * rows, LANES), bf16),
            pltpu.VMEM((width, 2 * half_width), bf16),
            pltpu.VMEM((planes, 2, pack.shape[0], pack.shape[1]), bf16),
            pltpu.VMEM((2 * tiles, 1, 2 * block), f32),
            pltpu.VMEM((2 * tiles, 1, 2 * block), f32),
            pltpu.VMEM((2 * tiles, LANES, 2 * block), f32),
            piece,
            piece,
            piece,
            piece,
        ]
        + [dma((planes - 1,))] * 4
        + [dma((2, planes))] * 2
        + [dma((4,))] * 2
        + [dma((5, planes - 1))] * 4
        + [dma((4, 2, planes))] * 2
        + [dma((4, 2))]
        + [dma((chunks,))] * 6
        + [dma((4,))],
        compiler_params=pltpu.CompilerParams(
            collective_id=1, has_side_effects=True, vmem_limit_bytes=VMEM_BYTES
        ),
        cost_estimate=pl.CostEstimate(
            flops=120_000_000_000, bytes_accessed=60_000_000, transcendentals=0
        ),
        name="front",
    )(prefix, x, pack, rest, spread, cosine, sine, w_project, w_gate, w_up, w_down)


def attend_back_kernel(
    final,
    meta_ref,
    carry_ref,
    first_ref,
    second_ref,
    q_ref,
    k_ref,
    v_ref,
    o_ref,
    do_ref,
    lse_ref,
    cos_ref,
    sin_ref,
    dq_ref,
    dkv_ref,
    delta_ref,
    acc_ref,
    dk_acc_ref,
    dv_acc_ref,
):
    query_tiles = lse_ref.shape[1]
    tile = q_ref.shape[0] // query_tiles
    key_tile = k_ref.shape[1]
    j = pl.program_id(1)

    def stacked(ref, i):
        rows = pl.ds(pl.multiple_of(i * tile, tile), tile)
        return jnp.concatenate([ref[rows, :LANES], ref[rows, LANES:]], axis=0)

    @pl.when(j == 0)
    def _():
        acc_ref[...] = carry_ref[0] if final else jnp.zeros_like(acc_ref)

        def one_delta(i, carry):
            product = stacked(o_ref, i).astype(jnp.float32) * stacked(do_ref, i).astype(jnp.float32)
            delta_ref[i] = jnp.sum(product.T, axis=0, keepdims=True)
            return carry

        lax.fori_loop(0, query_tiles, one_delta, 0)

    k_start = meta_ref[1 + query_tiles + (0 if final else pl.num_programs(1)) + j]
    keys = k_ref[0]
    values = v_ref[0]

    dk_acc_ref[...] = jnp.zeros_like(dk_acc_ref)
    dv_acc_ref[...] = jnp.zeros_like(dv_acc_ref)

    def one(i, carry):
        q_start = meta_ref[1 + i]
        prefix, whole, nothing = block_kinds(meta_ref, tile, key_tile, q_start, k_start)

        def some(masked):
            queries = stacked(q_ref, i)
            d_out = stacked(do_ref, i)
            scores = dot(keys, queries, ((1,), (1,)))
            if masked:
                scores = mask_scores(scores, prefix, q_start, k_start, tile)
            weights = jnp.exp2(scores - lse_ref[0, i])
            d_weights = dot(values, d_out, ((1,), (1,)))
            d_scores = (weights * (d_weights - delta_ref[i])).astype(jnp.bfloat16)
            dv_acc_ref[...] += dot(weights.astype(jnp.bfloat16), d_out, ((1,), (0,)))
            dk_acc_ref[...] += dot(d_scores, queries, ((1,), (0,)))
            acc_ref[i] += dot(keys, d_scores, ((0,), (0,)))

        @pl.when(whole)
        def _():
            some(False)

        @pl.when(jnp.logical_not(whole | nothing))
        def _():
            some(True)

        return carry

    lax.fori_loop(0, query_tiles, one, 0)
    dkv_ref[0, 0] = (dk_acc_ref[...] * (1.0 / LOG2E)).astype(jnp.bfloat16)
    dkv_ref[0, 1] = dv_acc_ref[...].astype(jnp.bfloat16)

    @pl.when(j == pl.num_programs(1) - 1)
    def _():
        scale = HD ** (-0.5)
        if not final:
            dq_ref[0] = acc_ref[...]
            return

        def one_out(i, carry):
            rows = pl.ds(pl.multiple_of(i * tile, tile), tile)
            turned = acc_ref[i].T * scale
            for head in range(2):
                part = turned[head * tile : (head + 1) * tile]
                part = part * cos_ref[rows, :] - pltpu.roll(part, SPAN, 1) * sin_ref[rows, :]
                dq_ref[rows, head * LANES : (head + 1) * LANES] = part.astype(jnp.bfloat16)
            return carry

        lax.fori_loop(0, query_tiles, one_out, 0)


def attend_back(meta, carry, first, second, q, kv, away, o, d_out, lse, cosine, sine, tile):
    rows, q_width = q.shape
    keys = kv.shape[1] // 2
    groups = q_width // (2 * LANES)
    query_tiles = rows // tile
    key_tiles = keys // tile
    skip = key_tiles if away else 0
    acc_block = pl.BlockSpec((1, query_tiles, LANES, 2 * tile), lambda g, j, m: (g, 0, 0, 0))
    acc_shape = jax.ShapeDtypeStruct((groups, query_tiles, LANES, 2 * tile), jnp.float32)
    if away:
        carry = jnp.zeros((1, 1, 8, LANES), jnp.float32)
        carry_block = pl.BlockSpec((1, 1, 8, LANES), lambda g, j, m: (0, 0, 0, 0))
    else:
        carry_block = acc_block
    whole_q = pl.BlockSpec((rows, 2 * LANES), lambda g, j, m: (0, g))
    return pl.pallas_call(
        functools.partial(attend_back_kernel, not away),
        grid_spec=pltpu.PrefetchScalarGridSpec(
            num_scalar_prefetch=1,
            grid=(groups, key_tiles),
            in_specs=[
                carry_block,
                pl.BlockSpec(memory_space=pl.ANY),
                pl.BlockSpec(memory_space=pl.ANY),
                whole_q,
                pl.BlockSpec((1, tile, LANES), lambda g, j, m: (g, skip + j, 0)),
                pl.BlockSpec((1, tile, LANES), lambda g, j, m: (groups + g, skip + j, 0)),
                whole_q,
                whole_q,
                pl.BlockSpec((1, query_tiles, 1, 2 * tile), lambda g, j, m: (g, 0, 0, 0)),
                pl.BlockSpec((rows, LANES), lambda g, j, m: (0, 0)),
                pl.BlockSpec((rows, LANES), lambda g, j, m: (0, 0)),
            ],
            out_specs=[
                acc_block if away else whole_q,
                pl.BlockSpec((1, 2, tile, LANES), lambda g, j, m: (g, 0, j, 0)),
            ],
            scratch_shapes=[
                pltpu.VMEM((query_tiles, 1, 2 * tile), jnp.float32),
                pltpu.VMEM((query_tiles, LANES, 2 * tile), jnp.float32),
                pltpu.VMEM((tile, LANES), jnp.float32),
                pltpu.VMEM((tile, LANES), jnp.float32),
            ],
        ),
        out_shape=[
            acc_shape if away else jax.ShapeDtypeStruct((rows, q_width), jnp.bfloat16),
            jax.ShapeDtypeStruct((groups, 2, keys, LANES), jnp.bfloat16),
        ],
        compiler_params=pltpu.CompilerParams(vmem_limit_bytes=VMEM_BYTES),
        cost_estimate=pl.CostEstimate(
            flops=20 * rows * keys * LANES * groups * 2, bytes_accessed=8_000_000, transcendentals=0
        ),
        name="attend_back_away" if away else "attend_back_own",
    )(meta, carry, first, second, q, kv, kv, o, d_out, lse, cosine, sine)


def middle_back_kernel(
    x_ref,
    project_ref,
    feed_ref,
    cot_ref,
    gain_ref,
    o_ref,
    wp_ref,
    grad_ref,
    d_out_ref,
    wp_grad_ref,
    gain_grad_ref,
    acc_ref,
):
    step = pl.program_id(0)
    last = pl.num_programs(0) - 1
    bf16, f32 = jnp.bfloat16, jnp.float32

    @pl.when(step == 0)
    def _():
        acc_ref[...] = jnp.zeros_like(acc_ref)
        gain_grad_ref[...] = jnp.zeros_like(gain_grad_ref)

    middle = x_ref[...].astype(f32) + project_ref[...].astype(f32)
    factor = lax.rsqrt(jnp.mean(middle * middle, axis=-1, keepdims=True) + EPSILON)
    feed_in = feed_ref[...].astype(f32)
    gain_grad_ref[...] += jnp.sum(feed_in * middle * factor, axis=0, keepdims=True)
    scaled = gain_ref[1:2, :].astype(f32) * feed_in
    grad = (
        cot_ref[...].astype(f32)
        + factor * scaled
        - middle * (factor * factor * factor * jnp.mean(scaled * middle, axis=-1, keepdims=True))
    )
    grad_ref[...] = grad
    low = grad.astype(bf16)
    d_out_ref[...] = dot(low, wp_ref[...], ((1,), (1,))).astype(bf16)
    acc_ref[...] += dot(o_ref[...], low, ((0,), (0,)))

    @pl.when(step == last)
    def _():
        for head in range(acc_ref.shape[0] // LANES):
            wp_grad_ref[head * HD : (head + 1) * HD, :] = acc_ref[
                head * LANES : head * LANES + HD, :
            ].astype(bf16)


def middle_back(x, project_sum, feed_sum, cot, gains, o, w_p):
    rows, width = x.shape
    tile = 256
    heads = o.shape[1] // LANES
    bf16, f32 = jnp.bfloat16, jnp.float32

    def rows_of(columns):
        return pl.BlockSpec((tile, columns), lambda i: (i, 0))

    def whole(array):
        return pl.BlockSpec(array.shape, lambda i: (0, 0))

    return pl.pallas_call(
        middle_back_kernel,
        grid=(rows // tile,),
        in_specs=[
            rows_of(width),
            rows_of(width),
            rows_of(width),
            rows_of(width),
            whole(gains),
            rows_of(o.shape[1]),
            whole(w_p),
        ],
        out_specs=[
            rows_of(width),
            rows_of(o.shape[1]),
            pl.BlockSpec((heads * HD, width), lambda i: (0, 0)),
            pl.BlockSpec((1, width), lambda i: (0, 0)),
        ],
        out_shape=[
            jax.ShapeDtypeStruct((rows, width), f32),
            jax.ShapeDtypeStruct(o.shape, bf16),
            jax.ShapeDtypeStruct((heads * HD, width), bf16),
            jax.ShapeDtypeStruct((1, width), f32),
        ],
        scratch_shapes=[pltpu.VMEM((o.shape[1], width), f32)],
        compiler_params=pltpu.CompilerParams(vmem_limit_bytes=VMEM_BYTES),
        cost_estimate=pl.CostEstimate(
            flops=5_000_000_000, bytes_accessed=26_000_000, transcendentals=0
        ),
        name="middle_back",
    )(x, project_sum, feed_sum, cot, gains, o, w_p)


def tail_kernel(
    down_hbm,
    gate_hbm,
    gate_away_hbm,
    gate_rest_hbm,
    up_hbm,
    up_away_hbm,
    q_low_ref,
    own_ref,
    away_ref,
    normed_hbm,
    wide_hbm,
    x_hbm,
    grad_hbm,
    gain_term_ref,
    gain_ref,
    project_ref,
    spread_ref,
    cos_ref,
    sin_ref,
    out_hbm,
    share_ref,
    project_share_ref,
    gate_share_ref,
    up_share_ref,
    gain_share_ref,
    down_away_hbm,
    normed_ref,
    wide_ref,
    x_ref,
    grad_ref,
    gate_ref,
    gate_away_ref,
    upw_ref,
    upw_away_ref,
    low_ref,
    close_ref,
    part_ref,
    x_in_ref,
    up_ref,
    down_ref,
    p_in_ref,
    p_up_ref,
    p_down_ref,
    g_up_ref,
    g_down_ref,
    u_up_ref,
    u_down_ref,
    give_ref,
    core_in_ref,
    chip_in_ref,
    total_ref,
    gain_sum_ref,
    gain_x_ref,
    gain_z_ref,
    x_send,
    x_recv,
    up_send,
    up_recv,
    down_send,
    down_recv,
    p_up_send,
    p_up_recv,
    p_down_send,
    p_down_recv,
    g_up_send,
    g_up_recv,
    g_down_send,
    g_down_recv,
    u_up_send,
    u_up_recv,
    u_down_send,
    u_down_recv,
    core_send,
    core_recv,
    chip_send,
    chip_recv,
    back_send,
    back_recv,
    last_send,
    last_recv,
    gain_send,
    gain_recv,
    load_sem,
):
    bf16, f32 = jnp.bfloat16, jnp.float32
    planes = part_ref.shape[1]
    rows, width = x_ref.shape
    depth = width // planes
    sent_rows = gate_away_hbm.shape[0]
    loads = [
        pltpu.make_async_copy(src, dst, load_sem.at[i])
        for i, (src, dst) in enumerate(
            (
                (gate_hbm, gate_ref),
                (gate_away_hbm, gate_away_ref.at[pl.ds(0, sent_rows)]),
                (gate_rest_hbm, gate_away_ref.at[pl.ds(sent_rows, width - sent_rows)]),
                (up_hbm, upw_ref),
                (up_away_hbm, upw_away_ref),
                (normed_hbm, normed_ref),
                (wide_hbm, wide_ref),
                (x_hbm, x_ref),
                (grad_hbm, grad_ref),
            )
        )
    ]
    for load in loads:
        load.start()
    half_rows = rows // 2
    chunks = give_ref.shape[0]
    chunk = half_rows // chunks
    half_width = low_ref.shape[2]
    z = lax.axis_index("fsdp")
    c = lax.axis_index("ctx")
    t = lax.axis_index("tp")
    core = lax.rem(t, 2)
    across = {"ctx": 1 - c}
    sibling = {"tp": t + 1 - 2 * core}
    partner = {"tp": lax.rem(t + 2, 4)}

    barrier = pltpu.get_barrier_semaphore()
    for device in (across, sibling, partner):
        pl.semaphore_signal(barrier, inc=1, device_id=device, device_id_type=MESH)
    for k in range(1, planes):
        pl.semaphore_signal(
            barrier, inc=1, device_id={"fsdp": lax.rem(z + k, planes)}, device_id_type=MESH
        )
    pl.semaphore_wait(barrier, 3 + planes - 1)

    def remote(src, dst, send, recv, device):
        return pltpu.make_async_remote_copy(
            src_ref=src,
            dst_ref=dst,
            send_sem=send,
            recv_sem=recv,
            device_id=device,
            device_id_type=MESH,
        )

    def plane_rows(d):
        return pl.ds(pl.multiple_of(d * depth, depth), depth)

    def pair_source(mine_ref, away_ref):
        def source(d):
            at = plane_rows(d)
            return (mine_ref[at, :].astype(f32) + away_ref[at, :].astype(f32)).astype(bf16)

        return source

    g_begin, g_relay, g_finish, g_sent = line_sum(
        z, planes, pair_source(gate_ref, gate_away_ref),
        g_up_ref, g_down_ref, g_up_send, g_up_recv, g_down_send, g_down_recv,
    )
    u_begin, u_relay, u_finish, u_sent = line_sum(
        z, planes, pair_source(upw_ref, upw_away_ref),
        u_up_ref, u_down_ref, u_up_send, u_up_recv, u_down_send, u_down_recv,
    )

    project_half = project_ref.shape[0] // 2

    def project_over():
        return remote(
            project_ref.at[pl.ds(project_half, project_half)], p_in_ref,
            last_send.at[2], last_recv.at[2], across,
        )

    def project_source(d):
        at = plane_rows(d)
        return (
            project_ref[0:project_half, at].astype(f32) + p_in_ref[:, at].astype(f32)
        ).astype(bf16)

    p_begin, p_relay, p_finish, p_sent = line_sum(
        z, planes, project_source, p_up_ref, p_down_ref, p_up_send, p_up_recv, p_down_send, p_down_recv
    )
    order = []
    for step in range((planes + 1) // 2):
        order += [planes - 1 - step, step]
    order = order[:planes]
    project_over().start()
    for load in loads[:3]:
        load.wait()
    g_begin(0)
    for load in loads[3:5]:
        load.wait()
    u_begin(0)

    block = 256

    def lower(i, carry):
        at = pl.ds(pl.multiple_of(i * block, block), block)
        for which in range(2):
            low_ref[which, at, : 2 * LANES] = q_low_ref[
                at, which * 2 * LANES : (which + 1) * 2 * LANES
            ]
            key = own_ref[which, 0, at, :].astype(f32) + away_ref[1 - which, 0, at, :].astype(f32)
            key = key * cos_ref[at, :] - pltpu.roll(key, SPAN, 1) * sin_ref[at, :]
            low_ref[which, at, 2 * LANES : 3 * LANES] = key.astype(bf16)
            value = own_ref[which, 1, at, :].astype(f32) + away_ref[1 - which, 1, at, :].astype(f32)
            low_ref[which, at, 3 * LANES :] = value.astype(bf16)
            close_ref[which, at, :] = dot(
                low_ref[which, at, :], spread_ref[...], ((1,), (1,))
            ).astype(bf16)
        return carry

    lax.fori_loop(0, rows // block, lower, 0)

    def weight_part(which, d):
        part_ref[which, d] = dot(
            normed_ref[:, d * depth : (d + 1) * depth], close_ref[which], ((0,), (0,))
        ).astype(bf16)

    def to_neighbour(d):
        return remote(part_ref.at[1, d], x_in_ref.at[d], x_send.at[d], x_recv.at[d], across)

    loads[5].wait()
    for d in order:
        weight_part(1, d)
        to_neighbour(d).start()

    def feature_rows(start):
        at = pl.ds(pl.multiple_of(start, chunk), chunk)
        return dot(low_ref[0, at, :], wide_ref[:, :half_width], ((1,), (1,))) + dot(
            low_ref[1, at, :], wide_ref[:, half_width:], ((1,), (1,))
        )

    loads[6].wait()
    give_start = (1 - core) * half_rows
    keep_start = core * half_rows

    def to_core(i):
        return remote(give_ref.at[i], core_in_ref.at[i], core_send.at[i], core_recv.at[i], sibling)

    def to_chip(i):
        return remote(total_ref.at[keep_at(i)], chip_in_ref.at[i], chip_send.at[i], chip_recv.at[i], partner)

    def keep_at(i):
        return pl.ds(pl.multiple_of(keep_start + i * chunk, chunk), chunk)

    def give_at(i):
        return pl.ds(pl.multiple_of(give_start + i * chunk, chunk), chunk)

    def back(i):
        return remote(
            total_ref.at[keep_at(i)],
            total_ref.at[keep_at(i)],
            back_send.at[i],
            back_recv.at[i],
            sibling,
        )

    def from_core(i):
        return remote(
            total_ref.at[give_at(i)],
            total_ref.at[give_at(i)],
            back_send.at[i],
            back_recv.at[i],
            sibling,
        )

    for i in range(chunks):
        give_ref[i] = feature_rows(give_start + i * chunk).astype(bf16)
        to_core(i).start()
    for i in range(chunks):
        kept = feature_rows(keep_start + i * chunk)
        to_core(i).wait_recv()
        total_ref[keep_at(i)] = (kept + core_in_ref[i].astype(f32)).astype(bf16)
        to_chip(i).start()

    g_begin(1)
    g_relay(0)
    u_begin(1)
    u_relay(0)
    for d in order:
        weight_part(0, d)

    def add_neighbour(d):
        to_neighbour(d).wait_recv()
        part_ref[0, d] = (part_ref[0, d].astype(f32) + x_in_ref[d].astype(f32)).astype(bf16)

    q_begin, q_relay, q_finish, q_sent = line_sum(
        z, planes, lambda d: part_ref[0, pl.ds(d, 1)][0], up_ref, down_ref, up_send, up_recv, down_send, down_recv
    )

    def finish_chunk(i):
        to_chip(i).wait()
        total_ref[keep_at(i)] = (
            total_ref[keep_at(i)].astype(f32) + chip_in_ref[i].astype(f32)
        ).astype(bf16)
        back(i).start()

    def last_share():
        return remote(
            share_ref.at[0], share_ref.at[1], last_send.at[0], last_recv.at[0], across
        )

    def last_project():
        return remote(
            project_share_ref.at[0], project_share_ref.at[1], last_send.at[1], last_recv.at[1], across
        )

    def down_over():
        return remote(down_hbm, down_away_hbm, last_send.at[5], last_recv.at[5], across)

    def last_of(ref, i):
        return remote(ref.at[0], ref.at[1], last_send.at[i], last_recv.at[i], across)

    g_begin(2)
    u_begin(2)
    g_relay(1)
    finish_chunk(0)
    u_relay(1)
    project_over().wait_recv()
    for step in range(planes - 1):
        p_begin(step)
    for d in order:
        add_neighbour(d)
    for step in range(planes - 1):
        q_begin(step)
    down_over().start()
    for load in loads[7:]:
        load.wait()
    gain_sum_ref[...] = jnp.zeros_like(gain_sum_ref)
    gain_sum_ref[1:2, :] = gain_term_ref[...]
    gain = gain_ref[0:1, :].astype(f32)

    def finish_rows(start):
        at = pl.ds(pl.multiple_of(start, chunk), chunk)
        x = x_ref[at, :].astype(f32)
        factor = lax.rsqrt(jnp.mean(x * x, axis=-1, keepdims=True) + EPSILON)
        normed_in = total_ref[at, :].astype(f32)
        gain_sum_ref[0:1, :] += jnp.sum(normed_in * x * factor, axis=0, keepdims=True)
        scaled = gain * normed_in
        x_ref[at, :] = (
            grad_ref[at, :]
            + factor * scaled
            - x * (factor * factor * factor * jnp.mean(scaled * x, axis=-1, keepdims=True))
        ).astype(bf16)

    finish_rows(keep_start)
    for i in range(1, chunks):
        finish_chunk(i)
    g_finish(gate_share_ref.at[0])
    last_of(gate_share_ref, 3).start()
    p_relay(0)
    u_finish(up_share_ref.at[0])
    last_of(up_share_ref, 4).start()
    q_relay(0)
    for i in range(1, chunks):
        finish_rows(keep_start + i * chunk)
    p_relay(1)
    q_relay(1)
    for i in range(chunks):
        from_core(i).wait_recv()
        finish_rows(give_start + i * chunk)
    out_copy = pltpu.make_async_copy(x_ref, out_hbm, load_sem.at[0])
    out_copy.start()

    gain_over = remote(gain_sum_ref, gain_x_ref, gain_send.at[0], gain_recv.at[0], across)
    gain_over.start()
    p_finish(project_share_ref.at[0])
    last_project().start()
    q_finish(share_ref.at[0])
    last_share().start()
    gain_over.wait()
    gain_sum_ref[...] = gain_sum_ref[...] + gain_x_ref[...]

    def gain_to(k):
        plane = lax.rem(z + k, planes)
        return remote(
            gain_sum_ref.at[:, pl.ds(pl.multiple_of(plane * depth, depth), depth)],
            gain_z_ref.at[k],
            gain_send.at[k],
            gain_recv.at[k],
            {"fsdp": plane},
        )

    for k in range(1, planes):
        gain_to(k).start()
    gain_share_ref[...] = gain_sum_ref[:, pl.ds(pl.multiple_of(z * depth, depth), depth)]
    for k in range(1, planes):
        gain_to(k).wait_recv()
        gain_share_ref[...] += gain_z_ref[k]

    last_share().wait()
    last_project().wait()
    last_of(gate_share_ref, 3).wait()
    last_of(up_share_ref, 4).wait()
    project_over().wait_send()
    down_over().wait()
    p_sent()
    g_sent()
    u_sent()
    q_sent()
    out_copy.wait()
    for k in range(1, planes):
        gain_to(k).wait_send()
    for i in range(chunks):
        to_core(i).wait_send()
        back(i).wait_send()
    for d in range(planes):
        to_neighbour(d).wait_send()


def tail(
    down_share, gate, gate_away, gate_rest, upw, up_away, q_low, own, away, normed, wide, x, grad,
    gain_term, gains, project, spread, cosine, sine, planes,
):
    rows, width = x.shape
    depth = width // planes
    half_width = wide.shape[1] // 2
    close_width = spread.shape[0]
    chunks = 2
    chunk = rows // 2 // chunks
    bf16, f32 = jnp.bfloat16, jnp.float32
    vmem = pl.BlockSpec(memory_space=pltpu.VMEM)
    dma = pltpu.SemaphoreType.DMA
    operands = (
        down_share, gate, gate_away, gate_rest, upw, up_away, q_low, own, away, normed, wide, x, grad,
        gain_term, gains, project, spread, cosine, sine,
    )
    units = gate.shape[1]
    unit_line = pltpu.VMEM((planes - 1, depth, units), bf16)
    anywhere = pl.BlockSpec(memory_space=pl.ANY)
    line = pltpu.VMEM((planes, depth, close_width), bf16)
    short_line = pltpu.VMEM((planes - 1, depth, close_width), bf16)
    project_line = pltpu.VMEM((planes - 1, project.shape[0] // 2, depth), bf16)
    return pl.pallas_call(
        tail_kernel,
        in_specs=[anywhere] * 6 + [vmem] * 3 + [anywhere] * 4 + [vmem] * (len(operands) - 13),
        out_specs=[anywhere] + [vmem] * 5 + [anywhere],
        out_shape=[
            jax.ShapeDtypeStruct((rows, width), bf16),
            jax.ShapeDtypeStruct((2, depth, close_width), bf16),
            jax.ShapeDtypeStruct((2, project.shape[0] // 2, depth), bf16),
            jax.ShapeDtypeStruct((2, depth, units), bf16),
            jax.ShapeDtypeStruct((2, depth, units), bf16),
            jax.ShapeDtypeStruct((8, depth), f32),
            jax.ShapeDtypeStruct(down_share.shape, bf16),
        ],
        scratch_shapes=[
            pltpu.VMEM((rows, width), bf16),
            pltpu.VMEM(wide.shape, bf16),
            pltpu.VMEM((rows, width), bf16),
            pltpu.VMEM((rows, width), f32),
            pltpu.VMEM((width, units), bf16),
            pltpu.VMEM((width, units), bf16),
            pltpu.VMEM((width, units), bf16),
            pltpu.VMEM((width, units), bf16),
            pltpu.VMEM((2, rows, half_width), bf16),
            pltpu.VMEM((2, rows, close_width), bf16),
            pltpu.VMEM((2, planes, depth, close_width), bf16),
            line,
            short_line,
            short_line,
            pltpu.VMEM((project.shape[0] // 2, width), bf16),
            project_line,
            project_line,
            unit_line,
            unit_line,
            unit_line,
            unit_line,
            pltpu.VMEM((chunks, chunk, width), bf16),
            pltpu.VMEM((chunks, chunk, width), bf16),
            pltpu.VMEM((chunks, chunk, width), bf16),
            pltpu.VMEM((rows, width), bf16),
            pltpu.VMEM((8, width), f32),
            pltpu.VMEM((8, width), f32),
            pltpu.VMEM((planes, 8, depth), f32),
        ]
        + [dma((planes,))] * 18
        + [dma((chunks,))] * 6
        + [dma((6,))] * 2
        + [dma((planes,))] * 2
        + [dma((9,))],
        compiler_params=pltpu.CompilerParams(
            collective_id=2, has_side_effects=True, vmem_limit_bytes=VMEM_BYTES + (3 << 19)
        ),
        cost_estimate=pl.CostEstimate(
            flops=60_000_000_000, bytes_accessed=24_000_000, transcendentals=0
        ),
        name="tail",
    )(*operands)


def feed_kernel(
    x_hbm,
    project_hbm,
    cot_hbm,
    gain_ref,
    gate_hbm,
    up_hbm,
    down_hbm,
    total_hbm,
    gate_m_hbm,
    gate_away_hbm,
    gate_rest_hbm,
    up_m_hbm,
    up_o_hbm,
    down_grad_hbm,
    down_rows_hbm,
    x_ref,
    project_ref,
    cot_ref,
    gate_ref,
    up_ref,
    down_ref,
    total_ref,
    grad_ref,
    down_grad_ref,
    down_rows_ref,
    gate_o_ref,
    normed_ref,
    turned_ref,
    hidden_ref,
    gate_back_ref,
    up_back_ref,
    give_ref,
    core_in_ref,
    keep_ref,
    chip_in_ref,
    load_sem,
    store_sem,
    core_send,
    core_recv,
    chip_send,
    chip_recv,
    back_send,
    back_recv,
    x_send,
    x_recv,
    over_send,
    over_recv,
):
    bf16, f32 = jnp.bfloat16, jnp.float32
    rows, width = x_ref.shape
    half_rows = rows // 2
    chunks, chunk, _ = give_ref.shape
    units = gate_ref.shape[2]
    c = lax.axis_index("ctx")
    t = lax.axis_index("tp")
    core = lax.rem(t, 2)
    across = {"ctx": 1 - c}
    sibling = {"tp": t + 1 - 2 * core}
    partner = {"tp": lax.rem(t + 2, 4)}

    loads = [
        pltpu.make_async_copy(src, dst, load_sem.at[i])
        for i, (src, dst) in enumerate(
            (
                (x_hbm, x_ref),
                (project_hbm, project_ref),
                (gate_hbm, gate_ref),
                (up_hbm, up_ref),
                (cot_hbm, cot_ref),
                (down_hbm, down_ref),
            )
        )
    ]
    for load in loads:
        load.start()

    barrier = pltpu.get_barrier_semaphore()
    for device in (across, sibling, partner):
        pl.semaphore_signal(barrier, inc=1, device_id=device, device_id_type=MESH)
    pl.semaphore_wait(barrier, 3)

    def remote(src, dst, send, recv, device):
        return pltpu.make_async_remote_copy(
            src_ref=src,
            dst_ref=dst,
            send_sem=send,
            recv_sem=recv,
            device_id=device,
            device_id_type=MESH,
        )

    give_start = (1 - core) * half_rows
    keep_start = core * half_rows
    gain = gain_ref[1:2, :].astype(f32)

    def feature_rows(start, first):
        at = pl.ds(pl.multiple_of(start, chunk), chunk)
        if first:
            loads[0].wait()
            loads[1].wait()
        middle = x_ref[at, :].astype(f32) + project_ref[at, :].astype(f32)
        factor = lax.rsqrt(jnp.mean(middle * middle, axis=-1, keepdims=True) + EPSILON)
        normed = (middle * factor * gain).astype(bf16)
        normed_ref[...] = normed
        turned_ref[:, at] = normed.T
        if first:
            for load in loads[2:]:
                load.wait()
        for which in range(2):
            cols = slice(which * units, (which + 1) * units)
            gate = dot(normed_ref[...], gate_ref[which], ((1,), (0,)))
            up = dot(normed_ref[...], up_ref[which], ((1,), (0,)))
            hidden_in = dot(cot_ref[at, :], down_ref[which], ((1,), (1,)))
            sigmoid = jax.nn.sigmoid(gate)
            silu = gate * sigmoid
            hidden_ref[at, cols] = (silu * up).astype(bf16)
            gate_back_ref[at, cols] = (
                hidden_in * up * sigmoid * (1.0 + gate * (1.0 - sigmoid))
            ).astype(bf16)
            up_back_ref[at, cols] = (hidden_in * silu).astype(bf16)
        return sum(
            dot(back_ref[at, which * units : (which + 1) * units], weight[which], ((1,), (1,)))
            for which in range(2)
            for back_ref, weight in ((gate_back_ref, gate_ref), (up_back_ref, up_ref))
        )

    def to_core(i):
        return remote(give_ref.at[i], core_in_ref.at[i], core_send.at[i], core_recv.at[i], sibling)

    def to_chip(i):
        return remote(keep_ref.at[i], chip_in_ref.at[i], chip_send.at[i], chip_recv.at[i], partner)

    def back(i, start):
        at = pl.ds(pl.multiple_of(start + i * chunk, chunk), chunk)
        return remote(
            total_ref.at[at], total_ref.at[at], back_send.at[i], back_recv.at[i], sibling
        )

    for i in range(chunks):
        give_ref[i] = feature_rows(give_start + i * chunk, i == 0).astype(bf16)
        to_core(i).start()
        kept = feature_rows(keep_start + i * chunk, False)
        to_core(i).wait_recv()
        keep_ref[i] = (kept + core_in_ref[i].astype(f32)).astype(bf16)
        to_chip(i).start()

    block = 256

    def weight_rows(back_ref, which, out_ref, begin, count, block=256):
        def some(i, carry):
            at = pl.ds(pl.multiple_of(i * block, block), block)
            out_ref[at, :] = dot(
                turned_ref[at, :], back_ref[:, which * units : (which + 1) * units], ((1,), (0,))
            ).astype(bf16)
            return carry

        lax.fori_loop(begin // block, (begin + count) // block, some, 0)

    def finish_chunk(i):
        to_chip(i).wait()
        at = pl.ds(pl.multiple_of(keep_start + i * chunk, chunk), chunk)
        total_ref[at, :] = (keep_ref[i].astype(f32) + chip_in_ref[i].astype(f32)).astype(bf16)
        back(i, keep_start).start()

    planes, _, depth = down_grad_ref.shape
    pieces = gate_away_hbm.shape[0] // depth

    def over(i):
        at = pl.ds(i * depth, depth)
        return remote(gate_o_ref.at[at], gate_away_hbm.at[at], x_send.at[i], x_recv.at[i], across)

    def down_over(i):
        at = pl.ds(pl.multiple_of(give_start + i * chunk, chunk), chunk)
        return remote(
            down_rows_ref.at[at], core_in_ref.at[i], over_send.at[i], over_recv.at[i], sibling
        )

    stores = []

    def store(src, dst):
        copy = pltpu.make_async_copy(src, dst, store_sem.at[len(stores)])
        copy.start()
        stores.append(copy)

    for i in range(pieces):
        weight_rows(gate_back_ref, 1, gate_o_ref, i * depth, depth, depth)
        over(i).start()
    weight_rows(gate_back_ref, 1, gate_o_ref, pieces * depth, width - pieces * depth, depth)
    store(gate_o_ref.at[pl.ds(pieces * depth, width - pieces * depth)], gate_rest_hbm)
    weight_rows(up_back_ref, 1, grad_ref.at[0], 0, width)
    store(grad_ref.at[0], up_o_hbm)
    for i in range(chunks // 2):
        finish_chunk(i)
    weight_rows(gate_back_ref, 0, grad_ref.at[1], 0, width)
    store(grad_ref.at[1], gate_m_hbm)
    weight_rows(up_back_ref, 0, grad_ref.at[2], 0, width)
    store(grad_ref.at[2], up_m_hbm)

    def down_grads(i, carry):
        at = pl.ds(pl.multiple_of(i * block, block), block)
        part = dot(hidden_ref[:, at], cot_ref[...], ((0,), (0,))).astype(bf16)
        planes, _, depth = down_grad_ref.shape
        for d in range(planes):
            down_grad_ref[d, at, :] = part[:, d * depth : (d + 1) * depth]
        return carry

    lax.fori_loop(0, 2 * units // block, down_grads, 0)
    store(down_grad_ref, down_grad_hbm)

    def down_features(i, carry):
        at = pl.ds(pl.multiple_of(i * block, block), block)
        down_rows_ref[at, :] = (
            dot(hidden_ref[at, :units], down_ref[0], ((1,), (0,)))
            + dot(hidden_ref[at, units:], down_ref[1], ((1,), (0,)))
        ).astype(bf16)
        return carry

    lax.fori_loop(0, rows // block, down_features, 0)
    for i in range(chunks // 2):
        back(i, give_start).wait_recv()
    for i in range(chunks):
        down_over(i).start()
    for i in range(chunks):
        to_core(i).wait_send()
        down_over(i).wait()
        at = pl.ds(pl.multiple_of(keep_start + i * chunk, chunk), chunk)
        give_ref[i] = (down_rows_ref[at, :].astype(f32) + core_in_ref[i].astype(f32)).astype(bf16)
    store(give_ref, down_rows_hbm)
    for i in range(chunks // 2, chunks):
        finish_chunk(i)
    for i in range(chunks // 2, chunks):
        back(i, give_start).wait_recv()
    store(total_ref, total_hbm)
    for i in range(chunks):
        back(i, keep_start).wait_send()
    for i in range(pieces):
        over(i).wait()
    for copy in stores:
        copy.wait()


def feed(x, project_sum, cot, gains, gate_w, up_w, down_w, planes):
    rows, width = x.shape
    units = gate_w.shape[2]
    chunk = 256
    chunks = rows // 2 // chunk
    depth = width // planes
    sent = 3 * depth
    bf16 = jnp.bfloat16
    vmem = pl.BlockSpec(memory_space=pltpu.VMEM)
    anywhere = pl.BlockSpec(memory_space=pl.ANY)
    dma = pltpu.SemaphoreType.DMA
    operands = (x, project_sum, cot, gains, gate_w, up_w, down_w)
    piece = pltpu.VMEM((chunks, chunk, width), bf16)
    rows_by_width = pltpu.VMEM((rows, width), bf16)
    rows_by_units = pltpu.VMEM((rows, 2 * units), bf16)
    weight = jax.ShapeDtypeStruct((width, units), bf16)
    return pl.pallas_call(
        feed_kernel,
        in_specs=[anywhere] * 3 + [vmem] + [anywhere] * 3,
        out_specs=[anywhere] * 8,
        out_shape=[
            jax.ShapeDtypeStruct((rows, width), bf16),
            weight,
            jax.ShapeDtypeStruct((sent, units), bf16),
            jax.ShapeDtypeStruct((width - sent, units), bf16),
            weight,
            weight,
            jax.ShapeDtypeStruct((planes, 2 * units, width // planes), bf16),
            jax.ShapeDtypeStruct((chunks, chunk, width), bf16),
        ],
        scratch_shapes=[
            rows_by_width,
            rows_by_width,
            rows_by_width,
            pltpu.VMEM(gate_w.shape, bf16),
            pltpu.VMEM(up_w.shape, bf16),
            pltpu.VMEM(down_w.shape, bf16),
            rows_by_width,
            pltpu.VMEM((3, width, units), bf16),
            pltpu.VMEM((planes, 2 * units, width // planes), bf16),
            rows_by_width,
            pltpu.VMEM((width, units), bf16),
            pltpu.VMEM((chunk, width), bf16),
            pltpu.VMEM((width, rows), bf16),
            rows_by_units,
            rows_by_units,
            rows_by_units,
            piece,
            piece,
            piece,
            piece,
            dma((6,)),
            dma((7,)),
        ]
        + [dma((chunks,))] * 6
        + [dma((sent // depth,))] * 2
        + [dma((chunks,))] * 2,
        compiler_params=pltpu.CompilerParams(
            collective_id=3, has_side_effects=True, vmem_limit_bytes=VMEM_BYTES
        ),
        cost_estimate=pl.CostEstimate(
            flops=50_000_000_000, bytes_accessed=40_000_000, transcendentals=0
        ),
        name="feed",
    )(*operands)


def add_kernel(first_ref, a_ref, b_ref, out_ref):
    out_ref[...] = (a_ref[...].astype(jnp.float32) + b_ref[...].astype(jnp.float32)).astype(
        out_ref.dtype
    )


def add_after(first, a, b):
    rows, width = a.shape
    tile = 256
    spec = pl.BlockSpec((tile, width), lambda i: (i, 0))
    return pl.pallas_call(
        add_kernel,
        grid=(rows // tile,),
        in_specs=[pl.BlockSpec(memory_space=pl.ANY), spec, spec],
        out_specs=spec,
        out_shape=jax.ShapeDtypeStruct(a.shape, a.dtype),
        name="add_after",
    )(first, a, b)


def paired_body(
    tokens,
    prefix_len,
    positions,
    gain_attend,
    w_query,
    w_key,
    w_value,
    w_project,
    gain_feed,
    w_gate,
    w_up,
    w_down,
    cotangent,
):
    seqs, rows, width = tokens.shape
    assert seqs == 1
    c = lax.axis_index("ctx")
    bf16, f32 = jnp.bfloat16, jnp.float32

    def half(array, axis, which=None):
        size = array.shape[axis] // 2
        which = c if which is None else which
        return lax.dynamic_slice_in_dim(array, which * size, size, axis)

    def ordered(mine, other, axis):
        return jnp.where(
            c == 0,
            jnp.concatenate([mine, other], axis=axis),
            jnp.concatenate([other, mine], axis=axis),
        )

    planes = lax.axis_size("fsdp")
    kv_half = w_key.shape[1] // 2
    q_half = w_query.shape[1] // 2

    def packed(which):
        return jnp.concatenate(
            [half(w_query, 1, which), half(w_key, 1, which), half(w_value, 1, which)], axis=1
        )

    gain_rows = jnp.pad(jnp.stack([gain_attend, gain_feed]), ((0, GAIN_ROWS - 2), (0, 0)))
    pack = jnp.concatenate([packed(c), gain_rows], axis=0)

    def parts(block):
        return (
            block[:, :q_half],
            block[:, q_half : q_half + kv_half],
            block[:, q_half + kv_half :],
        )

    half_heads = (q_half + 2 * kv_half) // HD
    spread = np.zeros((half_heads * HD, half_heads * LANES), np.float32)
    for head in range(half_heads):
        for lane in range(HD):
            turned = lane if lane < HALF or head == half_heads - 1 else lane - HALF + SPAN
            spread[head * HD + lane, head * LANES + turned] = 1.0
    spread = jnp.asarray(spread, bf16)

    frequency = ROPE_BASE ** (-(jnp.arange(HALF, dtype=f32) * 2.0 / HD))
    frequency = jnp.pad(frequency, (0, SPAN - HALF))
    angles = positions[0].astype(f32)[:, None] * frequency
    cosine = jnp.cos(angles)
    sine = jnp.sin(angles)
    cosine = jnp.concatenate([cosine, cosine], axis=1)
    sine = jnp.concatenate([-sine, sine], axis=1)

    block_len = rows // 2
    tile = min(256, block_len)
    query_tiles = rows // tile
    own = c * rows + tile * jnp.arange(query_tiles, dtype=jnp.int32)
    opposite = (1 - c) * rows + tile * jnp.arange(query_tiles, dtype=jnp.int32)
    own, opposite = natural_index(own, block_len, 2), natural_index(opposite, block_len, 2)
    meta = jnp.concatenate([prefix_len.astype(jnp.int32), own, own, opposite])

    x = tokens[0]
    cot = cotangent[0]
    (
        normed, q, kv_all, w_qkv, w_p, gains, o, lse, project_sum, wg, wu, wd,
    ) = front(
        prefix_len, x, pack, packed(1 - c), spread, cosine, sine,
        w_project.reshape(-1, HD, w_project.shape[1]), w_gate, w_up, w_down, planes,
    )
    w_p = w_p.reshape(-1, width)
    (
        feed_sum, gate_mine, gate_away, gate_rest, up_mine, up_other, down_part, down_rows,
    ) = feed(x, project_sum, cot, gains, wg, wu, wd, planes)

    gate_rest, up_away = swap_ctx(gate_rest), swap_ctx(up_other)
    down_share = lax.psum_scatter(down_part, "fsdp", scatter_dimension=0, tiled=False)
    middle_grad, d_out, project_part, gain_two_term = middle_back(
        x, project_sum, feed_sum, cot, gains, o, w_p
    )
    down_rows = down_rows.reshape(rows // 2, width)
    down_away = swap_chip(down_rows)
    dq_away, d_kv_away = attend_back(
        meta, None, d_out, d_out, q, kv_all, True, o, d_out, lse, cosine, sine, tile
    )
    d_kv_away = swap_ctx(d_kv_away)
    down_total = add_after(dq_away, down_rows, down_away)
    down_sum = by_core(down_total, swap_core(down_total))
    layer_output = (
        x.astype(f32) + project_sum.astype(f32) + down_sum.astype(f32)
    ).astype(bf16)
    q_low, d_kv_own = attend_back(
        meta, dq_away, gate_rest, up_away, q, kv_all, False, o, d_out, lse, cosine, sine, tile
    )
    tokens_grad, share, project_share, gate_share, up_share, gain_share, down_other_share = tail(
        down_share, gate_mine, gate_away, gate_rest, up_mine, up_away, q_low, d_kv_own, d_kv_away, normed, w_qkv, x, middle_grad,
        gain_two_term, gains, project_part, spread, cosine, sine, planes,
    )
    size = down_share.shape[0] // 2
    down_mine = down_share[:size].astype(f32) + down_other_share[size:].astype(f32)
    down_other = down_share[size:].astype(f32) + down_other_share[:size].astype(f32)
    down_grad = ordered(down_mine, down_other, 0)
    shares = [
        ordered(a, b, 1).astype(f32) for a, b in zip(parts(share[0]), parts(share[1]))
    ]
    return (
        layer_output[None],
        tokens_grad[None],
        gain_share[0],
        shares[0],
        shares[1],
        shares[2],
        ordered(project_share[0], project_share[1], 0).astype(f32),
        gain_share[1],
        ordered(gate_share[0], gate_share[1], 1).astype(f32),
        ordered(up_share[0], up_share[1], 1).astype(f32),
        down_grad,
    )


def solution(mesh):
    paired = mesh.shape["ctx"] == 2 and mesh.shape["tp"] == 4 and mesh.shape["fsdp"] == 4
    return jax.shard_map(
        paired_body if paired else general_body,
        mesh=mesh,
        in_specs=(
            P("fsdp", "ctx", None),
            P("fsdp"),
            P("fsdp", "ctx"),
            P("fsdp"),
            P("fsdp", "tp"),
            P("fsdp", "tp"),
            P("fsdp", "tp"),
            P("tp", "fsdp"),
            P("fsdp"),
            P("fsdp", "tp"),
            P("fsdp", "tp"),
            P("tp", "fsdp"),
            P("fsdp", "ctx", None),
        ),
        out_specs=(
            P("fsdp", "ctx", None),
            P("fsdp", "ctx", None),
            P("fsdp"),
            P("fsdp", "tp"),
            P("fsdp", "tp"),
            P("fsdp", "tp"),
            P("tp", "fsdp"),
            P("fsdp"),
            P("fsdp", "tp"),
            P("fsdp", "tp"),
            P("tp", "fsdp"),
        ),
        check_vma=False,
    )
```

```python
import functools
import math

import jax
import jax.numpy as jnp
import numpy as np
from jax import lax
from jax.experimental import pallas as pl
from jax.experimental.pallas import tpu as pltpu
from jax.sharding import PartitionSpec as P

HQ = 16
KVH = 8
HD = 96


EPSILON = 1e-05
ROPE_BASE = 100000.0
NEGATIVE = -1e30


def natural_index(stored, block_len, pair_count):
    device = stored // (2 * block_len)
    second_half = stored // block_len % 2
    within = stored % block_len
    block_id = jnp.where(second_half == 0, device, 2 * pair_count - 1 - device)
    return block_id * block_len + within


def rotate(values, cosine_table, sine_table):
    half_width = values.shape[-1] // 2
    leading = values[..., :half_width]
    trailing = values[..., half_width:]
    return jnp.concatenate(
        [
            leading * cosine_table - trailing * sine_table,
            trailing * cosine_table + leading * sine_table,
        ],
        axis=-1,
    )


def rotate_back(incoming, cosine_table, sine_table):
    half_width = incoming.shape[-1] // 2
    leading = incoming[..., :half_width]
    trailing = incoming[..., half_width:]
    return jnp.concatenate(
        [
            leading * cosine_table + trailing * sine_table,
            trailing * cosine_table - leading * sine_table,
        ],
        axis=-1,
    )


def rms_factor(values):
    return lax.rsqrt(jnp.mean(values * values, axis=-1, keepdims=True) + EPSILON)


def rms_back(values, factor, gain_row, incoming):
    scaled = gain_row * incoming
    return factor * scaled - values * factor**3 * jnp.mean(scaled * values, axis=-1, keepdims=True)


def tensor_sum(term_rows):
    return lax.psum(term_rows.astype(jnp.bfloat16), "tp").astype(jnp.float32)


def general_body(
    tokens,
    prefix_len,
    positions,
    gain_attend,
    w_query,
    w_key,
    w_value,
    w_project,
    gain_feed,
    w_gate,
    w_up,
    w_down,
    cotangent,
):
    (
        gain_one,
        query_weight_whole,
        key_weight_whole,
        value_weight_whole,
        project_weight_whole,
        gain_two,
        gate_weight_whole,
        up_weight_whole,
        down_weight_whole,
    ) = (
        lax.all_gather(gain_attend, "fsdp", axis=0, tiled=True),
        lax.all_gather(w_query, "fsdp", axis=0, tiled=True),
        lax.all_gather(w_key, "fsdp", axis=0, tiled=True),
        lax.all_gather(w_value, "fsdp", axis=0, tiled=True),
        lax.all_gather(w_project, "fsdp", axis=1, tiled=True),
        lax.all_gather(gain_feed, "fsdp", axis=0, tiled=True),
        lax.all_gather(w_gate, "fsdp", axis=0, tiled=True),
        lax.all_gather(w_up, "fsdp", axis=0, tiled=True),
        lax.all_gather(w_down, "fsdp", axis=1, tiled=True),
    )
    seq_count, rows_local, _ = tokens.shape
    pair_count = lax.axis_size("ctx")
    block_len = rows_local // 2
    query_width = query_weight_whole.shape[1]
    kv_width = key_weight_whole.shape[1]
    query_heads = query_width // HD
    kv_heads = kv_width // HD
    group_size = HQ // KVH
    score_scale = HD ** (-0.5)
    frequency = ROPE_BASE ** (-(jnp.arange(HD // 2, dtype=jnp.float32) * 2.0 / HD))
    angles = positions.astype(jnp.float32)[:, :, None] * frequency
    cosine_table = jnp.cos(angles)[:, :, None, :]
    sine_table = jnp.sin(angles)[:, :, None, :]
    stored_rows = lax.axis_index("ctx") * rows_local + jnp.arange(rows_local, dtype=jnp.int32)
    query_order = natural_index(stored_rows, block_len, pair_count)

    def visible_mask(key_order):
        causal = key_order[None, None, :] <= query_order[None, :, None]
        opened = key_order[None, None, :] < prefix_len[:, None, None]
        return (causal | opened)[:, :, None, None, :]

    inputs = tokens.astype(jnp.float32)
    factor_one = rms_factor(inputs)
    normed_hidden = (inputs * factor_one * gain_one.astype(jnp.float32)).astype(jnp.bfloat16)
    query_projected = jnp.einsum(
        "rxc,cf->rxf", normed_hidden, query_weight_whole, preferred_element_type=jnp.float32
    )
    key_projected = jnp.einsum(
        "rxc,cf->rxf", normed_hidden, key_weight_whole, preferred_element_type=jnp.float32
    )
    value_projected = jnp.einsum(
        "rxc,cf->rxf", normed_hidden, value_weight_whole, preferred_element_type=jnp.float32
    )
    queries = (
        rotate(
            query_projected.reshape(seq_count, rows_local, query_heads, HD),
            cosine_table,
            sine_table,
        )
        .astype(jnp.bfloat16)
        .reshape(seq_count, rows_local, kv_heads, group_size, HD)
    )
    keys_rot = (
        rotate(key_projected.reshape(seq_count, rows_local, kv_heads, HD), cosine_table, sine_table)
        .astype(jnp.bfloat16)
        .reshape(seq_count, rows_local, kv_width)
    )
    values_low = value_projected.astype(jnp.bfloat16)
    stat_shape = (seq_count, rows_local, kv_heads, group_size)
    initial = (
        jnp.full(stat_shape, NEGATIVE, jnp.float32),
        jnp.zeros(stat_shape, jnp.float32),
        jnp.zeros(stat_shape + (HD,), jnp.float32),
    )
    key_piece = lax.all_gather(keys_rot, "ctx", axis=1, tiled=True)
    value_piece = lax.all_gather(values_low, "ctx", axis=1, tiled=True)
    key_total = key_piece.shape[1]
    span_rows = math.gcd(key_total, rows_local)

    def one_span(span_index, running):
        run_max, run_sum, run_acc = running
        span_start = span_index * span_rows
        key_rows = lax.dynamic_slice_in_dim(key_piece, span_start, span_rows, 1).reshape(
            seq_count, span_rows, kv_heads, HD
        )
        value_rows = lax.dynamic_slice_in_dim(value_piece, span_start, span_rows, 1).reshape(
            seq_count, span_rows, kv_heads, HD
        )
        key_order = natural_index(
            span_start + jnp.arange(span_rows, dtype=jnp.int32), block_len, pair_count
        )
        visible = visible_mask(key_order)
        scores = (
            jnp.einsum("slhgd,skhd->slhgk", queries, key_rows, preferred_element_type=jnp.float32)
            * score_scale
        )
        new_max = jnp.maximum(run_max, jnp.max(jnp.where(visible, scores, NEGATIVE), axis=-1))
        weights_raw = jnp.where(visible, jnp.exp(scores - new_max[..., None]), 0.0)
        rescale = jnp.exp(run_max - new_max)
        run_sum = run_sum * rescale + jnp.sum(weights_raw, axis=-1)
        run_acc = run_acc * rescale[..., None] + jnp.einsum(
            "slhgk,skhd->slhgd",
            weights_raw.astype(jnp.bfloat16),
            value_rows,
            preferred_element_type=jnp.float32,
        )
        return (new_max, run_sum, run_acc)

    run_max, run_sum, run_acc = lax.fori_loop(0, key_total // span_rows, one_span, initial)
    attended = run_acc / run_sum[..., None]
    log_total = run_max + jnp.log(run_sum)
    attended_reduced = attended.reshape(seq_count, rows_local, query_width).astype(jnp.bfloat16)
    project_rows = jnp.einsum(
        "hxz,zm->hxm", attended_reduced, project_weight_whole, preferred_element_type=jnp.float32
    )
    middle = inputs + tensor_sum(project_rows)
    factor_two = rms_factor(middle)
    normed_feed_input = (middle * factor_two * gain_two.astype(jnp.float32)).astype(jnp.bfloat16)
    gate_activation = jnp.einsum(
        "qeh,hj->qej", normed_feed_input, gate_weight_whole, preferred_element_type=jnp.float32
    )
    up_activation = jnp.einsum(
        "qeh,hj->qej", normed_feed_input, up_weight_whole, preferred_element_type=jnp.float32
    )
    sigmoid_gate = jax.nn.sigmoid(gate_activation)
    silu_gate = gate_activation * sigmoid_gate
    hidden_state = (silu_gate * up_activation).astype(jnp.bfloat16)
    down_output_rows = jnp.einsum(
        "nct,tm->ncm", hidden_state, down_weight_whole, preferred_element_type=jnp.float32
    )
    layer_output = (middle + tensor_sum(down_output_rows)).astype(jnp.bfloat16)
    (
        gain_one,
        query_weight_whole,
        key_weight_whole,
        value_weight_whole,
        project_weight_whole,
        gain_two,
        gate_weight_whole,
        up_weight_whole,
        down_weight_whole,
    ) = (
        lax.all_gather(gain_attend, "fsdp", axis=0, tiled=True),
        lax.all_gather(w_query, "fsdp", axis=0, tiled=True),
        lax.all_gather(w_key, "fsdp", axis=0, tiled=True),
        lax.all_gather(w_value, "fsdp", axis=0, tiled=True),
        lax.all_gather(w_project, "fsdp", axis=1, tiled=True),
        lax.all_gather(gain_feed, "fsdp", axis=0, tiled=True),
        lax.all_gather(w_gate, "fsdp", axis=0, tiled=True),
        lax.all_gather(w_up, "fsdp", axis=0, tiled=True),
        lax.all_gather(w_down, "fsdp", axis=1, tiled=True),
    )
    hidden_grad = jnp.einsum(
        "ehv,iv->ehi", cotangent, down_weight_whole, preferred_element_type=jnp.float32
    )
    down_weight_part = jnp.einsum(
        "gqa,gqz->az", hidden_state, cotangent, preferred_element_type=jnp.float32
    )
    gate_reduced = (
        hidden_grad * up_activation * sigmoid_gate * (1.0 + gate_activation * (1.0 - sigmoid_gate))
    ).astype(jnp.bfloat16)
    up_reduced = (hidden_grad * silu_gate).astype(jnp.bfloat16)
    gate_weight_part = jnp.einsum(
        "bic,big->cg", normed_feed_input, gate_reduced, preferred_element_type=jnp.float32
    )
    up_weight_part = jnp.einsum(
        "bic,big->cg", normed_feed_input, up_reduced, preferred_element_type=jnp.float32
    )
    feed_rows = jnp.einsum(
        "vte,ce->vtc", gate_reduced, gate_weight_whole, preferred_element_type=jnp.float32
    ) + jnp.einsum("vte,ce->vtc", up_reduced, up_weight_whole, preferred_element_type=jnp.float32)
    feed_in = tensor_sum(feed_rows)
    gain_two_term = jnp.sum(feed_in * middle * factor_two, axis=(0, 1))
    middle_grad = cotangent.astype(jnp.float32) + rms_back(
        middle, factor_two, gain_two.astype(jnp.float32), feed_in
    )
    middle_reduced = middle_grad.astype(jnp.bfloat16)
    project_term = jnp.einsum(
        "xeh,xec->hc", attended_reduced, middle_reduced, preferred_element_type=jnp.float32
    )
    attended_grad = (
        jnp.einsum(
            "vhk,nk->vhn", middle_reduced, project_weight_whole, preferred_element_type=jnp.float32
        )
        .astype(jnp.bfloat16)
        .reshape(seq_count, rows_local, kv_heads, group_size, HD)
    )
    row_delta = jnp.sum(attended_grad.astype(jnp.float32) * attended, axis=-1)
    whole_keys, whole_values = (
        lax.all_gather(keys_rot[None], "ctx", axis=0, tiled=True),
        lax.all_gather(values_low[None], "ctx", axis=0, tiled=True),
    )

    def key_block(grad_acc, block_items):
        key_rows, value_rows, block_index = block_items
        key_rows = key_rows.reshape(seq_count, rows_local, kv_heads, HD)
        value_rows = value_rows.reshape(seq_count, rows_local, kv_heads, HD)
        key_order = natural_index(
            block_index * rows_local + jnp.arange(rows_local, dtype=jnp.int32),
            block_len,
            pair_count,
        )
        visible = visible_mask(key_order)
        scores = (
            jnp.einsum("slhgd,skhd->slhgk", queries, key_rows, preferred_element_type=jnp.float32)
            * score_scale
        )
        weights_norm = jnp.where(visible, jnp.exp(scores - log_total[..., None]), 0.0)
        prob_grad = jnp.einsum(
            "slhgd,skhd->slhgk", attended_grad, value_rows, preferred_element_type=jnp.float32
        )
        score_grad = (weights_norm * (prob_grad - row_delta[..., None])).astype(jnp.bfloat16)
        grad_acc = (
            grad_acc
            + jnp.einsum(
                "slhgk,skhd->slhgd", score_grad, key_rows, preferred_element_type=jnp.float32
            )
            * score_scale
        )
        key_grad = (
            jnp.einsum("slhgk,slhgd->skhd", score_grad, queries, preferred_element_type=jnp.float32)
            * score_scale
        )
        value_grad = jnp.einsum(
            "slhgk,slhgd->skhd",
            weights_norm.astype(jnp.bfloat16),
            attended_grad,
            preferred_element_type=jnp.float32,
        )
        return (
            grad_acc,
            (
                key_grad.reshape(seq_count, rows_local, kv_width),
                value_grad.reshape(seq_count, rows_local, kv_width),
            ),
        )

    block_ids = jnp.arange(pair_count, dtype=jnp.int32)
    query_grad, (key_terms, value_terms) = lax.scan(
        key_block, jnp.zeros(stat_shape + (HD,), jnp.float32), (whole_keys, whole_values, block_ids)
    )
    key_sum, value_sum = (
        lax.psum_scatter(
            key_terms.astype(jnp.bfloat16), "ctx", scatter_dimension=0, tiled=True
        ).astype(jnp.float32),
        lax.psum_scatter(
            value_terms.astype(jnp.bfloat16), "ctx", scatter_dimension=0, tiled=True
        ).astype(jnp.float32),
    )
    key_reduced = (
        rotate_back(
            key_sum[0].reshape(seq_count, rows_local, kv_heads, HD), cosine_table, sine_table
        )
        .astype(jnp.bfloat16)
        .reshape(seq_count, rows_local, kv_width)
    )
    value_backward = value_sum[0].astype(jnp.bfloat16)
    query_reduced = (
        rotate_back(
            query_grad.reshape(seq_count, rows_local, query_heads, HD), cosine_table, sine_table
        )
        .astype(jnp.bfloat16)
        .reshape(seq_count, rows_local, query_width)
    )
    query_weight_part = jnp.einsum(
        "prb,pro->bo", normed_hidden, query_reduced, preferred_element_type=jnp.float32
    )
    key_weight_part = jnp.einsum(
        "prb,pro->bo", normed_hidden, key_reduced, preferred_element_type=jnp.float32
    )
    value_weight_part = jnp.einsum(
        "prb,pro->bo", normed_hidden, value_backward, preferred_element_type=jnp.float32
    )
    normed_rows = (
        jnp.einsum(
            "kjw,iw->kji", query_reduced, query_weight_whole, preferred_element_type=jnp.float32
        )
        + jnp.einsum(
            "kjw,iw->kji", key_reduced, key_weight_whole, preferred_element_type=jnp.float32
        )
        + jnp.einsum(
            "kjw,iw->kji", value_backward, value_weight_whole, preferred_element_type=jnp.float32
        )
    )
    normed_grad = tensor_sum(normed_rows)
    gain_one_term = jnp.sum(normed_grad * inputs * factor_one, axis=(0, 1))
    tokens_grad = (
        middle_grad + rms_back(inputs, factor_one, gain_one.astype(jnp.float32), normed_grad)
    ).astype(jnp.bfloat16)
    (
        part_one,
        part_query,
        part_key,
        part_value,
        part_project,
        part_two,
        part_gate,
        part_up,
        part_down,
    ) = (
        lax.psum_scatter(gain_one_term, ("fsdp", "ctx"), scatter_dimension=0, tiled=True),
        lax.psum_scatter(query_weight_part, ("fsdp", "ctx"), scatter_dimension=0, tiled=True),
        lax.psum_scatter(key_weight_part, ("fsdp", "ctx"), scatter_dimension=0, tiled=True),
        lax.psum_scatter(value_weight_part, ("fsdp", "ctx"), scatter_dimension=0, tiled=True),
        lax.psum_scatter(project_term, ("fsdp", "ctx"), scatter_dimension=1, tiled=True),
        lax.psum_scatter(gain_two_term, ("fsdp", "ctx"), scatter_dimension=0, tiled=True),
        lax.psum_scatter(gate_weight_part, ("fsdp", "ctx"), scatter_dimension=0, tiled=True),
        lax.psum_scatter(up_weight_part, ("fsdp", "ctx"), scatter_dimension=0, tiled=True),
        lax.psum_scatter(down_weight_part, ("fsdp", "ctx"), scatter_dimension=1, tiled=True),
    )
    reduced = (
        lax.all_gather(part_one.astype(jnp.bfloat16), "ctx", axis=0, tiled=True).astype(
            part_one.dtype
        ),
        lax.all_gather(part_query.astype(jnp.bfloat16), "ctx", axis=0, tiled=True).astype(
            part_query.dtype
        ),
        lax.all_gather(part_key.astype(jnp.bfloat16), "ctx", axis=0, tiled=True).astype(
            part_key.dtype
        ),
        lax.all_gather(part_value.astype(jnp.bfloat16), "ctx", axis=0, tiled=True).astype(
            part_value.dtype
        ),
        lax.all_gather(part_project.astype(jnp.bfloat16), "ctx", axis=1, tiled=True).astype(
            part_project.dtype
        ),
        lax.all_gather(part_two.astype(jnp.bfloat16), "ctx", axis=0, tiled=True).astype(
            part_two.dtype
        ),
        lax.all_gather(part_gate.astype(jnp.bfloat16), "ctx", axis=0, tiled=True).astype(
            part_gate.dtype
        ),
        lax.all_gather(part_up.astype(jnp.bfloat16), "ctx", axis=0, tiled=True).astype(
            part_up.dtype
        ),
        lax.all_gather(part_down.astype(jnp.bfloat16), "ctx", axis=1, tiled=True).astype(
            part_down.dtype
        ),
    )
    return (layer_output, tokens_grad) + tuple(reduced)


LANES = 128
HALF = HD // 2
SPAN = LANES // 2
LOG2E = math.log2(math.e)
VMEM_BYTES = 60 * 1024 * 1024


def swap_ctx(block):
    return lax.ppermute(block, "ctx", [(0, 1), (1, 0)])


def swap_core(block):
    return lax.ppermute(block, "tp", [(0, 1), (1, 0), (2, 3), (3, 2)])


def swap_chip(block):
    return lax.ppermute(block, "tp", [(0, 2), (2, 0), (1, 3), (3, 1)])


def by_core(total, other):
    return jnp.where(
        lax.axis_index("tp") % 2 == 0,
        jnp.concatenate([total, other], axis=0),
        jnp.concatenate([other, total], axis=0),
    )


def dot(a, b, contract):
    return lax.dot_general(a, b, (contract, ((), ())), preferred_element_type=jnp.float32)


def block_kinds(meta_ref, query_tile, key_tile, q_start, k_start):
    prefix = meta_ref[0]
    whole = (k_start + (key_tile - 1) <= q_start) | (k_start + key_tile <= prefix)
    nothing = (k_start > q_start + (query_tile - 1)) & (k_start >= prefix)
    return prefix, whole, nothing


def mask_scores(scores, prefix, q_start, k_start, query_tile):
    key_ids = k_start + lax.broadcasted_iota(jnp.int32, scores.shape, 0)
    column = lax.broadcasted_iota(jnp.int32, scores.shape, 1)
    query_ids = q_start + jnp.bitwise_and(column, query_tile - 1)
    return jnp.where((key_ids <= query_ids) | (key_ids < prefix), scores, NEGATIVE)


MESH = pl.DeviceIdType.MESH
GAIN_ROWS = 16
PREFIX_MOST = 1024


def line_sum(z, planes, source, up_ref, down_ref, up_send, up_recv, down_send, down_recv):
    f32 = jnp.float32

    def up(d):
        return pltpu.make_async_remote_copy(
            src_ref=up_ref.at[d - 1],
            dst_ref=up_ref.at[d - 1],
            send_sem=up_send.at[d],
            recv_sem=up_recv.at[d],
            device_id={"fsdp": z + 1},
            device_id_type=MESH,
        )

    def down(d):
        return pltpu.make_async_remote_copy(
            src_ref=down_ref.at[d],
            dst_ref=down_ref.at[d],
            send_sem=down_send.at[d],
            recv_sem=down_recv.at[d],
            device_id={"fsdp": z - 1},
            device_id_type=MESH,
        )

    def begin(k):
        high, low = planes - 1 - k, k

        @pl.when(z == 0)
        def _():
            up_ref[high - 1] = source(high)
            up(high).start()

        @pl.when(z == planes - 1)
        def _():
            down_ref[low] = source(low)
            down(low).start()

    def relay(k):
        high, low = planes - 1 - k, k

        def pass_up():
            @pl.when((z > 0) & (z < high))
            def _():
                up(high).wait_recv()
                up_ref[high - 1] = (
                    up_ref[high - 1].astype(f32) + source(high).astype(f32)
                ).astype(up_ref.dtype)
                up(high).start()

        def pass_down():
            @pl.when((z < planes - 1) & (z > low))
            def _():
                down(low).wait_recv()
                down_ref[low] = (
                    down_ref[low].astype(f32) + source(low).astype(f32)
                ).astype(down_ref.dtype)
                down(low).start()

        @pl.when(2 * z < planes)
        def _():
            pass_up()
            pass_down()

        @pl.when(2 * z >= planes)
        def _():
            pass_down()
            pass_up()

    def finish(out_ref):
        out_ref[...] = source(z)

        @pl.when(z > 0)
        def _():
            up(z).wait_recv()
            out_ref[...] = (
                out_ref[...].astype(f32) + up_ref[pl.ds(z - 1, 1)][0].astype(f32)
            ).astype(out_ref.dtype)

        @pl.when(z < planes - 1)
        def _():
            down(z).wait_recv()
            out_ref[...] = (
                out_ref[...].astype(f32) + down_ref[pl.ds(z, 1)][0].astype(f32)
            ).astype(out_ref.dtype)

    def sent():
        for d in range(planes):

            @pl.when(z < d)
            def _():
                up(d).wait_send()

            @pl.when(z > d)
            def _():
                down(d).wait_send()

    return begin, relay, finish, sent


def front_kernel(
    prefix_ref,
    x_ref,
    pack_ref,
    rest_ref,
    spread_ref,
    cos_ref,
    sin_ref,
    w_project_ref,
    w_gate_ref,
    w_up_ref,
    w_down_ref,
    normed_hbm,
    q_hbm,
    kv_hbm,
    wide_hbm,
    project_ref,
    gain_ref,
    o_ref,
    lse_ref,
    total_ref,
    gate_ref,
    up_ref,
    down_ref,
    normed_ref,
    q_ref,
    kv_ref,
    wide_ref,
    buf_ref,
    max_ref,
    sum_ref,
    acc_ref,
    give_ref,
    core_in_ref,
    keep_ref,
    chip_in_ref,
    up_send,
    up_recv,
    down_send,
    down_recv,
    x_send,
    x_recv,
    kv_send,
    kv_recv,
    m_up_send,
    m_up_recv,
    m_down_send,
    m_down_recv,
    m_x_send,
    m_x_recv,
    local_sem,
    core_send,
    core_recv,
    chip_send,
    chip_recv,
    back_send,
    back_recv,
    store_sem,
):
    bf16, f32 = jnp.bfloat16, jnp.float32
    planes = buf_ref.shape[0]
    rows, width = x_ref.shape
    depth = width // planes
    half_width = wide_ref.shape[1] // 2
    matrix_rows = rest_ref.shape[0]
    heads_half = project_ref.shape[0] // 2
    units = gate_ref.shape[2]
    direct = units // 2
    z = lax.axis_index("fsdp")
    c = lax.axis_index("ctx")
    t = lax.axis_index("tp")
    core = lax.rem(t, 2)
    across = {"ctx": 1 - c}
    sibling = {"tp": t + 1 - 2 * core}
    partner = {"tp": lax.rem(t + 2, 4)}
    has_above = z < planes - 1
    has_below = z > 0

    def remote(src, dst, send, recv, device):
        return pltpu.make_async_remote_copy(
            src_ref=src,
            dst_ref=dst,
            send_sem=send,
            recv_sem=recv,
            device_id=device,
            device_id_type=MESH,
        )

    project_ref[:, HD:, :] = jnp.zeros(
        (project_ref.shape[0], LANES - HD, project_ref.shape[2]), bf16
    )

    barrier = pltpu.get_barrier_semaphore()

    @pl.when(has_above)
    def _():
        pl.semaphore_signal(barrier, inc=1, device_id={"fsdp": z + 1}, device_id_type=MESH)

    @pl.when(has_below)
    def _():
        pl.semaphore_signal(barrier, inc=1, device_id={"fsdp": z - 1}, device_id_type=MESH)

    for device in (across, sibling, partner):
        pl.semaphore_signal(barrier, inc=1, device_id=device, device_id_type=MESH)

    @pl.when(has_above & has_below)
    def _():
        pl.semaphore_wait(barrier, 5)

    @pl.when(jnp.logical_not(has_above & has_below))
    def _():
        pl.semaphore_wait(barrier, 4)

    def up(k):
        piece = z - k
        src = pack_ref if k == 0 else buf_ref.at[piece, 0]
        return remote(src, buf_ref.at[piece, 0], up_send.at[k], up_recv.at[k], {"fsdp": z + 1})

    def down(k):
        piece = z + k
        src = pack_ref if k == 0 else buf_ref.at[piece, 0]
        return remote(src, buf_ref.at[piece, 0], down_send.at[k], down_recv.at[k], {"fsdp": z - 1})

    def from_below(k):
        slot = buf_ref.at[z - 1 - k, 0]
        return remote(slot, slot, up_send.at[k], up_recv.at[k], {"fsdp": z - 1})

    def from_above(k):
        slot = buf_ref.at[z + 1 + k, 0]
        return remote(slot, slot, down_send.at[k], down_recv.at[k], {"fsdp": z + 1})

    def sideways(side, k):
        piece = z - k if side == 0 else z + k
        matrix = pl.ds(0, matrix_rows)
        return remote(
            buf_ref.at[piece, 0, matrix],
            buf_ref.at[piece, 1, matrix],
            x_send.at[side, k],
            x_recv.at[side, k],
            across,
        )

    def own_half(m, half):
        if m == 0:
            return w_gate_ref.at[:, pl.ds(pl.multiple_of(half * units, units), units)]
        if m == 1:
            return w_up_ref.at[:, pl.ds(pl.multiple_of(half * units, units), units)]
        if m == 2:
            return w_down_ref.at[pl.ds(pl.multiple_of(half * units, units), units), :]
        if m == 4:
            return w_down_ref.at[pl.ds(pl.multiple_of((1 - half) * units, units), direct), :]
        return w_project_ref.at[pl.ds(half * heads_half, heads_half)]

    def slot(m, which, piece):
        at = pl.ds(pl.multiple_of(piece * depth, depth), depth)
        if m == 0:
            return gate_ref.at[which, at]
        if m == 1:
            return up_ref.at[which, at]
        if m == 2:
            return down_ref.at[which, :, at]
        if m == 4:
            return down_ref.at[1, pl.ds(0, direct), at]
        return project_ref.at[pl.ds(which * heads_half, heads_half), pl.ds(0, HD), at]

    def m_up(m, k):
        piece = z - k
        src = own_half(m, c) if k == 0 else slot(m, 0, piece)
        return remote(
            src, slot(m, 0, piece), m_up_send.at[m, k], m_up_recv.at[m, k], {"fsdp": z + 1}
        )

    def m_down(m, k):
        piece = z + k
        src = own_half(m, c) if k == 0 else slot(m, 0, piece)
        return remote(
            src, slot(m, 0, piece), m_down_send.at[m, k], m_down_recv.at[m, k], {"fsdp": z - 1}
        )

    def m_below(m, k):
        at = slot(m, 0, z - 1 - k)
        return remote(at, at, m_up_send.at[m, k], m_up_recv.at[m, k], {"fsdp": z - 1})

    def m_above(m, k):
        at = slot(m, 0, z + 1 + k)
        return remote(at, at, m_down_send.at[m, k], m_down_recv.at[m, k], {"fsdp": z + 1})

    def m_side(m, side, k):
        piece = z - k if side == 0 else z + k
        src, dst = slot(m, 0, piece), slot(m, 1, piece)
        if m == 2:
            left = pl.ds(direct, units - direct)
            src, dst = src.at[left], dst.at[left]
        return remote(
            src,
            dst,
            m_x_send.at[m, side, k],
            m_x_recv.at[m, side, k],
            across,
        )

    groups = ((3,), (0,), (1,), (2, 4))

    def relay(group, k):
        for m in groups[group]:

            @pl.when(z - k >= 0)
            def _():
                m_below(m, k - 1).wait_recv()
                if k < planes - 1:

                    @pl.when(has_above)
                    def _():
                        m_up(m, k).start()

            @pl.when(z + k <= planes - 1)
            def _():
                m_above(m, k - 1).wait_recv()
                if k < planes - 1:

                    @pl.when(has_below)
                    def _():
                        m_down(m, k).start()

    def launch(group):
        for m in groups[group]:

            @pl.when(has_above)
            def _():
                m_up(m, 0).start()

            @pl.when(has_below)
            def _():
                m_down(m, 0).start()

    def cross(group, k):
        for m in groups[group]:
            if m == 4:
                continue

            @pl.when(z - k >= 0)
            def _():
                m_side(m, 0, k).start()

            @pl.when(z + k <= planes - 1)
            def _():
                m_side(m, 1, k).start()

    def crossed(m, k):
        @pl.when(z - k >= 0)
        def _():
            m_side(m, 0, k).wait_recv()

        @pl.when(z + k <= planes - 1)
        def _():
            m_side(m, 1, k).wait_recv()

    def local(m, which):
        half = c if which == 0 else 1 - c
        return pltpu.make_async_copy(own_half(m, half), slot(m, which, z), local_sem.at[m, which])

    spread = spread_ref[...]

    def place(block, piece, which):
        at = pl.ds(pl.multiple_of(piece * depth, depth), depth)
        wide_ref[at, which * half_width : (which + 1) * half_width] = dot(
            block[:depth], spread, ((1,), (0,))
        ).astype(bf16)

    def place_gain(block, piece):
        at = pl.ds(pl.multiple_of(piece * depth, depth), depth)
        gain_ref[:, at] = block[matrix_rows:]

    @pl.when(has_above)
    def _():
        up(0).start()

    @pl.when(has_below)
    def _():
        down(0).start()

    for m in (3, 0, 1, 2):
        for which in range(2):
            local(m, which).start()
    place(pack_ref, z, 0)
    place_gain(pack_ref, z)
    place(rest_ref, z, 1)

    for k in range(1, planes):
        below = z - k >= 0
        above = z + k <= planes - 1

        @pl.when(below)
        def _():
            from_below(k - 1).wait_recv()
            if k < planes - 1:

                @pl.when(has_above)
                def _():
                    up(k).start()

            sideways(0, k).start()

        @pl.when(above)
        def _():
            from_above(k - 1).wait_recv()
            if k < planes - 1:

                @pl.when(has_below)
                def _():
                    down(k).start()

            sideways(1, k).start()

        if k == max(1, planes - 2):
            launch(0)
            launch(1)

        @pl.when(below)
        def _():
            place(buf_ref.at[z - k, 0], z - k, 0)
            place_gain(buf_ref.at[z - k, 0], z - k)

        @pl.when(above)
        def _():
            place(buf_ref.at[z + k, 0], z + k, 0)
            place_gain(buf_ref.at[z + k, 0], z + k)

    relay(0, 1)
    cross(0, 1)
    tile = 128
    gain = gain_ref[0:1, :].astype(f32)

    def norm_rows(i, carry):
        at = pl.ds(pl.multiple_of(i * tile, tile), tile)
        x = x_ref[at, :].astype(f32)
        factor = lax.rsqrt(jnp.mean(x * x, axis=-1, keepdims=True) + EPSILON)
        normed_ref[at, :] = (x * factor * gain).astype(bf16)
        return carry

    lax.fori_loop(0, rows // tile, norm_rows, 0)
    relay(0, 2)
    cross(0, 2)
    launch(2)

    for k in range(1, planes):

        @pl.when(z - k >= 0)
        def _():
            sideways(0, k).wait_recv()
            place(buf_ref.at[z - k, 1], z - k, 1)

        @pl.when(z + k <= planes - 1)
        def _():
            sideways(1, k).wait_recv()
            place(buf_ref.at[z + k, 1], z + k, 1)

    block = 256

    def turn(part, at):
        return part * cos_ref[at, :] + pltpu.roll(part, SPAN, 1) * sin_ref[at, :]

    def key_rows(i, carry):
        at = pl.ds(pl.multiple_of(i * block, block), block)
        for which in range(2):
            lane = which * half_width + 2 * LANES
            both = dot(normed_ref[at, :], wide_ref[:, lane : lane + 2 * LANES], ((1,), (0,)))
            kv_ref[which, at, :] = turn(both[:, :LANES], at).astype(bf16)
            kv_ref[2 + which, at, :] = both[:, LANES:].astype(bf16)
        return carry

    lax.fori_loop(0, rows // block, key_rows, 0)

    def exchange(slab):
        return remote(
            kv_ref.at[slab, pl.ds(0, rows)],
            kv_ref.at[slab ^ 1, pl.ds(rows, rows)],
            kv_send.at[slab],
            kv_recv.at[slab ^ 1],
            across,
        )

    for slab in range(4):
        exchange(slab).start()
    relay(0, 3)
    cross(0, 3)
    relay(1, 1)
    launch(3)
    scale = HD ** (-0.5) * LOG2E

    def query_rows(i, carry):
        at = pl.ds(pl.multiple_of(i * block, block), block)
        for which in range(2):
            lane = which * half_width
            both = dot(normed_ref[at, :], wide_ref[:, lane : lane + 2 * LANES], ((1,), (0,)))
            for head in range(2):
                part = turn(both[:, head * LANES : (head + 1) * LANES], at)
                lane = (2 * which + head) * LANES
                q_ref[at, lane : lane + LANES] = (part * scale).astype(bf16)
        return carry

    lax.fori_loop(0, rows // block, query_rows, 0)
    stores = [
        pltpu.make_async_copy(src, dst, store_sem.at[i])
        for i, (src, dst) in enumerate(
            ((normed_ref, normed_hbm), (q_ref, q_hbm), (wide_ref, wide_hbm), (kv_ref, kv_hbm))
        )
    ]
    for store in stores[:3]:
        store.start()

    tiles = rows // block
    tiles_of_block = tiles // 2
    prefix = prefix_ref[0]
    max_ref[...] = jnp.full_like(max_ref, NEGATIVE)
    sum_ref[...] = jnp.zeros_like(sum_ref)
    acc_ref[...] = jnp.zeros_like(acc_ref)

    def start_of(device, tile_index):
        second = tile_index // tiles_of_block
        block_id = device + second * (3 - 2 * device)
        return (block_id * tiles_of_block + tile_index % tiles_of_block) * block

    def attend_group(g, away):
        key_device = 1 - c if away else c

        def one_tile(i, carry):
            at = pl.ds(pl.multiple_of(i * block, block), block)
            lane = 2 * g * LANES
            queries = jnp.concatenate(
                [q_ref[at, lane : lane + LANES], q_ref[at, lane + LANES : lane + 2 * LANES]],
                axis=0,
            )
            q_start = start_of(c, i)
            u = g * tiles + i

            def absorb(scores, values):
                old = max_ref[u]
                new = jnp.maximum(old, jnp.max(scores, axis=0, keepdims=True))
                weights = jnp.exp2(scores - new)
                rescale = jnp.exp2(old - new)
                max_ref[u] = new
                sum_ref[u] = sum_ref[u] * rescale + jnp.sum(weights, axis=0, keepdims=True)
                acc_ref[u] = acc_ref[u] * rescale + dot(values, weights.astype(bf16), ((0,), (0,)))

            def one(j, carry):
                k_start = start_of(key_device, j)
                first = (tiles if away else 0) + j
                keys_at = pl.ds(pl.multiple_of(first * block, block), block)
                whole = k_start + (block - 1) <= q_start
                nothing = (k_start > q_start + (block - 1)) & (k_start >= PREFIX_MOST)

                @pl.when(whole)
                def _():
                    absorb(dot(kv_ref[g, keys_at, :], queries, ((1,), (1,))), kv_ref[2 + g, keys_at, :])

                @pl.when(jnp.logical_not(whole | nothing))
                def _():
                    scores = dot(kv_ref[g, keys_at, :], queries, ((1,), (1,)))
                    absorb(
                        mask_scores(scores, prefix, q_start, k_start, block),
                        kv_ref[2 + g, keys_at, :],
                    )

                return carry

            lax.fori_loop(0, tiles, one, 0)
            if away:
                total = sum_ref[u]
                lse_ref[g, i] = max_ref[u] + jnp.log2(total)
                out = (acc_ref[u] / total).T.astype(bf16)
                o_ref[at, lane : lane + LANES] = out[:block]
                o_ref[at, lane + LANES : lane + 2 * LANES] = out[block:]
            return carry

        lax.fori_loop(0, tiles, one_tile, 0)

    attend_group(0, False)
    relay(2, 1)
    cross(1, 1)
    attend_group(1, False)
    relay(3, 1)
    for slab in range(4):
        exchange(slab).wait_recv()
    stores[3].start()
    cross(2, 1)
    cross(3, 1)
    attend_group(0, True)
    relay(1, 2)
    cross(1, 2)
    attend_group(1, True)
    relay(2, 2)
    cross(2, 2)

    chunks, chunk, _ = give_ref.shape
    half_rows = rows // 2
    give_start = (1 - core) * half_rows
    keep_start = core * half_rows
    for which in range(2):
        local(3, which).wait()
    for k in range(1, planes):
        crossed(3, k)
    w_project = project_ref[...].reshape(project_ref.shape[0] * LANES, width)

    def feature_rows(start):
        at = pl.ds(pl.multiple_of(start, chunk), chunk)
        return dot(o_ref[at, :], w_project, ((1,), (0,)))

    def to_core(i):
        return remote(give_ref.at[i], core_in_ref.at[i], core_send.at[i], core_recv.at[i], sibling)

    def to_chip(i):
        return remote(keep_ref.at[i], chip_in_ref.at[i], chip_send.at[i], chip_recv.at[i], partner)

    def back(i, start):
        at = pl.ds(pl.multiple_of(start + i * chunk, chunk), chunk)
        return remote(
            total_ref.at[at], total_ref.at[at], back_send.at[i], back_recv.at[i], sibling
        )

    for i in range(chunks):
        give_ref[i] = feature_rows(give_start + i * chunk).astype(bf16)
        to_core(i).start()
    for i in range(chunks):
        kept = feature_rows(keep_start + i * chunk)
        to_core(i).wait_recv()
        keep_ref[i] = (kept + core_in_ref[i].astype(f32)).astype(bf16)
        to_chip(i).start()

    def finish_chunk(i):
        to_chip(i).wait_recv()
        at = pl.ds(pl.multiple_of(keep_start + i * chunk, chunk), chunk)
        total_ref[at, :] = (keep_ref[i].astype(f32) + chip_in_ref[i].astype(f32)).astype(bf16)
        back(i, keep_start).start()

    relay(3, 2)
    cross(3, 2)
    for i in range(chunks):
        finish_chunk(i)
        if i < planes - 1:
            relay(i + 1, planes - 1)
            cross(i + 1, planes - 1)

    for store in stores:
        store.wait()
    for k in range(planes - 1):

        @pl.when((z - k >= 0) & has_above)
        def _():
            up(k).wait_send()
            for m in range(5):
                m_up(m, k).wait_send()

        @pl.when((z + k <= planes - 1) & has_below)
        def _():
            down(k).wait_send()
            for m in range(5):
                m_down(m, k).wait_send()

    for k in range(1, planes):

        @pl.when(z - k >= 0)
        def _():
            sideways(0, k).wait_send()
            for m in range(4):
                m_side(m, 0, k).wait_send()

        @pl.when(z + k <= planes - 1)
        def _():
            sideways(1, k).wait_send()
            for m in range(4):
                m_side(m, 1, k).wait_send()

        for m in range(3):
            crossed(m, k)

    for m in range(3):
        for which in range(2):
            local(m, which).wait()
    for slab in range(4):
        exchange(slab).wait_send()
    for i in range(chunks):
        to_core(i).wait_send()
        to_chip(i).wait_send()
        back(i, keep_start).wait_send()
        back(i, give_start).wait_recv()


def front(prefix, x, pack, rest, spread, cosine, sine, w_project, w_gate, w_up, w_down, planes):
    rows, width = x.shape
    half_width = spread.shape[1]
    units = w_gate.shape[1] // 2
    heads = w_project.shape[0]
    block = 256
    tiles = rows // block
    chunks = 4
    chunk = rows // 2 // chunks
    vmem = pl.BlockSpec(memory_space=pltpu.VMEM)
    anywhere = pl.BlockSpec(memory_space=pl.ANY)
    smem = pl.BlockSpec(memory_space=pltpu.SMEM)
    bf16, f32 = jnp.bfloat16, jnp.float32
    dma = pltpu.SemaphoreType.DMA
    piece = pltpu.VMEM((chunks, chunk, width), bf16)
    return pl.pallas_call(
        front_kernel,
        in_specs=[smem] + [vmem] * 6 + [anywhere] * 4,
        out_specs=[anywhere] * 4 + [vmem] * 5 + [anywhere] * 3,
        out_shape=[
            jax.ShapeDtypeStruct((rows, width), bf16),
            jax.ShapeDtypeStruct((rows, half_width), bf16),
            jax.ShapeDtypeStruct((4, 2 * rows, LANES), bf16),
            jax.ShapeDtypeStruct((width, 2 * half_width), bf16),
            jax.ShapeDtypeStruct((heads, LANES, width), bf16),
            jax.ShapeDtypeStruct((GAIN_ROWS, width), bf16),
            jax.ShapeDtypeStruct((rows, half_width), bf16),
            jax.ShapeDtypeStruct((2, tiles, 1, 2 * block), f32),
            jax.ShapeDtypeStruct((rows, width), bf16),
            jax.ShapeDtypeStruct((2, width, units), bf16),
            jax.ShapeDtypeStruct((2, width, units), bf16),
            jax.ShapeDtypeStruct((2, units, width), bf16),
        ],
        scratch_shapes=[
            pltpu.VMEM((rows, width), bf16),
            pltpu.VMEM((rows, half_width), bf16),
            pltpu.VMEM((4, 2 * rows, LANES), bf16),
            pltpu.VMEM((width, 2 * half_width), bf16),
            pltpu.VMEM((planes, 2, pack.shape[0], pack.shape[1]), bf16),
            pltpu.VMEM((2 * tiles, 1, 2 * block), f32),
            pltpu.VMEM((2 * tiles, 1, 2 * block), f32),
            pltpu.VMEM((2 * tiles, LANES, 2 * block), f32),
            piece,
            piece,
            piece,
            piece,
        ]
        + [dma((planes - 1,))] * 4
        + [dma((2, planes))] * 2
        + [dma((4,))] * 2
        + [dma((5, planes - 1))] * 4
        + [dma((4, 2, planes))] * 2
        + [dma((4, 2))]
        + [dma((chunks,))] * 6
        + [dma((4,))],
        compiler_params=pltpu.CompilerParams(
            collective_id=1, has_side_effects=True, vmem_limit_bytes=VMEM_BYTES
        ),
        cost_estimate=pl.CostEstimate(
            flops=120_000_000_000, bytes_accessed=60_000_000, transcendentals=0
        ),
        name="front",
    )(prefix, x, pack, rest, spread, cosine, sine, w_project, w_gate, w_up, w_down)


def attend_back_kernel(
    final,
    meta_ref,
    carry_ref,
    first_ref,
    second_ref,
    q_ref,
    k_ref,
    v_ref,
    o_ref,
    do_ref,
    lse_ref,
    cos_ref,
    sin_ref,
    dq_ref,
    dkv_ref,
    delta_ref,
    acc_ref,
    dk_acc_ref,
    dv_acc_ref,
):
    query_tiles = lse_ref.shape[1]
    tile = q_ref.shape[0] // query_tiles
    key_tile = k_ref.shape[1]
    j = pl.program_id(1)

    def stacked(ref, i):
        rows = pl.ds(pl.multiple_of(i * tile, tile), tile)
        return jnp.concatenate([ref[rows, :LANES], ref[rows, LANES:]], axis=0)

    @pl.when(j == 0)
    def _():
        acc_ref[...] = carry_ref[0] if final else jnp.zeros_like(acc_ref)

        def one_delta(i, carry):
            product = stacked(o_ref, i).astype(jnp.float32) * stacked(do_ref, i).astype(jnp.float32)
            delta_ref[i] = jnp.sum(product.T, axis=0, keepdims=True)
            return carry

        lax.fori_loop(0, query_tiles, one_delta, 0)

    k_start = meta_ref[1 + query_tiles + (0 if final else pl.num_programs(1)) + j]
    keys = k_ref[0]
    values = v_ref[0]

    dk_acc_ref[...] = jnp.zeros_like(dk_acc_ref)
    dv_acc_ref[...] = jnp.zeros_like(dv_acc_ref)

    def one(i, carry):
        q_start = meta_ref[1 + i]
        prefix, whole, nothing = block_kinds(meta_ref, tile, key_tile, q_start, k_start)

        def some(masked):
            queries = stacked(q_ref, i)
            d_out = stacked(do_ref, i)
            scores = dot(keys, queries, ((1,), (1,)))
            if masked:
                scores = mask_scores(scores, prefix, q_start, k_start, tile)
            weights = jnp.exp2(scores - lse_ref[0, i])
            d_weights = dot(values, d_out, ((1,), (1,)))
            d_scores = (weights * (d_weights - delta_ref[i])).astype(jnp.bfloat16)
            dv_acc_ref[...] += dot(weights.astype(jnp.bfloat16), d_out, ((1,), (0,)))
            dk_acc_ref[...] += dot(d_scores, queries, ((1,), (0,)))
            acc_ref[i] += dot(keys, d_scores, ((0,), (0,)))

        @pl.when(whole)
        def _():
            some(False)

        @pl.when(jnp.logical_not(whole | nothing))
        def _():
            some(True)

        return carry

    lax.fori_loop(0, query_tiles, one, 0)
    dkv_ref[0, 0] = (dk_acc_ref[...] * (1.0 / LOG2E)).astype(jnp.bfloat16)
    dkv_ref[0, 1] = dv_acc_ref[...].astype(jnp.bfloat16)

    @pl.when(j == pl.num_programs(1) - 1)
    def _():
        scale = HD ** (-0.5)
        if not final:
            dq_ref[0] = acc_ref[...]
            return

        def one_out(i, carry):
            rows = pl.ds(pl.multiple_of(i * tile, tile), tile)
            turned = acc_ref[i].T * scale
            for head in range(2):
                part = turned[head * tile : (head + 1) * tile]
                part = part * cos_ref[rows, :] - pltpu.roll(part, SPAN, 1) * sin_ref[rows, :]
                dq_ref[rows, head * LANES : (head + 1) * LANES] = part.astype(jnp.bfloat16)
            return carry

        lax.fori_loop(0, query_tiles, one_out, 0)


def attend_back(meta, carry, first, second, q, kv, away, o, d_out, lse, cosine, sine, tile):
    rows, q_width = q.shape
    keys = kv.shape[1] // 2
    groups = q_width // (2 * LANES)
    query_tiles = rows // tile
    key_tiles = keys // tile
    skip = key_tiles if away else 0
    acc_block = pl.BlockSpec((1, query_tiles, LANES, 2 * tile), lambda g, j, m: (g, 0, 0, 0))
    acc_shape = jax.ShapeDtypeStruct((groups, query_tiles, LANES, 2 * tile), jnp.float32)
    if away:
        carry = jnp.zeros((1, 1, 8, LANES), jnp.float32)
        carry_block = pl.BlockSpec((1, 1, 8, LANES), lambda g, j, m: (0, 0, 0, 0))
    else:
        carry_block = acc_block
    whole_q = pl.BlockSpec((rows, 2 * LANES), lambda g, j, m: (0, g))
    return pl.pallas_call(
        functools.partial(attend_back_kernel, not away),
        grid_spec=pltpu.PrefetchScalarGridSpec(
            num_scalar_prefetch=1,
            grid=(groups, key_tiles),
            in_specs=[
                carry_block,
                pl.BlockSpec(memory_space=pl.ANY),
                pl.BlockSpec(memory_space=pl.ANY),
                whole_q,
                pl.BlockSpec((1, tile, LANES), lambda g, j, m: (g, skip + j, 0)),
                pl.BlockSpec((1, tile, LANES), lambda g, j, m: (groups + g, skip + j, 0)),
                whole_q,
                whole_q,
                pl.BlockSpec((1, query_tiles, 1, 2 * tile), lambda g, j, m: (g, 0, 0, 0)),
                pl.BlockSpec((rows, LANES), lambda g, j, m: (0, 0)),
                pl.BlockSpec((rows, LANES), lambda g, j, m: (0, 0)),
            ],
            out_specs=[
                acc_block if away else whole_q,
                pl.BlockSpec((1, 2, tile, LANES), lambda g, j, m: (g, 0, j, 0)),
            ],
            scratch_shapes=[
                pltpu.VMEM((query_tiles, 1, 2 * tile), jnp.float32),
                pltpu.VMEM((query_tiles, LANES, 2 * tile), jnp.float32),
                pltpu.VMEM((tile, LANES), jnp.float32),
                pltpu.VMEM((tile, LANES), jnp.float32),
            ],
        ),
        out_shape=[
            acc_shape if away else jax.ShapeDtypeStruct((rows, q_width), jnp.bfloat16),
            jax.ShapeDtypeStruct((groups, 2, keys, LANES), jnp.bfloat16),
        ],
        compiler_params=pltpu.CompilerParams(vmem_limit_bytes=VMEM_BYTES),
        cost_estimate=pl.CostEstimate(
            flops=20 * rows * keys * LANES * groups * 2, bytes_accessed=8_000_000, transcendentals=0
        ),
        name="attend_back_away" if away else "attend_back_own",
    )(meta, carry, first, second, q, kv, kv, o, d_out, lse, cosine, sine)


def middle_back_kernel(
    x_ref,
    project_ref,
    feed_ref,
    cot_ref,
    gain_ref,
    o_ref,
    wp_ref,
    grad_ref,
    d_out_ref,
    wp_grad_ref,
    gain_grad_ref,
    acc_ref,
):
    step = pl.program_id(0)
    last = pl.num_programs(0) - 1
    bf16, f32 = jnp.bfloat16, jnp.float32

    @pl.when(step == 0)
    def _():
        acc_ref[...] = jnp.zeros_like(acc_ref)
        gain_grad_ref[...] = jnp.zeros_like(gain_grad_ref)

    middle = x_ref[...].astype(f32) + project_ref[...].astype(f32)
    factor = lax.rsqrt(jnp.mean(middle * middle, axis=-1, keepdims=True) + EPSILON)
    feed_in = feed_ref[...].astype(f32)
    gain_grad_ref[...] += jnp.sum(feed_in * middle * factor, axis=0, keepdims=True)
    scaled = gain_ref[1:2, :].astype(f32) * feed_in
    grad = (
        cot_ref[...].astype(f32)
        + factor * scaled
        - middle * (factor * factor * factor * jnp.mean(scaled * middle, axis=-1, keepdims=True))
    )
    grad_ref[...] = grad
    low = grad.astype(bf16)
    d_out_ref[...] = dot(low, wp_ref[...], ((1,), (1,))).astype(bf16)
    acc_ref[...] += dot(o_ref[...], low, ((0,), (0,)))

    @pl.when(step == last)
    def _():
        for head in range(acc_ref.shape[0] // LANES):
            wp_grad_ref[head * HD : (head + 1) * HD, :] = acc_ref[
                head * LANES : head * LANES + HD, :
            ].astype(bf16)


def middle_back(x, project_sum, feed_sum, cot, gains, o, w_p):
    rows, width = x.shape
    tile = 256
    heads = o.shape[1] // LANES
    bf16, f32 = jnp.bfloat16, jnp.float32

    def rows_of(columns):
        return pl.BlockSpec((tile, columns), lambda i: (i, 0))

    def whole(array):
        return pl.BlockSpec(array.shape, lambda i: (0, 0))

    return pl.pallas_call(
        middle_back_kernel,
        grid=(rows // tile,),
        in_specs=[
            rows_of(width),
            rows_of(width),
            rows_of(width),
            rows_of(width),
            whole(gains),
            rows_of(o.shape[1]),
            whole(w_p),
        ],
        out_specs=[
            rows_of(width),
            rows_of(o.shape[1]),
            pl.BlockSpec((heads * HD, width), lambda i: (0, 0)),
            pl.BlockSpec((1, width), lambda i: (0, 0)),
        ],
        out_shape=[
            jax.ShapeDtypeStruct((rows, width), f32),
            jax.ShapeDtypeStruct(o.shape, bf16),
            jax.ShapeDtypeStruct((heads * HD, width), bf16),
            jax.ShapeDtypeStruct((1, width), f32),
        ],
        scratch_shapes=[pltpu.VMEM((o.shape[1], width), f32)],
        compiler_params=pltpu.CompilerParams(vmem_limit_bytes=VMEM_BYTES),
        cost_estimate=pl.CostEstimate(
            flops=5_000_000_000, bytes_accessed=26_000_000, transcendentals=0
        ),
        name="middle_back",
    )(x, project_sum, feed_sum, cot, gains, o, w_p)


def tail_kernel(
    down_hbm,
    gate_hbm,
    gate_away_hbm,
    gate_rest_hbm,
    up_hbm,
    up_away_hbm,
    q_low_ref,
    own_ref,
    away_ref,
    normed_hbm,
    wide_hbm,
    x_hbm,
    grad_hbm,
    gain_term_ref,
    gain_ref,
    project_ref,
    spread_ref,
    cos_ref,
    sin_ref,
    out_hbm,
    share_ref,
    project_share_ref,
    gate_share_ref,
    up_share_ref,
    gain_share_ref,
    down_away_hbm,
    normed_ref,
    wide_ref,
    x_ref,
    grad_ref,
    gate_ref,
    gate_away_ref,
    upw_ref,
    upw_away_ref,
    low_ref,
    close_ref,
    part_ref,
    x_in_ref,
    up_ref,
    down_ref,
    p_in_ref,
    p_up_ref,
    p_down_ref,
    g_up_ref,
    g_down_ref,
    u_up_ref,
    u_down_ref,
    give_ref,
    core_in_ref,
    chip_in_ref,
    total_ref,
    gain_sum_ref,
    gain_x_ref,
    gain_z_ref,
    x_send,
    x_recv,
    up_send,
    up_recv,
    down_send,
    down_recv,
    p_up_send,
    p_up_recv,
    p_down_send,
    p_down_recv,
    g_up_send,
    g_up_recv,
    g_down_send,
    g_down_recv,
    u_up_send,
    u_up_recv,
    u_down_send,
    u_down_recv,
    core_send,
    core_recv,
    chip_send,
    chip_recv,
    back_send,
    back_recv,
    last_send,
    last_recv,
    gain_send,
    gain_recv,
    load_sem,
):
    bf16, f32 = jnp.bfloat16, jnp.float32
    planes = part_ref.shape[1]
    rows, width = x_ref.shape
    depth = width // planes
    sent_rows = gate_away_hbm.shape[0]
    loads = [
        pltpu.make_async_copy(src, dst, load_sem.at[i])
        for i, (src, dst) in enumerate(
            (
                (gate_hbm, gate_ref),
                (gate_away_hbm, gate_away_ref.at[pl.ds(0, sent_rows)]),
                (gate_rest_hbm, gate_away_ref.at[pl.ds(sent_rows, width - sent_rows)]),
                (up_hbm, upw_ref),
                (up_away_hbm, upw_away_ref),
                (normed_hbm, normed_ref),
                (wide_hbm, wide_ref),
                (x_hbm, x_ref),
                (grad_hbm, grad_ref),
            )
        )
    ]
    for load in loads:
        load.start()
    half_rows = rows // 2
    chunks = give_ref.shape[0]
    chunk = half_rows // chunks
    half_width = low_ref.shape[2]
    z = lax.axis_index("fsdp")
    c = lax.axis_index("ctx")
    t = lax.axis_index("tp")
    core = lax.rem(t, 2)
    across = {"ctx": 1 - c}
    sibling = {"tp": t + 1 - 2 * core}
    partner = {"tp": lax.rem(t + 2, 4)}

    barrier = pltpu.get_barrier_semaphore()
    for device in (across, sibling, partner):
        pl.semaphore_signal(barrier, inc=1, device_id=device, device_id_type=MESH)
    for k in range(1, planes):
        pl.semaphore_signal(
            barrier, inc=1, device_id={"fsdp": lax.rem(z + k, planes)}, device_id_type=MESH
        )
    pl.semaphore_wait(barrier, 3 + planes - 1)

    def remote(src, dst, send, recv, device):
        return pltpu.make_async_remote_copy(
            src_ref=src,
            dst_ref=dst,
            send_sem=send,
            recv_sem=recv,
            device_id=device,
            device_id_type=MESH,
        )

    def plane_rows(d):
        return pl.ds(pl.multiple_of(d * depth, depth), depth)

    def pair_source(mine_ref, away_ref):
        def source(d):
            at = plane_rows(d)
            return (mine_ref[at, :].astype(f32) + away_ref[at, :].astype(f32)).astype(bf16)

        return source

    g_begin, g_relay, g_finish, g_sent = line_sum(
        z, planes, pair_source(gate_ref, gate_away_ref),
        g_up_ref, g_down_ref, g_up_send, g_up_recv, g_down_send, g_down_recv,
    )
    u_begin, u_relay, u_finish, u_sent = line_sum(
        z, planes, pair_source(upw_ref, upw_away_ref),
        u_up_ref, u_down_ref, u_up_send, u_up_recv, u_down_send, u_down_recv,
    )

    project_half = project_ref.shape[0] // 2

    def project_over():
        return remote(
            project_ref.at[pl.ds(project_half, project_half)], p_in_ref,
            last_send.at[2], last_recv.at[2], across,
        )

    def project_source(d):
        at = plane_rows(d)
        return (
            project_ref[0:project_half, at].astype(f32) + p_in_ref[:, at].astype(f32)
        ).astype(bf16)

    p_begin, p_relay, p_finish, p_sent = line_sum(
        z, planes, project_source, p_up_ref, p_down_ref, p_up_send, p_up_recv, p_down_send, p_down_recv
    )
    order = []
    for step in range((planes + 1) // 2):
        order += [planes - 1 - step, step]
    order = order[:planes]
    for load in loads[:3]:
        load.wait()
    g_begin(0)
    for load in loads[3:5]:
        load.wait()
    u_begin(0)

    block = 256

    def lower(i, carry):
        at = pl.ds(pl.multiple_of(i * block, block), block)
        for which in range(2):
            low_ref[which, at, : 2 * LANES] = q_low_ref[
                at, which * 2 * LANES : (which + 1) * 2 * LANES
            ]
            key = own_ref[which, 0, at, :].astype(f32) + away_ref[1 - which, 0, at, :].astype(f32)
            key = key * cos_ref[at, :] - pltpu.roll(key, SPAN, 1) * sin_ref[at, :]
            low_ref[which, at, 2 * LANES : 3 * LANES] = key.astype(bf16)
            value = own_ref[which, 1, at, :].astype(f32) + away_ref[1 - which, 1, at, :].astype(f32)
            low_ref[which, at, 3 * LANES :] = value.astype(bf16)
            close_ref[which, at, :] = dot(
                low_ref[which, at, :], spread_ref[...], ((1,), (1,))
            ).astype(bf16)
        return carry

    lax.fori_loop(0, rows // block, lower, 0)

    def weight_part(which, d):
        part_ref[which, d] = dot(
            normed_ref[:, d * depth : (d + 1) * depth], close_ref[which], ((0,), (0,))
        ).astype(bf16)

    def to_neighbour(d):
        return remote(part_ref.at[1, d], x_in_ref.at[d], x_send.at[d], x_recv.at[d], across)

    loads[5].wait()
    for d in order:
        weight_part(1, d)
        to_neighbour(d).start()
    project_over().start()

    def feature_rows(start):
        at = pl.ds(pl.multiple_of(start, chunk), chunk)
        return dot(low_ref[0, at, :], wide_ref[:, :half_width], ((1,), (1,))) + dot(
            low_ref[1, at, :], wide_ref[:, half_width:], ((1,), (1,))
        )

    loads[6].wait()
    give_start = (1 - core) * half_rows
    keep_start = core * half_rows

    def to_core(i):
        return remote(give_ref.at[i], core_in_ref.at[i], core_send.at[i], core_recv.at[i], sibling)

    def to_chip(i):
        return remote(total_ref.at[keep_at(i)], chip_in_ref.at[i], chip_send.at[i], chip_recv.at[i], partner)

    def keep_at(i):
        return pl.ds(pl.multiple_of(keep_start + i * chunk, chunk), chunk)

    def give_at(i):
        return pl.ds(pl.multiple_of(give_start + i * chunk, chunk), chunk)

    def back(i):
        return remote(
            total_ref.at[keep_at(i)],
            total_ref.at[keep_at(i)],
            back_send.at[i],
            back_recv.at[i],
            sibling,
        )

    def from_core(i):
        return remote(
            total_ref.at[give_at(i)],
            total_ref.at[give_at(i)],
            back_send.at[i],
            back_recv.at[i],
            sibling,
        )

    for i in range(chunks):
        give_ref[i] = feature_rows(give_start + i * chunk).astype(bf16)
        to_core(i).start()
    for i in range(chunks):
        kept = feature_rows(keep_start + i * chunk)
        to_core(i).wait_recv()
        total_ref[keep_at(i)] = (kept + core_in_ref[i].astype(f32)).astype(bf16)
        to_chip(i).start()

    g_begin(1)
    g_relay(0)
    u_begin(1)
    u_relay(0)
    for d in order:
        weight_part(0, d)

    def add_neighbour(d):
        to_neighbour(d).wait_recv()
        part_ref[0, d] = (part_ref[0, d].astype(f32) + x_in_ref[d].astype(f32)).astype(bf16)

    q_begin, q_relay, q_finish, q_sent = line_sum(
        z, planes, lambda d: part_ref[0, pl.ds(d, 1)][0], up_ref, down_ref, up_send, up_recv, down_send, down_recv
    )

    def finish_chunk(i):
        to_chip(i).wait()
        total_ref[keep_at(i)] = (
            total_ref[keep_at(i)].astype(f32) + chip_in_ref[i].astype(f32)
        ).astype(bf16)
        back(i).start()

    def last_share():
        return remote(
            share_ref.at[0], share_ref.at[1], last_send.at[0], last_recv.at[0], across
        )

    def last_project():
        return remote(
            project_share_ref.at[0], project_share_ref.at[1], last_send.at[1], last_recv.at[1], across
        )

    def down_over():
        return remote(down_hbm, down_away_hbm, last_send.at[5], last_recv.at[5], across)

    def last_of(ref, i):
        return remote(ref.at[0], ref.at[1], last_send.at[i], last_recv.at[i], across)

    g_begin(2)
    u_begin(2)
    g_relay(1)
    finish_chunk(0)
    u_relay(1)
    for d in order:
        add_neighbour(d)
    for step in range(planes - 1):
        q_begin(step)
    down_over().start()
    project_over().wait_recv()
    for step in range(planes - 1):
        p_begin(step)
    for load in loads[7:]:
        load.wait()
    gain_sum_ref[...] = jnp.zeros_like(gain_sum_ref)
    gain_sum_ref[1:2, :] = gain_term_ref[...]
    gain = gain_ref[0:1, :].astype(f32)

    def finish_rows(start):
        at = pl.ds(pl.multiple_of(start, chunk), chunk)
        x = x_ref[at, :].astype(f32)
        factor = lax.rsqrt(jnp.mean(x * x, axis=-1, keepdims=True) + EPSILON)
        normed_in = total_ref[at, :].astype(f32)
        gain_sum_ref[0:1, :] += jnp.sum(normed_in * x * factor, axis=0, keepdims=True)
        scaled = gain * normed_in
        x_ref[at, :] = (
            grad_ref[at, :]
            + factor * scaled
            - x * (factor * factor * factor * jnp.mean(scaled * x, axis=-1, keepdims=True))
        ).astype(bf16)

    finish_rows(keep_start)
    for i in range(1, chunks):
        finish_chunk(i)
    g_finish(gate_share_ref.at[0])
    last_of(gate_share_ref, 3).start()
    u_finish(up_share_ref.at[0])
    last_of(up_share_ref, 4).start()
    q_relay(0)
    p_relay(0)
    for i in range(1, chunks):
        finish_rows(keep_start + i * chunk)
    q_relay(1)
    p_relay(1)
    for i in range(chunks):
        from_core(i).wait_recv()
        finish_rows(give_start + i * chunk)
    out_copy = pltpu.make_async_copy(x_ref, out_hbm, load_sem.at[0])
    out_copy.start()

    gain_over = remote(gain_sum_ref, gain_x_ref, gain_send.at[0], gain_recv.at[0], across)
    gain_over.start()
    p_finish(project_share_ref.at[0])
    last_project().start()
    q_finish(share_ref.at[0])
    last_share().start()
    gain_over.wait()
    gain_sum_ref[...] = gain_sum_ref[...] + gain_x_ref[...]

    def gain_to(k):
        plane = lax.rem(z + k, planes)
        return remote(
            gain_sum_ref.at[:, pl.ds(pl.multiple_of(plane * depth, depth), depth)],
            gain_z_ref.at[k],
            gain_send.at[k],
            gain_recv.at[k],
            {"fsdp": plane},
        )

    for k in range(1, planes):
        gain_to(k).start()
    gain_share_ref[...] = gain_sum_ref[:, pl.ds(pl.multiple_of(z * depth, depth), depth)]
    for k in range(1, planes):
        gain_to(k).wait_recv()
        gain_share_ref[...] += gain_z_ref[k]

    last_share().wait()
    last_project().wait()
    last_of(gate_share_ref, 3).wait()
    last_of(up_share_ref, 4).wait()
    project_over().wait_send()
    down_over().wait()
    p_sent()
    g_sent()
    u_sent()
    q_sent()
    out_copy.wait()
    for k in range(1, planes):
        gain_to(k).wait_send()
    for i in range(chunks):
        to_core(i).wait_send()
        back(i).wait_send()
    for d in range(planes):
        to_neighbour(d).wait_send()


def tail(
    down_share, gate, gate_away, gate_rest, upw, up_away, q_low, own, away, normed, wide, x, grad,
    gain_term, gains, project, spread, cosine, sine, planes,
):
    rows, width = x.shape
    depth = width // planes
    half_width = wide.shape[1] // 2
    close_width = spread.shape[0]
    chunks = 2
    chunk = rows // 2 // chunks
    bf16, f32 = jnp.bfloat16, jnp.float32
    vmem = pl.BlockSpec(memory_space=pltpu.VMEM)
    dma = pltpu.SemaphoreType.DMA
    operands = (
        down_share, gate, gate_away, gate_rest, upw, up_away, q_low, own, away, normed, wide, x, grad,
        gain_term, gains, project, spread, cosine, sine,
    )
    units = gate.shape[1]
    unit_line = pltpu.VMEM((planes - 1, depth, units), bf16)
    anywhere = pl.BlockSpec(memory_space=pl.ANY)
    line = pltpu.VMEM((planes, depth, close_width), bf16)
    short_line = pltpu.VMEM((planes - 1, depth, close_width), bf16)
    project_line = pltpu.VMEM((planes - 1, project.shape[0] // 2, depth), bf16)
    return pl.pallas_call(
        tail_kernel,
        in_specs=[anywhere] * 6 + [vmem] * 3 + [anywhere] * 4 + [vmem] * (len(operands) - 13),
        out_specs=[anywhere] + [vmem] * 5 + [anywhere],
        out_shape=[
            jax.ShapeDtypeStruct((rows, width), bf16),
            jax.ShapeDtypeStruct((2, depth, close_width), bf16),
            jax.ShapeDtypeStruct((2, project.shape[0] // 2, depth), bf16),
            jax.ShapeDtypeStruct((2, depth, units), bf16),
            jax.ShapeDtypeStruct((2, depth, units), bf16),
            jax.ShapeDtypeStruct((8, depth), f32),
            jax.ShapeDtypeStruct(down_share.shape, bf16),
        ],
        scratch_shapes=[
            pltpu.VMEM((rows, width), bf16),
            pltpu.VMEM(wide.shape, bf16),
            pltpu.VMEM((rows, width), bf16),
            pltpu.VMEM((rows, width), f32),
            pltpu.VMEM((width, units), bf16),
            pltpu.VMEM((width, units), bf16),
            pltpu.VMEM((width, units), bf16),
            pltpu.VMEM((width, units), bf16),
            pltpu.VMEM((2, rows, half_width), bf16),
            pltpu.VMEM((2, rows, close_width), bf16),
            pltpu.VMEM((2, planes, depth, close_width), bf16),
            line,
            short_line,
            short_line,
            pltpu.VMEM((project.shape[0] // 2, width), bf16),
            project_line,
            project_line,
            unit_line,
            unit_line,
            unit_line,
            unit_line,
            pltpu.VMEM((chunks, chunk, width), bf16),
            pltpu.VMEM((chunks, chunk, width), bf16),
            pltpu.VMEM((chunks, chunk, width), bf16),
            pltpu.VMEM((rows, width), bf16),
            pltpu.VMEM((8, width), f32),
            pltpu.VMEM((8, width), f32),
            pltpu.VMEM((planes, 8, depth), f32),
        ]
        + [dma((planes,))] * 18
        + [dma((chunks,))] * 6
        + [dma((6,))] * 2
        + [dma((planes,))] * 2
        + [dma((9,))],
        compiler_params=pltpu.CompilerParams(
            collective_id=2, has_side_effects=True, vmem_limit_bytes=VMEM_BYTES + (3 << 19)
        ),
        cost_estimate=pl.CostEstimate(
            flops=60_000_000_000, bytes_accessed=24_000_000, transcendentals=0
        ),
        name="tail",
    )(*operands)


def feed_kernel(
    x_hbm,
    project_hbm,
    cot_hbm,
    gain_ref,
    gate_hbm,
    up_hbm,
    down_hbm,
    total_hbm,
    gate_m_hbm,
    gate_away_hbm,
    gate_rest_hbm,
    up_m_hbm,
    up_o_hbm,
    down_grad_hbm,
    down_rows_hbm,
    x_ref,
    project_ref,
    cot_ref,
    gate_ref,
    up_ref,
    down_ref,
    total_ref,
    grad_ref,
    down_grad_ref,
    down_rows_ref,
    gate_o_ref,
    normed_ref,
    turned_ref,
    hidden_ref,
    gate_back_ref,
    up_back_ref,
    give_ref,
    core_in_ref,
    keep_ref,
    chip_in_ref,
    load_sem,
    store_sem,
    core_send,
    core_recv,
    chip_send,
    chip_recv,
    back_send,
    back_recv,
    x_send,
    x_recv,
    over_send,
    over_recv,
):
    bf16, f32 = jnp.bfloat16, jnp.float32
    rows, width = x_ref.shape
    half_rows = rows // 2
    chunks, chunk, _ = give_ref.shape
    units = gate_ref.shape[2]
    c = lax.axis_index("ctx")
    t = lax.axis_index("tp")
    core = lax.rem(t, 2)
    across = {"ctx": 1 - c}
    sibling = {"tp": t + 1 - 2 * core}
    partner = {"tp": lax.rem(t + 2, 4)}

    loads = [
        pltpu.make_async_copy(src, dst, load_sem.at[i])
        for i, (src, dst) in enumerate(
            (
                (x_hbm, x_ref),
                (project_hbm, project_ref),
                (gate_hbm, gate_ref),
                (up_hbm, up_ref),
                (cot_hbm, cot_ref),
                (down_hbm, down_ref),
            )
        )
    ]
    for load in loads:
        load.start()

    barrier = pltpu.get_barrier_semaphore()
    for device in (across, sibling, partner):
        pl.semaphore_signal(barrier, inc=1, device_id=device, device_id_type=MESH)
    pl.semaphore_wait(barrier, 3)

    def remote(src, dst, send, recv, device):
        return pltpu.make_async_remote_copy(
            src_ref=src,
            dst_ref=dst,
            send_sem=send,
            recv_sem=recv,
            device_id=device,
            device_id_type=MESH,
        )

    give_start = (1 - core) * half_rows
    keep_start = core * half_rows
    gain = gain_ref[1:2, :].astype(f32)

    def feature_rows(start, first):
        at = pl.ds(pl.multiple_of(start, chunk), chunk)
        if first:
            loads[0].wait()
            loads[1].wait()
        middle = x_ref[at, :].astype(f32) + project_ref[at, :].astype(f32)
        factor = lax.rsqrt(jnp.mean(middle * middle, axis=-1, keepdims=True) + EPSILON)
        normed = (middle * factor * gain).astype(bf16)
        normed_ref[...] = normed
        turned_ref[:, at] = normed.T
        if first:
            for load in loads[2:]:
                load.wait()
        for which in range(2):
            cols = slice(which * units, (which + 1) * units)
            gate = dot(normed_ref[...], gate_ref[which], ((1,), (0,)))
            up = dot(normed_ref[...], up_ref[which], ((1,), (0,)))
            hidden_in = dot(cot_ref[at, :], down_ref[which], ((1,), (1,)))
            sigmoid = jax.nn.sigmoid(gate)
            silu = gate * sigmoid
            hidden_ref[at, cols] = (silu * up).astype(bf16)
            gate_back_ref[at, cols] = (
                hidden_in * up * sigmoid * (1.0 + gate * (1.0 - sigmoid))
            ).astype(bf16)
            up_back_ref[at, cols] = (hidden_in * silu).astype(bf16)
        return sum(
            dot(back_ref[at, which * units : (which + 1) * units], weight[which], ((1,), (1,)))
            for which in range(2)
            for back_ref, weight in ((gate_back_ref, gate_ref), (up_back_ref, up_ref))
        )

    def to_core(i):
        return remote(give_ref.at[i], core_in_ref.at[i], core_send.at[i], core_recv.at[i], sibling)

    def to_chip(i):
        return remote(keep_ref.at[i], chip_in_ref.at[i], chip_send.at[i], chip_recv.at[i], partner)

    def back(i, start):
        at = pl.ds(pl.multiple_of(start + i * chunk, chunk), chunk)
        return remote(
            total_ref.at[at], total_ref.at[at], back_send.at[i], back_recv.at[i], sibling
        )

    for i in range(chunks):
        give_ref[i] = feature_rows(give_start + i * chunk, i == 0).astype(bf16)
        to_core(i).start()
        kept = feature_rows(keep_start + i * chunk, False)
        to_core(i).wait_recv()
        keep_ref[i] = (kept + core_in_ref[i].astype(f32)).astype(bf16)
        to_chip(i).start()

    block = 256

    def weight_rows(back_ref, which, out_ref, begin, count, block=256):
        def some(i, carry):
            at = pl.ds(pl.multiple_of(i * block, block), block)
            out_ref[at, :] = dot(
                turned_ref[at, :], back_ref[:, which * units : (which + 1) * units], ((1,), (0,))
            ).astype(bf16)
            return carry

        lax.fori_loop(begin // block, (begin + count) // block, some, 0)

    def finish_chunk(i):
        to_chip(i).wait()
        at = pl.ds(pl.multiple_of(keep_start + i * chunk, chunk), chunk)
        total_ref[at, :] = (keep_ref[i].astype(f32) + chip_in_ref[i].astype(f32)).astype(bf16)
        back(i, keep_start).start()

    planes, _, depth = down_grad_ref.shape
    pieces = gate_away_hbm.shape[0] // depth

    def over(i):
        at = pl.ds(i * depth, depth)
        return remote(gate_o_ref.at[at], gate_away_hbm.at[at], x_send.at[i], x_recv.at[i], across)

    def down_over(i):
        at = pl.ds(pl.multiple_of(give_start + i * chunk, chunk), chunk)
        return remote(
            down_rows_ref.at[at], core_in_ref.at[i], over_send.at[i], over_recv.at[i], sibling
        )

    stores = []

    def store(src, dst):
        copy = pltpu.make_async_copy(src, dst, store_sem.at[len(stores)])
        copy.start()
        stores.append(copy)

    for i in range(pieces):
        weight_rows(gate_back_ref, 1, gate_o_ref, i * depth, depth, depth)
        over(i).start()
    weight_rows(gate_back_ref, 1, gate_o_ref, pieces * depth, width - pieces * depth, depth)
    store(gate_o_ref.at[pl.ds(pieces * depth, width - pieces * depth)], gate_rest_hbm)
    weight_rows(up_back_ref, 1, grad_ref.at[0], 0, width)
    store(grad_ref.at[0], up_o_hbm)
    for i in range(chunks // 2):
        finish_chunk(i)
    weight_rows(gate_back_ref, 0, grad_ref.at[1], 0, width)
    store(grad_ref.at[1], gate_m_hbm)
    weight_rows(up_back_ref, 0, grad_ref.at[2], 0, width)
    store(grad_ref.at[2], up_m_hbm)

    def down_grads(i, carry):
        at = pl.ds(pl.multiple_of(i * block, block), block)
        part = dot(hidden_ref[:, at], cot_ref[...], ((0,), (0,))).astype(bf16)
        planes, _, depth = down_grad_ref.shape
        for d in range(planes):
            down_grad_ref[d, at, :] = part[:, d * depth : (d + 1) * depth]
        return carry

    lax.fori_loop(0, 2 * units // block, down_grads, 0)
    store(down_grad_ref, down_grad_hbm)

    def down_features(i, carry):
        at = pl.ds(pl.multiple_of(i * block, block), block)
        down_rows_ref[at, :] = (
            dot(hidden_ref[at, :units], down_ref[0], ((1,), (0,)))
            + dot(hidden_ref[at, units:], down_ref[1], ((1,), (0,)))
        ).astype(bf16)
        return carry

    lax.fori_loop(0, rows // block, down_features, 0)
    for i in range(chunks // 2):
        back(i, give_start).wait_recv()
    for i in range(chunks):
        down_over(i).start()
    for i in range(chunks):
        to_core(i).wait_send()
        down_over(i).wait()
        at = pl.ds(pl.multiple_of(keep_start + i * chunk, chunk), chunk)
        give_ref[i] = (down_rows_ref[at, :].astype(f32) + core_in_ref[i].astype(f32)).astype(bf16)
    store(give_ref, down_rows_hbm)
    for i in range(chunks // 2, chunks):
        finish_chunk(i)
    for i in range(chunks // 2, chunks):
        back(i, give_start).wait_recv()
    store(total_ref, total_hbm)
    for i in range(chunks):
        back(i, keep_start).wait_send()
    for i in range(pieces):
        over(i).wait()
    for copy in stores:
        copy.wait()


def feed(x, project_sum, cot, gains, gate_w, up_w, down_w, planes):
    rows, width = x.shape
    units = gate_w.shape[2]
    chunk = 256
    chunks = rows // 2 // chunk
    depth = width // planes
    sent = 3 * depth
    bf16 = jnp.bfloat16
    vmem = pl.BlockSpec(memory_space=pltpu.VMEM)
    anywhere = pl.BlockSpec(memory_space=pl.ANY)
    dma = pltpu.SemaphoreType.DMA
    operands = (x, project_sum, cot, gains, gate_w, up_w, down_w)
    piece = pltpu.VMEM((chunks, chunk, width), bf16)
    rows_by_width = pltpu.VMEM((rows, width), bf16)
    rows_by_units = pltpu.VMEM((rows, 2 * units), bf16)
    weight = jax.ShapeDtypeStruct((width, units), bf16)
    return pl.pallas_call(
        feed_kernel,
        in_specs=[anywhere] * 3 + [vmem] + [anywhere] * 3,
        out_specs=[anywhere] * 8,
        out_shape=[
            jax.ShapeDtypeStruct((rows, width), bf16),
            weight,
            jax.ShapeDtypeStruct((sent, units), bf16),
            jax.ShapeDtypeStruct((width - sent, units), bf16),
            weight,
            weight,
            jax.ShapeDtypeStruct((planes, 2 * units, width // planes), bf16),
            jax.ShapeDtypeStruct((chunks, chunk, width), bf16),
        ],
        scratch_shapes=[
            rows_by_width,
            rows_by_width,
            rows_by_width,
            pltpu.VMEM(gate_w.shape, bf16),
            pltpu.VMEM(up_w.shape, bf16),
            pltpu.VMEM(down_w.shape, bf16),
            rows_by_width,
            pltpu.VMEM((3, width, units), bf16),
            pltpu.VMEM((planes, 2 * units, width // planes), bf16),
            rows_by_width,
            pltpu.VMEM((width, units), bf16),
            pltpu.VMEM((chunk, width), bf16),
            pltpu.VMEM((width, rows), bf16),
            rows_by_units,
            rows_by_units,
            rows_by_units,
            piece,
            piece,
            piece,
            piece,
            dma((6,)),
            dma((7,)),
        ]
        + [dma((chunks,))] * 6
        + [dma((sent // depth,))] * 2
        + [dma((chunks,))] * 2,
        compiler_params=pltpu.CompilerParams(
            collective_id=3, has_side_effects=True, vmem_limit_bytes=VMEM_BYTES
        ),
        cost_estimate=pl.CostEstimate(
            flops=50_000_000_000, bytes_accessed=40_000_000, transcendentals=0
        ),
        name="feed",
    )(*operands)


def add_kernel(first_ref, a_ref, b_ref, out_ref):
    out_ref[...] = (a_ref[...].astype(jnp.float32) + b_ref[...].astype(jnp.float32)).astype(
        out_ref.dtype
    )


def add_after(first, a, b):
    rows, width = a.shape
    tile = 256
    spec = pl.BlockSpec((tile, width), lambda i: (i, 0))
    return pl.pallas_call(
        add_kernel,
        grid=(rows // tile,),
        in_specs=[pl.BlockSpec(memory_space=pl.ANY), spec, spec],
        out_specs=spec,
        out_shape=jax.ShapeDtypeStruct(a.shape, a.dtype),
        name="add_after",
    )(first, a, b)


def paired_body(
    tokens,
    prefix_len,
    positions,
    gain_attend,
    w_query,
    w_key,
    w_value,
    w_project,
    gain_feed,
    w_gate,
    w_up,
    w_down,
    cotangent,
):
    seqs, rows, width = tokens.shape
    assert seqs == 1
    c = lax.axis_index("ctx")
    bf16, f32 = jnp.bfloat16, jnp.float32

    def half(array, axis, which=None):
        size = array.shape[axis] // 2
        which = c if which is None else which
        return lax.dynamic_slice_in_dim(array, which * size, size, axis)

    def ordered(mine, other, axis):
        return jnp.where(
            c == 0,
            jnp.concatenate([mine, other], axis=axis),
            jnp.concatenate([other, mine], axis=axis),
        )

    planes = lax.axis_size("fsdp")
    kv_half = w_key.shape[1] // 2
    q_half = w_query.shape[1] // 2

    def packed(which):
        return jnp.concatenate(
            [half(w_query, 1, which), half(w_key, 1, which), half(w_value, 1, which)], axis=1
        )

    gain_rows = jnp.pad(jnp.stack([gain_attend, gain_feed]), ((0, GAIN_ROWS - 2), (0, 0)))
    pack = jnp.concatenate([packed(c), gain_rows], axis=0)

    def parts(block):
        return (
            block[:, :q_half],
            block[:, q_half : q_half + kv_half],
            block[:, q_half + kv_half :],
        )

    half_heads = (q_half + 2 * kv_half) // HD
    spread = np.zeros((half_heads * HD, half_heads * LANES), np.float32)
    for head in range(half_heads):
        for lane in range(HD):
            turned = lane if lane < HALF or head == half_heads - 1 else lane - HALF + SPAN
            spread[head * HD + lane, head * LANES + turned] = 1.0
    spread = jnp.asarray(spread, bf16)

    frequency = ROPE_BASE ** (-(jnp.arange(HALF, dtype=f32) * 2.0 / HD))
    frequency = jnp.pad(frequency, (0, SPAN - HALF))
    angles = positions[0].astype(f32)[:, None] * frequency
    cosine = jnp.cos(angles)
    sine = jnp.sin(angles)
    cosine = jnp.concatenate([cosine, cosine], axis=1)
    sine = jnp.concatenate([-sine, sine], axis=1)

    block_len = rows // 2
    tile = min(256, block_len)
    query_tiles = rows // tile
    own = c * rows + tile * jnp.arange(query_tiles, dtype=jnp.int32)
    opposite = (1 - c) * rows + tile * jnp.arange(query_tiles, dtype=jnp.int32)
    own, opposite = natural_index(own, block_len, 2), natural_index(opposite, block_len, 2)
    meta = jnp.concatenate([prefix_len.astype(jnp.int32), own, own, opposite])

    x = tokens[0]
    cot = cotangent[0]
    (
        normed, q, kv_all, w_qkv, w_p, gains, o, lse, project_sum, wg, wu, wd,
    ) = front(
        prefix_len, x, pack, packed(1 - c), spread, cosine, sine,
        w_project.reshape(-1, HD, w_project.shape[1]), w_gate, w_up, w_down, planes,
    )
    w_p = w_p.reshape(-1, width)
    (
        feed_sum, gate_mine, gate_away, gate_rest, up_mine, up_other, down_part, down_rows,
    ) = feed(x, project_sum, cot, gains, wg, wu, wd, planes)

    gate_rest, up_away = swap_ctx(gate_rest), swap_ctx(up_other)
    down_share = lax.psum_scatter(down_part, "fsdp", scatter_dimension=0, tiled=False)
    middle_grad, d_out, project_part, gain_two_term = middle_back(
        x, project_sum, feed_sum, cot, gains, o, w_p
    )
    down_rows = down_rows.reshape(rows // 2, width)
    down_away = swap_chip(down_rows)
    dq_away, d_kv_away = attend_back(
        meta, None, d_out, d_out, q, kv_all, True, o, d_out, lse, cosine, sine, tile
    )
    d_kv_away = swap_ctx(d_kv_away)
    down_total = add_after(dq_away, down_rows, down_away)
    down_sum = by_core(down_total, swap_core(down_total))
    layer_output = (
        x.astype(f32) + project_sum.astype(f32) + down_sum.astype(f32)
    ).astype(bf16)
    q_low, d_kv_own = attend_back(
        meta, dq_away, gate_rest, up_away, q, kv_all, False, o, d_out, lse, cosine, sine, tile
    )
    tokens_grad, share, project_share, gate_share, up_share, gain_share, down_other_share = tail(
        down_share, gate_mine, gate_away, gate_rest, up_mine, up_away, q_low, d_kv_own, d_kv_away, normed, w_qkv, x, middle_grad,
        gain_two_term, gains, project_part, spread, cosine, sine, planes,
    )
    size = down_share.shape[0] // 2
    down_mine = down_share[:size].astype(f32) + down_other_share[size:].astype(f32)
    down_other = down_share[size:].astype(f32) + down_other_share[:size].astype(f32)
    down_grad = ordered(down_mine, down_other, 0)
    shares = [
        ordered(a, b, 1).astype(f32) for a, b in zip(parts(share[0]), parts(share[1]))
    ]
    return (
        layer_output[None],
        tokens_grad[None],
        gain_share[0],
        shares[0],
        shares[1],
        shares[2],
        ordered(project_share[0], project_share[1], 0).astype(f32),
        gain_share[1],
        ordered(gate_share[0], gate_share[1], 1).astype(f32),
        ordered(up_share[0], up_share[1], 1).astype(f32),
        down_grad,
    )


def solution(mesh):
    paired = mesh.shape["ctx"] == 2 and mesh.shape["tp"] == 4 and mesh.shape["fsdp"] == 4
    return jax.shard_map(
        paired_body if paired else general_body,
        mesh=mesh,
        in_specs=(
            P("fsdp", "ctx", None),
            P("fsdp"),
            P("fsdp", "ctx"),
            P("fsdp"),
            P("fsdp", "tp"),
            P("fsdp", "tp"),
            P("fsdp", "tp"),
            P("tp", "fsdp"),
            P("fsdp"),
            P("fsdp", "tp"),
            P("fsdp", "tp"),
            P("tp", "fsdp"),
            P("fsdp", "ctx", None),
        ),
        out_specs=(
            P("fsdp", "ctx", None),
            P("fsdp", "ctx", None),
            P("fsdp"),
            P("fsdp", "tp"),
            P("fsdp", "tp"),
            P("fsdp", "tp"),
            P("tp", "fsdp"),
            P("fsdp"),
            P("fsdp", "tp"),
            P("fsdp", "tp"),
            P("tp", "fsdp"),
        ),
        check_vma=False,
    )
```
